32 devices in a mesh: dp: 16 (over z, y, core), tensor: 2 (over x).
Axes of the slice: x: 2, y: 2, z: 4, core: 2. Of those that a mesh axis runs over, the one named last changes fastest.
Arguments:
- block_input: float32 [2, 16, 1024, 1152], P(None, 'dp', 'tensor'), may hold values from -6 to 6
- image_ids: int32 [2, 16, 1024], P(None, 'dp', 'tensor'), may hold values from 0 to 7, as said below
- out_cotangent: float32 [2, 16, 1024, 1152], P(None, 'dp', 'tensor'), may hold values from -15 to 15
- qkv_master: float32 [1152, 3, 1152], P('dp', None, 'tensor'), may hold values from -0.1875 to 0.1875
- qkv_moment: bfloat16 [1152, 3, 1152], P('dp', None, 'tensor'), may hold values from -72 to 72
- qkv_second: float32 [1152, 3, 1152], P('dp', None, 'tensor'), may hold values from 1114.112 to 4423.68
- out_master: float32 [1152, 1152], P('tensor', 'dp'), may hold values from -0.625 to 0.625
- out_moment: bfloat16 [1152, 1152], P('tensor', 'dp'), may hold values from -27.125 to 27.125
- out_second: float32 [1152, 1152], P('tensor', 'dp'), may hold values from 154.0096 to 622.592
- up_master: float32 [1152, 4304], P('dp', 'tensor'), may hold values from -0.1875 to 0.1875
- up_moment: bfloat16 [1152, 4304], P('dp', 'tensor'), may hold values from -90.5 to 90.5
- up_second: float32 [1152, 4304], P('dp', 'tensor'), may hold values from 1736.704 to 6881.28
- down_master: float32 [4304, 1152], P('tensor', 'dp'), may hold values from -0.09375 to 0.09375
- down_moment: bfloat16 [4304, 1152], P('tensor', 'dp'), may hold values from -81 to 81
- down_second: float32 [4304, 1152], P('tensor', 'dp'), may hold values from 1409.024 to 5570.56
- vec_master: float32 [6, 1152], replicated, may hold values from -1 to 1.45, as said below
- vec_moment: bfloat16 [6, 1152], replicated, may hold values from -181 to 181
- vec_second: float32 [6, 1152], replicated, may hold values from 6881.28 to 27525.12
- bias_master: float32 [2, 3304], P('tensor'), may hold values from -1 to 1
- bias_moment: bfloat16 [2, 3304], P('tensor'), may hold values from -90.5 to 90.5
- bias_second: float32 [2, 3304], P('tensor'), may hold values from 1736.704 to 6881.28
Outputs:
- block_output: float32 [2, 16, 1024, 1152], P(None, 'dp', 'tensor')
- input_grad: float32 [2, 16, 1024, 1152], P(None, 'dp', 'tensor')
- qkv_grad: float32 [1152, 3, 1152], P('dp', None, 'tensor')
- qkv_second_new: float32 [1152, 3, 1152], P('dp', None, 'tensor')
- qkv_master_new: float32 [1152, 3, 1152], P('dp', None, 'tensor')
- out_grad: float32 [1152, 1152], P('tensor', 'dp')
- out_second_new: float32 [1152, 1152], P('tensor', 'dp')
- out_master_new: float32 [1152, 1152], P('tensor', 'dp')
- up_grad: float32 [1152, 4304], P('dp', 'tensor')
- up_second_new: float32 [1152, 4304], P('dp', 'tensor')
- up_master_new: float32 [1152, 4304], P('dp', 'tensor')
- down_grad: float32 [4304, 1152], P('tensor', 'dp')
- down_second_new: float32 [4304, 1152], P('tensor', 'dp')
- down_master_new: float32 [4304, 1152], P('tensor', 'dp')
- vec_grad: float32 [6, 1152], replicated
- vec_second_new: float32 [6, 1152], replicated
- vec_master_new: float32 [6, 1152], replicated
- bias_grad: float32 [2, 3304], P('tensor')
- bias_second_new: float32 [2, 3304], P('tensor')
- bias_master_new: float32 [2, 3304], P('tensor')
The draws below stay inside these ranges and needn't reach their ends.
Inputs may be any that keep to these rules, and one draw needn't show every extreme that they name: `image_ids`: within each row the ids never fall, and each of the 8 images has at least one token. `vec_master`: rows 0 and 3 are gains, the others biases.
All inputs are finite; a program needn't handle non-finite values.
Results may differ from the reference program's by a relative error of at most 0.022.
Values may be sent and summed in bfloat16 or wider, within the bound.
No kernel may reach another device: no remote copies, remote signals or barrier semaphores. Data moves between devices by JAX's collectives and lax.ppermute only.
A program may use at most 256 MiB of HBM per device.

```python
import math
import jax
import jax.numpy as jnp
from jax import lax

D = 1152
HEADS = 16
HEAD = 72
FF = 4304
MB = 2
IMGS = 8
STEP = 10
HH = 1152
ROW = 1024
SEQS = 16
TOKENS = 32768
SPLIT = 2
BG = 3304
JIT = 32


def draw_image_ids(key, part):
    key = jax.random.fold_in(key, 5)
    jitter = jax.random.randint(key, (MB, SEQS, IMGS - 1), -JIT, JIT + 1)
    boundaries = (jnp.arange(1, IMGS, dtype=jnp.int32) * (ROW // IMGS))[None, None, :] + jitter
    places = jnp.arange(ROW, dtype=jnp.int32)
    passed = (places[None, None, :, None] >= boundaries[:, :, None, :]).astype(jnp.int32)
    return jnp.sum(passed, -1).astype(jnp.int32)


def draw_out_cotangent(key, part):
    key = jax.random.fold_in(key, 7)
    along_seq = jnp.arange(SEQS, dtype=jnp.float32) / max(SEQS - 1, 1)
    along_row = jnp.arange(ROW, dtype=jnp.float32) / max(ROW - 1, 1)
    random_part = jnp.clip(jax.random.normal(key, (MB, SEQS, ROW, D), jnp.float32), -5.0, 5.0)
    growth = (1.0 + 2.0 * along_seq)[None, :, None, None] * (1.0 + 2.0 * along_row)[None, None, :, None] / 3.0
    return random_part * growth


def draw_vec_master(key, part):
    key = jax.random.fold_in(key, 11)
    random_rows = jnp.clip(jax.random.normal(key, (6, D), jnp.float32), -3.0, 3.0)
    row_index = jnp.arange(6)[:, None]
    gain_rows = (row_index == 0) | (row_index == 3)
    return jnp.where(gain_rows, 1.0 + 0.15 * random_rows, 0.2 * jnp.clip(random_rows, -5.0, 5.0))


def level_of(rng, dims, pieces, smallest, largest):
    factor_of, own = 1.0, jax.random.fold_in(rng, 6)
    for axis_at, parts in pieces:
        steps = jnp.exp(jax.random.uniform(jax.random.fold_in(own, axis_at), (parts,), jnp.float32, smallest / len(pieces), largest / len(pieces)))
        factor_of = factor_of * jnp.repeat(steps, dims[axis_at] // parts).reshape([-1 if axis == axis_at else 1 for axis in range(len(dims))])
    return factor_of


def gaussian(stream_key, shape, width, limit, pieces=(), kind=jnp.bfloat16):
    entries = width * jax.random.normal(stream_key, shape, jnp.float32)
    if pieces:
        entries = entries * level_of(stream_key, shape, pieces, -0.22, 0.18)
    return jnp.clip(entries, -limit, limit).astype(kind)


def setup_inputs(seed: int = 0) -> dict:
    arg_keys = jax.random.split(jax.random.key(seed), 22)
    block_input = gaussian(arg_keys[0], (MB, SEQS, ROW, D), 1.0, 6.0, ((1, 16), (2, 2)), jnp.float32)
    image_ids = draw_image_ids(jax.random.fold_in(arg_keys[21], 71), 0)
    out_cotangent = draw_out_cotangent(jax.random.fold_in(arg_keys[21], 71), 0)
    qkv_master = gaussian(arg_keys[3], (D, 3, HH), D ** -0.5, 0.1875, ((0, 16), (2, 2)), jnp.float32)
    qkv_moment = gaussian(arg_keys[4], (D, 3, HH), (0.089 * TOKENS ** 0.5), 72.0, ((0, 16), (2, 2)))
    qkv_second = jnp.clip(jnp.exp(math.log(4423.68) - 1.3789142 * jax.random.uniform(arg_keys[5], (D, 3, HH), jnp.float32) ** level_of(arg_keys[5], (D, 3, HH), ((0, 16), (2, 2)), -0.2, 0.2)), 1114.112, 4423.68)
    out_master = gaussian(arg_keys[6], (HH, D), (HH * 2 * (3 * IMGS + ROW // 100) // ROW) ** -0.5, 0.625, ((0, 2), (1, 16)), jnp.float32)
    out_moment = gaussian(arg_keys[7], (HH, D), (0.033 * TOKENS ** 0.5), 27.125, ((0, 2), (1, 16)))
    out_second = jnp.clip(jnp.exp(math.log(622.592) - 1.3968765 * jax.random.uniform(arg_keys[8], (HH, D), jnp.float32) ** level_of(arg_keys[8], (HH, D), ((0, 2), (1, 16)), -0.2, 0.2)), 154.0096, 622.592)
    up_master = gaussian(arg_keys[9], (D, FF), D ** -0.5, 0.1875, ((0, 16), (1, 2)), jnp.float32)
    up_moment = gaussian(arg_keys[10], (D, FF), (0.111 * TOKENS ** 0.5), 90.5, ((0, 16), (1, 2)))
    up_second = jnp.clip(jnp.exp(math.log(6881.28) - 1.3768156 * jax.random.uniform(arg_keys[11], (D, FF), jnp.float32) ** level_of(arg_keys[11], (D, FF), ((0, 16), (1, 2)), -0.2, 0.2)), 1736.704, 6881.28)
    down_master = gaussian(arg_keys[12], (FF, D), FF ** -0.5, 0.09375, ((0, 2), (1, 16)), jnp.float32)
    down_moment = gaussian(arg_keys[13], (FF, D), (0.1 * TOKENS ** 0.5), 81.0, ((0, 2), (1, 16)))
    down_second = jnp.clip(jnp.exp(math.log(5570.56) - 1.3745983 * jax.random.uniform(arg_keys[14], (FF, D), jnp.float32) ** level_of(arg_keys[14], (FF, D), ((0, 2), (1, 16)), -0.2, 0.2)), 1409.024, 5570.56)
    vec_master = draw_vec_master(jax.random.fold_in(arg_keys[21], 71), 0)
    vec_moment = gaussian(arg_keys[16], (6, D), (0.22 * TOKENS ** 0.5), 181.0)
    vec_second = jnp.clip(jnp.exp(jax.random.uniform(arg_keys[17], (6, D), jnp.float32, math.log(6881.28), math.log(27525.12))), 6881.28, 27525.12)
    bias_master = gaussian(arg_keys[18], (SPLIT, BG), 0.2, 1.0, ((0, 2),), jnp.float32)
    bias_moment = gaussian(arg_keys[19], (SPLIT, BG), (0.111 * TOKENS ** 0.5), 90.5, ((0, 2),))
    bias_second = jnp.clip(jnp.exp(math.log(6881.28) - 1.3768156 * jax.random.uniform(arg_keys[20], (SPLIT, BG), jnp.float32) ** level_of(arg_keys[20], (SPLIT, BG), ((0, 2),), -0.2, 0.2)), 1736.704, 6881.28)
    return {"block_input": block_input, "image_ids": image_ids, "out_cotangent": out_cotangent, "qkv_master": qkv_master, "qkv_moment": qkv_moment, "qkv_second": qkv_second, "out_master": out_master, "out_moment": out_moment, "out_second": out_second, "up_master": up_master, "up_moment": up_moment, "up_second": up_second, "down_master": down_master, "down_moment": down_moment, "down_second": down_second, "vec_master": vec_master, "vec_moment": vec_moment, "vec_second": vec_second, "bias_master": bias_master, "bias_moment": bias_moment, "bias_second": bias_second}


norm_eps = 1e-06
mask_fill = -1e+30
highest = lax.Precision.HIGHEST
beta_one = 0.9
beta_two = 0.95
adam_eps = 1e-08

@jax.custom_vjp
def low(v):
    return lax.optimization_barrier(v.astype(jnp.bfloat16)).astype(jnp.float32)

@jax.custom_vjp
def low_back(v):
    return v

def low_keep(v):
    return (low(v), None)

def low_pass(kept, grad):
    return (grad,)

def back_keep(v):
    return (v, None)

def back_low(kept, grad):
    return (low(grad),)
low.defvjp(low_keep, low_pass)
low_back.defvjp(back_keep, back_low)

def layer_norm(values, scale_vec, shift_vec):
    centre = values - lax.optimization_barrier(jnp.mean(values, -1, keepdims=True))
    spread = lax.optimization_barrier(jnp.mean(centre * centre, -1, keepdims=True))
    return centre * lax.rsqrt(spread + norm_eps) * scale_vec + shift_vec

def rounded(values):
    return low_back(low(values))

def sequence_forward(inputs, image_row, qkv_weight, out_weight, up_weight, down_weight, vectors, biases):
    groups = biases.shape[0]
    length = inputs.shape[0]
    features = inputs.shape[1]
    head_cols = qkv_weight.shape[2] // groups
    hidden_cols = up_weight.shape[1] // groups
    group_heads = HEADS // groups
    normed = low(layer_norm(inputs, vectors[0], vectors[1]))
    shared = low_back(jnp.broadcast_to(normed, (groups, length, features)))
    projected = jnp.einsum('gtd,dcge->cgte', shared, qkv_weight.reshape(features, 3, groups, head_cols), precision=highest)
    queries = rounded(projected[0] + biases[:, None, :head_cols])
    key_rows = rounded(projected[1])
    values = rounded(projected[2] + biases[:, None, head_cols:2 * head_cols])

    def to_heads(grouped):
        return grouped.reshape(groups, length, group_heads, HEAD).transpose(0, 2, 1, 3).reshape(HEADS, length, HEAD)
    query_heads = to_heads(queries)
    key_heads = to_heads(key_rows)
    value_heads = to_heads(values)
    block_rows = min(512, length)
    block_count = length // block_rows
    query_blocks = query_heads.reshape(HEADS, block_count, block_rows, HEAD).transpose(1, 0, 2, 3)
    image_blocks = image_row.reshape(block_count, block_rows)
    score_scale = HEAD ** (-0.5)

    def attend(block_pair):
        query_block, image_block = block_pair
        scores = low_back(jnp.einsum('hqe,hke->hqk', query_block, key_heads, precision=highest) * score_scale)
        same_image = image_block[:, None] == image_row[None, :]
        scores = jnp.where(same_image[None], scores, mask_fill)
        row_max = lax.optimization_barrier(jnp.max(scores, -1, keepdims=True))
        exp_scores = jnp.exp(scores - row_max)
        attn_probs = exp_scores / lax.optimization_barrier(jnp.sum(exp_scores, -1, keepdims=True))
        return jnp.einsum('hqk,hke->hqe', low(attn_probs), value_heads, precision=highest)
    attended_blocks = lax.map(jax.checkpoint(attend), (query_blocks, image_blocks))
    attended = attended_blocks.transpose(1, 0, 2, 3).reshape(HEADS, length, HEAD)
    grouped = rounded(attended.reshape(groups, group_heads, length, HEAD).transpose(0, 2, 1, 3).reshape(groups, length, head_cols))
    out_parts = rounded(jnp.einsum('gte,ged->gtd', grouped, out_weight.reshape(groups, head_cols, features), precision=highest))
    middle = inputs + lax.optimization_barrier(jnp.sum(out_parts, 0)) + vectors[2]
    normed_two = low(layer_norm(middle, vectors[3], vectors[4]))
    shared_two = low_back(jnp.broadcast_to(normed_two, (groups, length, features)))
    hidden = low_back(jnp.einsum('gtd,dgf->gtf', shared_two, up_weight.reshape(features, groups, hidden_cols), precision=highest) + biases[:, None, 2 * head_cols:])
    active = low(jax.nn.gelu(hidden, approximate=True))
    down_parts = rounded(jnp.einsum('gtf,gfd->gtd', active, down_weight.reshape(groups, hidden_cols, features), precision=highest))
    return middle + lax.optimization_barrier(jnp.sum(down_parts, 0)) + vectors[5]

def adam_update(master, moment, second, gradient, step_rate, weight_decay):
    first_moment = beta_one * moment.astype(jnp.float32) + (1.0 - beta_one) * gradient
    second_new = beta_two * second + (1.0 - beta_two) * gradient * gradient
    update = first_moment / (1.0 - beta_one ** STEP) / (jnp.sqrt(second_new / (1.0 - beta_two ** STEP)) + adam_eps) + weight_decay * master
    return (second_new, master - step_rate * update)

def reference(block_input, image_ids, out_cotangent, qkv_master, qkv_moment, qkv_second, out_master, out_moment, out_second, up_master, up_moment, up_second, down_master, down_moment, down_second, vec_master, vec_moment, vec_second, bias_master, bias_moment, bias_second):
    qkv_weight = low(qkv_master)
    out_weight = low(out_master)
    up_weight = low(up_master)
    down_weight = low(down_master)
    flat_inputs = block_input.reshape(MB * SEQS, ROW, D)
    flat_images = image_ids.reshape(MB * SEQS, ROW)
    flat_cotangents = out_cotangent.reshape(MB * SEQS, ROW, D)

    def one_sequence(totals, seq_item):
        inputs, image_row, cotangent = seq_item

        def forward(values, qkv_w, out_w, up_w, down_w, vectors, biases):
            return sequence_forward(values, image_row, qkv_w, out_w, up_w, down_w, vectors, biases)
        output, pull_back = jax.vjp(forward, inputs, qkv_weight, out_weight, up_weight, down_weight, vec_master, bias_master)
        gradients = pull_back(cotangent)
        summed = tuple((total + gradient for total, gradient in zip(totals, gradients[1:])))
        return (summed, (output, gradients[0]))
    zero_sums = tuple((jnp.zeros_like(array) for array in (qkv_weight, out_weight, up_weight, down_weight, vec_master, bias_master)))
    totals, (outputs, input_grads) = lax.scan(one_sequence, zero_sums, (flat_inputs, flat_images, flat_cotangents))
    qkv_grad, out_grad, up_grad, down_grad, vec_grad, bias_grad = totals
    qkv_second_new, qkv_master_new = adam_update(qkv_master, qkv_moment, qkv_second, qkv_grad, 0.09, 0.1)
    out_second_new, out_master_new = adam_update(out_master, out_moment, out_second, out_grad, 0.4, 0.1)
    up_second_new, up_master_new = adam_update(up_master, up_moment, up_second, up_grad, 0.09, 0.1)
    down_second_new, down_master_new = adam_update(down_master, down_moment, down_second, down_grad, 0.045, 0.1)
    vec_second_new, vec_master_new = adam_update(vec_master, vec_moment, vec_second, vec_grad, 0.6, 0.0)
    bias_second_new, bias_master_new = adam_update(bias_master, bias_moment, bias_second, bias_grad, 0.5, 0.0)
    return (outputs.reshape(MB, SEQS, ROW, D), input_grads.reshape(MB, SEQS, ROW, D), qkv_grad, qkv_second_new, qkv_master_new, out_grad, out_second_new, out_master_new, up_grad, up_second_new, up_master_new, down_grad, down_second_new, down_master_new, vec_grad, vec_second_new, vec_master_new, bias_grad, bias_second_new, bias_master_new)
```

```python
import math
from functools import partial

import jax
import jax.numpy as jnp
from jax import lax
from jax.experimental import pallas as pl
from jax.experimental.pallas import tpu as pltpu
from jax.sharding import PartitionSpec as P

HEAD = 72
STEP = 10


norm_eps = 1e-06
mask_fill = -1e30
beta_one = 0.9
beta_two = 0.95
adam_eps = 1e-08


def layer_norm(values, scale_vec, shift_vec):
    centre = values - jnp.mean(values, -1, keepdims=True)
    spread = jnp.mean(centre * centre, -1, keepdims=True)
    return centre * lax.rsqrt(spread + norm_eps) * scale_vec + shift_vec


def adam_update(master, moment, second, gradient, step_rate, weight_decay):
    first_moment = beta_one * moment.astype(jnp.float32) + (1.0 - beta_one) * gradient
    second_new = beta_two * second + (1.0 - beta_two) * gradient * gradient
    update = (
        first_moment
        / (1.0 - beta_one**STEP)
        / (jnp.sqrt(second_new / (1.0 - beta_two**STEP)) + adam_eps)
        + weight_decay * master
    )
    return (second_new, master - step_rate * update)


def split_layer(
    block_input,
    image_ids,
    out_cotangent,
    qkv_master,
    qkv_moment,
    qkv_second,
    out_master,
    out_moment,
    out_second,
    up_master,
    up_moment,
    up_second,
    down_master,
    down_moment,
    down_second,
    vec_master,
    vec_moment,
    vec_second,
    bias_master,
    bias_moment,
    bias_second,
):
    batches = block_input.shape[0]
    local_rows = block_input.shape[2]
    features = block_input.shape[3]
    splits = lax.axis_size("tensor")
    length = local_rows * splits
    head_cols = qkv_master.shape[2]
    local_heads = head_cols // HEAD
    block_rows = min(512, length)
    block_count = length // block_rows
    score_scale = HEAD ** (-0.5)
    biases = bias_master[0]
    query_bias = biases[:head_cols]
    value_bias = biases[head_cols : 2 * head_cols]
    hidden_bias = biases[2 * head_cols :]
    compute = (
        qkv_master.astype(jnp.bfloat16),
        out_master.astype(jnp.bfloat16),
        up_master.astype(jnp.bfloat16),
        down_master.astype(jnp.bfloat16),
    )
    gelu_tanh = partial(jax.nn.gelu, approximate=True)
    weight_sums = (
        jnp.zeros_like(qkv_master),
        jnp.zeros_like(out_master),
        jnp.zeros_like(up_master),
        jnp.zeros_like(down_master),
    )
    vector_terms = jnp.zeros((6, features), jnp.float32)
    bias_terms = jnp.zeros(biases.shape, jnp.float32)
    block_outputs = []
    input_grads = []
    for batch_index in range(batches):
        qkv_weight, out_weight, up_weight, down_weight = (
            lax.all_gather(compute[0], "dp", axis=0, tiled=True),
            lax.all_gather(compute[1], "dp", axis=1, tiled=True),
            lax.all_gather(compute[2], "dp", axis=0, tiled=True),
            lax.all_gather(compute[3], "dp", axis=1, tiled=True),
        )
        tokens_here = block_input[batch_index, 0]
        normed, norm_pull = jax.vjp(layer_norm, tokens_here, vec_master[0], vec_master[1])
        gathered, image_row = (
            lax.all_gather(normed.astype(jnp.bfloat16), "tensor", axis=0, tiled=True),
            lax.all_gather(image_ids[batch_index, 0], "tensor", axis=0, tiled=True),
        )
        projected = jnp.einsum(
            "td,dce->cte", gathered, qkv_weight, preferred_element_type=jnp.float32
        )
        queries = (projected[0] + query_bias).astype(jnp.bfloat16)
        key_rows = projected[1].astype(jnp.bfloat16)
        values = (projected[2] + value_bias).astype(jnp.bfloat16)
        key_heads = key_rows.reshape(length, local_heads, HEAD)
        value_heads = values.reshape(length, local_heads, HEAD)
        query_blocks = queries.reshape(block_count, block_rows, local_heads, HEAD)
        image_blocks = image_row.reshape(block_count, block_rows)

        def attend(block_pair):
            query_block, image_block = block_pair
            scores = (
                jnp.einsum(
                    "qhe,khe->hqk", query_block, key_heads, preferred_element_type=jnp.float32
                )
                * score_scale
            )
            same_image = image_block[:, None] == image_row[None, :]
            scores = jnp.where(same_image[None], scores, mask_fill)
            row_max = jnp.max(scores, -1, keepdims=True)
            exp_scores = jnp.exp(scores - row_max)
            exp_total = jnp.sum(exp_scores, -1, keepdims=True)
            attn_probs = exp_scores / exp_total
            result = jnp.einsum(
                "hqk,khe->qhe",
                attn_probs.astype(jnp.bfloat16),
                value_heads,
                preferred_element_type=jnp.float32,
            )
            return (result.reshape(block_rows, head_cols), (row_max + jnp.log(exp_total))[..., 0])

        attended_blocks, log_sums = lax.map(attend, (query_blocks, image_blocks))
        attended = attended_blocks.reshape(length, head_cols).astype(jnp.bfloat16)
        attn_sum = lax.psum_scatter(
            jnp.dot(attended, out_weight, preferred_element_type=jnp.float32).astype(jnp.bfloat16),
            "tensor",
            scatter_dimension=0,
            tiled=True,
        ).astype(jnp.float32)
        middle = tokens_here + attn_sum + vec_master[2]
        normed_two, norm_pull_two = jax.vjp(layer_norm, middle, vec_master[3], vec_master[4])
        gathered_two = lax.all_gather(normed_two.astype(jnp.bfloat16), "tensor", axis=0, tiled=True)
        hidden = jnp.dot(gathered_two, up_weight, preferred_element_type=jnp.float32) + hidden_bias
        active, gelu_pull = jax.vjp(gelu_tanh, hidden)
        active_low = active.astype(jnp.bfloat16)
        project_row_piece = lax.slice_in_dim(
            active_low, 0, local_rows * lax.axis_size("tensor"), axis=0
        )
        mlp_sum = lax.psum_scatter(
            jnp.dot(project_row_piece, down_weight, preferred_element_type=jnp.float32).astype(
                jnp.bfloat16
            ),
            "tensor",
            scatter_dimension=0,
            tiled=True,
        ).astype(jnp.float32)
        block_outputs.append(middle + mlp_sum + vec_master[5])
        qkv_weight, out_weight, up_weight, down_weight = (
            lax.all_gather(compute[0], "dp", axis=0, tiled=True),
            lax.all_gather(compute[1], "dp", axis=1, tiled=True),
            lax.all_gather(compute[2], "dp", axis=0, tiled=True),
            lax.all_gather(compute[3], "dp", axis=1, tiled=True),
        )
        cotangent = out_cotangent[batch_index, 0]
        cot_full = lax.all_gather(cotangent.astype(jnp.bfloat16), "tensor", axis=0, tiled=True)
        down_term = jnp.dot(active_low.T, cot_full, preferred_element_type=jnp.float32)
        d_active = jnp.dot(cot_full, down_weight.T, preferred_element_type=jnp.float32)
        d_hidden = gelu_pull(d_active)[0].astype(jnp.bfloat16)
        up_term = jnp.dot(gathered_two.T, d_hidden, preferred_element_type=jnp.float32)
        d_normed_two = lax.psum_scatter(
            jnp.dot(d_hidden, up_weight.T, preferred_element_type=jnp.float32).astype(jnp.bfloat16),
            "tensor",
            scatter_dimension=0,
            tiled=True,
        ).astype(jnp.float32)
        d_middle, gain_two_grad, shift_two_grad = norm_pull_two(d_normed_two)
        d_middle = d_middle + cotangent
        mid_full = lax.all_gather(d_middle.astype(jnp.bfloat16), "tensor", axis=0, tiled=True)
        out_term = jnp.dot(attended.T, mid_full, preferred_element_type=jnp.float32)
        d_attended = jnp.dot(mid_full, out_weight.T, preferred_element_type=jnp.float32).astype(
            jnp.bfloat16
        )
        d_blocks = d_attended.reshape(block_count, block_rows, local_heads, HEAD)

        def attend_back(running, block_item):
            d_keys, d_values = running
            query_block, image_block, block_sums, d_block = block_item
            scores = (
                jnp.einsum(
                    "qhe,khe->hqk", query_block, key_heads, preferred_element_type=jnp.float32
                )
                * score_scale
            )
            same_image = image_block[:, None] == image_row[None, :]
            scores = jnp.where(same_image[None], scores, mask_fill)
            attn_probs = jnp.exp(scores - block_sums[:, :, None])
            d_probs = jnp.einsum(
                "qhe,khe->hqk", d_block, value_heads, preferred_element_type=jnp.float32
            )
            row_delta = jnp.sum(attn_probs * d_probs, -1, keepdims=True)
            d_scores = (attn_probs * (d_probs - row_delta)).astype(jnp.bfloat16)
            d_query = (
                jnp.einsum("hqk,khe->qhe", d_scores, key_heads, preferred_element_type=jnp.float32)
                * score_scale
            )
            d_keys = (
                d_keys
                + jnp.einsum(
                    "hqk,qhe->khe", d_scores, query_block, preferred_element_type=jnp.float32
                )
                * score_scale
            )
            d_values = d_values + jnp.einsum(
                "hqk,qhe->khe",
                attn_probs.astype(jnp.bfloat16),
                d_block,
                preferred_element_type=jnp.float32,
            )
            return ((d_keys, d_values), d_query)

        zero_heads = jnp.zeros((length, local_heads, HEAD), jnp.float32)
        (d_keys, d_values), d_queries = lax.scan(
            attend_back, (zero_heads, zero_heads), (query_blocks, image_blocks, log_sums, d_blocks)
        )
        d_query_low = d_queries.reshape(length, head_cols).astype(jnp.bfloat16)
        d_key_low = d_keys.reshape(length, head_cols).astype(jnp.bfloat16)
        d_value_low = d_values.reshape(length, head_cols).astype(jnp.bfloat16)
        d_projected = jnp.stack([d_query_low, d_key_low, d_value_low])
        qkv_term = jnp.einsum(
            "td,cte->dce", gathered, d_projected, preferred_element_type=jnp.float32
        )
        d_normed = lax.psum_scatter(
            jnp.einsum(
                "cte,dce->td", d_projected, qkv_weight, preferred_element_type=jnp.float32
            ).astype(jnp.bfloat16),
            "tensor",
            scatter_dimension=0,
            tiled=True,
        ).astype(jnp.float32)
        d_tokens, gain_one_grad, shift_one_grad = norm_pull(d_normed)
        input_grads.append(d_tokens + d_middle)
        vector_terms = vector_terms + jnp.stack(
            [
                gain_one_grad,
                shift_one_grad,
                jnp.sum(d_middle, 0),
                gain_two_grad,
                shift_two_grad,
                jnp.sum(cotangent, 0),
            ]
        )
        bias_terms = bias_terms + jnp.concatenate(
            [
                jnp.sum(d_query_low, 0, dtype=jnp.float32),
                jnp.sum(d_value_low, 0, dtype=jnp.float32),
                jnp.sum(d_hidden, 0, dtype=jnp.float32),
            ]
        )
        local_terms = (qkv_term, out_term, up_term, down_term)
        owned = (
            lax.psum_scatter(
                local_terms[0].astype(jnp.bfloat16), "dp", scatter_dimension=0, tiled=True
            ).astype(jnp.float32),
            lax.psum_scatter(
                local_terms[1].astype(jnp.bfloat16), "dp", scatter_dimension=1, tiled=True
            ).astype(jnp.float32),
            lax.psum_scatter(
                local_terms[2].astype(jnp.bfloat16), "dp", scatter_dimension=0, tiled=True
            ).astype(jnp.float32),
            lax.psum_scatter(
                local_terms[3].astype(jnp.bfloat16), "dp", scatter_dimension=1, tiled=True
            ).astype(jnp.float32),
        )
        weight_sums = tuple((total + term for total, term in zip(weight_sums, owned)))
    qkv_grad, out_grad, up_grad, down_grad = weight_sums
    tensor_index = lax.axis_index("tensor")
    placed = jnp.where(jnp.arange(splits)[:, None] == tensor_index, bias_terms[None, :], 0.0)
    vec_grad, bias_table = lax.psum((vector_terms, placed), ("dp", "tensor"))
    bias_grad = lax.dynamic_slice_in_dim(bias_table, tensor_index, 1, 0)
    qkv_second_new, qkv_master_new = adam_update(
        qkv_master, qkv_moment, qkv_second, qkv_grad, 0.09, 0.1
    )
    out_second_new, out_master_new = adam_update(
        out_master, out_moment, out_second, out_grad, 0.4, 0.1
    )
    up_second_new, up_master_new = adam_update(up_master, up_moment, up_second, up_grad, 0.09, 0.1)
    down_second_new, down_master_new = adam_update(
        down_master, down_moment, down_second, down_grad, 0.045, 0.1
    )
    vec_second_new, vec_master_new = adam_update(
        vec_master, vec_moment, vec_second, vec_grad, 0.6, 0.0
    )
    bias_second_new, bias_master_new = adam_update(
        bias_master, bias_moment, bias_second, bias_grad, 0.5, 0.0
    )
    block_output = jnp.stack(block_outputs)[:, None]
    input_grad = jnp.stack(input_grads)[:, None]
    return (
        block_output,
        input_grad,
        qkv_grad,
        qkv_second_new,
        qkv_master_new,
        out_grad,
        out_second_new,
        out_master_new,
        up_grad,
        up_second_new,
        up_master_new,
        down_grad,
        down_second_new,
        down_master_new,
        vec_grad,
        vec_second_new,
        vec_master_new,
        bias_grad,
        bias_second_new,
        bias_master_new,
    )


LANES = 128
TILE = 128
SPAN = 256
WIDE = 1152


def lane_window(head):
    first = head * HEAD
    low = first // LANES * LANES
    high = -(-(first + HEAD) // LANES) * LANES
    return low, high


def head_mask(head, rows):
    low, high = lane_window(head)
    lane = lax.broadcasted_iota(jnp.int32, (rows, high - low), 1) + low
    return (lane >= head * HEAD) & (lane < head * HEAD + HEAD)


def padded(columns):
    return -(-columns // LANES) * LANES


def tile_spans(ids_smem, ids_ref, index, tiles):
    first_id = ids_smem[index * TILE]
    last_id = ids_smem[index * TILE + TILE - 1]
    ids = ids_ref[...]
    begin = jnp.sum((ids < first_id).astype(jnp.int32)) // TILE
    end = (jnp.sum((ids <= last_id).astype(jnp.int32)) + TILE - 1) // TILE
    count = (end - begin + 1) // 2
    return jnp.minimum(begin, tiles - 2 * count), count


def ids_column(ids_ref, index):
    row = ids_ref[:, pl.ds(pl.multiple_of(index * TILE, TILE), TILE)].astype(jnp.float32)
    square = jnp.broadcast_to(row, (TILE, TILE)).T
    return jnp.concatenate([square] * (SPAN // TILE), axis=1).astype(jnp.int32)


NT = (((1,), (1,)), ((), ()))
TN = (((0,), (0,)), ((), ()))


def attend_kernel(heads, length, ids_smem, ids_ref, q_ref, k_ref, v_ref, o_ref, lse_ref, top, total, acc):
    index = pl.program_id(0)
    columns = heads * HEAD
    scale = HEAD ** (-0.5) * math.log2(math.e)
    begin, count = tile_spans(ids_smem, ids_ref, index, length // TILE)
    own_ids = ids_column(ids_ref, index)
    top[...] = jnp.full(top.shape, mask_fill, jnp.float32)
    total[...] = jnp.zeros(total.shape, jnp.float32)
    acc[...] = jnp.zeros(acc.shape, jnp.float32)

    def window(low, high):
        return slice(low, min(high, columns))

    def step(item, carry):
        place = pl.multiple_of((begin + 2 * item) * TILE, TILE)
        keys = pl.ds(place, SPAN)
        same = own_ids == ids_ref[:, keys]
        for head in range(heads):
            low, high = lane_window(head)
            high = min(high, columns)
            cols = slice(low, high)
            mask = head_mask(head, TILE)[:, : high - low]
            query = q_ref[:, cols]
            query = jnp.where(mask, query, jnp.zeros_like(query))
            scores = lax.dot_general(query, k_ref[keys, cols], NT, preferred_element_type=jnp.float32)
            scores = jnp.where(same, scores * scale, mask_fill)
            before = top[head]
            now = jnp.maximum(before, jnp.max(scores, -1, keepdims=True))
            shrink = jnp.exp2(before - now)
            parts = jnp.exp2(scores - jnp.concatenate([now] * (SPAN // LANES), axis=1))
            total[head] = total[head] * shrink + jnp.sum(parts, -1, keepdims=True)
            top[head] = now
            mixed = jnp.dot(parts.astype(jnp.bfloat16), v_ref[keys, cols], preferred_element_type=jnp.float32)
            wide = jnp.concatenate([shrink] * ((high - low + LANES - 1) // LANES), axis=1)[:, : high - low]
            held = acc[:, cols]
            acc[:, cols] = jnp.where(mask, held * wide + mixed, held)
        return carry

    lax.fori_loop(0, count, step, 0)
    sums = jnp.zeros((TILE, LANES), jnp.float32)
    lane = lax.broadcasted_iota(jnp.int32, (TILE, LANES), 1)
    for head in range(heads):
        low, high = lane_window(head)
        high = min(high, columns)
        cols = slice(low, high)
        mask = head_mask(head, TILE)[:, : high - low]
        inverse = 1.0 / total[head]
        wide = jnp.concatenate([inverse] * ((high - low + LANES - 1) // LANES), axis=1)[:, : high - low]
        held = acc[:, cols]
        acc[:, cols] = jnp.where(mask, held * wide, held)
        sums = jnp.where(lane == head, top[head] + jnp.log2(total[head]), sums)
    o_ref[...] = acc[...].astype(o_ref.dtype)
    lse_ref[...] = sums.T[:heads]


def attend(ids, query, key, value):
    length, columns = query.shape
    heads = columns // HEAD
    tiles = length // TILE
    whole = pl.BlockSpec((length, columns), lambda i, s: (0, 0))
    block = pl.BlockSpec((TILE, columns), lambda i, s: (i, 0))
    return pl.pallas_call(
        partial(attend_kernel, heads, length),
        grid_spec=pltpu.PrefetchScalarGridSpec(
            num_scalar_prefetch=1,
            grid=(tiles,),
            in_specs=[pl.BlockSpec((1, length), lambda i, s: (0, 0)), block, whole, whole],
            out_specs=[block, pl.BlockSpec((heads, TILE), lambda i, s: (0, i))],
            scratch_shapes=[
                pltpu.VMEM((heads, TILE, LANES), jnp.float32),
                pltpu.VMEM((heads, TILE, LANES), jnp.float32),
                pltpu.VMEM((TILE, columns), jnp.float32),
            ],
        ),
        out_shape=[
            jax.ShapeDtypeStruct((length, columns), jnp.bfloat16),
            jax.ShapeDtypeStruct((heads, length), jnp.float32),
        ],
        compiler_params=pltpu.CompilerParams(vmem_limit_bytes=40 << 20),
        cost_estimate=pl.CostEstimate(flops=9 * 10**9, bytes_accessed=10**6, transcendentals=0),
    )(ids, ids.reshape(1, length), query, key, value)


def attend_back_kernel(
    heads, length, ids_smem, ids_ref, q_ref, k_ref, v_ref, o_ref, g_ref, lse_ref,
    dq_ref, dk_ref, dv_ref, delta, dq_acc, dk_acc, dv_acc,
):
    index = pl.program_id(0)
    columns = heads * HEAD
    natural = HEAD ** (-0.5)
    scale = natural * math.log2(math.e)
    tiles = length // TILE
    begin, count = tile_spans(ids_smem, ids_ref, index, tiles)
    own_ids = ids_column(ids_ref, index)

    @pl.when(index == 0)
    def _():
        dq_acc[...] = jnp.zeros(dq_acc.shape, jnp.float32)
        row = lax.broadcasted_iota(jnp.int32, (heads, columns), 0)
        lane = lax.broadcasted_iota(jnp.int32, (heads, columns), 1)
        pick = ((lane >= row * HEAD) & (lane < row * HEAD + HEAD)).astype(jnp.bfloat16)
        product = g_ref[...].astype(jnp.float32) * o_ref[...].astype(jnp.float32)
        coarse = product.astype(jnp.bfloat16)
        fine = (product - coarse.astype(jnp.float32)).astype(jnp.bfloat16)
        delta[...] = lax.dot_general(pick, coarse, NT, preferred_element_type=jnp.float32) + lax.dot_general(
            pick, fine, NT, preferred_element_type=jnp.float32
        )

    dk_acc[...] = jnp.zeros(dk_acc.shape, jnp.float32)
    dv_acc[...] = jnp.zeros(dv_acc.shape, jnp.float32)

    def step(item, carry):
        place = pl.multiple_of((begin + 2 * item) * TILE, TILE)
        rows = pl.ds(place, SPAN)
        same = own_ids == ids_ref[:, rows]
        for head in range(heads):
            low, high = lane_window(head)
            high = min(high, columns)
            cols = slice(low, high)
            mask = head_mask(head, TILE)[:, : high - low]
            key = k_ref[:, cols]
            key = jnp.where(mask, key, jnp.zeros_like(key))
            value = v_ref[:, cols]
            value = jnp.where(mask, value, jnp.zeros_like(value))
            query = q_ref[rows, cols]
            grad = g_ref[rows, cols]
            scores = lax.dot_general(key, query, NT, preferred_element_type=jnp.float32)
            probs = jnp.exp2(jnp.where(same, scores * scale, mask_fill) - lse_ref[head : head + 1, rows])
            d_probs = lax.dot_general(value, grad, NT, preferred_element_type=jnp.float32)
            d_scores = (probs * (d_probs - delta[head : head + 1, rows])).astype(jnp.bfloat16)
            d_value = jnp.dot(probs.astype(jnp.bfloat16), grad, preferred_element_type=jnp.float32)
            d_key = jnp.dot(d_scores, query, preferred_element_type=jnp.float32)
            dv_acc[:, cols] += jnp.where(mask, d_value, 0.0)
            dk_acc[:, cols] += jnp.where(mask, d_key, 0.0)
            dq_acc[rows, cols] += lax.dot_general(d_scores, key, TN, preferred_element_type=jnp.float32)
        return carry

    lax.fori_loop(0, count, step, 0)
    dk_ref[...] = (dk_acc[...] * natural).astype(dk_ref.dtype)
    dv_ref[...] = dv_acc[...].astype(dv_ref.dtype)

    @pl.when(index == tiles - 1)
    def _():
        dq_ref[...] = (dq_acc[...] * natural).astype(dq_ref.dtype)


def attend_back(ids, query, key, value, attended, grad, lse):
    length, columns = query.shape
    heads = columns // HEAD
    tiles = length // TILE
    whole = pl.BlockSpec((length, columns), lambda i, s: (0, 0))
    block = pl.BlockSpec((TILE, columns), lambda i, s: (i, 0))
    out = jax.ShapeDtypeStruct((length, columns), jnp.bfloat16)
    return pl.pallas_call(
        partial(attend_back_kernel, heads, length),
        grid_spec=pltpu.PrefetchScalarGridSpec(
            num_scalar_prefetch=1,
            grid=(tiles,),
            in_specs=[
                pl.BlockSpec((1, length), lambda i, s: (0, 0)),
                whole,
                block,
                block,
                whole,
                whole,
                pl.BlockSpec((heads, length), lambda i, s: (0, 0)),
            ],
            out_specs=[whole, block, block],
            scratch_shapes=[
                pltpu.VMEM((heads, length), jnp.float32),
                pltpu.VMEM((length, columns), jnp.float32),
                pltpu.VMEM((TILE, columns), jnp.float32),
                pltpu.VMEM((TILE, columns), jnp.float32),
            ],
        ),
        out_shape=[out, out, out],
        compiler_params=pltpu.CompilerParams(vmem_limit_bytes=40 << 20),
        cost_estimate=pl.CostEstimate(flops=9 * 10**9, bytes_accessed=10**6, transcendentals=0),
    )(ids, ids.reshape(1, length), query, key, value, attended, grad, lse)


def column_call(kernel, ins, outs, columns, flops, scratch=()):
    wide = min(WIDE, padded(columns))
    groups = outs[0].shape[0]

    def spec(shape, cut):
        if cut:
            return pl.BlockSpec((1, shape[1], wide), lambda g, i: (g, 0, i))
        return pl.BlockSpec(shape, lambda g, i: (0,) * len(shape))

    size = sum(math.prod(a.shape) * a.dtype.itemsize for a, _ in ins) + sum(
        math.prod(a.shape) * a.dtype.itemsize for a in outs
    )
    return pl.pallas_call(
        kernel,
        grid=(groups, -(-columns // wide)),
        in_specs=[spec(a.shape, cut) for a, cut in ins],
        out_specs=[spec(a.shape, True) for a in outs],
        out_shape=outs,
        scratch_shapes=list(scratch),
        compiler_params=pltpu.CompilerParams(vmem_limit_bytes=44 << 20),
        cost_estimate=pl.CostEstimate(flops=flops // 2, bytes_accessed=size // 2, transcendentals=0),
    )(*[a for a, _ in ins])


def hidden_kernel(x_ref, w_ref, b_ref, active_ref, slope_ref):
    rows = 256
    for block in range(x_ref.shape[0] // rows):
        part = pl.ds(block * rows, rows)
        value = jnp.dot(x_ref[part, :], w_ref[0], preferred_element_type=jnp.float32) + b_ref[0]
        active, slope = gelu_pair(value)
        active_ref[0, part, :] = active.astype(jnp.bfloat16)
        slope_ref[0, part, :] = slope.astype(jnp.bfloat16)


def hidden_units(x, weight, bias):
    groups, columns = bias.shape
    out = jax.ShapeDtypeStruct((groups, x.shape[0], columns), jnp.bfloat16)
    ins = [(x, False), (weight, True), (bias.reshape(groups, 1, columns), True)]
    return column_call(hidden_kernel, ins, [out, out], columns, 2 * groups * x.shape[0] * x.shape[1] * columns)


def hidden_back_kernel(x_ref, w_ref, slope_ref, grad_ref, sum_ref):
    rows = 256
    total = jnp.zeros(sum_ref.shape[1:], jnp.float32)
    for block in range(x_ref.shape[0] // rows):
        part = pl.ds(block * rows, rows)
        value = jnp.dot(x_ref[part, :], w_ref[0], preferred_element_type=jnp.float32)
        value = value * slope_ref[0, part, :].astype(jnp.float32)
        grad_ref[0, part, :] = value.astype(jnp.bfloat16)
        total = total + jnp.sum(value, 0, keepdims=True)
    sum_ref[0] = total


def hidden_back(x, weight, slope):
    groups, tokens, columns = slope.shape
    outs = [
        jax.ShapeDtypeStruct((groups, tokens, columns), jnp.bfloat16),
        jax.ShapeDtypeStruct((groups, 1, columns), jnp.float32),
    ]
    ins = [(x, False), (weight, True), (slope, True)]
    return column_call(hidden_back_kernel, ins, outs, columns, 2 * groups * tokens * x.shape[1] * columns)


def whole_grad_kernel(x_ref, dy_ref, out_ref, turned):
    @pl.when((pl.program_id(0) == 0) & (pl.program_id(1) == 0))
    def _():
        turned[...] = x_ref[...].T

    out_ref[0] = jnp.dot(turned[...], dy_ref[0], preferred_element_type=jnp.float32).astype(jnp.bfloat16)


def whole_grads(x, dy):
    groups, tokens, columns = dy.shape
    features = x.shape[1]
    out = jax.ShapeDtypeStruct((groups, features, columns), jnp.bfloat16)
    scratch = [pltpu.VMEM((features, tokens), jnp.bfloat16)]
    flops = 2 * groups * tokens * features * columns
    return column_call(whole_grad_kernel, [(x, False), (dy, True)], [out], columns, flops, scratch)[0]


def grad_kernel(chunks, x_ref, *refs):
    core = lax.axis_index("dp") % 2
    count = (len(refs) - 2) // 3
    dy_refs, sent_refs, kept_refs = refs[:count], refs[count : 2 * count], refs[2 * count : 3 * count]
    turned, result = refs[3 * count :]
    turned[...] = x_ref[...].T
    rows = turned.shape[0] // chunks
    for dy_ref, sent_ref, kept_ref in zip(dy_refs, sent_refs, kept_refs):
        result[...] = jnp.dot(turned[...], dy_ref[...], preferred_element_type=jnp.float32)
        for spot in range(chunks // 2):
            sent = pl.multiple_of((2 * spot + 1 - core) * rows, 8)
            kept = pl.multiple_of((2 * spot + core) * rows, 8)
            sent_ref[spot] = result[pl.ds(sent, rows), :].astype(jnp.bfloat16)
            kept_ref[spot] = result[pl.ds(kept, rows), :].astype(jnp.bfloat16)


def weight_grads(x, parts):
    tokens, features = x.shape
    columns = parts[0].shape[1]
    count = len(parts)
    out = jax.ShapeDtypeStruct((8, features // 16, columns), jnp.bfloat16)
    results = pl.pallas_call(
        partial(grad_kernel, 16),
        out_shape=[out] * (2 * count),
        scratch_shapes=[pltpu.VMEM((features, tokens), jnp.bfloat16), pltpu.VMEM((features, columns), jnp.float32)],
        compiler_params=pltpu.CompilerParams(vmem_limit_bytes=40 << 20),
        cost_estimate=pl.CostEstimate(
            flops=tokens * features * columns * count,
            bytes_accessed=tokens * features + count * columns * (tokens + features),
            transcendentals=0,
        ),
    )(x, *parts)
    return results[:count], results[count:]


def place_kernel(leads, ordered, steps, *refs):
    pieces = refs[: len(steps)]
    outs = refs[len(steps) : len(steps) + leads]
    sems = refs[len(steps) + leads]
    spot = lax.axis_index("dp")
    z, y, core = spot // 4, spot // 2 % 2, spot % 2
    copies = []
    for piece, (first_slot, y_step, core_step) in zip(pieces, steps):
        column = (y + y_step) % 2 * 2 + (core + core_step) % 2
        for slot in range(piece.shape[0]):
            number = first_slot + slot
            row = (number if ordered else (z + 4 - number) % 4) * 4 + column
            for lead in range(leads):
                copy = pltpu.make_async_copy(piece.at[slot, lead], outs[lead].at[row], sems.at[len(copies)])
                copy.start()
                copies.append(copy)
    for copy in copies:
        copy.wait()


def place(near, far, ordered):
    pieces = near + far
    leads, rows, columns = pieces[0].shape[1:]
    half = pieces[0].shape[0]
    steps = [(start, step % 2, step // 2) for start in (0, half) for step in range(4)]
    size = 16 * leads * rows * padded(columns) * 2
    placed = pl.pallas_call(
        partial(place_kernel, leads, ordered, steps),
        in_specs=[pl.BlockSpec(memory_space=pl.ANY)] * len(pieces),
        out_specs=[pl.BlockSpec(memory_space=pltpu.VMEM)] * leads,
        out_shape=[jax.ShapeDtypeStruct((16, rows, columns), jnp.bfloat16)] * leads,
        scratch_shapes=[pltpu.SemaphoreType.DMA((16 * leads,))],
        compiler_params=pltpu.CompilerParams(vmem_limit_bytes=size * 3 // 2 + (2 << 20)),
        cost_estimate=pl.CostEstimate(flops=0, bytes_accessed=size, transcendentals=0),
    )(*pieces)
    return [part.reshape(16 * rows, columns) for part in placed]


def swap_x(value):
    return lax.ppermute(value, "tensor", [(0, 1), (1, 0)])


def swap_y(value):
    return lax.ppermute(value, "dp", [(spot, spot ^ 2) for spot in range(16)])


def swap_core(value):
    return lax.ppermute(value, "dp", [(spot, spot ^ 1) for spot in range(16)])


def move_z(value, steps):
    return lax.ppermute(value, "dp", [(spot, (spot + 4 * steps) % 16) for spot in range(16)])


def after(value, *others):
    return lax.optimization_barrier((value,) + others)[0]


def exchange_z(shard):
    return [shard] + [move_z(shard, steps) for steps in (1, 2, 3)]


def gather_planes(near, far):
    near_x = swap_x(near)
    far_y = swap_y(far)
    near_y = swap_y(after(near, far_y))
    far_x = swap_x(after(far, near_x))
    near_xy = swap_y(after(near_x, near_y))
    far_yx = swap_x(after(far_y, far_x))
    return [near, near_y], [far, far_y], [near_x, near_xy], [far_x, far_yx]


def gather_cores(planes, ordered):
    planes = [parts + [swap_core(part) for part in parts] for parts in planes]
    return place(planes[0], planes[1], ordered), place(planes[2], planes[3], ordered)


def add_low(*terms):
    total = terms[0].astype(jnp.float32)
    for term in terms[1:]:
        total = total + term.astype(jnp.float32)
    return total.astype(jnp.bfloat16)


def part_of(value, index, axis):
    return lax.dynamic_index_in_dim(value, index, axis, keepdims=False)


def y_parts(value):
    spot = lax.axis_index("dp")
    split = value.reshape((4, 2) + value.shape[1:])
    return part_of(split, spot // 2 % 2, 1), part_of(split, 1 - spot // 2 % 2, 1)


def send_z(value):
    z = lax.axis_index("dp") // 4
    return [part_of(value, z, 0)] + [move_z(part_of(value, (z + steps) % 4, 0), steps) for steps in (1, 2, 3)]


def sum_terms(terms):
    total = terms[0].astype(jnp.float32)
    for term in terms[1:]:
        total = total + term.astype(jnp.float32)
    return total


def sum_everywhere(value):
    value = value + swap_core(value)
    value = value + swap_y(value)
    value = value + swap_x(value)
    return value + move_z(value, 1) + move_z(value, 2) + move_z(value, 3)


def norm_forward(values):
    centre = values - jnp.mean(values, -1, keepdims=True)
    inverse = lax.rsqrt(jnp.mean(centre * centre, -1, keepdims=True) + norm_eps)
    return centre * inverse, inverse


def norm_back(grad, hat, inverse, gain):
    scaled = grad * gain
    mean_one = jnp.mean(scaled, -1, keepdims=True)
    mean_two = jnp.mean(scaled * hat, -1, keepdims=True)
    return (scaled - mean_one - hat * mean_two) * inverse


def gelu_pair(value):
    inner = math.sqrt(2.0 / math.pi)
    squared = value * value
    bent = jnp.tanh(inner * (value + 0.044715 * value * squared))
    half = 0.5 * (1.0 + bent)
    slope = half + 0.5 * value * (1.0 - bent * bent) * inner * (1.0 + 3 * 0.044715 * squared)
    return value * half, slope


def row_layer(
    block_input,
    image_ids,
    out_cotangent,
    qkv_master,
    qkv_moment,
    qkv_second,
    out_master,
    out_moment,
    out_second,
    up_master,
    up_moment,
    up_second,
    down_master,
    down_moment,
    down_second,
    vec_master,
    vec_moment,
    vec_second,
    bias_master,
    bias_moment,
    bias_second,
):
    low = jnp.bfloat16
    wide = jnp.float32
    mine = lax.axis_index("tensor")
    first = mine == 0
    half = block_input.shape[2]
    features = block_input.shape[3]
    head_cols = qkv_master.shape[2]

    def pick(pair, index):
        return lax.dynamic_index_in_dim(pair, index, 0, keepdims=False)

    def in_order(own, other, axis=0):
        return jnp.concatenate([jnp.where(first, own, other), jnp.where(first, other, own)], axis)

    def dot(spec, left, right):
        return jnp.einsum(spec, left, right, preferred_element_type=wide)

    def gather(shard):
        return lax.all_gather(shard, ("tensor", "dp")).reshape(2, features, shard.shape[1])

    def scatter(terms):
        flat = terms.reshape(2 * features, terms.shape[2])
        return lax.psum_scatter(flat, ("tensor", "dp"), scatter_dimension=0, tiled=True)

    inputs_own = pick(block_input[:, 0], mine)
    inputs_sent = pick(block_input[:, 0], 1 - mine)
    cot_own = pick(out_cotangent[:, 0], mine)
    cot_sent = pick(out_cotangent[:, 0], 1 - mine)
    inputs = in_order(inputs_own, swap_x(inputs_sent.astype(low)).astype(wide))
    ids = in_order(pick(image_ids[:, 0], mine), swap_x(pick(image_ids[:, 0], 1 - mine)))
    biases = jnp.concatenate([bias_master, swap_x(bias_master)])
    early_shard = jnp.stack([qkv_master[:, 0], qkv_master[:, 1], qkv_master[:, 2]]).astype(low)
    early_z = exchange_z(early_shard)
    out_whole = gather(out_master.T.astype(low))
    up_weight = gather(after(up_master.astype(low), out_whole))
    down_weight = gather(after(down_master.T.astype(low), up_weight))
    early_planes = gather_planes(jnp.stack(early_z[:2]), jnp.stack(early_z[2:]))
    query_weight, key_weight, value_weight = list(zip(*gather_cores(early_planes, False)))
    out_weight = [pick(out_whole, mine), pick(out_whole, 1 - mine)]
    cot_row = in_order(cot_own, swap_x(after(cot_sent.astype(low), early_planes[3][1])).astype(wide))
    cot_low = cot_row.astype(low)

    hat_one, inverse_one = norm_forward(inputs)
    normed = (hat_one * vec_master[0] + vec_master[1]).astype(low)
    query = [(dot("td,de->te", normed, query_weight[g]) + biases[g, :head_cols]).astype(low) for g in range(2)]
    key = [dot("td,de->te", normed, key_weight[g]).astype(low) for g in range(2)]
    value = [
        (dot("td,de->te", normed, value_weight[g]) + biases[g, head_cols : 2 * head_cols]).astype(low)
        for g in range(2)
    ]
    attended, log_sums = [None, None], [None, None]
    attended[0], log_sums[0] = attend(ids, query[0], key[0], value[0])
    attended[1], log_sums[1] = attend(ids, query[1], key[1], value[1])
    attn_sum = sum(dot("te,de->td", attended[g], out_weight[g]) for g in range(2)) + vec_master[2]
    middle = inputs + attn_sum
    hat_two, inverse_two = norm_forward(middle)
    normed_two = (hat_two * vec_master[3] + vec_master[4]).astype(low)
    hidden_biases = in_order(biases[:1, 2 * head_cols :], biases[1:, 2 * head_cols :])
    active, slope = hidden_units(normed_two, up_weight, hidden_biases)
    added = attn_sum + sum(dot("tf,df->td", active[g], down_weight[g]) for g in range(2)) + vec_master[5]
    added = added.reshape(2, half, features)
    out_here = inputs_own + pick(added, mine)
    out_there = pick(block_input[:, 0], 1 - mine) + swap_x(pick(added, 1 - mine).astype(low)).astype(wide)
    block_output = in_order(out_here[None], out_there[None])[:, None]

    own, other = 0, 1
    down_term = scatter(whole_grads(cot_low, active))
    d_hidden, hidden_sums = hidden_back(cot_low, down_weight, slope)
    up_term = scatter(whole_grads(normed_two, d_hidden))
    d_normed_two = sum(dot("tf,df->td", d_hidden[g], up_weight[g]) for g in range(2))
    mid_added = norm_back(d_normed_two, hat_two, inverse_two, vec_master[3])
    d_middle = cot_row + mid_added
    mid_low = d_middle.astype(low)
    d_attended = [dot("td,de->te", mid_low, out_weight[g]).astype(low) for g in range(2)]
    out_sent, out_kept = weight_grads(mid_low, attended)
    out_core = [swap_core(part) for part in out_sent]

    def back(g, grad):
        return attend_back(ids, query[g], key[g], value[g], attended[g], grad, log_sums[g])

    out_here = [y_parts(add_low(out_kept[g], out_core[g])) for g in range(2)]
    d_other = back(other, after(d_attended[other], out_here[0][1], out_here[1][1]))
    qkv_sent, qkv_kept = [None, None], [None, None]
    qkv_sent[other], qkv_kept[other] = weight_grads(normed, d_other)
    qkv_core_other = swap_core(jnp.stack(qkv_sent[other]))
    out_y = swap_y(jnp.stack([part[1] for part in out_here]))
    qkv_other_here, qkv_other_there = zip(
        *[y_parts(part) for part in add_low(jnp.stack(qkv_kept[other]), qkv_core_other)]
    )
    qkv_y_other = swap_y(jnp.stack(qkv_other_there))
    d_own = back(own, after(d_attended[own], qkv_y_other, out_y))
    qkv_other = add_low(jnp.stack(qkv_other_here), qkv_y_other)
    qkv_x = swap_x(qkv_other)
    out_x = swap_x(add_low(out_here[other][0], out_y[other]))
    qkv_sent[own], qkv_kept[own] = weight_grads(after(normed, qkv_other), d_own)
    qkv_core_own = swap_core(jnp.stack(qkv_sent[own]))
    d_own_late = after(tuple(d_own), *qkv_sent[own])
    d_normed = sum(
        dot("te,de->td", part[g], weight[g])
        for part, weight in zip(zip(d_own_late, d_other), (query_weight, key_weight, value_weight))
        for g in range(2)
    )
    qkv_here, qkv_there = zip(*[y_parts(part) for part in add_low(jnp.stack(qkv_kept[own]), qkv_core_own)])
    qkv_y = swap_y(jnp.stack(qkv_there))
    out_terms = send_z(add_low(out_here[own][0], out_y[own], out_x))
    qkv_terms = send_z(add_low(jnp.stack(qkv_here), qkv_y, qkv_x).transpose(1, 0, 2, 3))
    down_grad = down_term.astype(wide).T
    up_grad = up_term.astype(wide)
    out_grad = sum_terms(out_terms).T
    qkv_grad = sum_terms(qkv_terms).transpose(1, 0, 2)
    in_added = (mid_added + norm_back(d_normed, hat_one, inverse_one, vec_master[0])).reshape(2, half, features)
    grad_here = cot_own + pick(in_added, mine)
    grad_there = cot_sent + swap_x(pick(in_added, 1 - mine).astype(low)).astype(wide)
    input_grad = in_order(grad_here[None], grad_there[None])[:, None]

    early = jnp.concatenate(
        [
            jnp.sum(d_middle, 0),
            jnp.sum(d_normed_two * hat_two, 0),
            jnp.sum(d_normed_two, 0),
            jnp.sum(out_cotangent[:, 0], (0, 1)),
        ]
    )

    def bias_rows(sums):
        return jnp.where(first, jnp.concatenate(sums), jnp.concatenate(sums[::-1]))

    sums = sum_everywhere(
        jnp.concatenate(
            [
                jnp.sum(d_normed * hat_one, 0),
                jnp.sum(d_normed, 0),
                early,
                bias_rows([jnp.sum(part[0], 0, dtype=wide) for part in (d_own, d_other)]),
                bias_rows([jnp.sum(part[2], 0, dtype=wide) for part in (d_own, d_other)]),
                hidden_sums.reshape(-1),
            ]
        )[None]
    )[0]
    vec_grad = sums[: 6 * features].reshape(6, features)

    def group(start, size):
        return pick(sums[start : start + 2 * size].reshape(2, size), mine)

    start = 6 * features
    bias_grad = jnp.concatenate(
        [
            group(start, head_cols),
            group(start + 2 * head_cols, head_cols),
            group(start + 4 * head_cols, up_master.shape[1]),
        ]
    )[None]

    results = [block_output, input_grad]
    for master, moment, second, grad, rate, decay in (
        (qkv_master, qkv_moment, qkv_second, qkv_grad, 0.09, 0.1),
        (out_master, out_moment, out_second, out_grad, 0.4, 0.1),
        (up_master, up_moment, up_second, up_grad, 0.09, 0.1),
        (down_master, down_moment, down_second, down_grad, 0.045, 0.1),
        (vec_master, vec_moment, vec_second, vec_grad, 0.6, 0.0),
        (bias_master, bias_moment, bias_second, bias_grad, 0.5, 0.0),
    ):
        second_new, master_new = adam_update(master, moment, second, grad, rate, decay)
        results += [grad, second_new, master_new]
    return tuple(results)


def solution(mesh):
    placed = (
        P(None, "dp", "tensor", None),
        P(None, "dp", "tensor"),
        P(None, "dp", "tensor", None),
        P("dp", None, "tensor"),
        P("dp", None, "tensor"),
        P("dp", None, "tensor"),
        P("tensor", "dp"),
        P("tensor", "dp"),
        P("tensor", "dp"),
        P("dp", "tensor"),
        P("dp", "tensor"),
        P("dp", "tensor"),
        P("tensor", "dp"),
        P("tensor", "dp"),
        P("tensor", "dp"),
        P(),
        P(),
        P(),
        P("tensor", None),
        P("tensor", None),
        P("tensor", None),
    )
    by_rows = dict(mesh.shape) == {"dp": 16, "tensor": 2}
    return jax.shard_map(
        row_layer if by_rows else split_layer,
        mesh=mesh,
        in_specs=placed,
        out_specs=(
            P(None, "dp", "tensor", None),
            P(None, "dp", "tensor", None),
            P("dp", None, "tensor"),
            P("dp", None, "tensor"),
            P("dp", None, "tensor"),
            P("tensor", "dp"),
            P("tensor", "dp"),
            P("tensor", "dp"),
            P("dp", "tensor"),
            P("dp", "tensor"),
            P("dp", "tensor"),
            P("tensor", "dp"),
            P("tensor", "dp"),
            P("tensor", "dp"),
            P(),
            P(),
            P(),
            P("tensor", None),
            P("tensor", None),
            P("tensor", None),
        ),
        check_vma=False,
    )
```

```python
import math
from functools import partial

import jax
import jax.numpy as jnp
from jax import lax
from jax.experimental import pallas as pl
from jax.experimental.pallas import tpu as pltpu
from jax.sharding import PartitionSpec as P

HEAD = 72
STEP = 10


norm_eps = 1e-06
mask_fill = -1e30
beta_one = 0.9
beta_two = 0.95
adam_eps = 1e-08


def layer_norm(values, scale_vec, shift_vec):
    centre = values - jnp.mean(values, -1, keepdims=True)
    spread = jnp.mean(centre * centre, -1, keepdims=True)
    return centre * lax.rsqrt(spread + norm_eps) * scale_vec + shift_vec


def adam_update(master, moment, second, gradient, step_rate, weight_decay):
    first_moment = beta_one * moment.astype(jnp.float32) + (1.0 - beta_one) * gradient
    second_new = beta_two * second + (1.0 - beta_two) * gradient * gradient
    update = (
        first_moment
        / (1.0 - beta_one**STEP)
        / (jnp.sqrt(second_new / (1.0 - beta_two**STEP)) + adam_eps)
        + weight_decay * master
    )
    return (second_new, master - step_rate * update)


def split_layer(
    block_input,
    image_ids,
    out_cotangent,
    qkv_master,
    qkv_moment,
    qkv_second,
    out_master,
    out_moment,
    out_second,
    up_master,
    up_moment,
    up_second,
    down_master,
    down_moment,
    down_second,
    vec_master,
    vec_moment,
    vec_second,
    bias_master,
    bias_moment,
    bias_second,
):
    batches = block_input.shape[0]
    local_rows = block_input.shape[2]
    features = block_input.shape[3]
    splits = lax.axis_size("tensor")
    length = local_rows * splits
    head_cols = qkv_master.shape[2]
    local_heads = head_cols // HEAD
    block_rows = min(512, length)
    block_count = length // block_rows
    score_scale = HEAD ** (-0.5)
    biases = bias_master[0]
    query_bias = biases[:head_cols]
    value_bias = biases[head_cols : 2 * head_cols]
    hidden_bias = biases[2 * head_cols :]
    compute = (
        qkv_master.astype(jnp.bfloat16),
        out_master.astype(jnp.bfloat16),
        up_master.astype(jnp.bfloat16),
        down_master.astype(jnp.bfloat16),
    )
    gelu_tanh = partial(jax.nn.gelu, approximate=True)
    weight_sums = (
        jnp.zeros_like(qkv_master),
        jnp.zeros_like(out_master),
        jnp.zeros_like(up_master),
        jnp.zeros_like(down_master),
    )
    vector_terms = jnp.zeros((6, features), jnp.float32)
    bias_terms = jnp.zeros(biases.shape, jnp.float32)
    block_outputs = []
    input_grads = []
    for batch_index in range(batches):
        qkv_weight, out_weight, up_weight, down_weight = (
            lax.all_gather(compute[0], "dp", axis=0, tiled=True),
            lax.all_gather(compute[1], "dp", axis=1, tiled=True),
            lax.all_gather(compute[2], "dp", axis=0, tiled=True),
            lax.all_gather(compute[3], "dp", axis=1, tiled=True),
        )
        tokens_here = block_input[batch_index, 0]
        normed, norm_pull = jax.vjp(layer_norm, tokens_here, vec_master[0], vec_master[1])
        gathered, image_row = (
            lax.all_gather(normed.astype(jnp.bfloat16), "tensor", axis=0, tiled=True),
            lax.all_gather(image_ids[batch_index, 0], "tensor", axis=0, tiled=True),
        )
        projected = jnp.einsum(
            "td,dce->cte", gathered, qkv_weight, preferred_element_type=jnp.float32
        )
        queries = (projected[0] + query_bias).astype(jnp.bfloat16)
        key_rows = projected[1].astype(jnp.bfloat16)
        values = (projected[2] + value_bias).astype(jnp.bfloat16)
        key_heads = key_rows.reshape(length, local_heads, HEAD)
        value_heads = values.reshape(length, local_heads, HEAD)
        query_blocks = queries.reshape(block_count, block_rows, local_heads, HEAD)
        image_blocks = image_row.reshape(block_count, block_rows)

        def attend(block_pair):
            query_block, image_block = block_pair
            scores = (
                jnp.einsum(
                    "qhe,khe->hqk", query_block, key_heads, preferred_element_type=jnp.float32
                )
                * score_scale
            )
            same_image = image_block[:, None] == image_row[None, :]
            scores = jnp.where(same_image[None], scores, mask_fill)
            row_max = jnp.max(scores, -1, keepdims=True)
            exp_scores = jnp.exp(scores - row_max)
            exp_total = jnp.sum(exp_scores, -1, keepdims=True)
            attn_probs = exp_scores / exp_total
            result = jnp.einsum(
                "hqk,khe->qhe",
                attn_probs.astype(jnp.bfloat16),
                value_heads,
                preferred_element_type=jnp.float32,
            )
            return (result.reshape(block_rows, head_cols), (row_max + jnp.log(exp_total))[..., 0])

        attended_blocks, log_sums = lax.map(attend, (query_blocks, image_blocks))
        attended = attended_blocks.reshape(length, head_cols).astype(jnp.bfloat16)
        attn_sum = lax.psum_scatter(
            jnp.dot(attended, out_weight, preferred_element_type=jnp.float32).astype(jnp.bfloat16),
            "tensor",
            scatter_dimension=0,
            tiled=True,
        ).astype(jnp.float32)
        middle = tokens_here + attn_sum + vec_master[2]
        normed_two, norm_pull_two = jax.vjp(layer_norm, middle, vec_master[3], vec_master[4])
        gathered_two = lax.all_gather(normed_two.astype(jnp.bfloat16), "tensor", axis=0, tiled=True)
        hidden = jnp.dot(gathered_two, up_weight, preferred_element_type=jnp.float32) + hidden_bias
        active, gelu_pull = jax.vjp(gelu_tanh, hidden)
        active_low = active.astype(jnp.bfloat16)
        project_row_piece = lax.slice_in_dim(
            active_low, 0, local_rows * lax.axis_size("tensor"), axis=0
        )
        mlp_sum = lax.psum_scatter(
            jnp.dot(project_row_piece, down_weight, preferred_element_type=jnp.float32).astype(
                jnp.bfloat16
            ),
            "tensor",
            scatter_dimension=0,
            tiled=True,
        ).astype(jnp.float32)
        block_outputs.append(middle + mlp_sum + vec_master[5])
        qkv_weight, out_weight, up_weight, down_weight = (
            lax.all_gather(compute[0], "dp", axis=0, tiled=True),
            lax.all_gather(compute[1], "dp", axis=1, tiled=True),
            lax.all_gather(compute[2], "dp", axis=0, tiled=True),
            lax.all_gather(compute[3], "dp", axis=1, tiled=True),
        )
        cotangent = out_cotangent[batch_index, 0]
        cot_full = lax.all_gather(cotangent.astype(jnp.bfloat16), "tensor", axis=0, tiled=True)
        down_term = jnp.dot(active_low.T, cot_full, preferred_element_type=jnp.float32)
        d_active = jnp.dot(cot_full, down_weight.T, preferred_element_type=jnp.float32)
        d_hidden = gelu_pull(d_active)[0].astype(jnp.bfloat16)
        up_term = jnp.dot(gathered_two.T, d_hidden, preferred_element_type=jnp.float32)
        d_normed_two = lax.psum_scatter(
            jnp.dot(d_hidden, up_weight.T, preferred_element_type=jnp.float32).astype(jnp.bfloat16),
            "tensor",
            scatter_dimension=0,
            tiled=True,
        ).astype(jnp.float32)
        d_middle, gain_two_grad, shift_two_grad = norm_pull_two(d_normed_two)
        d_middle = d_middle + cotangent
        mid_full = lax.all_gather(d_middle.astype(jnp.bfloat16), "tensor", axis=0, tiled=True)
        out_term = jnp.dot(attended.T, mid_full, preferred_element_type=jnp.float32)
        d_attended = jnp.dot(mid_full, out_weight.T, preferred_element_type=jnp.float32).astype(
            jnp.bfloat16
        )
        d_blocks = d_attended.reshape(block_count, block_rows, local_heads, HEAD)

        def attend_back(running, block_item):
            d_keys, d_values = running
            query_block, image_block, block_sums, d_block = block_item
            scores = (
                jnp.einsum(
                    "qhe,khe->hqk", query_block, key_heads, preferred_element_type=jnp.float32
                )
                * score_scale
            )
            same_image = image_block[:, None] == image_row[None, :]
            scores = jnp.where(same_image[None], scores, mask_fill)
            attn_probs = jnp.exp(scores - block_sums[:, :, None])
            d_probs = jnp.einsum(
                "qhe,khe->hqk", d_block, value_heads, preferred_element_type=jnp.float32
            )
            row_delta = jnp.sum(attn_probs * d_probs, -1, keepdims=True)
            d_scores = (attn_probs * (d_probs - row_delta)).astype(jnp.bfloat16)
            d_query = (
                jnp.einsum("hqk,khe->qhe", d_scores, key_heads, preferred_element_type=jnp.float32)
                * score_scale
            )
            d_keys = (
                d_keys
                + jnp.einsum(
                    "hqk,qhe->khe", d_scores, query_block, preferred_element_type=jnp.float32
                )
                * score_scale
            )
            d_values = d_values + jnp.einsum(
                "hqk,qhe->khe",
                attn_probs.astype(jnp.bfloat16),
                d_block,
                preferred_element_type=jnp.float32,
            )
            return ((d_keys, d_values), d_query)

        zero_heads = jnp.zeros((length, local_heads, HEAD), jnp.float32)
        (d_keys, d_values), d_queries = lax.scan(
            attend_back, (zero_heads, zero_heads), (query_blocks, image_blocks, log_sums, d_blocks)
        )
        d_query_low = d_queries.reshape(length, head_cols).astype(jnp.bfloat16)
        d_key_low = d_keys.reshape(length, head_cols).astype(jnp.bfloat16)
        d_value_low = d_values.reshape(length, head_cols).astype(jnp.bfloat16)
        d_projected = jnp.stack([d_query_low, d_key_low, d_value_low])
        qkv_term = jnp.einsum(
            "td,cte->dce", gathered, d_projected, preferred_element_type=jnp.float32
        )
        d_normed = lax.psum_scatter(
            jnp.einsum(
                "cte,dce->td", d_projected, qkv_weight, preferred_element_type=jnp.float32
            ).astype(jnp.bfloat16),
            "tensor",
            scatter_dimension=0,
            tiled=True,
        ).astype(jnp.float32)
        d_tokens, gain_one_grad, shift_one_grad = norm_pull(d_normed)
        input_grads.append(d_tokens + d_middle)
        vector_terms = vector_terms + jnp.stack(
            [
                gain_one_grad,
                shift_one_grad,
                jnp.sum(d_middle, 0),
                gain_two_grad,
                shift_two_grad,
                jnp.sum(cotangent, 0),
            ]
        )
        bias_terms = bias_terms + jnp.concatenate(
            [
                jnp.sum(d_query_low, 0, dtype=jnp.float32),
                jnp.sum(d_value_low, 0, dtype=jnp.float32),
                jnp.sum(d_hidden, 0, dtype=jnp.float32),
            ]
        )
        local_terms = (qkv_term, out_term, up_term, down_term)
        owned = (
            lax.psum_scatter(
                local_terms[0].astype(jnp.bfloat16), "dp", scatter_dimension=0, tiled=True
            ).astype(jnp.float32),
            lax.psum_scatter(
                local_terms[1].astype(jnp.bfloat16), "dp", scatter_dimension=1, tiled=True
            ).astype(jnp.float32),
            lax.psum_scatter(
                local_terms[2].astype(jnp.bfloat16), "dp", scatter_dimension=0, tiled=True
            ).astype(jnp.float32),
            lax.psum_scatter(
                local_terms[3].astype(jnp.bfloat16), "dp", scatter_dimension=1, tiled=True
            ).astype(jnp.float32),
        )
        weight_sums = tuple((total + term for total, term in zip(weight_sums, owned)))
    qkv_grad, out_grad, up_grad, down_grad = weight_sums
    tensor_index = lax.axis_index("tensor")
    placed = jnp.where(jnp.arange(splits)[:, None] == tensor_index, bias_terms[None, :], 0.0)
    vec_grad, bias_table = lax.psum((vector_terms, placed), ("dp", "tensor"))
    bias_grad = lax.dynamic_slice_in_dim(bias_table, tensor_index, 1, 0)
    qkv_second_new, qkv_master_new = adam_update(
        qkv_master, qkv_moment, qkv_second, qkv_grad, 0.09, 0.1
    )
    out_second_new, out_master_new = adam_update(
        out_master, out_moment, out_second, out_grad, 0.4, 0.1
    )
    up_second_new, up_master_new = adam_update(up_master, up_moment, up_second, up_grad, 0.09, 0.1)
    down_second_new, down_master_new = adam_update(
        down_master, down_moment, down_second, down_grad, 0.045, 0.1
    )
    vec_second_new, vec_master_new = adam_update(
        vec_master, vec_moment, vec_second, vec_grad, 0.6, 0.0
    )
    bias_second_new, bias_master_new = adam_update(
        bias_master, bias_moment, bias_second, bias_grad, 0.5, 0.0
    )
    block_output = jnp.stack(block_outputs)[:, None]
    input_grad = jnp.stack(input_grads)[:, None]
    return (
        block_output,
        input_grad,
        qkv_grad,
        qkv_second_new,
        qkv_master_new,
        out_grad,
        out_second_new,
        out_master_new,
        up_grad,
        up_second_new,
        up_master_new,
        down_grad,
        down_second_new,
        down_master_new,
        vec_grad,
        vec_second_new,
        vec_master_new,
        bias_grad,
        bias_second_new,
        bias_master_new,
    )


LANES = 128
TILE = 128
SPAN = 256
WIDE = 1152
BATCH = 8


def lane_window(head):
    first = head * HEAD
    low = first // LANES * LANES
    high = -(-(first + HEAD) // LANES) * LANES
    return low, high


def head_mask(head, rows):
    low, high = lane_window(head)
    lane = lax.broadcasted_iota(jnp.int32, (rows, high - low), 1) + low
    return (lane >= head * HEAD) & (lane < head * HEAD + HEAD)


def head_columns(head, columns):
    low, high = lane_window(head)
    high = min(high, columns)
    return slice(low, high), head_mask(head, TILE)[:, : high - low]


def padded(columns):
    return -(-columns // LANES) * LANES


def tile_spans(ids_smem, ids_ref, index, tiles):
    first_id = ids_smem[index * TILE]
    last_id = ids_smem[index * TILE + TILE - 1]
    ids = ids_ref[...]
    begin = jnp.sum((ids < first_id).astype(jnp.int32)) // TILE
    end = (jnp.sum((ids <= last_id).astype(jnp.int32)) + TILE - 1) // TILE
    count = (end - begin + 1) // 2
    return jnp.minimum(begin, tiles - 2 * count), count


def ids_column(ids_ref, index):
    row = ids_ref[:, pl.ds(pl.multiple_of(index * TILE, TILE), TILE)].astype(jnp.float32)
    square = jnp.broadcast_to(row, (TILE, TILE)).T
    return jnp.concatenate([square] * (SPAN // TILE), axis=1).astype(jnp.int32)


NT = (((1,), (1,)), ((), ()))
TN = (((0,), (0,)), ((), ()))


def attend_kernel(heads, length, ids_smem, ids_ref, q_ref, k_ref, v_ref, o_ref, lse_ref, top, total, acc):
    index = pl.program_id(0)
    columns = heads * HEAD
    scale = HEAD ** (-0.5) * math.log2(math.e)
    begin, count = tile_spans(ids_smem, ids_ref, index, length // TILE)
    own_ids = ids_column(ids_ref, index)
    top[...] = jnp.full(top.shape, mask_fill, jnp.float32)
    total[...] = jnp.zeros(total.shape, jnp.float32)
    acc[...] = jnp.zeros(acc.shape, jnp.float32)

    def window(low, high):
        return slice(low, min(high, columns))

    def step(item, carry):
        place = pl.multiple_of((begin + 2 * item) * TILE, TILE)
        keys = pl.ds(place, SPAN)
        same = own_ids == ids_ref[:, keys]
        for first in range(0, heads, BATCH):
            batch = range(first, min(first + BATCH, heads))
            held_scores = []
            for head in batch:
                cols, mask = head_columns(head, columns)
                query = q_ref[:, cols]
                query = jnp.where(mask, query, jnp.zeros_like(query))
                scores = lax.dot_general(query, k_ref[keys, cols], NT, preferred_element_type=jnp.float32)
                held_scores.append(jnp.where(same, scores * scale, mask_fill))
            tops = [jnp.maximum(top[head], jnp.max(scores, -1, keepdims=True)) for head, scores in zip(batch, held_scores)]
            parts = [
                jnp.exp2(scores - jnp.concatenate([now] * (SPAN // LANES), axis=1)) for now, scores in zip(tops, held_scores)
            ]
            sums = [jnp.sum(part, -1, keepdims=True) for part in parts]
            mixes = [
                jnp.dot(part.astype(jnp.bfloat16), v_ref[keys, head_columns(head, columns)[0]], preferred_element_type=jnp.float32)
                for head, part in zip(batch, parts)
            ]
            for head, now, part_sum, mixed in zip(batch, tops, sums, mixes):
                cols, mask = head_columns(head, columns)
                shrink = jnp.exp2(top[head] - now)
                total[head] = total[head] * shrink + part_sum
                top[head] = now
                width = cols.stop - cols.start
                wide = jnp.concatenate([shrink] * ((width + LANES - 1) // LANES), axis=1)[:, :width]
                held = acc[:, cols]
                acc[:, cols] = jnp.where(mask, held * wide + mixed, held)
        return carry

    lax.fori_loop(0, count, step, 0)
    sums = jnp.zeros((TILE, LANES), jnp.float32)
    lane = lax.broadcasted_iota(jnp.int32, (TILE, LANES), 1)
    for head in range(heads):
        low, high = lane_window(head)
        high = min(high, columns)
        cols = slice(low, high)
        mask = head_mask(head, TILE)[:, : high - low]
        inverse = 1.0 / total[head]
        wide = jnp.concatenate([inverse] * ((high - low + LANES - 1) // LANES), axis=1)[:, : high - low]
        held = acc[:, cols]
        acc[:, cols] = jnp.where(mask, held * wide, held)
        sums = jnp.where(lane == head, top[head] + jnp.log2(total[head]), sums)
    o_ref[...] = acc[...].astype(o_ref.dtype)
    lse_ref[...] = sums.T[:heads]


def attend(ids, query, key, value):
    length, columns = query.shape
    heads = columns // HEAD
    tiles = length // TILE
    whole = pl.BlockSpec((length, columns), lambda i, s: (0, 0))
    block = pl.BlockSpec((TILE, columns), lambda i, s: (i, 0))
    return pl.pallas_call(
        partial(attend_kernel, heads, length),
        grid_spec=pltpu.PrefetchScalarGridSpec(
            num_scalar_prefetch=1,
            grid=(tiles,),
            in_specs=[pl.BlockSpec((1, length), lambda i, s: (0, 0)), block, whole, whole],
            out_specs=[block, pl.BlockSpec((heads, TILE), lambda i, s: (0, i))],
            scratch_shapes=[
                pltpu.VMEM((heads, TILE, LANES), jnp.float32),
                pltpu.VMEM((heads, TILE, LANES), jnp.float32),
                pltpu.VMEM((TILE, columns), jnp.float32),
            ],
        ),
        out_shape=[
            jax.ShapeDtypeStruct((length, columns), jnp.bfloat16),
            jax.ShapeDtypeStruct((heads, length), jnp.float32),
        ],
        compiler_params=pltpu.CompilerParams(vmem_limit_bytes=36 << 20),
        cost_estimate=pl.CostEstimate(flops=4 * 10**9, bytes_accessed=10**6, transcendentals=0),
    )(ids, ids.reshape(1, length), query, key, value)


def attend_back_kernel(
    heads, length, ids_smem, ids_ref, q_ref, k_ref, v_ref, o_ref, g_ref, lse_ref,
    dq_ref, dk_ref, dv_ref, delta, dq_acc, dk_acc, dv_acc,
):
    index = pl.program_id(0)
    columns = heads * HEAD
    natural = HEAD ** (-0.5)
    scale = natural * math.log2(math.e)
    tiles = length // TILE
    begin, count = tile_spans(ids_smem, ids_ref, index, tiles)
    own_ids = ids_column(ids_ref, index)

    @pl.when(index == 0)
    def _():
        dq_acc[...] = jnp.zeros(dq_acc.shape, jnp.float32)
        row = lax.broadcasted_iota(jnp.int32, (heads, columns), 0)
        lane = lax.broadcasted_iota(jnp.int32, (heads, columns), 1)
        pick = ((lane >= row * HEAD) & (lane < row * HEAD + HEAD)).astype(jnp.bfloat16)
        product = g_ref[...].astype(jnp.float32) * o_ref[...].astype(jnp.float32)
        coarse = product.astype(jnp.bfloat16)
        fine = (product - coarse.astype(jnp.float32)).astype(jnp.bfloat16)
        delta[...] = lax.dot_general(pick, coarse, NT, preferred_element_type=jnp.float32) + lax.dot_general(
            pick, fine, NT, preferred_element_type=jnp.float32
        )

    dk_acc[...] = jnp.zeros(dk_acc.shape, jnp.float32)
    dv_acc[...] = jnp.zeros(dv_acc.shape, jnp.float32)

    def step(item, carry):
        place = pl.multiple_of((begin + 2 * item) * TILE, TILE)
        rows = pl.ds(place, SPAN)
        same = own_ids == ids_ref[:, rows]
        for first in range(0, heads, BATCH):
            batch = range(first, min(first + BATCH, heads))
            keys, scores, d_probs = [], [], []
            for head in batch:
                cols, mask = head_columns(head, columns)
                key = k_ref[:, cols]
                keys.append(jnp.where(mask, key, jnp.zeros_like(key)))
                value = v_ref[:, cols]
                value = jnp.where(mask, value, jnp.zeros_like(value))
                scores.append(lax.dot_general(keys[-1], q_ref[rows, cols], NT, preferred_element_type=jnp.float32))
                d_probs.append(lax.dot_general(value, g_ref[rows, cols], NT, preferred_element_type=jnp.float32))
            probs = [
                jnp.exp2(jnp.where(same, score * scale, mask_fill) - lse_ref[head : head + 1, rows])
                for head, score in zip(batch, scores)
            ]
            d_scores = [
                (prob * (d_prob - delta[head : head + 1, rows])).astype(jnp.bfloat16)
                for head, prob, d_prob in zip(batch, probs, d_probs)
            ]
            for head, key, prob, d_score in zip(batch, keys, probs, d_scores):
                cols, mask = head_columns(head, columns)
                d_value = jnp.dot(prob.astype(jnp.bfloat16), g_ref[rows, cols], preferred_element_type=jnp.float32)
                d_key = jnp.dot(d_score, q_ref[rows, cols], preferred_element_type=jnp.float32)
                d_query = lax.dot_general(d_score, key, TN, preferred_element_type=jnp.float32)
                dv_acc[:, cols] += jnp.where(mask, d_value, 0.0)
                dk_acc[:, cols] += jnp.where(mask, d_key, 0.0)
                dq_acc[rows, cols] += d_query
        return carry

    lax.fori_loop(0, count, step, 0)
    dk_ref[...] = (dk_acc[...] * natural).astype(dk_ref.dtype)
    dv_ref[...] = dv_acc[...].astype(dv_ref.dtype)

    @pl.when(index == tiles - 1)
    def _():
        dq_ref[...] = (dq_acc[...] * natural).astype(dq_ref.dtype)


def attend_back(ids, query, key, value, attended, grad, lse):
    length, columns = query.shape
    heads = columns // HEAD
    tiles = length // TILE
    whole = pl.BlockSpec((length, columns), lambda i, s: (0, 0))
    block = pl.BlockSpec((TILE, columns), lambda i, s: (i, 0))
    out = jax.ShapeDtypeStruct((length, columns), jnp.bfloat16)
    return pl.pallas_call(
        partial(attend_back_kernel, heads, length),
        grid_spec=pltpu.PrefetchScalarGridSpec(
            num_scalar_prefetch=1,
            grid=(tiles,),
            in_specs=[
                pl.BlockSpec((1, length), lambda i, s: (0, 0)),
                whole,
                block,
                block,
                whole,
                whole,
                pl.BlockSpec((heads, length), lambda i, s: (0, 0)),
            ],
            out_specs=[whole, block, block],
            scratch_shapes=[
                pltpu.VMEM((heads, length), jnp.float32),
                pltpu.VMEM((length, columns), jnp.float32),
                pltpu.VMEM((TILE, columns), jnp.float32),
                pltpu.VMEM((TILE, columns), jnp.float32),
            ],
        ),
        out_shape=[out, out, out],
        compiler_params=pltpu.CompilerParams(vmem_limit_bytes=36 << 20),
        cost_estimate=pl.CostEstimate(flops=2 * 10**9, bytes_accessed=10**6, transcendentals=0),
    )(ids, ids.reshape(1, length), query, key, value, attended, grad, lse)


def column_call(kernel, ins, outs, columns, flops, scratch=()):
    wide = min(WIDE, padded(columns))
    steps = -(-columns // wide)

    def spec(shape, cut):
        if cut:
            return pl.BlockSpec(shape[:-1] + (wide,), lambda i: (0,) * (len(shape) - 1) + (i,))
        return pl.BlockSpec(shape, lambda i: (0,) * len(shape))

    size = sum(math.prod(a.shape) * a.dtype.itemsize for a, _ in ins) + sum(
        math.prod(a.shape) * a.dtype.itemsize for a in outs
    )
    return pl.pallas_call(
        kernel,
        grid=(steps,),
        in_specs=[spec(a.shape, cut) for a, cut in ins],
        out_specs=[spec(a.shape, True) for a in outs],
        out_shape=outs,
        scratch_shapes=list(scratch),
        compiler_params=pltpu.CompilerParams(vmem_limit_bytes=44 << 20),
        cost_estimate=pl.CostEstimate(flops=flops // 8, bytes_accessed=size // 8, transcendentals=0),
    )(*[a for a, _ in ins])


def hidden_kernel(x_ref, w_ref, b_ref, active_ref, slope_ref):
    rows = 256
    for block in range(x_ref.shape[0] // rows):
        part = pl.ds(block * rows, rows)
        value = jnp.dot(x_ref[part, :], w_ref[...], preferred_element_type=jnp.float32) + b_ref[...]
        active, slope = gelu_pair(value)
        active_ref[part, :] = active.astype(jnp.bfloat16)
        slope_ref[part, :] = slope.astype(jnp.bfloat16)


def hidden_units(x, weight, bias):
    tokens, columns = x.shape[0], weight.shape[1]
    out = jax.ShapeDtypeStruct((tokens, columns), jnp.bfloat16)
    ins = [(x, False), (weight, True), (bias.reshape(1, columns), True)]
    return column_call(hidden_kernel, ins, [out, out], columns, 2 * tokens * x.shape[1] * columns)


def hidden_back_kernel(x_ref, w_ref, slope_ref, grad_ref, sum_ref):
    rows = 256
    total = jnp.zeros(sum_ref.shape, jnp.float32)
    for block in range(x_ref.shape[0] // rows):
        part = pl.ds(block * rows, rows)
        value = jnp.dot(x_ref[part, :], w_ref[...], preferred_element_type=jnp.float32)
        value = value * slope_ref[part, :].astype(jnp.float32)
        grad_ref[part, :] = value.astype(jnp.bfloat16)
        total = total + jnp.sum(value, 0, keepdims=True)
    sum_ref[...] = total


def hidden_back(x, weight, slope):
    tokens, columns = x.shape[0], weight.shape[1]
    outs = [jax.ShapeDtypeStruct((tokens, columns), jnp.bfloat16), jax.ShapeDtypeStruct((1, columns), jnp.float32)]
    ins = [(x, False), (weight, True), (slope, True)]
    return column_call(hidden_back_kernel, ins, outs, columns, 2 * tokens * x.shape[1] * columns)


def grad_kernel(chunks, stacked, x_ref, *refs):
    core = lax.axis_index("dp") % 2
    count = len(refs) - 4 if stacked else (len(refs) - 2) // 3
    turned, result = refs[-2:]
    dy_refs = refs[:count]
    outs = refs[count:-2]

    @pl.when(pl.program_id(0) == 0)
    def _():
        turned[...] = x_ref[...].T

    rows = turned.shape[0] // chunks
    for number, dy_ref in enumerate(dy_refs):
        if stacked:
            sent_ref, kept_ref = outs[0].at[number], outs[1].at[number]
        else:
            sent_ref, kept_ref = outs[number], outs[count + number]
        result[...] = jnp.dot(turned[...], dy_ref[...], preferred_element_type=jnp.float32)
        for spot in range(chunks // 2):
            sent = pl.multiple_of((2 * spot + 1 - core) * rows, 8)
            kept = pl.multiple_of((2 * spot + core) * rows, 8)
            sent_ref[spot] = result[pl.ds(sent, rows), :].astype(jnp.bfloat16)
            kept_ref[spot] = result[pl.ds(kept, rows), :].astype(jnp.bfloat16)


def weight_grads(x, parts, stacked=False):
    tokens, features = x.shape
    columns = parts[0].shape[1]
    count = len(parts)
    wide = min(WIDE, padded(columns))
    shape = (8, features // 16, columns)
    outs = [jax.ShapeDtypeStruct(shape, jnp.bfloat16)] * (2 * count)
    if stacked:
        outs = [jax.ShapeDtypeStruct((count,) + shape, jnp.bfloat16)] * 2
    results = column_call(
        partial(grad_kernel, 16, stacked),
        [(x, False)] + [(part, True) for part in parts],
        outs,
        columns,
        2 * tokens * features * columns * count,
        [pltpu.VMEM((features, tokens), jnp.bfloat16), pltpu.VMEM((features, wide), jnp.float32)],
    )
    return results if stacked else (results[:count], results[count:])


def place_kernel(leads, ordered, steps, *refs):
    pieces = refs[: len(steps)]
    outs = refs[len(steps) : len(steps) + leads]
    sems = refs[len(steps) + leads]
    spot = lax.axis_index("dp")
    z, y, core = spot // 4, spot // 2 % 2, spot % 2
    copies = []
    for piece, (first_slot, y_step, core_step) in zip(pieces, steps):
        column = (y + y_step) % 2 * 2 + (core + core_step) % 2
        for slot in range(piece.shape[0]):
            number = first_slot + slot
            row = (number if ordered else (z + 4 - number) % 4) * 4 + column
            for lead in range(leads):
                copy = pltpu.make_async_copy(piece.at[slot, lead], outs[lead].at[row], sems.at[len(copies)])
                copy.start()
                copies.append(copy)
    for copy in copies:
        copy.wait()


def place(planes, ordered):
    pieces = sum(planes, [])
    leads, rows, columns = pieces[0].shape[1:]
    slots = pieces[0].shape[0]
    steps = [(start, step % 2, step // 2) for start in range(0, 4, slots) for step in range(4)]
    size = 16 * leads * rows * padded(columns) * 2
    placed = pl.pallas_call(
        partial(place_kernel, leads, ordered, steps),
        in_specs=[pl.BlockSpec(memory_space=pl.ANY)] * len(pieces),
        out_specs=[pl.BlockSpec(memory_space=pltpu.VMEM)] * leads,
        out_shape=[jax.ShapeDtypeStruct((16, rows, columns), jnp.bfloat16)] * leads,
        scratch_shapes=[pltpu.SemaphoreType.DMA((16 * leads,))],
        compiler_params=pltpu.CompilerParams(vmem_limit_bytes=size * 3 // 2 + (2 << 20)),
        cost_estimate=pl.CostEstimate(flops=0, bytes_accessed=size // 4, transcendentals=0),
    )(*pieces)
    return [part.reshape(16 * rows, columns) for part in placed]


def swap_x(value):
    return lax.ppermute(value, "tensor", [(0, 1), (1, 0)])


def swap_y(value):
    return lax.ppermute(value, "dp", [(spot, spot ^ 2) for spot in range(16)])


def swap_core(value):
    return lax.ppermute(value, "dp", [(spot, spot ^ 1) for spot in range(16)])


def move_z(value, steps):
    return lax.ppermute(value, "dp", [(spot, (spot + 4 * steps) % 16) for spot in range(16)])


def tie(*values):
    return lax.optimization_barrier(values)


def both_cores(parts):
    return parts + [swap_core(part) for part in parts]


def add_low(*terms):
    total = terms[0].astype(jnp.float32)
    for term in terms[1:]:
        total = total + term.astype(jnp.float32)
    return total.astype(jnp.bfloat16)


def part_of(value, index, axis):
    return lax.dynamic_index_in_dim(value, index, axis, keepdims=False)


def y_parts(value):
    spot = lax.axis_index("dp")
    split = value.reshape((value.shape[0] // 2, 2) + value.shape[1:])
    return part_of(split, spot // 2 % 2, 1), part_of(split, 1 - spot // 2 % 2, 1)


class Planes:
    def __init__(self, own, other):
        half = own.shape[0] // 2
        self.near_own, near_own = y_parts(own[:half])
        self.near_other, near_other = y_parts(other[:half])
        self.far_own = own[half:]
        self.sent = [jnp.stack([near_own, near_other]), other[half:]]

    def first(self):
        self.got = [swap_y(self.sent[0]), swap_x(self.sent[1])]

    def middle(self):
        self.near_own = add_low(self.near_own, self.got[0][0])
        self.far_own, far = y_parts(add_low(self.far_own, self.got[1]))
        self.sent = [add_low(self.near_other, self.got[0][1]), far]

    def second(self):
        self.got = [swap_x(self.sent[0]), swap_y(self.sent[1])]

    def total(self):
        return jnp.concatenate([add_low(self.near_own, self.got[0]), add_low(self.far_own, self.got[1])])


def scatter_z(value):
    groups = [[spot + 4 * z for z in range(4)] for spot in range(4)]
    return lax.psum_scatter(value, "dp", axis_index_groups=groups)


def send_z(value):
    z = lax.axis_index("dp") // 4
    return [part_of(value, z, 0)] + [move_z(part_of(value, (z + steps) % 4, 0), steps) for steps in (1, 2, 3)]


def sum_terms(terms):
    total = terms[0].astype(jnp.float32)
    for term in terms[1:]:
        total = total + term.astype(jnp.float32)
    return total


def sum_everywhere(value):
    value = value + swap_core(value)
    value = value + swap_y(value)
    value = value + swap_x(value)
    return value + move_z(value, 1) + move_z(value, 2) + move_z(value, 3)


def norm_forward(values):
    centre = values - jnp.mean(values, -1, keepdims=True)
    inverse = lax.rsqrt(jnp.mean(centre * centre, -1, keepdims=True) + norm_eps)
    return centre * inverse, inverse


def norm_back(grad, hat, inverse, gain):
    scaled = grad * gain
    mean_one = jnp.mean(scaled, -1, keepdims=True)
    mean_two = jnp.mean(scaled * hat, -1, keepdims=True)
    return (scaled - mean_one - hat * mean_two) * inverse


def gelu_pair(value):
    inner = math.sqrt(2.0 / math.pi)
    squared = value * value
    bent = jnp.tanh(inner * (value + 0.044715 * value * squared))
    half = 0.5 * (1.0 + bent)
    slope = half + 0.5 * value * (1.0 - bent * bent) * inner * (1.0 + 3 * 0.044715 * squared)
    return value * half, slope


def row_layer(
    block_input,
    image_ids,
    out_cotangent,
    qkv_master,
    qkv_moment,
    qkv_second,
    out_master,
    out_moment,
    out_second,
    up_master,
    up_moment,
    up_second,
    down_master,
    down_moment,
    down_second,
    vec_master,
    vec_moment,
    vec_second,
    bias_master,
    bias_moment,
    bias_second,
):
    low = jnp.bfloat16
    wide = jnp.float32
    mine = lax.axis_index("tensor")
    first = mine == 0
    half = block_input.shape[2]
    features = block_input.shape[3]
    head_cols = qkv_master.shape[2]

    def pick(pair, index):
        return lax.dynamic_index_in_dim(pair, index, 0, keepdims=False)

    def in_order(own, other, axis=0):
        return jnp.concatenate([jnp.where(first, own, other), jnp.where(first, other, own)], axis)

    def dot(spec, left, right):
        return jnp.einsum(spec, left, right, preferred_element_type=wide)

    inputs_own = pick(block_input[:, 0], mine)
    inputs_sent = pick(block_input[:, 0], 1 - mine)
    cot_own = pick(out_cotangent[:, 0], mine)
    cot_sent = pick(out_cotangent[:, 0], 1 - mine)
    inputs_low = inputs_sent.astype(low)
    early_shard = jnp.stack([qkv_master[:, 0], qkv_master[:, 1], qkv_master[:, 2]]).astype(low)
    early_shard, inputs_low = tie(early_shard, inputs_low)
    inputs_got = swap_x(inputs_low)
    out_whole = lax.all_gather(out_master.T.astype(low), ("tensor", "dp")).reshape(2, features, head_cols)
    early_one = move_z(early_shard, 1)
    early_three = move_z(early_shard, 3)
    ids_got = swap_x(pick(image_ids[:, 0], 1 - mine))
    biases_got = swap_x(bias_master)
    early_shard, early_one = tie(early_shard, early_one)
    early_two = move_z(early_shard, 2)
    near = jnp.stack([early_shard, early_one])
    near_y, near_x = swap_y(near), swap_x(near)
    late_shard = jnp.stack([up_master, down_master.T]).astype(low)
    late_shard, early_two, inputs_got = tie(late_shard, early_two, inputs_got)
    late_one = move_z(late_shard, 1)
    late_three = move_z(late_shard, 3)
    far = jnp.stack([early_two, early_three])
    far_y, far_x = swap_y(far), swap_x(far)
    near_xy, far_yx = swap_y(near_x), swap_x(far_y)
    early_own = place([both_cores([near, near_y]), both_cores([far, far_y])], False)
    late_shard, late_one, late_three = tie(late_shard, late_one, late_three)
    late_two = move_z(late_shard, 2)
    inputs = in_order(inputs_own, inputs_got.astype(wide))
    ids = in_order(pick(image_ids[:, 0], mine), ids_got)
    biases = jnp.concatenate([bias_master, biases_got])

    hat_one, inverse_one = norm_forward(inputs)
    normed = (hat_one * vec_master[0] + vec_master[1]).astype(low)
    def project(g, weights):
        query = (dot("td,de->te", normed, weights[0]) + biases[g, :head_cols]).astype(low)
        key = dot("td,de->te", normed, weights[1]).astype(low)
        value = (dot("td,de->te", normed, weights[2]) + biases[g, head_cols : 2 * head_cols]).astype(low)
        return query, key, value

    projected = [project(0, early_own), None]
    attended, log_sums = [None, None], [None, None]
    attended[0], log_sums[0] = attend(ids, *projected[0])
    others = [both_cores([near_x, near_xy]), both_cores([far_x, far_yx])]
    others, attended[0], late_two = tie(others, attended[0], late_two)
    early_other = place(others, False)
    late_z = [late_shard, late_one, late_two, late_three]
    up_z = jnp.stack([part[:1] for part in late_z])
    down_z = jnp.stack([part[1:] for part in late_z])
    early_other, up_z, down_z = tie(early_other, up_z, down_z)
    up_x, up_y = swap_x(up_z), swap_y(up_z)
    projected[1] = project(1, early_other)
    attended[1], log_sums[1] = attend(ids, *projected[1])
    query_weight, key_weight, value_weight = zip(early_own, early_other)
    attended[1], up_x, up_y = tie(attended[1], up_x, up_y)
    up_xy = swap_y(up_x)
    down_x = swap_x(down_z)
    out_weight = [pick(out_whole, mine), pick(out_whole, 1 - mine)]
    attn_sum = sum(dot("te,de->td", attended[g], out_weight[g]) for g in range(2)) + vec_master[2]
    middle = inputs + attn_sum
    hat_two, inverse_two = norm_forward(middle)
    normed_two = (hat_two * vec_master[3] + vec_master[4]).astype(low)
    normed_two, up_xy, down_x = tie(normed_two, up_xy, down_x)
    down_y = swap_y(down_z)
    cot_got = swap_x(cot_sent.astype(low))
    up_weight = [place([both_cores([up_z, up_y])], False)[0], place([both_cores([up_x, up_xy])], False)[0]]
    active, slope = [None, None], [None, None]
    active[0], slope[0] = hidden_units(normed_two, up_weight[0], biases[0, 2 * head_cols :])
    normed_two, active[0], down_y, cot_got = tie(normed_two, active[0], down_y, cot_got)
    down_xy = swap_y(down_x)
    active[1], slope[1] = hidden_units(normed_two, up_weight[1], biases[1, 2 * head_cols :])
    cot_row = in_order(cot_own, cot_got.astype(wide))
    cot_low = cot_row.astype(low)
    down_sent, down_kept = weight_grads(cot_low, active)
    down_weight = [place([both_cores([down_z, down_y])], False)[0], place([both_cores([down_x, down_xy])], False)[0]]
    added = attn_sum + sum(dot("tf,df->td", active[g], down_weight[g]) for g in range(2)) + vec_master[5]
    added = added.reshape(2, half, features)
    out_here = inputs_own + pick(added, mine)
    out_there = pick(block_input[:, 0], 1 - mine) + swap_x(pick(added, 1 - mine).astype(low)).astype(wide)
    block_output = in_order(out_here[None], out_there[None])[:, None]

    own, other = 0, 1
    down_core = [swap_core(part) for part in down_sent]
    d_hidden, hidden_sums = [None, None], [None, None]
    d_hidden[own], hidden_sums[own] = hidden_back(cot_low, down_weight[own], slope[own])
    d_hidden[own], down_core = tie(d_hidden[own], down_core)
    down = Planes(*[add_low(down_kept[g], down_core[g]) for g in range(2)])
    cot_late, down.sent = tie(cot_low, down.sent)
    down.first()
    d_hidden[other], hidden_sums[other] = hidden_back(cot_late, down_weight[other], slope[other])
    up_sent, up_kept = weight_grads(normed_two, d_hidden)
    up_sent, down.got = tie(up_sent, down.got)
    up_core = [swap_core(part) for part in up_sent]
    down.middle()
    d_hidden, down.sent = tie(d_hidden, down.sent)
    down.second()
    d_normed_two = sum(dot("tf,df->td", d_hidden[g], up_weight[g]) for g in range(2))
    d_normed_two, up_core, down.got = tie(d_normed_two, up_core, down.got)
    up = Planes(*[add_low(up_kept[g], up_core[g]) for g in range(2)])
    down_total = down.total()
    d_normed_two, up.sent, down_total = tie(d_normed_two, up.sent, down_total)
    up.first()
    down_term = scatter_z(down_total)
    mid_added = norm_back(d_normed_two, hat_two, inverse_two, vec_master[3])
    d_middle = cot_row + mid_added
    mid_low = d_middle.astype(low)
    d_attended = [dot("td,de->te", mid_low, out_weight[g]).astype(low) for g in range(2)]
    out_sent, out_kept = weight_grads(mid_low, attended)
    d_attended[other], out_sent = tie(d_attended[other], out_sent)
    out_core = [swap_core(part) for part in out_sent]

    def back(g, grad):
        return attend_back(ids, *projected[g], attended[g], grad, log_sums[g])

    d_other = back(other, d_attended[other])
    d_other, out_core, up.got = tie(d_other, out_core, up.got)
    up.middle()
    out_other = add_low(out_kept[other], out_core[other])
    out_own = add_low(out_kept[own], out_core[own])
    d_other, up.sent, out_other = tie(d_other, up.sent, out_other)
    up.second()
    out_there_x = swap_x(out_other)
    qkv_sent, qkv_kept = [None, None], [None, None]
    qkv_sent[other], qkv_kept[other] = weight_grads(normed, d_other, True)

    def normed_part(parts, g):
        weights = (query_weight, key_weight, value_weight)
        return sum(dot("te,de->td", part, weight[g]) for part, weight in zip(parts, weights))

    d_other, qkv_sent[other] = tie(d_other, qkv_sent[other])
    qkv_core_other = swap_core(qkv_sent[other])
    d_normed_other = normed_part(d_other, other)
    d_normed_other, up.got, out_there_x, qkv_core_other = tie(d_normed_other, up.got, out_there_x, qkv_core_other)
    up_total = up.total()
    out_here, out_there = y_parts(add_low(out_own, out_there_x))
    qkv_other_here, qkv_other_there = zip(*[y_parts(part) for part in add_low(qkv_kept[other], qkv_core_other)])
    qkv_other_there = jnp.stack(qkv_other_there)
    d_attended[own], up_total, out_there, qkv_other_there = tie(
        d_attended[own], up_total, out_there, qkv_other_there
    )
    up_term = scatter_z(up_total)
    out_there_y = swap_y(out_there)
    qkv_there_y = swap_y(qkv_other_there)
    d_own = back(own, d_attended[own])
    d_own, qkv_there_y, out_there_y = tie(tuple(d_own), qkv_there_y, out_there_y)
    qkv_other = add_low(jnp.stack(qkv_other_here), qkv_there_y)
    out_total = add_low(out_here, out_there_y)
    d_own, qkv_other, out_total = tie(d_own, qkv_other, out_total)
    qkv_there_x = swap_x(qkv_other)
    out_term = scatter_z(out_total)
    qkv_sent[own], qkv_kept[own] = weight_grads(normed, d_own, True)
    d_own, qkv_sent[own] = tie(d_own, qkv_sent[own])
    qkv_core_own = swap_core(qkv_sent[own])
    d_normed_own = normed_part(d_own, own)
    d_normed_own, qkv_core_own = tie(d_normed_own, qkv_core_own)
    qkv_here, qkv_there = zip(*[y_parts(part) for part in add_low(qkv_kept[own], qkv_core_own)])
    qkv_there = jnp.stack(qkv_there)
    d_normed_own, qkv_there = tie(d_normed_own, qkv_there)
    qkv_there_y = swap_y(qkv_there)
    d_normed = d_normed_other + d_normed_own
    down_grad = down_term.astype(wide).T
    up_grad = up_term.astype(wide)
    out_grad = out_term.astype(wide).T
    in_added = (mid_added + norm_back(d_normed, hat_one, inverse_one, vec_master[0])).reshape(2, half, features)
    grad_here = cot_own + pick(in_added, mine)
    grad_there = cot_sent + swap_x(pick(in_added, 1 - mine).astype(low)).astype(wide)
    input_grad = in_order(grad_here[None], grad_there[None])[:, None]

    early = jnp.concatenate(
        [
            jnp.sum(d_middle, 0),
            jnp.sum(d_normed_two * hat_two, 0),
            jnp.sum(d_normed_two, 0),
            jnp.sum(out_cotangent[:, 0], (0, 1)),
        ]
    )

    def bias_rows(sums):
        return jnp.where(first, jnp.concatenate(sums), jnp.concatenate(sums[::-1]))

    sums = jnp.concatenate(
        [
            jnp.sum(d_normed * hat_one, 0),
            jnp.sum(d_normed, 0),
            early,
            bias_rows([jnp.sum(part[0], 0, dtype=wide) for part in (d_own, d_other)]),
            bias_rows([jnp.sum(part[2], 0, dtype=wide) for part in (d_own, d_other)]),
            bias_rows([part[0] for part in hidden_sums]),
        ]
    )
    sums, qkv_there_y, qkv_there_x = tie(sums, qkv_there_y, qkv_there_x)
    qkv_terms = send_z(add_low(jnp.stack(qkv_here), qkv_there_y, qkv_there_x).transpose(1, 0, 2, 3))
    qkv_grad = sum_terms(qkv_terms).transpose(1, 0, 2)
    sums = sum_everywhere(sums[None])[0]
    vec_grad = sums[: 6 * features].reshape(6, features)

    def group(start, size):
        return pick(sums[start : start + 2 * size].reshape(2, size), mine)

    start = 6 * features
    bias_grad = jnp.concatenate(
        [
            group(start, head_cols),
            group(start + 2 * head_cols, head_cols),
            group(start + 4 * head_cols, up_master.shape[1]),
        ]
    )[None]

    results = [block_output, input_grad]
    for master, moment, second, grad, rate, decay in (
        (qkv_master, qkv_moment, qkv_second, qkv_grad, 0.09, 0.1),
        (out_master, out_moment, out_second, out_grad, 0.4, 0.1),
        (up_master, up_moment, up_second, up_grad, 0.09, 0.1),
        (down_master, down_moment, down_second, down_grad, 0.045, 0.1),
        (vec_master, vec_moment, vec_second, vec_grad, 0.6, 0.0),
        (bias_master, bias_moment, bias_second, bias_grad, 0.5, 0.0),
    ):
        second_new, master_new = adam_update(master, moment, second, grad, rate, decay)
        results += [grad, second_new, master_new]
    return tuple(results)


def solution(mesh):
    placed = (
        P(None, "dp", "tensor", None),
        P(None, "dp", "tensor"),
        P(None, "dp", "tensor", None),
        P("dp", None, "tensor"),
        P("dp", None, "tensor"),
        P("dp", None, "tensor"),
        P("tensor", "dp"),
        P("tensor", "dp"),
        P("tensor", "dp"),
        P("dp", "tensor"),
        P("dp", "tensor"),
        P("dp", "tensor"),
        P("tensor", "dp"),
        P("tensor", "dp"),
        P("tensor", "dp"),
        P(),
        P(),
        P(),
        P("tensor", None),
        P("tensor", None),
        P("tensor", None),
    )
    by_rows = dict(mesh.shape) == {"dp": 16, "tensor": 2}
    return jax.shard_map(
        row_layer if by_rows else split_layer,
        mesh=mesh,
        in_specs=placed,
        out_specs=(
            P(None, "dp", "tensor", None),
            P(None, "dp", "tensor", None),
            P("dp", None, "tensor"),
            P("dp", None, "tensor"),
            P("dp", None, "tensor"),
            P("tensor", "dp"),
            P("tensor", "dp"),
            P("tensor", "dp"),
            P("dp", "tensor"),
            P("dp", "tensor"),
            P("dp", "tensor"),
            P("tensor", "dp"),
            P("tensor", "dp"),
            P("tensor", "dp"),
            P(),
            P(),
            P(),
            P("tensor", None),
            P("tensor", None),
            P("tensor", None),
        ),
        check_vma=False,
    )
```

```python
import math
from functools import partial

import jax
import jax.numpy as jnp
from jax import lax
from jax.experimental import pallas as pl
from jax.experimental.pallas import tpu as pltpu
from jax.sharding import PartitionSpec as P

HEAD = 72
STEP = 10


norm_eps = 1e-06
mask_fill = -1e30
beta_one = 0.9
beta_two = 0.95
adam_eps = 1e-08


def layer_norm(values, scale_vec, shift_vec):
    centre = values - jnp.mean(values, -1, keepdims=True)
    spread = jnp.mean(centre * centre, -1, keepdims=True)
    return centre * lax.rsqrt(spread + norm_eps) * scale_vec + shift_vec


def adam_update(master, moment, second, gradient, step_rate, weight_decay):
    first_moment = beta_one * moment.astype(jnp.float32) + (1.0 - beta_one) * gradient
    second_new = beta_two * second + (1.0 - beta_two) * gradient * gradient
    update = (
        first_moment
        / (1.0 - beta_one**STEP)
        / (jnp.sqrt(second_new / (1.0 - beta_two**STEP)) + adam_eps)
        + weight_decay * master
    )
    return (second_new, master - step_rate * update)


def split_layer(
    block_input,
    image_ids,
    out_cotangent,
    qkv_master,
    qkv_moment,
    qkv_second,
    out_master,
    out_moment,
    out_second,
    up_master,
    up_moment,
    up_second,
    down_master,
    down_moment,
    down_second,
    vec_master,
    vec_moment,
    vec_second,
    bias_master,
    bias_moment,
    bias_second,
):
    batches = block_input.shape[0]
    local_rows = block_input.shape[2]
    features = block_input.shape[3]
    splits = lax.axis_size("tensor")
    length = local_rows * splits
    head_cols = qkv_master.shape[2]
    local_heads = head_cols // HEAD
    block_rows = min(512, length)
    block_count = length // block_rows
    score_scale = HEAD ** (-0.5)
    biases = bias_master[0]
    query_bias = biases[:head_cols]
    value_bias = biases[head_cols : 2 * head_cols]
    hidden_bias = biases[2 * head_cols :]
    compute = (
        qkv_master.astype(jnp.bfloat16),
        out_master.astype(jnp.bfloat16),
        up_master.astype(jnp.bfloat16),
        down_master.astype(jnp.bfloat16),
    )
    gelu_tanh = partial(jax.nn.gelu, approximate=True)
    weight_sums = (
        jnp.zeros_like(qkv_master),
        jnp.zeros_like(out_master),
        jnp.zeros_like(up_master),
        jnp.zeros_like(down_master),
    )
    vector_terms = jnp.zeros((6, features), jnp.float32)
    bias_terms = jnp.zeros(biases.shape, jnp.float32)
    block_outputs = []
    input_grads = []
    for batch_index in range(batches):
        qkv_weight, out_weight, up_weight, down_weight = (
            lax.all_gather(compute[0], "dp", axis=0, tiled=True),
            lax.all_gather(compute[1], "dp", axis=1, tiled=True),
            lax.all_gather(compute[2], "dp", axis=0, tiled=True),
            lax.all_gather(compute[3], "dp", axis=1, tiled=True),
        )
        tokens_here = block_input[batch_index, 0]
        normed, norm_pull = jax.vjp(layer_norm, tokens_here, vec_master[0], vec_master[1])
        gathered, image_row = (
            lax.all_gather(normed.astype(jnp.bfloat16), "tensor", axis=0, tiled=True),
            lax.all_gather(image_ids[batch_index, 0], "tensor", axis=0, tiled=True),
        )
        projected = jnp.einsum(
            "td,dce->cte", gathered, qkv_weight, preferred_element_type=jnp.float32
        )
        queries = (projected[0] + query_bias).astype(jnp.bfloat16)
        key_rows = projected[1].astype(jnp.bfloat16)
        values = (projected[2] + value_bias).astype(jnp.bfloat16)
        key_heads = key_rows.reshape(length, local_heads, HEAD)
        value_heads = values.reshape(length, local_heads, HEAD)
        query_blocks = queries.reshape(block_count, block_rows, local_heads, HEAD)
        image_blocks = image_row.reshape(block_count, block_rows)

        def attend(block_pair):
            query_block, image_block = block_pair
            scores = (
                jnp.einsum(
                    "qhe,khe->hqk", query_block, key_heads, preferred_element_type=jnp.float32
                )
                * score_scale
            )
            same_image = image_block[:, None] == image_row[None, :]
            scores = jnp.where(same_image[None], scores, mask_fill)
            row_max = jnp.max(scores, -1, keepdims=True)
            exp_scores = jnp.exp(scores - row_max)
            exp_total = jnp.sum(exp_scores, -1, keepdims=True)
            attn_probs = exp_scores / exp_total
            result = jnp.einsum(
                "hqk,khe->qhe",
                attn_probs.astype(jnp.bfloat16),
                value_heads,
                preferred_element_type=jnp.float32,
            )
            return (result.reshape(block_rows, head_cols), (row_max + jnp.log(exp_total))[..., 0])

        attended_blocks, log_sums = lax.map(attend, (query_blocks, image_blocks))
        attended = attended_blocks.reshape(length, head_cols).astype(jnp.bfloat16)
        attn_sum = lax.psum_scatter(
            jnp.dot(attended, out_weight, preferred_element_type=jnp.float32).astype(jnp.bfloat16),
            "tensor",
            scatter_dimension=0,
            tiled=True,
        ).astype(jnp.float32)
        middle = tokens_here + attn_sum + vec_master[2]
        normed_two, norm_pull_two = jax.vjp(layer_norm, middle, vec_master[3], vec_master[4])
        gathered_two = lax.all_gather(normed_two.astype(jnp.bfloat16), "tensor", axis=0, tiled=True)
        hidden = jnp.dot(gathered_two, up_weight, preferred_element_type=jnp.float32) + hidden_bias
        active, gelu_pull = jax.vjp(gelu_tanh, hidden)
        active_low = active.astype(jnp.bfloat16)
        project_row_piece = lax.slice_in_dim(
            active_low, 0, local_rows * lax.axis_size("tensor"), axis=0
        )
        mlp_sum = lax.psum_scatter(
            jnp.dot(project_row_piece, down_weight, preferred_element_type=jnp.float32).astype(
                jnp.bfloat16
            ),
            "tensor",
            scatter_dimension=0,
            tiled=True,
        ).astype(jnp.float32)
        block_outputs.append(middle + mlp_sum + vec_master[5])
        qkv_weight, out_weight, up_weight, down_weight = (
            lax.all_gather(compute[0], "dp", axis=0, tiled=True),
            lax.all_gather(compute[1], "dp", axis=1, tiled=True),
            lax.all_gather(compute[2], "dp", axis=0, tiled=True),
            lax.all_gather(compute[3], "dp", axis=1, tiled=True),
        )
        cotangent = out_cotangent[batch_index, 0]
        cot_full = lax.all_gather(cotangent.astype(jnp.bfloat16), "tensor", axis=0, tiled=True)
        down_term = jnp.dot(active_low.T, cot_full, preferred_element_type=jnp.float32)
        d_active = jnp.dot(cot_full, down_weight.T, preferred_element_type=jnp.float32)
        d_hidden = gelu_pull(d_active)[0].astype(jnp.bfloat16)
        up_term = jnp.dot(gathered_two.T, d_hidden, preferred_element_type=jnp.float32)
        d_normed_two = lax.psum_scatter(
            jnp.dot(d_hidden, up_weight.T, preferred_element_type=jnp.float32).astype(jnp.bfloat16),
            "tensor",
            scatter_dimension=0,
            tiled=True,
        ).astype(jnp.float32)
        d_middle, gain_two_grad, shift_two_grad = norm_pull_two(d_normed_two)
        d_middle = d_middle + cotangent
        mid_full = lax.all_gather(d_middle.astype(jnp.bfloat16), "tensor", axis=0, tiled=True)
        out_term = jnp.dot(attended.T, mid_full, preferred_element_type=jnp.float32)
        d_attended = jnp.dot(mid_full, out_weight.T, preferred_element_type=jnp.float32).astype(
            jnp.bfloat16
        )
        d_blocks = d_attended.reshape(block_count, block_rows, local_heads, HEAD)

        def attend_back(running, block_item):
            d_keys, d_values = running
            query_block, image_block, block_sums, d_block = block_item
            scores = (
                jnp.einsum(
                    "qhe,khe->hqk", query_block, key_heads, preferred_element_type=jnp.float32
                )
                * score_scale
            )
            same_image = image_block[:, None] == image_row[None, :]
            scores = jnp.where(same_image[None], scores, mask_fill)
            attn_probs = jnp.exp(scores - block_sums[:, :, None])
            d_probs = jnp.einsum(
                "qhe,khe->hqk", d_block, value_heads, preferred_element_type=jnp.float32
            )
            row_delta = jnp.sum(attn_probs * d_probs, -1, keepdims=True)
            d_scores = (attn_probs * (d_probs - row_delta)).astype(jnp.bfloat16)
            d_query = (
                jnp.einsum("hqk,khe->qhe", d_scores, key_heads, preferred_element_type=jnp.float32)
                * score_scale
            )
            d_keys = (
                d_keys
                + jnp.einsum(
                    "hqk,qhe->khe", d_scores, query_block, preferred_element_type=jnp.float32
                )
                * score_scale
            )
            d_values = d_values + jnp.einsum(
                "hqk,qhe->khe",
                attn_probs.astype(jnp.bfloat16),
                d_block,
                preferred_element_type=jnp.float32,
            )
            return ((d_keys, d_values), d_query)

        zero_heads = jnp.zeros((length, local_heads, HEAD), jnp.float32)
        (d_keys, d_values), d_queries = lax.scan(
            attend_back, (zero_heads, zero_heads), (query_blocks, image_blocks, log_sums, d_blocks)
        )
        d_query_low = d_queries.reshape(length, head_cols).astype(jnp.bfloat16)
        d_key_low = d_keys.reshape(length, head_cols).astype(jnp.bfloat16)
        d_value_low = d_values.reshape(length, head_cols).astype(jnp.bfloat16)
        d_projected = jnp.stack([d_query_low, d_key_low, d_value_low])
        qkv_term = jnp.einsum(
            "td,cte->dce", gathered, d_projected, preferred_element_type=jnp.float32
        )
        d_normed = lax.psum_scatter(
            jnp.einsum(
                "cte,dce->td", d_projected, qkv_weight, preferred_element_type=jnp.float32
            ).astype(jnp.bfloat16),
            "tensor",
            scatter_dimension=0,
            tiled=True,
        ).astype(jnp.float32)
        d_tokens, gain_one_grad, shift_one_grad = norm_pull(d_normed)
        input_grads.append(d_tokens + d_middle)
        vector_terms = vector_terms + jnp.stack(
            [
                gain_one_grad,
                shift_one_grad,
                jnp.sum(d_middle, 0),
                gain_two_grad,
                shift_two_grad,
                jnp.sum(cotangent, 0),
            ]
        )
        bias_terms = bias_terms + jnp.concatenate(
            [
                jnp.sum(d_query_low, 0, dtype=jnp.float32),
                jnp.sum(d_value_low, 0, dtype=jnp.float32),
                jnp.sum(d_hidden, 0, dtype=jnp.float32),
            ]
        )
        local_terms = (qkv_term, out_term, up_term, down_term)
        owned = (
            lax.psum_scatter(
                local_terms[0].astype(jnp.bfloat16), "dp", scatter_dimension=0, tiled=True
            ).astype(jnp.float32),
            lax.psum_scatter(
                local_terms[1].astype(jnp.bfloat16), "dp", scatter_dimension=1, tiled=True
            ).astype(jnp.float32),
            lax.psum_scatter(
                local_terms[2].astype(jnp.bfloat16), "dp", scatter_dimension=0, tiled=True
            ).astype(jnp.float32),
            lax.psum_scatter(
                local_terms[3].astype(jnp.bfloat16), "dp", scatter_dimension=1, tiled=True
            ).astype(jnp.float32),
        )
        weight_sums = tuple((total + term for total, term in zip(weight_sums, owned)))
    qkv_grad, out_grad, up_grad, down_grad = weight_sums
    tensor_index = lax.axis_index("tensor")
    placed = jnp.where(jnp.arange(splits)[:, None] == tensor_index, bias_terms[None, :], 0.0)
    vec_grad, bias_table = lax.psum((vector_terms, placed), ("dp", "tensor"))
    bias_grad = lax.dynamic_slice_in_dim(bias_table, tensor_index, 1, 0)
    qkv_second_new, qkv_master_new = adam_update(
        qkv_master, qkv_moment, qkv_second, qkv_grad, 0.09, 0.1
    )
    out_second_new, out_master_new = adam_update(
        out_master, out_moment, out_second, out_grad, 0.4, 0.1
    )
    up_second_new, up_master_new = adam_update(up_master, up_moment, up_second, up_grad, 0.09, 0.1)
    down_second_new, down_master_new = adam_update(
        down_master, down_moment, down_second, down_grad, 0.045, 0.1
    )
    vec_second_new, vec_master_new = adam_update(
        vec_master, vec_moment, vec_second, vec_grad, 0.6, 0.0
    )
    bias_second_new, bias_master_new = adam_update(
        bias_master, bias_moment, bias_second, bias_grad, 0.5, 0.0
    )
    block_output = jnp.stack(block_outputs)[:, None]
    input_grad = jnp.stack(input_grads)[:, None]
    return (
        block_output,
        input_grad,
        qkv_grad,
        qkv_second_new,
        qkv_master_new,
        out_grad,
        out_second_new,
        out_master_new,
        up_grad,
        up_second_new,
        up_master_new,
        down_grad,
        down_second_new,
        down_master_new,
        vec_grad,
        vec_second_new,
        vec_master_new,
        bias_grad,
        bias_second_new,
        bias_master_new,
    )


LANES = 128
TILE = 128
SPAN = 256
WIDE = 1152
BATCH = 8


def lane_window(head):
    first = head * HEAD
    low = first // LANES * LANES
    high = -(-(first + HEAD) // LANES) * LANES
    return low, high


def head_mask(head, rows):
    low, high = lane_window(head)
    lane = lax.broadcasted_iota(jnp.int32, (rows, high - low), 1) + low
    return (lane >= head * HEAD) & (lane < head * HEAD + HEAD)


def head_columns(head, columns):
    low, high = lane_window(head)
    high = min(high, columns)
    return slice(low, high), head_mask(head, TILE)[:, : high - low]


def padded(columns):
    return -(-columns // LANES) * LANES


def tile_spans(ids_smem, ids_ref, index, tiles):
    first_id = ids_smem[index * TILE]
    last_id = ids_smem[index * TILE + TILE - 1]
    ids = ids_ref[...]
    begin = jnp.sum((ids < first_id).astype(jnp.int32)) // TILE
    end = (jnp.sum((ids <= last_id).astype(jnp.int32)) + TILE - 1) // TILE
    count = (end - begin + 1) // 2
    return jnp.minimum(begin, tiles - 2 * count), count


def ids_column(ids_ref, index):
    row = ids_ref[:, pl.ds(pl.multiple_of(index * TILE, TILE), TILE)].astype(jnp.float32)
    square = jnp.broadcast_to(row, (TILE, TILE)).T
    return jnp.concatenate([square] * (SPAN // TILE), axis=1).astype(jnp.int32)


NT = (((1,), (1,)), ((), ()))
TN = (((0,), (0,)), ((), ()))


def attend_kernel(heads, length, ids_smem, ids_ref, q_ref, k_ref, v_ref, o_ref, lse_ref, top, total, acc):
    index = pl.program_id(0)
    columns = heads * HEAD
    scale = HEAD ** (-0.5) * math.log2(math.e)
    begin, count = tile_spans(ids_smem, ids_ref, index, length // TILE)
    own_ids = ids_column(ids_ref, index)
    top[...] = jnp.full(top.shape, mask_fill, jnp.float32)
    total[...] = jnp.zeros(total.shape, jnp.float32)
    acc[...] = jnp.zeros(acc.shape, jnp.float32)

    def window(low, high):
        return slice(low, min(high, columns))

    def step(item, carry):
        place = pl.multiple_of((begin + 2 * item) * TILE, TILE)
        keys = pl.ds(place, SPAN)
        same = own_ids == ids_ref[:, keys]
        for first in range(0, heads, BATCH):
            batch = range(first, min(first + BATCH, heads))
            held_scores = []
            for head in batch:
                cols, mask = head_columns(head, columns)
                query = q_ref[:, cols]
                query = jnp.where(mask, query, jnp.zeros_like(query))
                scores = lax.dot_general(query, k_ref[keys, cols], NT, preferred_element_type=jnp.float32)
                held_scores.append(jnp.where(same, scores * scale, mask_fill))
            tops = [jnp.maximum(top[head], jnp.max(scores, -1, keepdims=True)) for head, scores in zip(batch, held_scores)]
            parts = [
                jnp.exp2(scores - jnp.concatenate([now] * (SPAN // LANES), axis=1)) for now, scores in zip(tops, held_scores)
            ]
            sums = [jnp.sum(part, -1, keepdims=True) for part in parts]
            mixes = [
                jnp.dot(part.astype(jnp.bfloat16), v_ref[keys, head_columns(head, columns)[0]], preferred_element_type=jnp.float32)
                for head, part in zip(batch, parts)
            ]
            for head, now, part_sum, mixed in zip(batch, tops, sums, mixes):
                cols, mask = head_columns(head, columns)
                shrink = jnp.exp2(top[head] - now)
                total[head] = total[head] * shrink + part_sum
                top[head] = now
                width = cols.stop - cols.start
                wide = jnp.concatenate([shrink] * ((width + LANES - 1) // LANES), axis=1)[:, :width]
                held = acc[:, cols]
                acc[:, cols] = jnp.where(mask, held * wide + mixed, held)
        return carry

    lax.fori_loop(0, count, step, 0)
    sums = jnp.zeros((TILE, LANES), jnp.float32)
    lane = lax.broadcasted_iota(jnp.int32, (TILE, LANES), 1)
    for head in range(heads):
        low, high = lane_window(head)
        high = min(high, columns)
        cols = slice(low, high)
        mask = head_mask(head, TILE)[:, : high - low]
        inverse = 1.0 / total[head]
        wide = jnp.concatenate([inverse] * ((high - low + LANES - 1) // LANES), axis=1)[:, : high - low]
        held = acc[:, cols]
        acc[:, cols] = jnp.where(mask, held * wide, held)
        sums = jnp.where(lane == head, top[head] + jnp.log2(total[head]), sums)
    o_ref[...] = acc[...].astype(o_ref.dtype)
    lse_ref[...] = sums.T[:heads]


def attend(ids, query, key, value):
    length, columns = query.shape
    heads = columns // HEAD
    tiles = length // TILE
    whole = pl.BlockSpec((length, columns), lambda i, s: (0, 0))
    block = pl.BlockSpec((TILE, columns), lambda i, s: (i, 0))
    return pl.pallas_call(
        partial(attend_kernel, heads, length),
        grid_spec=pltpu.PrefetchScalarGridSpec(
            num_scalar_prefetch=1,
            grid=(tiles,),
            in_specs=[pl.BlockSpec((1, length), lambda i, s: (0, 0)), block, whole, whole],
            out_specs=[block, pl.BlockSpec((heads, TILE), lambda i, s: (0, i))],
            scratch_shapes=[
                pltpu.VMEM((heads, TILE, LANES), jnp.float32),
                pltpu.VMEM((heads, TILE, LANES), jnp.float32),
                pltpu.VMEM((TILE, columns), jnp.float32),
            ],
        ),
        out_shape=[
            jax.ShapeDtypeStruct((length, columns), jnp.bfloat16),
            jax.ShapeDtypeStruct((heads, length), jnp.float32),
        ],
        compiler_params=pltpu.CompilerParams(vmem_limit_bytes=36 << 20),
        cost_estimate=pl.CostEstimate(flops=4 * 10**9, bytes_accessed=10**6, transcendentals=0),
    )(ids, ids.reshape(1, length), query, key, value)


def attend_back_kernel(
    heads, length, ids_smem, ids_ref, q_ref, k_ref, v_ref, o_ref, g_ref, lse_ref,
    dq_ref, dk_ref, dv_ref, delta, dq_acc, dk_acc, dv_acc,
):
    index = pl.program_id(0)
    columns = heads * HEAD
    natural = HEAD ** (-0.5)
    scale = natural * math.log2(math.e)
    tiles = length // TILE
    begin, count = tile_spans(ids_smem, ids_ref, index, tiles)
    own_ids = ids_column(ids_ref, index)

    @pl.when(index == 0)
    def _():
        dq_acc[...] = jnp.zeros(dq_acc.shape, jnp.float32)
        row = lax.broadcasted_iota(jnp.int32, (heads, columns), 0)
        lane = lax.broadcasted_iota(jnp.int32, (heads, columns), 1)
        pick = ((lane >= row * HEAD) & (lane < row * HEAD + HEAD)).astype(jnp.bfloat16)
        product = g_ref[...].astype(jnp.float32) * o_ref[...].astype(jnp.float32)
        coarse = product.astype(jnp.bfloat16)
        fine = (product - coarse.astype(jnp.float32)).astype(jnp.bfloat16)
        delta[...] = lax.dot_general(pick, coarse, NT, preferred_element_type=jnp.float32) + lax.dot_general(
            pick, fine, NT, preferred_element_type=jnp.float32
        )

    dk_acc[...] = jnp.zeros(dk_acc.shape, jnp.float32)
    dv_acc[...] = jnp.zeros(dv_acc.shape, jnp.float32)

    def step(item, carry):
        place = pl.multiple_of((begin + 2 * item) * TILE, TILE)
        rows = pl.ds(place, SPAN)
        same = own_ids == ids_ref[:, rows]
        for first in range(0, heads, BATCH):
            batch = range(first, min(first + BATCH, heads))
            keys, scores, d_probs = [], [], []
            for head in batch:
                cols, mask = head_columns(head, columns)
                key = k_ref[:, cols]
                keys.append(jnp.where(mask, key, jnp.zeros_like(key)))
                value = v_ref[:, cols]
                value = jnp.where(mask, value, jnp.zeros_like(value))
                scores.append(lax.dot_general(keys[-1], q_ref[rows, cols], NT, preferred_element_type=jnp.float32))
                d_probs.append(lax.dot_general(value, g_ref[rows, cols], NT, preferred_element_type=jnp.float32))
            probs = [
                jnp.exp2(jnp.where(same, score * scale, mask_fill) - lse_ref[head : head + 1, rows])
                for head, score in zip(batch, scores)
            ]
            d_scores = [
                (prob * (d_prob - delta[head : head + 1, rows])).astype(jnp.bfloat16)
                for head, prob, d_prob in zip(batch, probs, d_probs)
            ]
            for head, key, prob, d_score in zip(batch, keys, probs, d_scores):
                cols, mask = head_columns(head, columns)
                d_value = jnp.dot(prob.astype(jnp.bfloat16), g_ref[rows, cols], preferred_element_type=jnp.float32)
                d_key = jnp.dot(d_score, q_ref[rows, cols], preferred_element_type=jnp.float32)
                d_query = lax.dot_general(d_score, key, TN, preferred_element_type=jnp.float32)
                dv_acc[:, cols] += jnp.where(mask, d_value, 0.0)
                dk_acc[:, cols] += jnp.where(mask, d_key, 0.0)
                dq_acc[rows, cols] += d_query
        return carry

    lax.fori_loop(0, count, step, 0)
    dk_ref[...] = (dk_acc[...] * natural).astype(dk_ref.dtype)
    dv_ref[...] = dv_acc[...].astype(dv_ref.dtype)

    @pl.when(index == tiles - 1)
    def _():
        dq_ref[...] = (dq_acc[...] * natural).astype(dq_ref.dtype)


def attend_back(ids, query, key, value, attended, grad, lse):
    length, columns = query.shape
    heads = columns // HEAD
    tiles = length // TILE
    whole = pl.BlockSpec((length, columns), lambda i, s: (0, 0))
    block = pl.BlockSpec((TILE, columns), lambda i, s: (i, 0))
    out = jax.ShapeDtypeStruct((length, columns), jnp.bfloat16)
    return pl.pallas_call(
        partial(attend_back_kernel, heads, length),
        grid_spec=pltpu.PrefetchScalarGridSpec(
            num_scalar_prefetch=1,
            grid=(tiles,),
            in_specs=[
                pl.BlockSpec((1, length), lambda i, s: (0, 0)),
                whole,
                block,
                block,
                whole,
                whole,
                pl.BlockSpec((heads, length), lambda i, s: (0, 0)),
            ],
            out_specs=[whole, block, block],
            scratch_shapes=[
                pltpu.VMEM((heads, length), jnp.float32),
                pltpu.VMEM((length, columns), jnp.float32),
                pltpu.VMEM((TILE, columns), jnp.float32),
                pltpu.VMEM((TILE, columns), jnp.float32),
            ],
        ),
        out_shape=[out, out, out],
        compiler_params=pltpu.CompilerParams(vmem_limit_bytes=36 << 20),
        cost_estimate=pl.CostEstimate(flops=2 * 10**9, bytes_accessed=10**6, transcendentals=0),
    )(ids, ids.reshape(1, length), query, key, value, attended, grad, lse)


def column_call(kernel, ins, outs, columns, flops, scratch=()):
    wide = min(WIDE, padded(columns))
    steps = -(-columns // wide)

    def spec(shape, cut):
        if cut:
            return pl.BlockSpec(shape[:-1] + (wide,), lambda i: (0,) * (len(shape) - 1) + (i,))
        return pl.BlockSpec(shape, lambda i: (0,) * len(shape))

    size = sum(math.prod(a.shape) * a.dtype.itemsize for a, _ in ins) + sum(
        math.prod(a.shape) * a.dtype.itemsize for a in outs
    )
    return pl.pallas_call(
        kernel,
        grid=(steps,),
        in_specs=[spec(a.shape, cut) for a, cut in ins],
        out_specs=[spec(a.shape, True) for a in outs],
        out_shape=outs,
        scratch_shapes=list(scratch),
        compiler_params=pltpu.CompilerParams(vmem_limit_bytes=44 << 20),
        cost_estimate=pl.CostEstimate(flops=flops // 8, bytes_accessed=size // 8, transcendentals=0),
    )(*[a for a, _ in ins])


def hidden_kernel(x_ref, w_ref, b_ref, active_ref, slope_ref):
    rows = 256
    for block in range(x_ref.shape[0] // rows):
        part = pl.ds(block * rows, rows)
        value = jnp.dot(x_ref[part, :], w_ref[...], preferred_element_type=jnp.float32) + b_ref[...]
        active, slope = gelu_pair(value)
        active_ref[part, :] = active.astype(jnp.bfloat16)
        slope_ref[part, :] = slope.astype(jnp.bfloat16)


def hidden_units(x, weight, bias):
    tokens, columns = x.shape[0], weight.shape[1]
    out = jax.ShapeDtypeStruct((tokens, columns), jnp.bfloat16)
    ins = [(x, False), (weight, True), (bias.reshape(1, columns), True)]
    return column_call(hidden_kernel, ins, [out, out], columns, 2 * tokens * x.shape[1] * columns)


def hidden_back_kernel(x_ref, w_ref, slope_ref, grad_ref, sum_ref):
    rows = 256
    total = jnp.zeros(sum_ref.shape, jnp.float32)
    for block in range(x_ref.shape[0] // rows):
        part = pl.ds(block * rows, rows)
        value = jnp.dot(x_ref[part, :], w_ref[...], preferred_element_type=jnp.float32)
        value = value * slope_ref[part, :].astype(jnp.float32)
        grad_ref[part, :] = value.astype(jnp.bfloat16)
        total = total + jnp.sum(value, 0, keepdims=True)
    sum_ref[...] = total


def hidden_back(x, weight, slope):
    tokens, columns = x.shape[0], weight.shape[1]
    outs = [jax.ShapeDtypeStruct((tokens, columns), jnp.bfloat16), jax.ShapeDtypeStruct((1, columns), jnp.float32)]
    ins = [(x, False), (weight, True), (slope, True)]
    return column_call(hidden_back_kernel, ins, outs, columns, 2 * tokens * x.shape[1] * columns)


def grad_kernel(chunks, stacked, x_ref, *refs):
    core = lax.axis_index("dp") % 2
    count = len(refs) - 4 if stacked else (len(refs) - 2) // 3
    turned, result = refs[-2:]
    dy_refs = refs[:count]
    outs = refs[count:-2]

    @pl.when(pl.program_id(0) == 0)
    def _():
        turned[...] = x_ref[...].T

    rows = turned.shape[0] // chunks
    for number, dy_ref in enumerate(dy_refs):
        if stacked:
            sent_ref, kept_ref = outs[0].at[number], outs[1].at[number]
        else:
            sent_ref, kept_ref = outs[number], outs[count + number]
        result[...] = jnp.dot(turned[...], dy_ref[...], preferred_element_type=jnp.float32)
        for spot in range(chunks // 2):
            sent = pl.multiple_of((2 * spot + 1 - core) * rows, 8)
            kept = pl.multiple_of((2 * spot + core) * rows, 8)
            sent_ref[spot] = result[pl.ds(sent, rows), :].astype(jnp.bfloat16)
            kept_ref[spot] = result[pl.ds(kept, rows), :].astype(jnp.bfloat16)


def weight_grads(x, parts, stacked=False):
    tokens, features = x.shape
    columns = parts[0].shape[1]
    count = len(parts)
    wide = min(WIDE, padded(columns))
    shape = (8, features // 16, columns)
    outs = [jax.ShapeDtypeStruct(shape, jnp.bfloat16)] * (2 * count)
    if stacked:
        outs = [jax.ShapeDtypeStruct((count,) + shape, jnp.bfloat16)] * 2
    results = column_call(
        partial(grad_kernel, 16, stacked),
        [(x, False)] + [(part, True) for part in parts],
        outs,
        columns,
        2 * tokens * features * columns * count,
        [pltpu.VMEM((features, tokens), jnp.bfloat16), pltpu.VMEM((features, wide), jnp.float32)],
    )
    return results if stacked else (results[:count], results[count:])


def place_kernel(leads, ordered, steps, *refs):
    pieces = refs[: len(steps)]
    outs = refs[len(steps) : len(steps) + leads]
    sems = refs[len(steps) + leads]
    spot = lax.axis_index("dp")
    z, y, core = spot // 4, spot // 2 % 2, spot % 2
    copies = []
    for piece, (first_slot, y_step, core_step) in zip(pieces, steps):
        column = (y + y_step) % 2 * 2 + (core + core_step) % 2
        for slot in range(piece.shape[0]):
            number = first_slot + slot
            row = (number if ordered else (z + 4 - number) % 4) * 4 + column
            for lead in range(leads):
                copy = pltpu.make_async_copy(piece.at[slot, lead], outs[lead].at[row], sems.at[len(copies)])
                copy.start()
                copies.append(copy)
    for copy in copies:
        copy.wait()


def place(planes, ordered):
    pieces = sum(planes, [])
    leads, rows, columns = pieces[0].shape[1:]
    slots = pieces[0].shape[0]
    steps = [(start, step % 2, step // 2) for start in range(0, 4, slots) for step in range(4)]
    size = 16 * leads * rows * padded(columns) * 2
    placed = pl.pallas_call(
        partial(place_kernel, leads, ordered, steps),
        in_specs=[pl.BlockSpec(memory_space=pl.ANY)] * len(pieces),
        out_specs=[pl.BlockSpec(memory_space=pltpu.VMEM)] * leads,
        out_shape=[jax.ShapeDtypeStruct((16, rows, columns), jnp.bfloat16)] * leads,
        scratch_shapes=[pltpu.SemaphoreType.DMA((16 * leads,))],
        compiler_params=pltpu.CompilerParams(vmem_limit_bytes=size * 3 // 2 + (2 << 20)),
        cost_estimate=pl.CostEstimate(flops=0, bytes_accessed=size // 4, transcendentals=0),
    )(*pieces)
    return [part.reshape(16 * rows, columns) for part in placed]


def swap_x(value):
    return lax.ppermute(value, "tensor", [(0, 1), (1, 0)])


def swap_y(value):
    return lax.ppermute(value, "dp", [(spot, spot ^ 2) for spot in range(16)])


def swap_core(value):
    return lax.ppermute(value, "dp", [(spot, spot ^ 1) for spot in range(16)])


def move_z(value, steps):
    return lax.ppermute(value, "dp", [(spot, (spot + 4 * steps) % 16) for spot in range(16)])


def tie(*values):
    return lax.optimization_barrier(values)


def gather_z(shard):
    groups = [[spot + 4 * z for z in range(4)] for spot in range(4)]
    return lax.all_gather(shard, "dp", axis_index_groups=groups)


def both_cores(parts):
    return parts + [swap_core(part) for part in parts]


def add_low(*terms):
    total = terms[0].astype(jnp.float32)
    for term in terms[1:]:
        total = total + term.astype(jnp.float32)
    return total.astype(jnp.bfloat16)


def part_of(value, index, axis):
    return lax.dynamic_index_in_dim(value, index, axis, keepdims=False)


def y_parts(value):
    spot = lax.axis_index("dp")
    split = value.reshape((value.shape[0] // 2, 2) + value.shape[1:])
    return part_of(split, spot // 2 % 2, 1), part_of(split, 1 - spot // 2 % 2, 1)


class Planes:
    def __init__(self, own, other):
        half = own.shape[0] // 2
        self.near_own, near_own = y_parts(own[:half])
        self.near_other, near_other = y_parts(other[:half])
        self.far_own = own[half:]
        self.sent = [jnp.stack([near_own, near_other]), other[half:]]

    def first(self):
        self.got = [swap_y(self.sent[0]), swap_x(self.sent[1])]

    def middle(self):
        self.near_own = add_low(self.near_own, self.got[0][0])
        self.far_own, far = y_parts(add_low(self.far_own, self.got[1]))
        self.sent = [add_low(self.near_other, self.got[0][1]), far]

    def second(self):
        self.got = [swap_x(self.sent[0]), swap_y(self.sent[1])]

    def total(self):
        return jnp.concatenate([add_low(self.near_own, self.got[0]), add_low(self.far_own, self.got[1])])


def scatter_z(value):
    groups = [[spot + 4 * z for z in range(4)] for spot in range(4)]
    return lax.psum_scatter(value, "dp", axis_index_groups=groups)


def send_z(value):
    z = lax.axis_index("dp") // 4
    return [part_of(value, z, 0)] + [move_z(part_of(value, (z + steps) % 4, 0), steps) for steps in (1, 2, 3)]


def sum_terms(terms):
    total = terms[0].astype(jnp.float32)
    for term in terms[1:]:
        total = total + term.astype(jnp.float32)
    return total


def sum_everywhere(value):
    value = value + swap_core(value)
    value = value + swap_y(value)
    return value + move_z(value, 1) + move_z(value, 2) + move_z(value, 3)


def norm_forward(values):
    centre = values - jnp.mean(values, -1, keepdims=True)
    inverse = lax.rsqrt(jnp.mean(centre * centre, -1, keepdims=True) + norm_eps)
    return centre * inverse, inverse


def norm_back(grad, hat, inverse, gain):
    scaled = grad * gain
    mean_one = jnp.mean(scaled, -1, keepdims=True)
    mean_two = jnp.mean(scaled * hat, -1, keepdims=True)
    return (scaled - mean_one - hat * mean_two) * inverse


def gelu_pair(value):
    inner = math.sqrt(2.0 / math.pi)
    squared = value * value
    bent = jnp.tanh(inner * (value + 0.044715 * value * squared))
    half = 0.5 * (1.0 + bent)
    slope = half + 0.5 * value * (1.0 - bent * bent) * inner * (1.0 + 3 * 0.044715 * squared)
    return value * half, slope


def row_layer(
    block_input,
    image_ids,
    out_cotangent,
    qkv_master,
    qkv_moment,
    qkv_second,
    out_master,
    out_moment,
    out_second,
    up_master,
    up_moment,
    up_second,
    down_master,
    down_moment,
    down_second,
    vec_master,
    vec_moment,
    vec_second,
    bias_master,
    bias_moment,
    bias_second,
):
    low = jnp.bfloat16
    wide = jnp.float32
    mine = lax.axis_index("tensor")
    first = mine == 0
    half = block_input.shape[2]
    features = block_input.shape[3]
    head_cols = qkv_master.shape[2]

    def pick(pair, index):
        return lax.dynamic_index_in_dim(pair, index, 0, keepdims=False)

    def in_order(own, other, axis=0):
        return jnp.concatenate([jnp.where(first, own, other), jnp.where(first, other, own)], axis)

    def dot(spec, left, right):
        return jnp.einsum(spec, left, right, preferred_element_type=wide)

    inputs_own = pick(block_input[:, 0], mine)
    inputs_sent = pick(block_input[:, 0], 1 - mine)
    cot_own = pick(out_cotangent[:, 0], mine)
    cot_sent = pick(out_cotangent[:, 0], 1 - mine)
    inputs_low = inputs_sent.astype(low)
    early_shard = jnp.stack([qkv_master[:, 0], qkv_master[:, 1], qkv_master[:, 2]]).astype(low)
    early_shard, inputs_low = tie(early_shard, inputs_low)
    inputs_got = swap_x(inputs_low)
    early_one = move_z(early_shard, 1)
    early_three = move_z(early_shard, 3)
    early_shard, early_one = tie(early_shard, early_one)
    early_two = move_z(early_shard, 2)
    near = jnp.stack([early_shard, early_one])
    near_y, near_x = swap_y(near), swap_x(near)
    late_shard = jnp.stack([up_master, down_master.T]).astype(low)
    small = jnp.concatenate([pick(image_ids[:, 0], 1 - mine).astype(wide), bias_master[0]])
    late_shard, small, early_two, early_three, inputs_got = tie(late_shard, small, early_two, early_three, inputs_got)
    small_got = swap_x(small[None])[0]
    late_z = gather_z(late_shard)
    out_shard, late_z = tie(out_master.T.astype(low), late_z)
    out_whole = lax.all_gather(out_shard, ("tensor", "dp")).reshape(2, features, head_cols)
    far = jnp.stack([early_two, early_three])
    far_y, far_x = swap_y(far), swap_x(far)
    near_xy, far_yx = swap_y(near_x), swap_x(far_y)
    early_own = place([both_cores([near, near_y]), both_cores([far, far_y])], False)
    inputs = in_order(inputs_own, inputs_got.astype(wide))
    ids = in_order(pick(image_ids[:, 0], mine), small_got[:half].astype(jnp.int32))
    biases = jnp.stack([bias_master[0], small_got[half:]])

    hat_one, inverse_one = norm_forward(inputs)
    normed = (hat_one * vec_master[0] + vec_master[1]).astype(low)
    def project(g, weights):
        query = (dot("td,de->te", normed, weights[0]) + biases[g, :head_cols]).astype(low)
        key = dot("td,de->te", normed, weights[1]).astype(low)
        value = (dot("td,de->te", normed, weights[2]) + biases[g, head_cols : 2 * head_cols]).astype(low)
        return query, key, value

    projected = [project(0, early_own), None]
    attended, log_sums = [None, None], [None, None]
    attended[0], log_sums[0] = attend(ids, *projected[0])
    others = [both_cores([near_x, near_xy]), both_cores([far_x, far_yx])]
    others, attended[0] = tie(others, attended[0])
    early_other = place(others, False)
    up_near, up_far = [late_z[start : start + 2, :1] for start in (0, 2)]
    down_near, down_far = [late_z[start : start + 2, 1:] for start in (0, 2)]
    early_other, up_near, up_far = tie(early_other, up_near, up_far)
    up_near_x, up_far_y = swap_x(up_near), swap_y(up_far)
    projected[1] = project(1, early_other)
    query_weight, key_weight, value_weight = zip(early_own, early_other)
    projected[1], up_near, up_far, up_near_x, up_far_y = tie(projected[1], up_near, up_far, up_near_x, up_far_y)
    up_near_y, up_far_x = swap_y(up_near), swap_x(up_far)
    attended[1], log_sums[1] = attend(ids, *projected[1])
    attended[1], up_near_x, up_far_y, up_near_y, up_far_x = tie(
        attended[1], up_near_x, up_far_y, up_near_y, up_far_x
    )
    up_near_xy, up_far_yx = swap_y(up_near_x), swap_x(up_far_y)
    cot_got = swap_x(cot_sent.astype(low))
    out_weight = [pick(out_whole, mine), pick(out_whole, 1 - mine)]
    attn_sum = sum(dot("te,de->td", attended[g], out_weight[g]) for g in range(2)) + vec_master[2]
    middle = inputs + attn_sum
    hat_two, inverse_two = norm_forward(middle)
    normed_two = (hat_two * vec_master[3] + vec_master[4]).astype(low)
    normed_two, up_near_xy, up_far_yx, down_near, down_far = tie(
        normed_two, up_near_xy, up_far_yx, down_near, down_far
    )
    down_near_x, down_far_y = swap_x(down_near), swap_y(down_far)
    up_weight = [
        place([both_cores([up_near, up_near_y]), both_cores([up_far, up_far_y])], True)[0],
        place([both_cores([up_near_x, up_near_xy]), both_cores([up_far_x, up_far_yx])], True)[0],
    ]
    active, slope = [None, None], [None, None]
    active[0], slope[0] = hidden_units(normed_two, up_weight[0], biases[0, 2 * head_cols :])
    normed_two, active[0], down_near, down_far, down_near_x, down_far_y = tie(
        normed_two, active[0], down_near, down_far, down_near_x, down_far_y
    )
    down_near_y, down_far_x = swap_y(down_near), swap_x(down_far)
    active[1], slope[1] = hidden_units(normed_two, up_weight[1], biases[1, 2 * head_cols :])
    active[1], down_near_x, down_far_y, down_near_y, down_far_x = tie(
        active[1], down_near_x, down_far_y, down_near_y, down_far_x
    )
    down_weight = [place([both_cores([down_near, down_near_y]), both_cores([down_far, down_far_y])], True)[0], None]
    active[1], down_weight[0], down_near_x, down_far_y = tie(active[1], down_weight[0], down_near_x, down_far_y)
    down_near_xy, down_far_yx = swap_y(down_near_x), swap_x(down_far_y)
    cot_row = in_order(cot_own, cot_got.astype(wide))
    cot_low = cot_row.astype(low)
    down_sent, down_kept = weight_grads(cot_low, active)
    down_sent, down_near_xy, down_far_yx = tie(down_sent, down_near_xy, down_far_yx)
    down_weight[1] = place(
        [both_cores([down_near_x, down_near_xy]), both_cores([down_far_x, down_far_yx])], True
    )[0]
    added = attn_sum + sum(dot("tf,df->td", active[g], down_weight[g]) for g in range(2)) + vec_master[5]
    added = added.reshape(2, half, features)
    added_got = swap_x(pick(added, 1 - mine).astype(low))

    own, other = 0, 1
    down_core = [swap_core(part) for part in down_sent]
    d_hidden, hidden_sums = [None, None], [None, None]
    d_hidden[own], hidden_sums[own] = hidden_back(cot_low, down_weight[own], slope[own])
    d_hidden[own], down_core = tie(d_hidden[own], down_core)
    down = Planes(*[add_low(down_kept[g], down_core[g]) for g in range(2)])
    cot_late, down.sent = tie(cot_low, down.sent)
    down.first()
    d_hidden[other], hidden_sums[other] = hidden_back(cot_late, down_weight[other], slope[other])
    up_sent, up_kept = weight_grads(normed_two, d_hidden)
    up_sent, down.got = tie(up_sent, down.got)
    up_core = [swap_core(part) for part in up_sent]
    down.middle()
    d_hidden, down.sent = tie(d_hidden, down.sent)
    down.second()
    d_normed_two = sum(dot("tf,df->td", d_hidden[g], up_weight[g]) for g in range(2))
    d_normed_two, up_core, down.got = tie(d_normed_two, up_core, down.got)
    up = Planes(*[add_low(up_kept[g], up_core[g]) for g in range(2)])
    down_total = down.total()
    d_normed_two, up.sent, down_total = tie(d_normed_two, up.sent, down_total)
    up.first()
    down_term = scatter_z(down_total)
    mid_added = norm_back(d_normed_two, hat_two, inverse_two, vec_master[3])
    d_middle = cot_row + mid_added
    mid_low = d_middle.astype(low)
    d_attended = [dot("td,de->te", mid_low, out_weight[g]).astype(low) for g in range(2)]
    out_sent, out_kept = weight_grads(mid_low, attended)
    d_attended[other], out_sent, added_got = tie(d_attended[other], out_sent, added_got)
    out_here = inputs_own + pick(added, mine)
    out_there = pick(block_input[:, 0], 1 - mine) + added_got.astype(wide)
    block_output = in_order(out_here[None], out_there[None])[:, None]
    out_core = [swap_core(part) for part in out_sent]

    def back(g, grad):
        return attend_back(ids, *projected[g], attended[g], grad, log_sums[g])

    d_other = back(other, d_attended[other])
    d_other, out_core, up.got = tie(d_other, out_core, up.got)
    up.middle()
    out_other = add_low(out_kept[other], out_core[other])
    out_own = add_low(out_kept[own], out_core[own])
    d_other, up.sent, out_other = tie(d_other, up.sent, out_other)
    up.second()
    out_there_x = swap_x(out_other)
    qkv_sent, qkv_kept = [None, None], [None, None]
    qkv_sent[other], qkv_kept[other] = weight_grads(normed, d_other, True)

    def normed_part(parts, g):
        weights = (query_weight, key_weight, value_weight)
        return sum(dot("te,de->td", part, weight[g]) for part, weight in zip(parts, weights))

    d_other, qkv_sent[other] = tie(d_other, qkv_sent[other])
    qkv_core_other = swap_core(qkv_sent[other])
    d_normed_other = normed_part(d_other, other)
    d_normed_other, up.got, qkv_core_other = tie(d_normed_other, up.got, qkv_core_other)
    up_total = up.total()
    qkv_other_here, qkv_other_there = zip(*[y_parts(part) for part in add_low(qkv_kept[other], qkv_core_other)])
    qkv_other_there = jnp.stack(qkv_other_there)
    d_attended[own], up_total, qkv_other_there = tie(d_attended[own], up_total, qkv_other_there)
    up_term = scatter_z(up_total)
    qkv_there_y = swap_y(qkv_other_there)
    d_own = back(own, d_attended[own])
    d_own, qkv_there_y, out_there_x = tie(tuple(d_own), qkv_there_y, out_there_x)
    qkv_other = add_low(jnp.stack(qkv_other_here), qkv_there_y)
    out_here, out_there = y_parts(add_low(out_own, out_there_x))
    d_own, qkv_other, out_there = tie(d_own, qkv_other, out_there)
    qkv_there_x = swap_x(qkv_other)
    out_there_y = swap_y(out_there)
    qkv_sent[own], qkv_kept[own] = weight_grads(normed, d_own, True)
    d_own, qkv_sent[own], out_there_y = tie(d_own, qkv_sent[own], out_there_y)
    out_terms = send_z(add_low(out_here, out_there_y))
    qkv_core_own = swap_core(qkv_sent[own])
    d_normed_own = normed_part(d_own, own)
    d_normed_own, qkv_core_own = tie(d_normed_own, qkv_core_own)
    qkv_here, qkv_there = zip(*[y_parts(part) for part in add_low(qkv_kept[own], qkv_core_own)])
    qkv_there = jnp.stack(qkv_there)
    d_normed_own, qkv_there = tie(d_normed_own, qkv_there)
    qkv_there_y = swap_y(qkv_there)
    d_normed = d_normed_other + d_normed_own
    early = jnp.concatenate(
        [
            jnp.sum(d_middle, 0),
            jnp.sum(d_normed_two * hat_two, 0),
            jnp.sum(d_normed_two, 0),
            jnp.sum(out_cotangent[:, 0], (0, 1)),
        ]
    )

    def bias_rows(sums):
        return jnp.where(first, jnp.concatenate(sums), jnp.concatenate(sums[::-1]))

    sums = jnp.concatenate(
        [
            jnp.sum(d_normed * hat_one, 0),
            jnp.sum(d_normed, 0),
            early,
            bias_rows([jnp.sum(part[0], 0, dtype=wide) for part in (d_own, d_other)]),
            bias_rows([jnp.sum(part[2], 0, dtype=wide) for part in (d_own, d_other)]),
            bias_rows([part[0] for part in hidden_sums]),
        ]
    )
    in_added = (mid_added + norm_back(d_normed, hat_one, inverse_one, vec_master[0])).reshape(2, half, features)
    in_sent = pick(in_added, 1 - mine).astype(low)
    sums = sums + swap_x(sums[None])[0]
    sums, in_sent = tie(sums, in_sent)
    in_got = swap_x(in_sent)
    sums, qkv_there_y, qkv_there_x = tie(sums, qkv_there_y, qkv_there_x)
    qkv_terms = send_z(add_low(jnp.stack(qkv_here), qkv_there_y, qkv_there_x).transpose(1, 0, 2, 3))
    sums = sum_everywhere(sums[None])[0]
    sums, qkv_terms, down_term, up_term, out_terms = tie(sums, qkv_terms, down_term, up_term, out_terms)
    down_grad = down_term.astype(wide).T
    up_grad = up_term.astype(wide)
    out_grad = sum_terms(out_terms).T
    qkv_grad = sum_terms(qkv_terms).transpose(1, 0, 2)
    grad_here = cot_own + pick(in_added, mine)
    grad_there = cot_sent + in_got.astype(wide)
    input_grad = in_order(grad_here[None], grad_there[None])[:, None]
    vec_grad = sums[: 6 * features].reshape(6, features)

    def group(start, size):
        return pick(sums[start : start + 2 * size].reshape(2, size), mine)

    start = 6 * features
    bias_grad = jnp.concatenate(
        [
            group(start, head_cols),
            group(start + 2 * head_cols, head_cols),
            group(start + 4 * head_cols, up_master.shape[1]),
        ]
    )[None]

    results = [block_output, input_grad]
    for master, moment, second, grad, rate, decay in (
        (qkv_master, qkv_moment, qkv_second, qkv_grad, 0.09, 0.1),
        (out_master, out_moment, out_second, out_grad, 0.4, 0.1),
        (up_master, up_moment, up_second, up_grad, 0.09, 0.1),
        (down_master, down_moment, down_second, down_grad, 0.045, 0.1),
        (vec_master, vec_moment, vec_second, vec_grad, 0.6, 0.0),
        (bias_master, bias_moment, bias_second, bias_grad, 0.5, 0.0),
    ):
        second_new, master_new = adam_update(master, moment, second, grad, rate, decay)
        results += [grad, second_new, master_new]
    return tuple(results)


def solution(mesh):
    placed = (
        P(None, "dp", "tensor", None),
        P(None, "dp", "tensor"),
        P(None, "dp", "tensor", None),
        P("dp", None, "tensor"),
        P("dp", None, "tensor"),
        P("dp", None, "tensor"),
        P("tensor", "dp"),
        P("tensor", "dp"),
        P("tensor", "dp"),
        P("dp", "tensor"),
        P("dp", "tensor"),
        P("dp", "tensor"),
        P("tensor", "dp"),
        P("tensor", "dp"),
        P("tensor", "dp"),
        P(),
        P(),
        P(),
        P("tensor", None),
        P("tensor", None),
        P("tensor", None),
    )
    by_rows = dict(mesh.shape) == {"dp": 16, "tensor": 2}
    return jax.shard_map(
        row_layer if by_rows else split_layer,
        mesh=mesh,
        in_specs=placed,
        out_specs=(
            P(None, "dp", "tensor", None),
            P(None, "dp", "tensor", None),
            P("dp", None, "tensor"),
            P("dp", None, "tensor"),
            P("dp", None, "tensor"),
            P("tensor", "dp"),
            P("tensor", "dp"),
            P("tensor", "dp"),
            P("dp", "tensor"),
            P("dp", "tensor"),
            P("dp", "tensor"),
            P("tensor", "dp"),
            P("tensor", "dp"),
            P("tensor", "dp"),
            P(),
            P(),
            P(),
            P("tensor", None),
            P("tensor", None),
            P("tensor", None),
        ),
        check_vma=False,
    )
```

```python
import math
from functools import partial

import jax
import jax.numpy as jnp
from jax import lax
from jax.experimental import pallas as pl
from jax.experimental.pallas import tpu as pltpu
from jax.sharding import PartitionSpec as P

HEAD = 72
STEP = 10


norm_eps = 1e-06
mask_fill = -1e30
beta_one = 0.9
beta_two = 0.95
adam_eps = 1e-08


def layer_norm(values, scale_vec, shift_vec):
    centre = values - jnp.mean(values, -1, keepdims=True)
    spread = jnp.mean(centre * centre, -1, keepdims=True)
    return centre * lax.rsqrt(spread + norm_eps) * scale_vec + shift_vec


def adam_update(master, moment, second, gradient, step_rate, weight_decay):
    first_moment = beta_one * moment.astype(jnp.float32) + (1.0 - beta_one) * gradient
    second_new = beta_two * second + (1.0 - beta_two) * gradient * gradient
    update = (
        first_moment
        / (1.0 - beta_one**STEP)
        / (jnp.sqrt(second_new / (1.0 - beta_two**STEP)) + adam_eps)
        + weight_decay * master
    )
    return (second_new, master - step_rate * update)


def split_layer(
    block_input,
    image_ids,
    out_cotangent,
    qkv_master,
    qkv_moment,
    qkv_second,
    out_master,
    out_moment,
    out_second,
    up_master,
    up_moment,
    up_second,
    down_master,
    down_moment,
    down_second,
    vec_master,
    vec_moment,
    vec_second,
    bias_master,
    bias_moment,
    bias_second,
):
    batches = block_input.shape[0]
    local_rows = block_input.shape[2]
    features = block_input.shape[3]
    splits = lax.axis_size("tensor")
    length = local_rows * splits
    head_cols = qkv_master.shape[2]
    local_heads = head_cols // HEAD
    block_rows = min(512, length)
    block_count = length // block_rows
    score_scale = HEAD ** (-0.5)
    biases = bias_master[0]
    query_bias = biases[:head_cols]
    value_bias = biases[head_cols : 2 * head_cols]
    hidden_bias = biases[2 * head_cols :]
    compute = (
        qkv_master.astype(jnp.bfloat16),
        out_master.astype(jnp.bfloat16),
        up_master.astype(jnp.bfloat16),
        down_master.astype(jnp.bfloat16),
    )
    gelu_tanh = partial(jax.nn.gelu, approximate=True)
    weight_sums = (
        jnp.zeros_like(qkv_master),
        jnp.zeros_like(out_master),
        jnp.zeros_like(up_master),
        jnp.zeros_like(down_master),
    )
    vector_terms = jnp.zeros((6, features), jnp.float32)
    bias_terms = jnp.zeros(biases.shape, jnp.float32)
    block_outputs = []
    input_grads = []
    for batch_index in range(batches):
        qkv_weight, out_weight, up_weight, down_weight = (
            lax.all_gather(compute[0], "dp", axis=0, tiled=True),
            lax.all_gather(compute[1], "dp", axis=1, tiled=True),
            lax.all_gather(compute[2], "dp", axis=0, tiled=True),
            lax.all_gather(compute[3], "dp", axis=1, tiled=True),
        )
        tokens_here = block_input[batch_index, 0]
        normed, norm_pull = jax.vjp(layer_norm, tokens_here, vec_master[0], vec_master[1])
        gathered, image_row = (
            lax.all_gather(normed.astype(jnp.bfloat16), "tensor", axis=0, tiled=True),
            lax.all_gather(image_ids[batch_index, 0], "tensor", axis=0, tiled=True),
        )
        projected = jnp.einsum(
            "td,dce->cte", gathered, qkv_weight, preferred_element_type=jnp.float32
        )
        queries = (projected[0] + query_bias).astype(jnp.bfloat16)
        key_rows = projected[1].astype(jnp.bfloat16)
        values = (projected[2] + value_bias).astype(jnp.bfloat16)
        key_heads = key_rows.reshape(length, local_heads, HEAD)
        value_heads = values.reshape(length, local_heads, HEAD)
        query_blocks = queries.reshape(block_count, block_rows, local_heads, HEAD)
        image_blocks = image_row.reshape(block_count, block_rows)

        def attend(block_pair):
            query_block, image_block = block_pair
            scores = (
                jnp.einsum(
                    "qhe,khe->hqk", query_block, key_heads, preferred_element_type=jnp.float32
                )
                * score_scale
            )
            same_image = image_block[:, None] == image_row[None, :]
            scores = jnp.where(same_image[None], scores, mask_fill)
            row_max = jnp.max(scores, -1, keepdims=True)
            exp_scores = jnp.exp(scores - row_max)
            exp_total = jnp.sum(exp_scores, -1, keepdims=True)
            attn_probs = exp_scores / exp_total
            result = jnp.einsum(
                "hqk,khe->qhe",
                attn_probs.astype(jnp.bfloat16),
                value_heads,
                preferred_element_type=jnp.float32,
            )
            return (result.reshape(block_rows, head_cols), (row_max + jnp.log(exp_total))[..., 0])

        attended_blocks, log_sums = lax.map(attend, (query_blocks, image_blocks))
        attended = attended_blocks.reshape(length, head_cols).astype(jnp.bfloat16)
        attn_sum = lax.psum_scatter(
            jnp.dot(attended, out_weight, preferred_element_type=jnp.float32).astype(jnp.bfloat16),
            "tensor",
            scatter_dimension=0,
            tiled=True,
        ).astype(jnp.float32)
        middle = tokens_here + attn_sum + vec_master[2]
        normed_two, norm_pull_two = jax.vjp(layer_norm, middle, vec_master[3], vec_master[4])
        gathered_two = lax.all_gather(normed_two.astype(jnp.bfloat16), "tensor", axis=0, tiled=True)
        hidden = jnp.dot(gathered_two, up_weight, preferred_element_type=jnp.float32) + hidden_bias
        active, gelu_pull = jax.vjp(gelu_tanh, hidden)
        active_low = active.astype(jnp.bfloat16)
        project_row_piece = lax.slice_in_dim(
            active_low, 0, local_rows * lax.axis_size("tensor"), axis=0
        )
        mlp_sum = lax.psum_scatter(
            jnp.dot(project_row_piece, down_weight, preferred_element_type=jnp.float32).astype(
                jnp.bfloat16
            ),
            "tensor",
            scatter_dimension=0,
            tiled=True,
        ).astype(jnp.float32)
        block_outputs.append(middle + mlp_sum + vec_master[5])
        qkv_weight, out_weight, up_weight, down_weight = (
            lax.all_gather(compute[0], "dp", axis=0, tiled=True),
            lax.all_gather(compute[1], "dp", axis=1, tiled=True),
            lax.all_gather(compute[2], "dp", axis=0, tiled=True),
            lax.all_gather(compute[3], "dp", axis=1, tiled=True),
        )
        cotangent = out_cotangent[batch_index, 0]
        cot_full = lax.all_gather(cotangent.astype(jnp.bfloat16), "tensor", axis=0, tiled=True)
        down_term = jnp.dot(active_low.T, cot_full, preferred_element_type=jnp.float32)
        d_active = jnp.dot(cot_full, down_weight.T, preferred_element_type=jnp.float32)
        d_hidden = gelu_pull(d_active)[0].astype(jnp.bfloat16)
        up_term = jnp.dot(gathered_two.T, d_hidden, preferred_element_type=jnp.float32)
        d_normed_two = lax.psum_scatter(
            jnp.dot(d_hidden, up_weight.T, preferred_element_type=jnp.float32).astype(jnp.bfloat16),
            "tensor",
            scatter_dimension=0,
            tiled=True,
        ).astype(jnp.float32)
        d_middle, gain_two_grad, shift_two_grad = norm_pull_two(d_normed_two)
        d_middle = d_middle + cotangent
        mid_full = lax.all_gather(d_middle.astype(jnp.bfloat16), "tensor", axis=0, tiled=True)
        out_term = jnp.dot(attended.T, mid_full, preferred_element_type=jnp.float32)
        d_attended = jnp.dot(mid_full, out_weight.T, preferred_element_type=jnp.float32).astype(
            jnp.bfloat16
        )
        d_blocks = d_attended.reshape(block_count, block_rows, local_heads, HEAD)

        def attend_back(running, block_item):
            d_keys, d_values = running
            query_block, image_block, block_sums, d_block = block_item
            scores = (
                jnp.einsum(
                    "qhe,khe->hqk", query_block, key_heads, preferred_element_type=jnp.float32
                )
                * score_scale
            )
            same_image = image_block[:, None] == image_row[None, :]
            scores = jnp.where(same_image[None], scores, mask_fill)
            attn_probs = jnp.exp(scores - block_sums[:, :, None])
            d_probs = jnp.einsum(
                "qhe,khe->hqk", d_block, value_heads, preferred_element_type=jnp.float32
            )
            row_delta = jnp.sum(attn_probs * d_probs, -1, keepdims=True)
            d_scores = (attn_probs * (d_probs - row_delta)).astype(jnp.bfloat16)
            d_query = (
                jnp.einsum("hqk,khe->qhe", d_scores, key_heads, preferred_element_type=jnp.float32)
                * score_scale
            )
            d_keys = (
                d_keys
                + jnp.einsum(
                    "hqk,qhe->khe", d_scores, query_block, preferred_element_type=jnp.float32
                )
                * score_scale
            )
            d_values = d_values + jnp.einsum(
                "hqk,qhe->khe",
                attn_probs.astype(jnp.bfloat16),
                d_block,
                preferred_element_type=jnp.float32,
            )
            return ((d_keys, d_values), d_query)

        zero_heads = jnp.zeros((length, local_heads, HEAD), jnp.float32)
        (d_keys, d_values), d_queries = lax.scan(
            attend_back, (zero_heads, zero_heads), (query_blocks, image_blocks, log_sums, d_blocks)
        )
        d_query_low = d_queries.reshape(length, head_cols).astype(jnp.bfloat16)
        d_key_low = d_keys.reshape(length, head_cols).astype(jnp.bfloat16)
        d_value_low = d_values.reshape(length, head_cols).astype(jnp.bfloat16)
        d_projected = jnp.stack([d_query_low, d_key_low, d_value_low])
        qkv_term = jnp.einsum(
            "td,cte->dce", gathered, d_projected, preferred_element_type=jnp.float32
        )
        d_normed = lax.psum_scatter(
            jnp.einsum(
                "cte,dce->td", d_projected, qkv_weight, preferred_element_type=jnp.float32
            ).astype(jnp.bfloat16),
            "tensor",
            scatter_dimension=0,
            tiled=True,
        ).astype(jnp.float32)
        d_tokens, gain_one_grad, shift_one_grad = norm_pull(d_normed)
        input_grads.append(d_tokens + d_middle)
        vector_terms = vector_terms + jnp.stack(
            [
                gain_one_grad,
                shift_one_grad,
                jnp.sum(d_middle, 0),
                gain_two_grad,
                shift_two_grad,
                jnp.sum(cotangent, 0),
            ]
        )
        bias_terms = bias_terms + jnp.concatenate(
            [
                jnp.sum(d_query_low, 0, dtype=jnp.float32),
                jnp.sum(d_value_low, 0, dtype=jnp.float32),
                jnp.sum(d_hidden, 0, dtype=jnp.float32),
            ]
        )
        local_terms = (qkv_term, out_term, up_term, down_term)
        owned = (
            lax.psum_scatter(
                local_terms[0].astype(jnp.bfloat16), "dp", scatter_dimension=0, tiled=True
            ).astype(jnp.float32),
            lax.psum_scatter(
                local_terms[1].astype(jnp.bfloat16), "dp", scatter_dimension=1, tiled=True
            ).astype(jnp.float32),
            lax.psum_scatter(
                local_terms[2].astype(jnp.bfloat16), "dp", scatter_dimension=0, tiled=True
            ).astype(jnp.float32),
            lax.psum_scatter(
                local_terms[3].astype(jnp.bfloat16), "dp", scatter_dimension=1, tiled=True
            ).astype(jnp.float32),
        )
        weight_sums = tuple((total + term for total, term in zip(weight_sums, owned)))
    qkv_grad, out_grad, up_grad, down_grad = weight_sums
    tensor_index = lax.axis_index("tensor")
    placed = jnp.where(jnp.arange(splits)[:, None] == tensor_index, bias_terms[None, :], 0.0)
    vec_grad, bias_table = lax.psum((vector_terms, placed), ("dp", "tensor"))
    bias_grad = lax.dynamic_slice_in_dim(bias_table, tensor_index, 1, 0)
    qkv_second_new, qkv_master_new = adam_update(
        qkv_master, qkv_moment, qkv_second, qkv_grad, 0.09, 0.1
    )
    out_second_new, out_master_new = adam_update(
        out_master, out_moment, out_second, out_grad, 0.4, 0.1
    )
    up_second_new, up_master_new = adam_update(up_master, up_moment, up_second, up_grad, 0.09, 0.1)
    down_second_new, down_master_new = adam_update(
        down_master, down_moment, down_second, down_grad, 0.045, 0.1
    )
    vec_second_new, vec_master_new = adam_update(
        vec_master, vec_moment, vec_second, vec_grad, 0.6, 0.0
    )
    bias_second_new, bias_master_new = adam_update(
        bias_master, bias_moment, bias_second, bias_grad, 0.5, 0.0
    )
    block_output = jnp.stack(block_outputs)[:, None]
    input_grad = jnp.stack(input_grads)[:, None]
    return (
        block_output,
        input_grad,
        qkv_grad,
        qkv_second_new,
        qkv_master_new,
        out_grad,
        out_second_new,
        out_master_new,
        up_grad,
        up_second_new,
        up_master_new,
        down_grad,
        down_second_new,
        down_master_new,
        vec_grad,
        vec_second_new,
        vec_master_new,
        bias_grad,
        bias_second_new,
        bias_master_new,
    )


LANES = 128
TILE = 128
SPAN = 256
WIDE = 1152
BATCH = 8


def lane_window(head):
    first = head * HEAD
    low = first // LANES * LANES
    high = -(-(first + HEAD) // LANES) * LANES
    return low, high


def head_mask(head, rows):
    low, high = lane_window(head)
    lane = lax.broadcasted_iota(jnp.int32, (rows, high - low), 1) + low
    return (lane >= head * HEAD) & (lane < head * HEAD + HEAD)


def head_columns(head, columns):
    low, high = lane_window(head)
    high = min(high, columns)
    return slice(low, high), head_mask(head, TILE)[:, : high - low]


def padded(columns):
    return -(-columns // LANES) * LANES


def tile_spans(ids_smem, ids_ref, index, tiles):
    first_id = ids_smem[index * TILE]
    last_id = ids_smem[index * TILE + TILE - 1]
    ids = ids_ref[...]
    begin = jnp.sum((ids < first_id).astype(jnp.int32)) // TILE
    end = (jnp.sum((ids <= last_id).astype(jnp.int32)) + TILE - 1) // TILE
    count = (end - begin + 1) // 2
    return jnp.minimum(begin, tiles - 2 * count), count


def ids_column(ids_ref, index):
    row = ids_ref[:, pl.ds(pl.multiple_of(index * TILE, TILE), TILE)].astype(jnp.float32)
    square = jnp.broadcast_to(row, (TILE, TILE)).T
    return jnp.concatenate([square] * (SPAN // TILE), axis=1).astype(jnp.int32)


NT = (((1,), (1,)), ((), ()))
TN = (((0,), (0,)), ((), ()))


def attend_kernel(heads, length, ids_smem, ids_ref, q_ref, k_ref, v_ref, o_ref, lse_ref, top, total, acc):
    index = pl.program_id(0)
    columns = heads * HEAD
    scale = HEAD ** (-0.5) * math.log2(math.e)
    begin, count = tile_spans(ids_smem, ids_ref, index, length // TILE)
    own_ids = ids_column(ids_ref, index)
    top[...] = jnp.full(top.shape, mask_fill, jnp.float32)
    total[...] = jnp.zeros(total.shape, jnp.float32)
    acc[...] = jnp.zeros(acc.shape, jnp.float32)

    def window(low, high):
        return slice(low, min(high, columns))

    def step(item, carry):
        place = pl.multiple_of((begin + 2 * item) * TILE, TILE)
        keys = pl.ds(place, SPAN)
        same = own_ids == ids_ref[:, keys]
        for first in range(0, heads, BATCH):
            batch = range(first, min(first + BATCH, heads))
            held_scores = []
            for head in batch:
                cols, mask = head_columns(head, columns)
                query = q_ref[:, cols]
                query = jnp.where(mask, query, jnp.zeros_like(query))
                scores = lax.dot_general(query, k_ref[keys, cols], NT, preferred_element_type=jnp.float32)
                held_scores.append(jnp.where(same, scores * scale, mask_fill))
            tops = [jnp.maximum(top[head], jnp.max(scores, -1, keepdims=True)) for head, scores in zip(batch, held_scores)]
            parts = [
                jnp.exp2(scores - jnp.concatenate([now] * (SPAN // LANES), axis=1)) for now, scores in zip(tops, held_scores)
            ]
            sums = [jnp.sum(part, -1, keepdims=True) for part in parts]
            mixes = [
                jnp.dot(part.astype(jnp.bfloat16), v_ref[keys, head_columns(head, columns)[0]], preferred_element_type=jnp.float32)
                for head, part in zip(batch, parts)
            ]
            for head, now, part_sum, mixed in zip(batch, tops, sums, mixes):
                cols, mask = head_columns(head, columns)
                shrink = jnp.exp2(top[head] - now)
                total[head] = total[head] * shrink + part_sum
                top[head] = now
                width = cols.stop - cols.start
                wide = jnp.concatenate([shrink] * ((width + LANES - 1) // LANES), axis=1)[:, :width]
                held = acc[:, cols]
                acc[:, cols] = jnp.where(mask, held * wide + mixed, held)
        return carry

    lax.fori_loop(0, count, step, 0)
    sums = jnp.zeros((TILE, LANES), jnp.float32)
    lane = lax.broadcasted_iota(jnp.int32, (TILE, LANES), 1)
    for head in range(heads):
        low, high = lane_window(head)
        high = min(high, columns)
        cols = slice(low, high)
        mask = head_mask(head, TILE)[:, : high - low]
        inverse = 1.0 / total[head]
        wide = jnp.concatenate([inverse] * ((high - low + LANES - 1) // LANES), axis=1)[:, : high - low]
        held = acc[:, cols]
        acc[:, cols] = jnp.where(mask, held * wide, held)
        sums = jnp.where(lane == head, top[head] + jnp.log2(total[head]), sums)
    o_ref[...] = acc[...].astype(o_ref.dtype)
    lse_ref[...] = sums.T[:heads]


def attend(ids, query, key, value):
    length, columns = query.shape
    heads = columns // HEAD
    tiles = length // TILE
    whole = pl.BlockSpec((length, columns), lambda i, s: (0, 0))
    block = pl.BlockSpec((TILE, columns), lambda i, s: (i, 0))
    return pl.pallas_call(
        partial(attend_kernel, heads, length),
        grid_spec=pltpu.PrefetchScalarGridSpec(
            num_scalar_prefetch=1,
            grid=(tiles,),
            in_specs=[pl.BlockSpec((1, length), lambda i, s: (0, 0)), block, whole, whole],
            out_specs=[block, pl.BlockSpec((heads, TILE), lambda i, s: (0, i))],
            scratch_shapes=[
                pltpu.VMEM((heads, TILE, LANES), jnp.float32),
                pltpu.VMEM((heads, TILE, LANES), jnp.float32),
                pltpu.VMEM((TILE, columns), jnp.float32),
            ],
        ),
        out_shape=[
            jax.ShapeDtypeStruct((length, columns), jnp.bfloat16),
            jax.ShapeDtypeStruct((heads, length), jnp.float32),
        ],
        compiler_params=pltpu.CompilerParams(vmem_limit_bytes=36 << 20),
        cost_estimate=pl.CostEstimate(flops=4 * 10**9, bytes_accessed=10**6, transcendentals=0),
    )(ids, ids.reshape(1, length), query, key, value)


def attend_back_kernel(
    heads, length, ids_smem, ids_ref, q_ref, k_ref, v_ref, o_ref, g_ref, lse_ref,
    dq_ref, dk_ref, dv_ref, delta, dq_acc, dk_acc, dv_acc,
):
    index = pl.program_id(0)
    columns = heads * HEAD
    natural = HEAD ** (-0.5)
    scale = natural * math.log2(math.e)
    tiles = length // TILE
    begin, count = tile_spans(ids_smem, ids_ref, index, tiles)
    own_ids = ids_column(ids_ref, index)

    @pl.when(index == 0)
    def _():
        dq_acc[...] = jnp.zeros(dq_acc.shape, jnp.float32)
        row = lax.broadcasted_iota(jnp.int32, (heads, columns), 0)
        lane = lax.broadcasted_iota(jnp.int32, (heads, columns), 1)
        pick = ((lane >= row * HEAD) & (lane < row * HEAD + HEAD)).astype(jnp.bfloat16)
        product = g_ref[...].astype(jnp.float32) * o_ref[...].astype(jnp.float32)
        coarse = product.astype(jnp.bfloat16)
        fine = (product - coarse.astype(jnp.float32)).astype(jnp.bfloat16)
        delta[...] = lax.dot_general(pick, coarse, NT, preferred_element_type=jnp.float32) + lax.dot_general(
            pick, fine, NT, preferred_element_type=jnp.float32
        )

    dk_acc[...] = jnp.zeros(dk_acc.shape, jnp.float32)
    dv_acc[...] = jnp.zeros(dv_acc.shape, jnp.float32)

    def step(item, carry):
        place = pl.multiple_of((begin + 2 * item) * TILE, TILE)
        rows = pl.ds(place, SPAN)
        same = own_ids == ids_ref[:, rows]
        for first in range(0, heads, BATCH):
            batch = range(first, min(first + BATCH, heads))
            keys, scores, d_probs = [], [], []
            for head in batch:
                cols, mask = head_columns(head, columns)
                key = k_ref[:, cols]
                keys.append(jnp.where(mask, key, jnp.zeros_like(key)))
                value = v_ref[:, cols]
                value = jnp.where(mask, value, jnp.zeros_like(value))
                scores.append(lax.dot_general(keys[-1], q_ref[rows, cols], NT, preferred_element_type=jnp.float32))
                d_probs.append(lax.dot_general(value, g_ref[rows, cols], NT, preferred_element_type=jnp.float32))
            probs = [
                jnp.exp2(jnp.where(same, score * scale, mask_fill) - lse_ref[head : head + 1, rows])
                for head, score in zip(batch, scores)
            ]
            d_scores = [
                (prob * (d_prob - delta[head : head + 1, rows])).astype(jnp.bfloat16)
                for head, prob, d_prob in zip(batch, probs, d_probs)
            ]
            for head, key, prob, d_score in zip(batch, keys, probs, d_scores):
                cols, mask = head_columns(head, columns)
                d_value = jnp.dot(prob.astype(jnp.bfloat16), g_ref[rows, cols], preferred_element_type=jnp.float32)
                d_key = jnp.dot(d_score, q_ref[rows, cols], preferred_element_type=jnp.float32)
                d_query = lax.dot_general(d_score, key, TN, preferred_element_type=jnp.float32)
                dv_acc[:, cols] += jnp.where(mask, d_value, 0.0)
                dk_acc[:, cols] += jnp.where(mask, d_key, 0.0)
                dq_acc[rows, cols] += d_query
        return carry

    lax.fori_loop(0, count, step, 0)
    dk_ref[...] = (dk_acc[...] * natural).astype(dk_ref.dtype)
    dv_ref[...] = dv_acc[...].astype(dv_ref.dtype)

    @pl.when(index == tiles - 1)
    def _():
        dq_ref[...] = (dq_acc[...] * natural).astype(dq_ref.dtype)


def attend_back(ids, query, key, value, attended, grad, lse):
    length, columns = query.shape
    heads = columns // HEAD
    tiles = length // TILE
    whole = pl.BlockSpec((length, columns), lambda i, s: (0, 0))
    block = pl.BlockSpec((TILE, columns), lambda i, s: (i, 0))
    out = jax.ShapeDtypeStruct((length, columns), jnp.bfloat16)
    return pl.pallas_call(
        partial(attend_back_kernel, heads, length),
        grid_spec=pltpu.PrefetchScalarGridSpec(
            num_scalar_prefetch=1,
            grid=(tiles,),
            in_specs=[
                pl.BlockSpec((1, length), lambda i, s: (0, 0)),
                whole,
                block,
                block,
                whole,
                whole,
                pl.BlockSpec((heads, length), lambda i, s: (0, 0)),
            ],
            out_specs=[whole, block, block],
            scratch_shapes=[
                pltpu.VMEM((heads, length), jnp.float32),
                pltpu.VMEM((length, columns), jnp.float32),
                pltpu.VMEM((TILE, columns), jnp.float32),
                pltpu.VMEM((TILE, columns), jnp.float32),
            ],
        ),
        out_shape=[out, out, out],
        compiler_params=pltpu.CompilerParams(vmem_limit_bytes=36 << 20),
        cost_estimate=pl.CostEstimate(flops=2 * 10**9, bytes_accessed=10**6, transcendentals=0),
    )(ids, ids.reshape(1, length), query, key, value, attended, grad, lse)


def column_call(kernel, ins, outs, columns, flops, scratch=()):
    wide = min(WIDE, padded(columns))
    steps = -(-columns // wide)

    def spec(shape, cut):
        if cut:
            return pl.BlockSpec(shape[:-1] + (wide,), lambda i: (0,) * (len(shape) - 1) + (i,))
        return pl.BlockSpec(shape, lambda i: (0,) * len(shape))

    size = sum(math.prod(a.shape) * a.dtype.itemsize for a, _ in ins) + sum(
        math.prod(a.shape) * a.dtype.itemsize for a in outs
    )
    return pl.pallas_call(
        kernel,
        grid=(steps,),
        in_specs=[spec(a.shape, cut) for a, cut in ins],
        out_specs=[spec(a.shape, True) for a in outs],
        out_shape=outs,
        scratch_shapes=list(scratch),
        compiler_params=pltpu.CompilerParams(vmem_limit_bytes=44 << 20),
        cost_estimate=pl.CostEstimate(flops=flops // 8, bytes_accessed=size // 8, transcendentals=0),
    )(*[a for a, _ in ins])


def hidden_kernel(x_ref, w_ref, b_ref, active_ref, slope_ref):
    rows = 256
    for block in range(x_ref.shape[0] // rows):
        part = pl.ds(block * rows, rows)
        value = jnp.dot(x_ref[part, :], w_ref[...], preferred_element_type=jnp.float32) + b_ref[...]
        active, slope = gelu_pair(value)
        active_ref[part, :] = active.astype(jnp.bfloat16)
        slope_ref[part, :] = slope.astype(jnp.bfloat16)


def hidden_units(x, weight, bias):
    tokens, columns = x.shape[0], weight.shape[1]
    out = jax.ShapeDtypeStruct((tokens, columns), jnp.bfloat16)
    ins = [(x, False), (weight, True), (bias.reshape(1, columns), True)]
    return column_call(hidden_kernel, ins, [out, out], columns, 2 * tokens * x.shape[1] * columns)


def hidden_back_kernel(x_ref, w_ref, slope_ref, grad_ref, sum_ref):
    rows = 256
    total = jnp.zeros(sum_ref.shape, jnp.float32)
    for block in range(x_ref.shape[0] // rows):
        part = pl.ds(block * rows, rows)
        value = jnp.dot(x_ref[part, :], w_ref[...], preferred_element_type=jnp.float32)
        value = value * slope_ref[part, :].astype(jnp.float32)
        grad_ref[part, :] = value.astype(jnp.bfloat16)
        total = total + jnp.sum(value, 0, keepdims=True)
    sum_ref[...] = total


def hidden_back(x, weight, slope):
    tokens, columns = x.shape[0], weight.shape[1]
    outs = [jax.ShapeDtypeStruct((tokens, columns), jnp.bfloat16), jax.ShapeDtypeStruct((1, columns), jnp.float32)]
    ins = [(x, False), (weight, True), (slope, True)]
    return column_call(hidden_back_kernel, ins, outs, columns, 2 * tokens * x.shape[1] * columns)


def grad_kernel(chunks, stacked, x_ref, *refs):
    core = lax.axis_index("dp") % 2
    count = len(refs) - 4 if stacked else (len(refs) - 2) // 3
    turned, result = refs[-2:]
    dy_refs = refs[:count]
    outs = refs[count:-2]

    @pl.when(pl.program_id(0) == 0)
    def _():
        turned[...] = x_ref[...].T

    rows = turned.shape[0] // chunks
    for number, dy_ref in enumerate(dy_refs):
        if stacked:
            sent_ref, kept_ref = outs[0].at[number], outs[1].at[number]
        else:
            sent_ref, kept_ref = outs[number], outs[count + number]
        result[...] = jnp.dot(turned[...], dy_ref[...], preferred_element_type=jnp.float32)
        for spot in range(chunks // 2):
            sent = pl.multiple_of((2 * spot + 1 - core) * rows, 8)
            kept = pl.multiple_of((2 * spot + core) * rows, 8)
            sent_ref[spot] = result[pl.ds(sent, rows), :].astype(jnp.bfloat16)
            kept_ref[spot] = result[pl.ds(kept, rows), :].astype(jnp.bfloat16)


def weight_grads(x, parts, stacked=False):
    tokens, features = x.shape
    columns = parts[0].shape[1]
    count = len(parts)
    wide = min(WIDE, padded(columns))
    shape = (8, features // 16, columns)
    outs = [jax.ShapeDtypeStruct(shape, jnp.bfloat16)] * (2 * count)
    if stacked:
        outs = [jax.ShapeDtypeStruct((count,) + shape, jnp.bfloat16)] * 2
    results = column_call(
        partial(grad_kernel, 16, stacked),
        [(x, False)] + [(part, True) for part in parts],
        outs,
        columns,
        2 * tokens * features * columns * count,
        [pltpu.VMEM((features, tokens), jnp.bfloat16), pltpu.VMEM((features, wide), jnp.float32)],
    )
    return results if stacked else (results[:count], results[count:])


def place_kernel(leads, ordered, steps, *refs):
    pieces = refs[: len(steps)]
    outs = refs[len(steps) : len(steps) + leads]
    sems = refs[len(steps) + leads]
    spot = lax.axis_index("dp")
    z, y, core = spot // 4, spot // 2 % 2, spot % 2
    copies = []
    for piece, (first_slot, y_step, core_step) in zip(pieces, steps):
        column = (y + y_step) % 2 * 2 + (core + core_step) % 2
        for slot in range(piece.shape[0]):
            number = first_slot + slot
            row = (number if ordered else (z + 4 - number) % 4) * 4 + column
            for lead in range(leads):
                copy = pltpu.make_async_copy(piece.at[slot, lead], outs[lead].at[row], sems.at[len(copies)])
                copy.start()
                copies.append(copy)
    for copy in copies:
        copy.wait()


def place(planes, ordered):
    pieces = sum(planes, [])
    leads, rows, columns = pieces[0].shape[1:]
    slots = pieces[0].shape[0]
    steps = [(start, step % 2, step // 2) for start in range(0, 4, slots) for step in range(4)]
    size = 16 * leads * rows * padded(columns) * 2
    placed = pl.pallas_call(
        partial(place_kernel, leads, ordered, steps),
        in_specs=[pl.BlockSpec(memory_space=pl.ANY)] * len(pieces),
        out_specs=[pl.BlockSpec(memory_space=pltpu.VMEM)] * leads,
        out_shape=[jax.ShapeDtypeStruct((16, rows, columns), jnp.bfloat16)] * leads,
        scratch_shapes=[pltpu.SemaphoreType.DMA((16 * leads,))],
        compiler_params=pltpu.CompilerParams(vmem_limit_bytes=size * 3 // 2 + (2 << 20)),
        cost_estimate=pl.CostEstimate(flops=0, bytes_accessed=size // 4, transcendentals=0),
    )(*pieces)
    return [part.reshape(16 * rows, columns) for part in placed]


def swap_x(value):
    return lax.ppermute(value, "tensor", [(0, 1), (1, 0)])


def swap_y(value):
    return lax.ppermute(value, "dp", [(spot, spot ^ 2) for spot in range(16)])


def swap_core(value):
    return lax.ppermute(value, "dp", [(spot, spot ^ 1) for spot in range(16)])


def move_z(value, steps):
    return lax.ppermute(value, "dp", [(spot, (spot + 4 * steps) % 16) for spot in range(16)])


def tie(*values):
    return lax.optimization_barrier(values)


def gather_z(shard):
    groups = [[spot + 4 * z for z in range(4)] for spot in range(4)]
    return lax.all_gather(shard, "dp", axis_index_groups=groups)


def both_cores(parts):
    return parts + [swap_core(part) for part in parts]


def add_low(*terms):
    total = terms[0].astype(jnp.float32)
    for term in terms[1:]:
        total = total + term.astype(jnp.float32)
    return total.astype(jnp.bfloat16)


def part_of(value, index, axis):
    return lax.dynamic_index_in_dim(value, index, axis, keepdims=False)


def y_parts(value):
    spot = lax.axis_index("dp")
    split = value.reshape((value.shape[0] // 2, 2) + value.shape[1:])
    return part_of(split, spot // 2 % 2, 1), part_of(split, 1 - spot // 2 % 2, 1)


class Planes:
    def __init__(self, own, other):
        half = own.shape[0] // 2
        self.near_own, near_own = y_parts(own[:half])
        self.near_other, near_other = y_parts(other[:half])
        self.far_own = own[half:]
        self.sent = [jnp.stack([near_own, near_other]), other[half:]]

    def first(self):
        self.got = [swap_y(self.sent[0]), swap_x(self.sent[1])]

    def middle(self):
        self.near_own = add_low(self.near_own, self.got[0][0])
        self.far_own, far = y_parts(add_low(self.far_own, self.got[1]))
        self.sent = [add_low(self.near_other, self.got[0][1]), far]

    def second(self):
        self.got = [swap_x(self.sent[0]), swap_y(self.sent[1])]

    def total(self):
        return jnp.concatenate([add_low(self.near_own, self.got[0]), add_low(self.far_own, self.got[1])])


def scatter_z(value):
    groups = [[spot + 4 * z for z in range(4)] for spot in range(4)]
    return lax.psum_scatter(value, "dp", axis_index_groups=groups)


def send_z(value):
    z = lax.axis_index("dp") // 4
    return [part_of(value, z, 0)] + [move_z(part_of(value, (z + steps) % 4, 0), steps) for steps in (1, 2, 3)]


def sum_terms(terms):
    total = terms[0].astype(jnp.float32)
    for term in terms[1:]:
        total = total + term.astype(jnp.float32)
    return total


def norm_forward(values):
    centre = values - jnp.mean(values, -1, keepdims=True)
    inverse = lax.rsqrt(jnp.mean(centre * centre, -1, keepdims=True) + norm_eps)
    return centre * inverse, inverse


def norm_back(grad, hat, inverse, gain):
    scaled = grad * gain
    mean_one = jnp.mean(scaled, -1, keepdims=True)
    mean_two = jnp.mean(scaled * hat, -1, keepdims=True)
    return (scaled - mean_one - hat * mean_two) * inverse


def gelu_pair(value):
    inner = math.sqrt(2.0 / math.pi)
    squared = value * value
    bent = jnp.tanh(inner * (value + 0.044715 * value * squared))
    half = 0.5 * (1.0 + bent)
    slope = half + 0.5 * value * (1.0 - bent * bent) * inner * (1.0 + 3 * 0.044715 * squared)
    return value * half, slope


def row_layer(
    block_input,
    image_ids,
    out_cotangent,
    qkv_master,
    qkv_moment,
    qkv_second,
    out_master,
    out_moment,
    out_second,
    up_master,
    up_moment,
    up_second,
    down_master,
    down_moment,
    down_second,
    vec_master,
    vec_moment,
    vec_second,
    bias_master,
    bias_moment,
    bias_second,
):
    low = jnp.bfloat16
    wide = jnp.float32
    mine = lax.axis_index("tensor")
    first = mine == 0
    half = block_input.shape[2]
    features = block_input.shape[3]
    head_cols = qkv_master.shape[2]

    def pick(pair, index):
        return lax.dynamic_index_in_dim(pair, index, 0, keepdims=False)

    def in_order(own, other, axis=0):
        return jnp.concatenate([jnp.where(first, own, other), jnp.where(first, other, own)], axis)

    def dot(spec, left, right):
        return jnp.einsum(spec, left, right, preferred_element_type=wide)

    inputs_own = pick(block_input[:, 0], mine)
    inputs_sent = pick(block_input[:, 0], 1 - mine)
    cot_own = pick(out_cotangent[:, 0], mine)
    cot_sent = pick(out_cotangent[:, 0], 1 - mine)
    inputs_low = inputs_sent.astype(low)
    early_shard = jnp.stack([qkv_master[:, 0], qkv_master[:, 1], qkv_master[:, 2]]).astype(low)
    early_shard, inputs_low = tie(early_shard, inputs_low)
    inputs_got = swap_x(inputs_low)
    early_one = move_z(early_shard, 1)
    early_three = move_z(early_shard, 3)
    early_shard, early_one = tie(early_shard, early_one)
    early_two = move_z(early_shard, 2)
    near = jnp.stack([early_shard, early_one])
    near_y, near_x = swap_y(near), swap_x(near)
    late_shard = jnp.stack([up_master, down_master.T]).astype(low)
    small = jnp.concatenate([pick(image_ids[:, 0], 1 - mine).astype(wide), bias_master[0]])
    cot_sum = jnp.sum(out_cotangent[:, 0], (0, 1))
    late_shard, small, cot_sum, early_two, early_three, inputs_got, near_x, near_y = tie(
        late_shard, small, cot_sum, early_two, early_three, inputs_got, near_x, near_y
    )
    small_got = swap_x(small[None])[0]
    late_z = gather_z(late_shard)
    far = jnp.stack([early_two, early_three])
    far_y, far_x = swap_y(far), swap_x(far)
    near_xy, far_yx = swap_y(near_x), swap_x(far_y)
    early_own = place([both_cores([near, near_y]), both_cores([far, far_y])], False)
    out_shard, early_own = tie(out_master.T.astype(low), early_own)
    out_whole = lax.all_gather(out_shard, ("tensor", "dp")).reshape(2, features, head_cols)
    inputs = in_order(inputs_own, inputs_got.astype(wide))
    ids = in_order(pick(image_ids[:, 0], mine), small_got[:half].astype(jnp.int32))
    biases = jnp.stack([bias_master[0], small_got[half:]])

    hat_one, inverse_one = norm_forward(inputs)
    normed = (hat_one * vec_master[0] + vec_master[1]).astype(low)
    def project(g, weights):
        query = (dot("td,de->te", normed, weights[0]) + biases[g, :head_cols]).astype(low)
        key = dot("td,de->te", normed, weights[1]).astype(low)
        value = (dot("td,de->te", normed, weights[2]) + biases[g, head_cols : 2 * head_cols]).astype(low)
        return query, key, value

    projected = [project(0, early_own), None]
    attended, log_sums = [None, None], [None, None]
    attended[0], log_sums[0] = attend(ids, *projected[0])
    others = [both_cores([near_x, near_xy]), both_cores([far_x, far_yx])]
    others, attended[0] = tie(others, attended[0])
    early_other = place(others, False)
    up_near, up_far = [late_z[start : start + 2, :1] for start in (0, 2)]
    down_near, down_far = [late_z[start : start + 2, 1:] for start in (0, 2)]
    early_other, up_near, up_far = tie(early_other, up_near, up_far)
    up_near_x, up_far_y = swap_x(up_near), swap_y(up_far)
    projected[1] = project(1, early_other)
    query_weight, key_weight, value_weight = zip(early_own, early_other)
    projected[1], up_near, up_far, up_near_x, up_far_y = tie(projected[1], up_near, up_far, up_near_x, up_far_y)
    up_near_y, up_far_x = swap_y(up_near), swap_x(up_far)
    attended[1], log_sums[1] = attend(ids, *projected[1])
    attended[1], up_near_x, up_far_y, up_near_y, up_far_x = tie(
        attended[1], up_near_x, up_far_y, up_near_y, up_far_x
    )
    up_near_xy, up_far_yx = swap_y(up_near_x), swap_x(up_far_y)
    cot_got = swap_x(cot_sent.astype(low))
    out_weight = [pick(out_whole, mine), pick(out_whole, 1 - mine)]
    attn_sum = sum(dot("te,de->td", attended[g], out_weight[g]) for g in range(2)) + vec_master[2]
    middle = inputs + attn_sum
    hat_two, inverse_two = norm_forward(middle)
    normed_two = (hat_two * vec_master[3] + vec_master[4]).astype(low)
    normed_two, up_near_xy, up_far_yx, down_near, down_far = tie(
        normed_two, up_near_xy, up_far_yx, down_near, down_far
    )
    down_near_x, down_far_y = swap_x(down_near), swap_y(down_far)
    up_weight = [
        place([both_cores([up_near, up_near_y]), both_cores([up_far, up_far_y])], True)[0],
        place([both_cores([up_near_x, up_near_xy]), both_cores([up_far_x, up_far_yx])], True)[0],
    ]
    active, slope = [None, None], [None, None]
    active[0], slope[0] = hidden_units(normed_two, up_weight[0], biases[0, 2 * head_cols :])
    normed_two, active[0], down_near, down_far, down_near_x, down_far_y = tie(
        normed_two, active[0], down_near, down_far, down_near_x, down_far_y
    )
    down_near_y, down_far_x = swap_y(down_near), swap_x(down_far)
    active[1], slope[1] = hidden_units(normed_two, up_weight[1], biases[1, 2 * head_cols :])
    active[1], down_near_x, down_far_y, down_near_y, down_far_x = tie(
        active[1], down_near_x, down_far_y, down_near_y, down_far_x
    )
    down_weight = [place([both_cores([down_near, down_near_y]), both_cores([down_far, down_far_y])], True)[0], None]
    active[1], down_weight[0], down_near_x, down_far_y = tie(active[1], down_weight[0], down_near_x, down_far_y)
    down_near_xy, down_far_yx = swap_y(down_near_x), swap_x(down_far_y)
    cot_row = in_order(cot_own, cot_got.astype(wide))
    cot_low = cot_row.astype(low)
    down_sent, down_kept = weight_grads(cot_low, active)
    down_sent, down_near_xy, down_far_yx = tie(down_sent, down_near_xy, down_far_yx)
    down_weight[1] = place(
        [both_cores([down_near_x, down_near_xy]), both_cores([down_far_x, down_far_yx])], True
    )[0]
    added = attn_sum + sum(dot("tf,df->td", active[g], down_weight[g]) for g in range(2)) + vec_master[5]
    added = added.reshape(2, half, features)
    added_got = swap_x(pick(added, 1 - mine).astype(low))

    own, other = 0, 1
    down_core = [swap_core(part) for part in down_sent]
    d_hidden, hidden_sums = [None, None], [None, None]
    d_hidden[own], hidden_sums[own] = hidden_back(cot_low, down_weight[own], slope[own])
    d_hidden[own], down_core = tie(d_hidden[own], down_core)
    down = Planes(*[add_low(down_kept[g], down_core[g]) for g in range(2)])
    cot_late, down.sent = tie(cot_low, down.sent)
    down.first()
    d_hidden[other], hidden_sums[other] = hidden_back(cot_late, down_weight[other], slope[other])
    up_sent, up_kept = weight_grads(normed_two, d_hidden)
    up_sent, down.got = tie(up_sent, down.got)
    up_core = [swap_core(part) for part in up_sent]
    down.middle()
    d_hidden, down.sent = tie(d_hidden, down.sent)
    down.second()
    d_normed_two = sum(dot("tf,df->td", d_hidden[g], up_weight[g]) for g in range(2))
    d_normed_two, up_core, down.got = tie(d_normed_two, up_core, down.got)
    up = Planes(*[add_low(up_kept[g], up_core[g]) for g in range(2)])
    down_total = down.total()
    d_normed_two, up.sent, down_total = tie(d_normed_two, up.sent, down_total)
    up.first()
    down_term = scatter_z(down_total)
    mid_added = norm_back(d_normed_two, hat_two, inverse_two, vec_master[3])
    d_middle = cot_row + mid_added
    mid_low = d_middle.astype(low)
    d_attended = [dot("td,de->te", mid_low, out_weight[g]).astype(low) for g in range(2)]
    out_sent, out_kept = weight_grads(mid_low, attended)
    d_attended[other], out_sent, added_got = tie(d_attended[other], out_sent, added_got)
    out_core = [swap_core(part) for part in out_sent]

    def back(g, grad):
        return attend_back(ids, *projected[g], attended[g], grad, log_sums[g])

    d_other = back(other, d_attended[other])
    d_other, out_core, up.got = tie(d_other, out_core, up.got)
    up.middle()
    out_other = add_low(out_kept[other], out_core[other])
    out_own = add_low(out_kept[own], out_core[own])
    d_other, up.sent, out_other = tie(d_other, up.sent, out_other)
    up.second()
    out_there_x = swap_x(out_other)
    qkv_sent, qkv_kept = [None, None], [None, None]
    qkv_sent[other], qkv_kept[other] = weight_grads(normed, d_other, True)

    def normed_part(parts, g):
        weights = (query_weight, key_weight, value_weight)
        return sum(dot("te,de->td", part, weight[g]) for part, weight in zip(parts, weights))

    d_other, qkv_sent[other] = tie(d_other, qkv_sent[other])
    qkv_core_other = swap_core(qkv_sent[other])
    d_normed_other = normed_part(d_other, other)
    d_normed_other, up.got, qkv_core_other = tie(d_normed_other, up.got, qkv_core_other)
    up_total = up.total()
    qkv_other_here, qkv_other_there = zip(*[y_parts(part) for part in add_low(qkv_kept[other], qkv_core_other)])
    qkv_other_there = jnp.stack(qkv_other_there)
    d_attended[own], up_total, qkv_other_there = tie(d_attended[own], up_total, qkv_other_there)
    up_term = scatter_z(up_total)
    qkv_there_y = swap_y(qkv_other_there)
    d_own = back(own, d_attended[own])
    d_own, qkv_there_y, out_there_x = tie(tuple(d_own), qkv_there_y, out_there_x)
    qkv_other = add_low(jnp.stack(qkv_other_here), qkv_there_y)
    out_here, out_there = y_parts(add_low(out_own, out_there_x))
    d_own, qkv_other, out_there = tie(d_own, qkv_other, out_there)
    qkv_there_x = swap_x(qkv_other)
    out_there_y = swap_y(out_there)
    qkv_sent[own], qkv_kept[own] = weight_grads(normed, d_own, True)
    d_own, qkv_sent[own], out_there_y = tie(d_own, qkv_sent[own], out_there_y)
    out_terms = send_z(add_low(out_here, out_there_y))
    qkv_core_own = swap_core(qkv_sent[own])
    d_normed_own = normed_part(d_own, own)
    d_normed_own, qkv_core_own, qkv_there_x, out_terms = tie(d_normed_own, qkv_core_own, qkv_there_x, out_terms)
    qkv_here, qkv_there = zip(*[y_parts(part) for part in add_low(qkv_kept[own], qkv_core_own)])
    qkv_there = [jnp.stack(qkv_there[:1]), jnp.stack(qkv_there[1:])]
    d_normed_own, qkv_there = tie(d_normed_own, qkv_there)
    qkv_there_y = [swap_y(part) for part in qkv_there]
    d_normed = d_normed_other + d_normed_own
    early = jnp.concatenate(
        [
            jnp.sum(d_middle, 0),
            jnp.sum(d_normed_two * hat_two, 0),
            jnp.sum(d_normed_two, 0),
            cot_sum,
        ]
    )

    def bias_rows(sums):
        return jnp.where(first, jnp.concatenate(sums), jnp.concatenate(sums[::-1]))

    sums = jnp.concatenate(
        [
            jnp.sum(d_normed * hat_one, 0),
            jnp.sum(d_normed, 0),
            early,
            bias_rows([jnp.sum(part[0], 0, dtype=wide) for part in (d_own, d_other)]),
            bias_rows([jnp.sum(part[2], 0, dtype=wide) for part in (d_own, d_other)]),
            bias_rows([part[0] for part in hidden_sums]),
        ]
    )
    sums, qkv_there_y[0] = tie(sums, qkv_there_y[0])
    in_added = (mid_added + norm_back(d_normed, hat_one, inverse_one, vec_master[0])).reshape(2, half, features)
    in_sent = pick(in_added, 1 - mine).astype(low)
    sums = sums[None]
    sums = sums + move_z(sums, 1) + move_z(sums, 2) + move_z(sums, 3)
    in_got = swap_x(in_sent)
    sums, qkv_there_y, in_got, added_got = tie(sums, qkv_there_y, in_got, added_got)
    qkv_terms = send_z(add_low(jnp.stack(qkv_here), jnp.concatenate(qkv_there_y), qkv_there_x).transpose(1, 0, 2, 3))
    sums = sums + swap_core(sums)
    sums = sums + swap_y(sums)
    sums = (sums + swap_x(sums))[0]
    block_here = inputs_own + pick(added, mine)
    block_there = pick(block_input[:, 0], 1 - mine) + added_got.astype(wide)
    block_output = in_order(block_here[None], block_there[None])[:, None]
    down_term, up_term, out_terms, added_got = tie(down_term, up_term, out_terms, added_got)
    down_grad = down_term.astype(wide).T
    up_grad = up_term.astype(wide)
    out_grad = sum_terms(out_terms).T
    qkv_grad = sum_terms(qkv_terms).transpose(1, 0, 2)
    grad_here = cot_own + pick(in_added, mine)
    grad_there = cot_sent + in_got.astype(wide)
    input_grad = in_order(grad_here[None], grad_there[None])[:, None]
    vec_grad = sums[: 6 * features].reshape(6, features)

    def group(start, size):
        return pick(sums[start : start + 2 * size].reshape(2, size), mine)

    start = 6 * features
    bias_grad = jnp.concatenate(
        [
            group(start, head_cols),
            group(start + 2 * head_cols, head_cols),
            group(start + 4 * head_cols, up_master.shape[1]),
        ]
    )[None]

    results = [block_output, input_grad]
    for master, moment, second, grad, rate, decay in (
        (qkv_master, qkv_moment, qkv_second, qkv_grad, 0.09, 0.1),
        (out_master, out_moment, out_second, out_grad, 0.4, 0.1),
        (up_master, up_moment, up_second, up_grad, 0.09, 0.1),
        (down_master, down_moment, down_second, down_grad, 0.045, 0.1),
        (vec_master, vec_moment, vec_second, vec_grad, 0.6, 0.0),
        (bias_master, bias_moment, bias_second, bias_grad, 0.5, 0.0),
    ):
        second_new, master_new = adam_update(master, moment, second, grad, rate, decay)
        results += [grad, second_new, master_new]
    return tuple(results)


def solution(mesh):
    placed = (
        P(None, "dp", "tensor", None),
        P(None, "dp", "tensor"),
        P(None, "dp", "tensor", None),
        P("dp", None, "tensor"),
        P("dp", None, "tensor"),
        P("dp", None, "tensor"),
        P("tensor", "dp"),
        P("tensor", "dp"),
        P("tensor", "dp"),
        P("dp", "tensor"),
        P("dp", "tensor"),
        P("dp", "tensor"),
        P("tensor", "dp"),
        P("tensor", "dp"),
        P("tensor", "dp"),
        P(),
        P(),
        P(),
        P("tensor", None),
        P("tensor", None),
        P("tensor", None),
    )
    by_rows = dict(mesh.shape) == {"dp": 16, "tensor": 2}
    return jax.shard_map(
        row_layer if by_rows else split_layer,
        mesh=mesh,
        in_specs=placed,
        out_specs=(
            P(None, "dp", "tensor", None),
            P(None, "dp", "tensor", None),
            P("dp", None, "tensor"),
            P("dp", None, "tensor"),
            P("dp", None, "tensor"),
            P("tensor", "dp"),
            P("tensor", "dp"),
            P("tensor", "dp"),
            P("dp", "tensor"),
            P("dp", "tensor"),
            P("dp", "tensor"),
            P("tensor", "dp"),
            P("tensor", "dp"),
            P("tensor", "dp"),
            P(),
            P(),
            P(),
            P("tensor", None),
            P("tensor", None),
            P("tensor", None),
        ),
        check_vma=False,
    )
```

```python
import math
from functools import partial

import jax
import jax.numpy as jnp
from jax import lax
from jax.experimental import pallas as pl
from jax.experimental.pallas import tpu as pltpu
from jax.sharding import PartitionSpec as P

HEAD = 72
STEP = 10


norm_eps = 1e-06
mask_fill = -1e30
beta_one = 0.9
beta_two = 0.95
adam_eps = 1e-08


def layer_norm(values, scale_vec, shift_vec):
    centre = values - jnp.mean(values, -1, keepdims=True)
    spread = jnp.mean(centre * centre, -1, keepdims=True)
    return centre * lax.rsqrt(spread + norm_eps) * scale_vec + shift_vec


def adam_update(master, moment, second, gradient, step_rate, weight_decay):
    first_moment = beta_one * moment.astype(jnp.float32) + (1.0 - beta_one) * gradient
    second_new = beta_two * second + (1.0 - beta_two) * gradient * gradient
    update = (
        first_moment
        / (1.0 - beta_one**STEP)
        / (jnp.sqrt(second_new / (1.0 - beta_two**STEP)) + adam_eps)
        + weight_decay * master
    )
    return (second_new, master - step_rate * update)


def split_layer(
    block_input,
    image_ids,
    out_cotangent,
    qkv_master,
    qkv_moment,
    qkv_second,
    out_master,
    out_moment,
    out_second,
    up_master,
    up_moment,
    up_second,
    down_master,
    down_moment,
    down_second,
    vec_master,
    vec_moment,
    vec_second,
    bias_master,
    bias_moment,
    bias_second,
):
    batches = block_input.shape[0]
    local_rows = block_input.shape[2]
    features = block_input.shape[3]
    splits = lax.axis_size("tensor")
    length = local_rows * splits
    head_cols = qkv_master.shape[2]
    local_heads = head_cols // HEAD
    block_rows = min(512, length)
    block_count = length // block_rows
    score_scale = HEAD ** (-0.5)
    biases = bias_master[0]
    query_bias = biases[:head_cols]
    value_bias = biases[head_cols : 2 * head_cols]
    hidden_bias = biases[2 * head_cols :]
    compute = (
        qkv_master.astype(jnp.bfloat16),
        out_master.astype(jnp.bfloat16),
        up_master.astype(jnp.bfloat16),
        down_master.astype(jnp.bfloat16),
    )
    gelu_tanh = partial(jax.nn.gelu, approximate=True)
    weight_sums = (
        jnp.zeros_like(qkv_master),
        jnp.zeros_like(out_master),
        jnp.zeros_like(up_master),
        jnp.zeros_like(down_master),
    )
    vector_terms = jnp.zeros((6, features), jnp.float32)
    bias_terms = jnp.zeros(biases.shape, jnp.float32)
    block_outputs = []
    input_grads = []
    for batch_index in range(batches):
        qkv_weight, out_weight, up_weight, down_weight = (
            lax.all_gather(compute[0], "dp", axis=0, tiled=True),
            lax.all_gather(compute[1], "dp", axis=1, tiled=True),
            lax.all_gather(compute[2], "dp", axis=0, tiled=True),
            lax.all_gather(compute[3], "dp", axis=1, tiled=True),
        )
        tokens_here = block_input[batch_index, 0]
        normed, norm_pull = jax.vjp(layer_norm, tokens_here, vec_master[0], vec_master[1])
        gathered, image_row = (
            lax.all_gather(normed.astype(jnp.bfloat16), "tensor", axis=0, tiled=True),
            lax.all_gather(image_ids[batch_index, 0], "tensor", axis=0, tiled=True),
        )
        projected = jnp.einsum(
            "td,dce->cte", gathered, qkv_weight, preferred_element_type=jnp.float32
        )
        queries = (projected[0] + query_bias).astype(jnp.bfloat16)
        key_rows = projected[1].astype(jnp.bfloat16)
        values = (projected[2] + value_bias).astype(jnp.bfloat16)
        key_heads = key_rows.reshape(length, local_heads, HEAD)
        value_heads = values.reshape(length, local_heads, HEAD)
        query_blocks = queries.reshape(block_count, block_rows, local_heads, HEAD)
        image_blocks = image_row.reshape(block_count, block_rows)

        def attend(block_pair):
            query_block, image_block = block_pair
            scores = (
                jnp.einsum(
                    "qhe,khe->hqk", query_block, key_heads, preferred_element_type=jnp.float32
                )
                * score_scale
            )
            same_image = image_block[:, None] == image_row[None, :]
            scores = jnp.where(same_image[None], scores, mask_fill)
            row_max = jnp.max(scores, -1, keepdims=True)
            exp_scores = jnp.exp(scores - row_max)
            exp_total = jnp.sum(exp_scores, -1, keepdims=True)
            attn_probs = exp_scores / exp_total
            result = jnp.einsum(
                "hqk,khe->qhe",
                attn_probs.astype(jnp.bfloat16),
                value_heads,
                preferred_element_type=jnp.float32,
            )
            return (result.reshape(block_rows, head_cols), (row_max + jnp.log(exp_total))[..., 0])

        attended_blocks, log_sums = lax.map(attend, (query_blocks, image_blocks))
        attended = attended_blocks.reshape(length, head_cols).astype(jnp.bfloat16)
        attn_sum = lax.psum_scatter(
            jnp.dot(attended, out_weight, preferred_element_type=jnp.float32).astype(jnp.bfloat16),
            "tensor",
            scatter_dimension=0,
            tiled=True,
        ).astype(jnp.float32)
        middle = tokens_here + attn_sum + vec_master[2]
        normed_two, norm_pull_two = jax.vjp(layer_norm, middle, vec_master[3], vec_master[4])
        gathered_two = lax.all_gather(normed_two.astype(jnp.bfloat16), "tensor", axis=0, tiled=True)
        hidden = jnp.dot(gathered_two, up_weight, preferred_element_type=jnp.float32) + hidden_bias
        active, gelu_pull = jax.vjp(gelu_tanh, hidden)
        active_low = active.astype(jnp.bfloat16)
        project_row_piece = lax.slice_in_dim(
            active_low, 0, local_rows * lax.axis_size("tensor"), axis=0
        )
        mlp_sum = lax.psum_scatter(
            jnp.dot(project_row_piece, down_weight, preferred_element_type=jnp.float32).astype(
                jnp.bfloat16
            ),
            "tensor",
            scatter_dimension=0,
            tiled=True,
        ).astype(jnp.float32)
        block_outputs.append(middle + mlp_sum + vec_master[5])
        qkv_weight, out_weight, up_weight, down_weight = (
            lax.all_gather(compute[0], "dp", axis=0, tiled=True),
            lax.all_gather(compute[1], "dp", axis=1, tiled=True),
            lax.all_gather(compute[2], "dp", axis=0, tiled=True),
            lax.all_gather(compute[3], "dp", axis=1, tiled=True),
        )
        cotangent = out_cotangent[batch_index, 0]
        cot_full = lax.all_gather(cotangent.astype(jnp.bfloat16), "tensor", axis=0, tiled=True)
        down_term = jnp.dot(active_low.T, cot_full, preferred_element_type=jnp.float32)
        d_active = jnp.dot(cot_full, down_weight.T, preferred_element_type=jnp.float32)
        d_hidden = gelu_pull(d_active)[0].astype(jnp.bfloat16)
        up_term = jnp.dot(gathered_two.T, d_hidden, preferred_element_type=jnp.float32)
        d_normed_two = lax.psum_scatter(
            jnp.dot(d_hidden, up_weight.T, preferred_element_type=jnp.float32).astype(jnp.bfloat16),
            "tensor",
            scatter_dimension=0,
            tiled=True,
        ).astype(jnp.float32)
        d_middle, gain_two_grad, shift_two_grad = norm_pull_two(d_normed_two)
        d_middle = d_middle + cotangent
        mid_full = lax.all_gather(d_middle.astype(jnp.bfloat16), "tensor", axis=0, tiled=True)
        out_term = jnp.dot(attended.T, mid_full, preferred_element_type=jnp.float32)
        d_attended = jnp.dot(mid_full, out_weight.T, preferred_element_type=jnp.float32).astype(
            jnp.bfloat16
        )
        d_blocks = d_attended.reshape(block_count, block_rows, local_heads, HEAD)

        def attend_back(running, block_item):
            d_keys, d_values = running
            query_block, image_block, block_sums, d_block = block_item
            scores = (
                jnp.einsum(
                    "qhe,khe->hqk", query_block, key_heads, preferred_element_type=jnp.float32
                )
                * score_scale
            )
            same_image = image_block[:, None] == image_row[None, :]
            scores = jnp.where(same_image[None], scores, mask_fill)
            attn_probs = jnp.exp(scores - block_sums[:, :, None])
            d_probs = jnp.einsum(
                "qhe,khe->hqk", d_block, value_heads, preferred_element_type=jnp.float32
            )
            row_delta = jnp.sum(attn_probs * d_probs, -1, keepdims=True)
            d_scores = (attn_probs * (d_probs - row_delta)).astype(jnp.bfloat16)
            d_query = (
                jnp.einsum("hqk,khe->qhe", d_scores, key_heads, preferred_element_type=jnp.float32)
                * score_scale
            )
            d_keys = (
                d_keys
                + jnp.einsum(
                    "hqk,qhe->khe", d_scores, query_block, preferred_element_type=jnp.float32
                )
                * score_scale
            )
            d_values = d_values + jnp.einsum(
                "hqk,qhe->khe",
                attn_probs.astype(jnp.bfloat16),
                d_block,
                preferred_element_type=jnp.float32,
            )
            return ((d_keys, d_values), d_query)

        zero_heads = jnp.zeros((length, local_heads, HEAD), jnp.float32)
        (d_keys, d_values), d_queries = lax.scan(
            attend_back, (zero_heads, zero_heads), (query_blocks, image_blocks, log_sums, d_blocks)
        )
        d_query_low = d_queries.reshape(length, head_cols).astype(jnp.bfloat16)
        d_key_low = d_keys.reshape(length, head_cols).astype(jnp.bfloat16)
        d_value_low = d_values.reshape(length, head_cols).astype(jnp.bfloat16)
        d_projected = jnp.stack([d_query_low, d_key_low, d_value_low])
        qkv_term = jnp.einsum(
            "td,cte->dce", gathered, d_projected, preferred_element_type=jnp.float32
        )
        d_normed = lax.psum_scatter(
            jnp.einsum(
                "cte,dce->td", d_projected, qkv_weight, preferred_element_type=jnp.float32
            ).astype(jnp.bfloat16),
            "tensor",
            scatter_dimension=0,
            tiled=True,
        ).astype(jnp.float32)
        d_tokens, gain_one_grad, shift_one_grad = norm_pull(d_normed)
        input_grads.append(d_tokens + d_middle)
        vector_terms = vector_terms + jnp.stack(
            [
                gain_one_grad,
                shift_one_grad,
                jnp.sum(d_middle, 0),
                gain_two_grad,
                shift_two_grad,
                jnp.sum(cotangent, 0),
            ]
        )
        bias_terms = bias_terms + jnp.concatenate(
            [
                jnp.sum(d_query_low, 0, dtype=jnp.float32),
                jnp.sum(d_value_low, 0, dtype=jnp.float32),
                jnp.sum(d_hidden, 0, dtype=jnp.float32),
            ]
        )
        local_terms = (qkv_term, out_term, up_term, down_term)
        owned = (
            lax.psum_scatter(
                local_terms[0].astype(jnp.bfloat16), "dp", scatter_dimension=0, tiled=True
            ).astype(jnp.float32),
            lax.psum_scatter(
                local_terms[1].astype(jnp.bfloat16), "dp", scatter_dimension=1, tiled=True
            ).astype(jnp.float32),
            lax.psum_scatter(
                local_terms[2].astype(jnp.bfloat16), "dp", scatter_dimension=0, tiled=True
            ).astype(jnp.float32),
            lax.psum_scatter(
                local_terms[3].astype(jnp.bfloat16), "dp", scatter_dimension=1, tiled=True
            ).astype(jnp.float32),
        )
        weight_sums = tuple((total + term for total, term in zip(weight_sums, owned)))
    qkv_grad, out_grad, up_grad, down_grad = weight_sums
    tensor_index = lax.axis_index("tensor")
    placed = jnp.where(jnp.arange(splits)[:, None] == tensor_index, bias_terms[None, :], 0.0)
    vec_grad, bias_table = lax.psum((vector_terms, placed), ("dp", "tensor"))
    bias_grad = lax.dynamic_slice_in_dim(bias_table, tensor_index, 1, 0)
    qkv_second_new, qkv_master_new = adam_update(
        qkv_master, qkv_moment, qkv_second, qkv_grad, 0.09, 0.1
    )
    out_second_new, out_master_new = adam_update(
        out_master, out_moment, out_second, out_grad, 0.4, 0.1
    )
    up_second_new, up_master_new = adam_update(up_master, up_moment, up_second, up_grad, 0.09, 0.1)
    down_second_new, down_master_new = adam_update(
        down_master, down_moment, down_second, down_grad, 0.045, 0.1
    )
    vec_second_new, vec_master_new = adam_update(
        vec_master, vec_moment, vec_second, vec_grad, 0.6, 0.0
    )
    bias_second_new, bias_master_new = adam_update(
        bias_master, bias_moment, bias_second, bias_grad, 0.5, 0.0
    )
    block_output = jnp.stack(block_outputs)[:, None]
    input_grad = jnp.stack(input_grads)[:, None]
    return (
        block_output,
        input_grad,
        qkv_grad,
        qkv_second_new,
        qkv_master_new,
        out_grad,
        out_second_new,
        out_master_new,
        up_grad,
        up_second_new,
        up_master_new,
        down_grad,
        down_second_new,
        down_master_new,
        vec_grad,
        vec_second_new,
        vec_master_new,
        bias_grad,
        bias_second_new,
        bias_master_new,
    )


LANES = 128
TILE = 128
SPAN = 256
WIDE = 1152
BATCH = 8


def lane_window(head):
    first = head * HEAD
    low = first // LANES * LANES
    high = -(-(first + HEAD) // LANES) * LANES
    return low, high


def head_mask(head, rows):
    low, high = lane_window(head)
    lane = lax.broadcasted_iota(jnp.int32, (rows, high - low), 1) + low
    return (lane >= head * HEAD) & (lane < head * HEAD + HEAD)


def head_columns(head, columns):
    low, high = lane_window(head)
    high = min(high, columns)
    return slice(low, high), head_mask(head, TILE)[:, : high - low]


def padded(columns):
    return -(-columns // LANES) * LANES


def tile_spans(ids_smem, ids_ref, index, tiles):
    first_id = ids_smem[index * TILE]
    last_id = ids_smem[index * TILE + TILE - 1]
    ids = ids_ref[...]
    begin = jnp.sum((ids < first_id).astype(jnp.int32)) // TILE
    end = (jnp.sum((ids <= last_id).astype(jnp.int32)) + TILE - 1) // TILE
    count = (end - begin + 1) // 2
    return jnp.minimum(begin, tiles - 2 * count), count


def ids_column(ids_ref, index):
    row = ids_ref[:, pl.ds(pl.multiple_of(index * TILE, TILE), TILE)].astype(jnp.float32)
    square = jnp.broadcast_to(row, (TILE, TILE)).T
    return jnp.concatenate([square] * (SPAN // TILE), axis=1).astype(jnp.int32)


NT = (((1,), (1,)), ((), ()))
TN = (((0,), (0,)), ((), ()))


def attend_kernel(heads, length, ids_smem, ids_ref, q_ref, k_ref, v_ref, o_ref, lse_ref, top, total, acc):
    index = pl.program_id(0)
    columns = heads * HEAD
    scale = HEAD ** (-0.5) * math.log2(math.e)
    begin, count = tile_spans(ids_smem, ids_ref, index, length // TILE)
    own_ids = ids_column(ids_ref, index)
    top[...] = jnp.full(top.shape, mask_fill, jnp.float32)
    total[...] = jnp.zeros(total.shape, jnp.float32)
    acc[...] = jnp.zeros(acc.shape, jnp.float32)

    def window(low, high):
        return slice(low, min(high, columns))

    def step(item, carry):
        place = pl.multiple_of((begin + 2 * item) * TILE, TILE)
        keys = pl.ds(place, SPAN)
        same = own_ids == ids_ref[:, keys]
        for first in range(0, heads, BATCH):
            batch = range(first, min(first + BATCH, heads))
            held_scores = []
            for head in batch:
                cols, mask = head_columns(head, columns)
                query = q_ref[:, cols]
                query = jnp.where(mask, query, jnp.zeros_like(query))
                scores = lax.dot_general(query, k_ref[keys, cols], NT, preferred_element_type=jnp.float32)
                held_scores.append(jnp.where(same, scores * scale, mask_fill))
            tops = [jnp.maximum(top[head], jnp.max(scores, -1, keepdims=True)) for head, scores in zip(batch, held_scores)]
            parts = [
                jnp.exp2(scores - jnp.concatenate([now] * (SPAN // LANES), axis=1)) for now, scores in zip(tops, held_scores)
            ]
            sums = [jnp.sum(part, -1, keepdims=True) for part in parts]
            mixes = [
                jnp.dot(part.astype(jnp.bfloat16), v_ref[keys, head_columns(head, columns)[0]], preferred_element_type=jnp.float32)
                for head, part in zip(batch, parts)
            ]
            for head, now, part_sum, mixed in zip(batch, tops, sums, mixes):
                cols, mask = head_columns(head, columns)
                shrink = jnp.exp2(top[head] - now)
                total[head] = total[head] * shrink + part_sum
                top[head] = now
                width = cols.stop - cols.start
                wide = jnp.concatenate([shrink] * ((width + LANES - 1) // LANES), axis=1)[:, :width]
                held = acc[:, cols]
                acc[:, cols] = jnp.where(mask, held * wide + mixed, held)
        return carry

    lax.fori_loop(0, count, step, 0)
    sums = jnp.zeros((TILE, LANES), jnp.float32)
    lane = lax.broadcasted_iota(jnp.int32, (TILE, LANES), 1)
    for head in range(heads):
        low, high = lane_window(head)
        high = min(high, columns)
        cols = slice(low, high)
        mask = head_mask(head, TILE)[:, : high - low]
        inverse = 1.0 / total[head]
        wide = jnp.concatenate([inverse] * ((high - low + LANES - 1) // LANES), axis=1)[:, : high - low]
        held = acc[:, cols]
        acc[:, cols] = jnp.where(mask, held * wide, held)
        sums = jnp.where(lane == head, top[head] + jnp.log2(total[head]), sums)
    o_ref[...] = acc[...].astype(o_ref.dtype)
    lse_ref[...] = sums.T[:heads]


def attend(ids, query, key, value):
    length, columns = query.shape
    heads = columns // HEAD
    tiles = length // TILE
    whole = pl.BlockSpec((length, columns), lambda i, s: (0, 0))
    block = pl.BlockSpec((TILE, columns), lambda i, s: (i, 0))
    return pl.pallas_call(
        partial(attend_kernel, heads, length),
        grid_spec=pltpu.PrefetchScalarGridSpec(
            num_scalar_prefetch=1,
            grid=(tiles,),
            in_specs=[pl.BlockSpec((1, length), lambda i, s: (0, 0)), block, whole, whole],
            out_specs=[block, pl.BlockSpec((heads, TILE), lambda i, s: (0, i))],
            scratch_shapes=[
                pltpu.VMEM((heads, TILE, LANES), jnp.float32),
                pltpu.VMEM((heads, TILE, LANES), jnp.float32),
                pltpu.VMEM((TILE, columns), jnp.float32),
            ],
        ),
        out_shape=[
            jax.ShapeDtypeStruct((length, columns), jnp.bfloat16),
            jax.ShapeDtypeStruct((heads, length), jnp.float32),
        ],
        compiler_params=pltpu.CompilerParams(vmem_limit_bytes=36 << 20),
        cost_estimate=pl.CostEstimate(flops=4 * 10**9, bytes_accessed=10**6, transcendentals=0),
    )(ids, ids.reshape(1, length), query, key, value)


def attend_back_kernel(
    heads, length, ids_smem, ids_ref, q_ref, k_ref, v_ref, o_ref, g_ref, lse_ref,
    dq_ref, dk_ref, dv_ref, delta, dq_acc, dk_acc, dv_acc,
):
    index = pl.program_id(0)
    columns = heads * HEAD
    natural = HEAD ** (-0.5)
    scale = natural * math.log2(math.e)
    tiles = length // TILE
    begin, count = tile_spans(ids_smem, ids_ref, index, tiles)
    own_ids = ids_column(ids_ref, index)

    @pl.when(index == 0)
    def _():
        dq_acc[...] = jnp.zeros(dq_acc.shape, jnp.float32)
        row = lax.broadcasted_iota(jnp.int32, (heads, columns), 0)
        lane = lax.broadcasted_iota(jnp.int32, (heads, columns), 1)
        pick = ((lane >= row * HEAD) & (lane < row * HEAD + HEAD)).astype(jnp.bfloat16)
        product = g_ref[...].astype(jnp.float32) * o_ref[...].astype(jnp.float32)
        coarse = product.astype(jnp.bfloat16)
        fine = (product - coarse.astype(jnp.float32)).astype(jnp.bfloat16)
        delta[...] = lax.dot_general(pick, coarse, NT, preferred_element_type=jnp.float32) + lax.dot_general(
            pick, fine, NT, preferred_element_type=jnp.float32
        )

    dk_acc[...] = jnp.zeros(dk_acc.shape, jnp.float32)
    dv_acc[...] = jnp.zeros(dv_acc.shape, jnp.float32)

    def step(item, carry):
        place = pl.multiple_of((begin + 2 * item) * TILE, TILE)
        rows = pl.ds(place, SPAN)
        same = own_ids == ids_ref[:, rows]
        for first in range(0, heads, BATCH):
            batch = range(first, min(first + BATCH, heads))
            keys, scores, d_probs = [], [], []
            for head in batch:
                cols, mask = head_columns(head, columns)
                key = k_ref[:, cols]
                keys.append(jnp.where(mask, key, jnp.zeros_like(key)))
                value = v_ref[:, cols]
                value = jnp.where(mask, value, jnp.zeros_like(value))
                scores.append(lax.dot_general(keys[-1], q_ref[rows, cols], NT, preferred_element_type=jnp.float32))
                d_probs.append(lax.dot_general(value, g_ref[rows, cols], NT, preferred_element_type=jnp.float32))
            probs = [
                jnp.exp2(jnp.where(same, score * scale, mask_fill) - lse_ref[head : head + 1, rows])
                for head, score in zip(batch, scores)
            ]
            d_scores = [
                (prob * (d_prob - delta[head : head + 1, rows])).astype(jnp.bfloat16)
                for head, prob, d_prob in zip(batch, probs, d_probs)
            ]
            for head, key, prob, d_score in zip(batch, keys, probs, d_scores):
                cols, mask = head_columns(head, columns)
                d_value = jnp.dot(prob.astype(jnp.bfloat16), g_ref[rows, cols], preferred_element_type=jnp.float32)
                d_key = jnp.dot(d_score, q_ref[rows, cols], preferred_element_type=jnp.float32)
                d_query = lax.dot_general(d_score, key, TN, preferred_element_type=jnp.float32)
                dv_acc[:, cols] += jnp.where(mask, d_value, 0.0)
                dk_acc[:, cols] += jnp.where(mask, d_key, 0.0)
                dq_acc[rows, cols] += d_query
        return carry

    lax.fori_loop(0, count, step, 0)
    dk_ref[...] = (dk_acc[...] * natural).astype(dk_ref.dtype)
    dv_ref[...] = dv_acc[...].astype(dv_ref.dtype)

    @pl.when(index == tiles - 1)
    def _():
        dq_ref[...] = (dq_acc[...] * natural).astype(dq_ref.dtype)


def attend_back(ids, query, key, value, attended, grad, lse):
    length, columns = query.shape
    heads = columns // HEAD
    tiles = length // TILE
    whole = pl.BlockSpec((length, columns), lambda i, s: (0, 0))
    block = pl.BlockSpec((TILE, columns), lambda i, s: (i, 0))
    out = jax.ShapeDtypeStruct((length, columns), jnp.bfloat16)
    return pl.pallas_call(
        partial(attend_back_kernel, heads, length),
        grid_spec=pltpu.PrefetchScalarGridSpec(
            num_scalar_prefetch=1,
            grid=(tiles,),
            in_specs=[
                pl.BlockSpec((1, length), lambda i, s: (0, 0)),
                whole,
                block,
                block,
                whole,
                whole,
                pl.BlockSpec((heads, length), lambda i, s: (0, 0)),
            ],
            out_specs=[whole, block, block],
            scratch_shapes=[
                pltpu.VMEM((heads, length), jnp.float32),
                pltpu.VMEM((length, columns), jnp.float32),
                pltpu.VMEM((TILE, columns), jnp.float32),
                pltpu.VMEM((TILE, columns), jnp.float32),
            ],
        ),
        out_shape=[out, out, out],
        compiler_params=pltpu.CompilerParams(vmem_limit_bytes=36 << 20),
        cost_estimate=pl.CostEstimate(flops=2 * 10**9, bytes_accessed=10**6, transcendentals=0),
    )(ids, ids.reshape(1, length), query, key, value, attended, grad, lse)


def column_call(kernel, ins, outs, columns, flops, scratch=()):
    wide = min(WIDE, padded(columns))
    steps = -(-columns // wide)

    def spec(shape, cut):
        if cut:
            return pl.BlockSpec(shape[:-1] + (wide,), lambda i: (0,) * (len(shape) - 1) + (i,))
        return pl.BlockSpec(shape, lambda i: (0,) * len(shape))

    size = sum(math.prod(a.shape) * a.dtype.itemsize for a, _ in ins) + sum(
        math.prod(a.shape) * a.dtype.itemsize for a in outs
    )
    return pl.pallas_call(
        kernel,
        grid=(steps,),
        in_specs=[spec(a.shape, cut) for a, cut in ins],
        out_specs=[spec(a.shape, True) for a in outs],
        out_shape=outs,
        scratch_shapes=list(scratch),
        compiler_params=pltpu.CompilerParams(vmem_limit_bytes=44 << 20),
        cost_estimate=pl.CostEstimate(flops=flops // 8, bytes_accessed=size // 8, transcendentals=0),
    )(*[a for a, _ in ins])


def hidden_kernel(x_ref, w_ref, b_ref, active_ref, slope_ref):
    rows = 256
    for block in range(x_ref.shape[0] // rows):
        part = pl.ds(block * rows, rows)
        value = jnp.dot(x_ref[part, :], w_ref[...], preferred_element_type=jnp.float32) + b_ref[...]
        active, slope = gelu_pair(value)
        active_ref[part, :] = active.astype(jnp.bfloat16)
        slope_ref[part, :] = slope.astype(jnp.bfloat16)


def hidden_units(x, weight, bias):
    tokens, columns = x.shape[0], weight.shape[1]
    out = jax.ShapeDtypeStruct((tokens, columns), jnp.bfloat16)
    ins = [(x, False), (weight, True), (bias.reshape(1, columns), True)]
    return column_call(hidden_kernel, ins, [out, out], columns, 2 * tokens * x.shape[1] * columns)


def hidden_back_kernel(x_ref, w_ref, slope_ref, grad_ref, sum_ref):
    rows = 256
    total = jnp.zeros(sum_ref.shape, jnp.float32)
    for block in range(x_ref.shape[0] // rows):
        part = pl.ds(block * rows, rows)
        value = jnp.dot(x_ref[part, :], w_ref[...], preferred_element_type=jnp.float32)
        value = value * slope_ref[part, :].astype(jnp.float32)
        grad_ref[part, :] = value.astype(jnp.bfloat16)
        total = total + jnp.sum(value, 0, keepdims=True)
    sum_ref[...] = total


def hidden_back(x, weight, slope):
    tokens, columns = x.shape[0], weight.shape[1]
    outs = [jax.ShapeDtypeStruct((tokens, columns), jnp.bfloat16), jax.ShapeDtypeStruct((1, columns), jnp.float32)]
    ins = [(x, False), (weight, True), (slope, True)]
    return column_call(hidden_back_kernel, ins, outs, columns, 2 * tokens * x.shape[1] * columns)


def grad_kernel(chunks, stacked, x_ref, *refs):
    core = lax.axis_index("dp") % 2
    count = len(refs) - 4 if stacked else (len(refs) - 2) // 3
    turned, result = refs[-2:]
    dy_refs = refs[:count]
    outs = refs[count:-2]

    @pl.when(pl.program_id(0) == 0)
    def _():
        turned[...] = x_ref[...].T

    rows = turned.shape[0] // chunks
    for number, dy_ref in enumerate(dy_refs):
        if stacked:
            sent_ref, kept_ref = outs[0].at[number], outs[1].at[number]
        else:
            sent_ref, kept_ref = outs[number], outs[count + number]
        result[...] = jnp.dot(turned[...], dy_ref[...], preferred_element_type=jnp.float32)
        for spot in range(chunks // 2):
            sent = pl.multiple_of((2 * spot + 1 - core) * rows, 8)
            kept = pl.multiple_of((2 * spot + core) * rows, 8)
            sent_ref[spot] = result[pl.ds(sent, rows), :].astype(jnp.bfloat16)
            kept_ref[spot] = result[pl.ds(kept, rows), :].astype(jnp.bfloat16)


def weight_grads(x, parts, stacked=False):
    tokens, features = x.shape
    columns = parts[0].shape[1]
    count = len(parts)
    wide = min(WIDE, padded(columns))
    shape = (8, features // 16, columns)
    outs = [jax.ShapeDtypeStruct(shape, jnp.bfloat16)] * (2 * count)
    if stacked:
        outs = [jax.ShapeDtypeStruct((count,) + shape, jnp.bfloat16)] * 2
    results = column_call(
        partial(grad_kernel, 16, stacked),
        [(x, False)] + [(part, True) for part in parts],
        outs,
        columns,
        2 * tokens * features * columns * count,
        [pltpu.VMEM((features, tokens), jnp.bfloat16), pltpu.VMEM((features, wide), jnp.float32)],
    )
    return results if stacked else (results[:count], results[count:])


def block_call(kernel, ins, outs, columns):
    wide = min(768, padded(columns))

    def spec(shape):
        return pl.BlockSpec(shape[:-1] + (wide,), lambda i: (0,) * (len(shape) - 1) + (i,))

    size = sum(math.prod(a.shape) * 2 for a in list(ins) + list(outs))
    return pl.pallas_call(
        kernel,
        grid=(-(-columns // wide),),
        in_specs=[spec(a.shape) for a in ins],
        out_specs=[spec(a.shape) for a in outs],
        out_shape=outs,
        compiler_params=pltpu.CompilerParams(vmem_limit_bytes=40 << 20),
        cost_estimate=pl.CostEstimate(flops=0, bytes_accessed=size // 4, transcendentals=0),
    )(*ins)


def low_sum(*refs):
    total = refs[0].astype(jnp.float32)
    for ref in refs[1:]:
        total = total + ref.astype(jnp.float32)
    return total.astype(jnp.bfloat16)


def first_sums_kernel(kept_own, kept_other, core_own, core_other, near_own, near_other, far_own, near_sent, far_sent):
    y = lax.axis_index("dp") // 2 % 2
    for z in range(2):
        keep, send = 2 * z + y, 2 * z + 1 - y
        near_own[z] = low_sum(kept_own[keep], core_own[keep])
        near_other[z] = low_sum(kept_other[keep], core_other[keep])
        near_sent[0, z] = low_sum(kept_own[send], core_own[send])
        near_sent[1, z] = low_sum(kept_other[send], core_other[send])
    for spot in range(4):
        far_own[spot] = low_sum(kept_own[4 + spot], core_own[4 + spot])
        far_sent[spot] = low_sum(kept_other[4 + spot], core_other[4 + spot])


def middle_sums_kernel(near_own, near_other, near_got, far_own, far_got, own, far, near_sent, far_sent):
    y = lax.axis_index("dp") // 2 % 2
    for z in range(2):
        keep, send = 2 * z + y, 2 * z + 1 - y
        own[z] = low_sum(near_own[z], near_got[0, z])
        near_sent[z] = low_sum(near_other[z], near_got[1, z])
        far[z] = low_sum(far_own[keep], far_got[keep])
        far_sent[z] = low_sum(far_own[send], far_got[send])


def core_sums_kernel(kept, got, here, there):
    y = lax.axis_index("dp") // 2 % 2
    for lead in range(kept.shape[0]):
        for z in range(4):
            keep, send = 2 * z + y, 2 * z + 1 - y
            here[lead, z] = low_sum(kept[lead, keep], got[lead, keep])
            there[lead, z] = low_sum(kept[lead, send], got[lead, send])


def core_sums(kept, got):
    leads, rows, columns = kept.shape[0], kept.shape[2], kept.shape[3]
    out = jax.ShapeDtypeStruct((leads, 4, rows, columns), jnp.bfloat16)
    return block_call(core_sums_kernel, [kept, got], [out, out], columns)


def place_kernel(leads, ordered, steps, *refs):
    pieces = refs[: len(steps)]
    outs = refs[len(steps) : len(steps) + leads]
    sems = refs[len(steps) + leads]
    spot = lax.axis_index("dp")
    z, y, core = spot // 4, spot // 2 % 2, spot % 2
    copies = []
    for piece, (first_slot, y_step, core_step) in zip(pieces, steps):
        column = (y + y_step) % 2 * 2 + (core + core_step) % 2
        for slot in range(piece.shape[0]):
            number = first_slot + slot
            row = (number if ordered else (z + 4 - number) % 4) * 4 + column
            for lead in range(leads):
                copy = pltpu.make_async_copy(piece.at[slot, lead], outs[lead].at[row], sems.at[len(copies)])
                copy.start()
                copies.append(copy)
    for copy in copies:
        copy.wait()


def place(planes, ordered):
    pieces = sum(planes, [])
    leads, rows, columns = pieces[0].shape[1:]
    slots = pieces[0].shape[0]
    steps = [(start, step % 2, step // 2) for start in range(0, 4, slots) for step in range(4)]
    size = 16 * leads * rows * padded(columns) * 2
    placed = pl.pallas_call(
        partial(place_kernel, leads, ordered, steps),
        in_specs=[pl.BlockSpec(memory_space=pl.ANY)] * len(pieces),
        out_specs=[pl.BlockSpec(memory_space=pltpu.VMEM)] * leads,
        out_shape=[jax.ShapeDtypeStruct((16, rows, columns), jnp.bfloat16)] * leads,
        scratch_shapes=[pltpu.SemaphoreType.DMA((16 * leads,))],
        compiler_params=pltpu.CompilerParams(vmem_limit_bytes=size * 3 // 2 + (2 << 20)),
        cost_estimate=pl.CostEstimate(flops=0, bytes_accessed=size // 4, transcendentals=0),
    )(*pieces)
    return [part.reshape(16 * rows, columns) for part in placed]


def swap_x(value):
    return lax.ppermute(value, "tensor", [(0, 1), (1, 0)])


def swap_y(value):
    return lax.ppermute(value, "dp", [(spot, spot ^ 2) for spot in range(16)])


def swap_core(value):
    return lax.ppermute(value, "dp", [(spot, spot ^ 1) for spot in range(16)])


def move_z(value, steps):
    return lax.ppermute(value, "dp", [(spot, (spot + 4 * steps) % 16) for spot in range(16)])


def tie(*values):
    return lax.optimization_barrier(values)


def gather_z(shard):
    groups = [[spot + 4 * z for z in range(4)] for spot in range(4)]
    return lax.all_gather(shard, "dp", axis_index_groups=groups)


def both_cores(parts):
    return parts + [swap_core(part) for part in parts]


def add_low(*terms):
    total = terms[0].astype(jnp.float32)
    for term in terms[1:]:
        total = total + term.astype(jnp.float32)
    return total.astype(jnp.bfloat16)


def part_of(value, index, axis):
    return lax.dynamic_index_in_dim(value, index, axis, keepdims=False)


def y_parts(value):
    spot = lax.axis_index("dp")
    split = value.reshape((value.shape[0] // 2, 2) + value.shape[1:])
    return part_of(split, spot // 2 % 2, 1), part_of(split, 1 - spot // 2 % 2, 1)


class Planes:
    def __init__(self, kept, core):
        rows, self.columns = kept[0].shape[1:]
        self.two, self.four = [jax.ShapeDtypeStruct((n, rows, self.columns), jnp.bfloat16) for n in (2, 4)]
        pair = jax.ShapeDtypeStruct((2, 2, rows, self.columns), jnp.bfloat16)
        self.near_own, self.near_other, self.far_own, *self.sent = block_call(
            first_sums_kernel, [*kept, *core], [self.two, self.two, self.four, pair, self.four], self.columns
        )

    def first(self):
        self.got = [swap_y(self.sent[0]), swap_x(self.sent[1])]

    def middle(self):
        self.near_own, self.far_own, *self.sent = block_call(
            middle_sums_kernel,
            [self.near_own, self.near_other, self.got[0], self.far_own, self.got[1]],
            [self.two] * 4,
            self.columns,
        )

    def second(self):
        self.got = [swap_x(self.sent[0]), swap_y(self.sent[1])]

    def total(self):
        return jnp.concatenate([add_low(self.near_own, self.got[0]), add_low(self.far_own, self.got[1])])


def scatter_z(value):
    groups = [[spot + 4 * z for z in range(4)] for spot in range(4)]
    return lax.psum_scatter(value, "dp", axis_index_groups=groups)


def send_z(value):
    z = lax.axis_index("dp") // 4
    return [part_of(value, z, 0)] + [move_z(part_of(value, (z + steps) % 4, 0), steps) for steps in (1, 2, 3)]


def sum_terms(terms):
    total = terms[0].astype(jnp.float32)
    for term in terms[1:]:
        total = total + term.astype(jnp.float32)
    return total


def norm_forward(values):
    centre = values - jnp.mean(values, -1, keepdims=True)
    inverse = lax.rsqrt(jnp.mean(centre * centre, -1, keepdims=True) + norm_eps)
    return centre * inverse, inverse


def norm_back(grad, hat, inverse, gain):
    scaled = grad * gain
    mean_one = jnp.mean(scaled, -1, keepdims=True)
    mean_two = jnp.mean(scaled * hat, -1, keepdims=True)
    return (scaled - mean_one - hat * mean_two) * inverse


def gelu_pair(value):
    inner = math.sqrt(2.0 / math.pi)
    squared = value * value
    bent = jnp.tanh(inner * (value + 0.044715 * value * squared))
    half = 0.5 * (1.0 + bent)
    slope = half + 0.5 * value * (1.0 - bent * bent) * inner * (1.0 + 3 * 0.044715 * squared)
    return value * half, slope


def row_layer(
    block_input,
    image_ids,
    out_cotangent,
    qkv_master,
    qkv_moment,
    qkv_second,
    out_master,
    out_moment,
    out_second,
    up_master,
    up_moment,
    up_second,
    down_master,
    down_moment,
    down_second,
    vec_master,
    vec_moment,
    vec_second,
    bias_master,
    bias_moment,
    bias_second,
):
    low = jnp.bfloat16
    wide = jnp.float32
    mine = lax.axis_index("tensor")
    first = mine == 0
    half = block_input.shape[2]
    features = block_input.shape[3]
    head_cols = qkv_master.shape[2]

    def pick(pair, index):
        return lax.dynamic_index_in_dim(pair, index, 0, keepdims=False)

    def in_order(own, other, axis=0):
        return jnp.concatenate([jnp.where(first, own, other), jnp.where(first, other, own)], axis)

    def dot(spec, left, right):
        return jnp.einsum(spec, left, right, preferred_element_type=wide)

    inputs_own = pick(block_input[:, 0], mine)
    inputs_sent = pick(block_input[:, 0], 1 - mine)
    cot_own = pick(out_cotangent[:, 0], mine)
    cot_sent = pick(out_cotangent[:, 0], 1 - mine)
    inputs_low = inputs_sent.astype(low)
    early_shard = jnp.stack([qkv_master[:, 0], qkv_master[:, 1], qkv_master[:, 2]]).astype(low)
    early_shard, inputs_low = tie(early_shard, inputs_low)
    inputs_got = swap_x(inputs_low)
    early_one = move_z(early_shard, 1)
    early_three = move_z(early_shard, 3)
    early_shard, early_one = tie(early_shard, early_one)
    early_two = move_z(early_shard, 2)
    near = jnp.stack([early_shard, early_one])
    near_y, near_x = swap_y(near), swap_x(near)
    late_shard = jnp.stack([up_master, down_master.T]).astype(low)
    small = jnp.concatenate([pick(image_ids[:, 0], 1 - mine).astype(wide), bias_master[0]])
    cot_sum = jnp.sum(out_cotangent[:, 0], (0, 1))
    cot_low_sent = cot_sent.astype(low)
    late_shard, small, cot_sum, cot_low_sent, early_two, early_three, inputs_got, near_x, near_y = tie(
        late_shard, small, cot_sum, cot_low_sent, early_two, early_three, inputs_got, near_x, near_y
    )
    small_got = swap_x(small[None])[0]
    late_z = gather_z(late_shard)
    far = jnp.stack([early_two, early_three])
    far_y, far_x = swap_y(far), swap_x(far)
    near_xy, far_yx = swap_y(near_x), swap_x(far_y)
    early_own = place([both_cores([near, near_y]), both_cores([far, far_y])], False)
    out_shard, early_own = tie(out_master.T.astype(low), early_own)
    out_whole = lax.all_gather(out_shard, ("tensor", "dp")).reshape(2, features, head_cols)
    inputs = in_order(inputs_own, inputs_got.astype(wide))
    ids = in_order(pick(image_ids[:, 0], mine), small_got[:half].astype(jnp.int32))
    biases = jnp.stack([bias_master[0], small_got[half:]])

    hat_one, inverse_one = norm_forward(inputs)
    normed = (hat_one * vec_master[0] + vec_master[1]).astype(low)
    def project(g, weights):
        query = (dot("td,de->te", normed, weights[0]) + biases[g, :head_cols]).astype(low)
        key = dot("td,de->te", normed, weights[1]).astype(low)
        value = (dot("td,de->te", normed, weights[2]) + biases[g, head_cols : 2 * head_cols]).astype(low)
        return query, key, value

    projected = [project(0, early_own), None]
    projected[0], near_x, near_xy, far_x = tie(projected[0], near_x, near_xy, far_x)
    others = [both_cores([near_x, near_xy]), [far_x, swap_core(far_x)]]
    attended, log_sums = [None, None], [None, None]
    attended[0], log_sums[0] = attend(ids, *projected[0])
    up_near, up_far = [late_z[start : start + 2, :1] for start in (0, 2)]
    others, attended[0], far_yx, up_near, up_far = tie(others, attended[0], far_yx, up_near, up_far)
    others[1] = [others[1][0], far_yx, others[1][1], swap_core(far_yx)]
    early_other = place(others, False)
    down_near, down_far = [late_z[start : start + 2, 1:] for start in (0, 2)]
    early_other, up_near, up_far = tie(early_other, up_near, up_far)
    up_near_x, up_far_y = swap_x(up_near), swap_y(up_far)
    projected[1] = project(1, early_other)
    query_weight, key_weight, value_weight = zip(early_own, early_other)
    projected[1], up_near, up_far, up_near_x, up_far_y = tie(projected[1], up_near, up_far, up_near_x, up_far_y)
    up_near_y, up_far_x = swap_y(up_near), swap_x(up_far)
    attended[1], log_sums[1] = attend(ids, *projected[1])
    attended[1], up_near_x, up_far_y, up_near_y, up_far_x = tie(
        attended[1], up_near_x, up_far_y, up_near_y, up_far_x
    )
    up_near_xy, up_far_yx = swap_y(up_near_x), swap_x(up_far_y)
    cot_got = swap_x(cot_low_sent)
    out_weight = [pick(out_whole, mine), pick(out_whole, 1 - mine)]
    attn_sum = sum(dot("te,de->td", attended[g], out_weight[g]) for g in range(2)) + vec_master[2]
    middle = inputs + attn_sum
    hat_two, inverse_two = norm_forward(middle)
    normed_two = (hat_two * vec_master[3] + vec_master[4]).astype(low)
    normed_two, up_near_xy, up_far_yx, down_near, down_far = tie(
        normed_two, up_near_xy, up_far_yx, down_near, down_far
    )
    down_near_x, down_far_y = swap_x(down_near), swap_y(down_far)
    up_weight = [
        place([both_cores([up_near, up_near_y]), both_cores([up_far, up_far_y])], True)[0],
        place([both_cores([up_near_x, up_near_xy]), both_cores([up_far_x, up_far_yx])], True)[0],
    ]
    active, slope = [None, None], [None, None]
    active[0], slope[0] = hidden_units(normed_two, up_weight[0], biases[0, 2 * head_cols :])
    normed_two, active[0], down_near, down_far, down_near_x, down_far_y = tie(
        normed_two, active[0], down_near, down_far, down_near_x, down_far_y
    )
    down_near_y, down_far_x = swap_y(down_near), swap_x(down_far)
    active[1], slope[1] = hidden_units(normed_two, up_weight[1], biases[1, 2 * head_cols :])
    active[1], down_near_x, down_far_y, down_near_y, down_far_x = tie(
        active[1], down_near_x, down_far_y, down_near_y, down_far_x
    )
    down_weight = [place([both_cores([down_near, down_near_y]), both_cores([down_far, down_far_y])], True)[0], None]
    active[1], down_weight[0], down_near_x, down_far_y = tie(active[1], down_weight[0], down_near_x, down_far_y)
    down_near_xy, down_far_yx = swap_y(down_near_x), swap_x(down_far_y)
    cot_row = in_order(cot_own, cot_got.astype(wide))
    cot_low = cot_row.astype(low)
    down_sent, down_kept = weight_grads(cot_low, active)
    down_sent, down_near_xy, down_far_yx = tie(down_sent, down_near_xy, down_far_yx)
    down_weight[1] = place(
        [both_cores([down_near_x, down_near_xy]), both_cores([down_far_x, down_far_yx])], True
    )[0]
    added = attn_sum + sum(dot("tf,df->td", active[g], down_weight[g]) for g in range(2)) + vec_master[5]
    added = added.reshape(2, half, features)
    added_got = swap_x(pick(added, 1 - mine).astype(low))

    own, other = 0, 1
    down_core = [swap_core(part) for part in down_sent]
    d_hidden, hidden_sums = [None, None], [None, None]
    d_hidden[own], hidden_sums[own] = hidden_back(cot_low, down_weight[own], slope[own])
    d_hidden[own], down_core = tie(d_hidden[own], down_core)
    down = Planes(down_kept, down_core)
    cot_late, down.sent = tie(cot_low, down.sent)
    down.first()
    d_hidden[other], hidden_sums[other] = hidden_back(cot_late, down_weight[other], slope[other])
    up_sent, up_kept = weight_grads(normed_two, d_hidden)
    up_sent, down.got = tie(up_sent, down.got)
    up_core = [swap_core(part) for part in up_sent]
    down.middle()
    d_hidden, down.sent = tie(d_hidden, down.sent)
    down.second()
    d_normed_two = sum(dot("tf,df->td", d_hidden[g], up_weight[g]) for g in range(2))
    d_normed_two, up_core, down.got = tie(d_normed_two, up_core, down.got)
    up = Planes(up_kept, up_core)
    down_total = down.total()
    d_normed_two, up.sent, down_total = tie(d_normed_two, up.sent, down_total)
    up.first()
    down_term = scatter_z(down_total)
    mid_added = norm_back(d_normed_two, hat_two, inverse_two, vec_master[3])
    d_middle = cot_row + mid_added
    mid_low = d_middle.astype(low)
    d_attended = [dot("td,de->te", mid_low, out_weight[g]).astype(low) for g in range(2)]
    out_sent, out_kept = weight_grads(mid_low, attended)
    d_attended[other], out_sent, added_got = tie(d_attended[other], out_sent, added_got)
    out_core = [swap_core(part) for part in out_sent]

    def back(g, grad):
        return attend_back(ids, *projected[g], attended[g], grad, log_sums[g])

    d_other = back(other, d_attended[other])
    d_other, out_core, up.got = tie(d_other, out_core, up.got)
    up.middle()
    out_other = add_low(out_kept[other], out_core[other])
    out_own = add_low(out_kept[own], out_core[own])
    d_other, up.sent, out_other = tie(d_other, up.sent, out_other)
    up.second()
    out_there_x = swap_x(out_other)
    qkv_sent, qkv_kept = [None, None], [None, None]
    qkv_sent[other], qkv_kept[other] = weight_grads(normed, d_other, True)

    def normed_part(parts, g):
        weights = (query_weight, key_weight, value_weight)
        return sum(dot("te,de->td", part, weight[g]) for part, weight in zip(parts, weights))

    d_other, qkv_sent[other] = tie(d_other, qkv_sent[other])
    qkv_core_other = swap_core(qkv_sent[other])
    d_normed_other = normed_part(d_other, other)
    d_normed_other, up.got, qkv_core_other = tie(d_normed_other, up.got, qkv_core_other)
    up_total = up.total()
    qkv_other_here, qkv_other_there = core_sums(qkv_kept[other], qkv_core_other)
    d_attended[own], up_total, qkv_other_there = tie(d_attended[own], up_total, qkv_other_there)
    up_term = scatter_z(up_total)
    qkv_there_y = swap_y(qkv_other_there)
    d_own = back(own, d_attended[own])
    d_own, qkv_there_y, out_there_x = tie(tuple(d_own), qkv_there_y, out_there_x)
    qkv_other = add_low(qkv_other_here, qkv_there_y)
    out_here, out_there = y_parts(add_low(out_own, out_there_x))
    d_own, qkv_other, out_there = tie(d_own, qkv_other, out_there)
    qkv_there_x = swap_x(qkv_other)
    out_there_y = swap_y(out_there)
    qkv_sent[own], qkv_kept[own] = weight_grads(normed, d_own, True)
    d_own, qkv_sent[own], out_there_y = tie(d_own, qkv_sent[own], out_there_y)
    out_terms = send_z(add_low(out_here, out_there_y))
    qkv_core_own = swap_core(qkv_sent[own])
    d_normed_own = normed_part(d_own, own)
    d_normed_own, qkv_core_own, qkv_there_x, out_terms = tie(d_normed_own, qkv_core_own, qkv_there_x, out_terms)
    qkv_here, qkv_there = core_sums(qkv_kept[own], qkv_core_own)
    d_normed_own, qkv_there = tie(d_normed_own, qkv_there)
    qkv_there_y = swap_y(qkv_there)
    d_normed = d_normed_other + d_normed_own
    early = jnp.concatenate(
        [
            jnp.sum(d_middle, 0),
            jnp.sum(d_normed_two * hat_two, 0),
            jnp.sum(d_normed_two, 0),
            cot_sum,
        ]
    )

    def bias_rows(sums):
        return jnp.where(first, jnp.concatenate(sums), jnp.concatenate(sums[::-1]))

    sums = jnp.concatenate(
        [
            jnp.sum(d_normed * hat_one, 0),
            jnp.sum(d_normed, 0),
            early,
            bias_rows([jnp.sum(part[0], 0, dtype=wide) for part in (d_own, d_other)]),
            bias_rows([jnp.sum(part[2], 0, dtype=wide) for part in (d_own, d_other)]),
            bias_rows([part[0] for part in hidden_sums]),
        ]
    )
    in_added = (mid_added + norm_back(d_normed, hat_one, inverse_one, vec_master[0])).reshape(2, half, features)
    in_sent = pick(in_added, 1 - mine).astype(low)
    in_got = swap_x(in_sent)
    down_term, up_term, out_terms, added_got, in_sent = tie(down_term, up_term, out_terms, added_got, in_sent)
    block_here = inputs_own + pick(added, mine)
    block_there = pick(block_input[:, 0], 1 - mine) + added_got.astype(wide)
    block_output = in_order(block_here[None], block_there[None])[:, None]

    def update(name, grad):
        master, moment, second, rate, decay = states[name]
        second_new, master_new = adam_update(master, moment, second, grad, rate, decay)
        return grad, second_new, master_new

    states = {
        "qkv": (qkv_master, qkv_moment, qkv_second, 0.09, 0.1),
        "out": (out_master, out_moment, out_second, 0.4, 0.1),
        "up": (up_master, up_moment, up_second, 0.09, 0.1),
        "down": (down_master, down_moment, down_second, 0.045, 0.1),
        "vec": (vec_master, vec_moment, vec_second, 0.6, 0.0),
        "bias": (bias_master, bias_moment, bias_second, 0.5, 0.0),
    }
    up_new = update("up", up_term.astype(wide))
    down_new = update("down", down_term.astype(wide).T)
    out_new = update("out", sum_terms(out_terms).T)
    sums, qkv_there_y, in_got, block_output, up_new, down_new, out_new = tie(
        sums, qkv_there_y, in_got, block_output, up_new, down_new, out_new
    )
    qkv_terms = send_z(add_low(qkv_here, qkv_there_y, qkv_there_x).transpose(1, 0, 2, 3))
    sums = sums[None]
    sums = sums + move_z(sums, 1) + move_z(sums, 2) + move_z(sums, 3)
    sums = sums + swap_core(sums)
    sums = sums + swap_y(sums)
    sums = (sums + swap_x(sums))[0]
    qkv_new = update("qkv", sum_terms(qkv_terms).transpose(1, 0, 2))
    grad_here = cot_own + pick(in_added, mine)
    grad_there = cot_sent + in_got.astype(wide)
    input_grad = in_order(grad_here[None], grad_there[None])[:, None]
    vec_grad = sums[: 6 * features].reshape(6, features)

    def group(start, size):
        return pick(sums[start : start + 2 * size].reshape(2, size), mine)

    start = 6 * features
    bias_grad = jnp.concatenate(
        [
            group(start, head_cols),
            group(start + 2 * head_cols, head_cols),
            group(start + 4 * head_cols, up_master.shape[1]),
        ]
    )[None]

    vec_new = update("vec", vec_grad)
    bias_new = update("bias", bias_grad)
    return (block_output, input_grad, *qkv_new, *out_new, *up_new, *down_new, *vec_new, *bias_new)


def solution(mesh):
    placed = (
        P(None, "dp", "tensor", None),
        P(None, "dp", "tensor"),
        P(None, "dp", "tensor", None),
        P("dp", None, "tensor"),
        P("dp", None, "tensor"),
        P("dp", None, "tensor"),
        P("tensor", "dp"),
        P("tensor", "dp"),
        P("tensor", "dp"),
        P("dp", "tensor"),
        P("dp", "tensor"),
        P("dp", "tensor"),
        P("tensor", "dp"),
        P("tensor", "dp"),
        P("tensor", "dp"),
        P(),
        P(),
        P(),
        P("tensor", None),
        P("tensor", None),
        P("tensor", None),
    )
    by_rows = dict(mesh.shape) == {"dp": 16, "tensor": 2}
    return jax.shard_map(
        row_layer if by_rows else split_layer,
        mesh=mesh,
        in_specs=placed,
        out_specs=(
            P(None, "dp", "tensor", None),
            P(None, "dp", "tensor", None),
            P("dp", None, "tensor"),
            P("dp", None, "tensor"),
            P("dp", None, "tensor"),
            P("tensor", "dp"),
            P("tensor", "dp"),
            P("tensor", "dp"),
            P("dp", "tensor"),
            P("dp", "tensor"),
            P("dp", "tensor"),
            P("tensor", "dp"),
            P("tensor", "dp"),
            P("tensor", "dp"),
            P(),
            P(),
            P(),
            P("tensor", None),
            P("tensor", None),
            P("tensor", None),
        ),
        check_vma=False,
    )
```

```python
import math
from functools import partial

import jax
import jax.numpy as jnp
from jax import lax
from jax.experimental import pallas as pl
from jax.experimental.pallas import tpu as pltpu
from jax.sharding import PartitionSpec as P

HEAD = 72
STEP = 10


norm_eps = 1e-06
mask_fill = -1e30
beta_one = 0.9
beta_two = 0.95
adam_eps = 1e-08


def layer_norm(values, scale_vec, shift_vec):
    centre = values - jnp.mean(values, -1, keepdims=True)
    spread = jnp.mean(centre * centre, -1, keepdims=True)
    return centre * lax.rsqrt(spread + norm_eps) * scale_vec + shift_vec


def adam_update(master, moment, second, gradient, step_rate, weight_decay):
    first_moment = beta_one * moment.astype(jnp.float32) + (1.0 - beta_one) * gradient
    second_new = beta_two * second + (1.0 - beta_two) * gradient * gradient
    update = (
        first_moment
        / (1.0 - beta_one**STEP)
        / (jnp.sqrt(second_new / (1.0 - beta_two**STEP)) + adam_eps)
        + weight_decay * master
    )
    return (second_new, master - step_rate * update)


def split_layer(
    block_input,
    image_ids,
    out_cotangent,
    qkv_master,
    qkv_moment,
    qkv_second,
    out_master,
    out_moment,
    out_second,
    up_master,
    up_moment,
    up_second,
    down_master,
    down_moment,
    down_second,
    vec_master,
    vec_moment,
    vec_second,
    bias_master,
    bias_moment,
    bias_second,
):
    batches = block_input.shape[0]
    local_rows = block_input.shape[2]
    features = block_input.shape[3]
    splits = lax.axis_size("tensor")
    length = local_rows * splits
    head_cols = qkv_master.shape[2]
    local_heads = head_cols // HEAD
    block_rows = min(512, length)
    block_count = length // block_rows
    score_scale = HEAD ** (-0.5)
    biases = bias_master[0]
    query_bias = biases[:head_cols]
    value_bias = biases[head_cols : 2 * head_cols]
    hidden_bias = biases[2 * head_cols :]
    compute = (
        qkv_master.astype(jnp.bfloat16),
        out_master.astype(jnp.bfloat16),
        up_master.astype(jnp.bfloat16),
        down_master.astype(jnp.bfloat16),
    )
    gelu_tanh = partial(jax.nn.gelu, approximate=True)
    weight_sums = (
        jnp.zeros_like(qkv_master),
        jnp.zeros_like(out_master),
        jnp.zeros_like(up_master),
        jnp.zeros_like(down_master),
    )
    vector_terms = jnp.zeros((6, features), jnp.float32)
    bias_terms = jnp.zeros(biases.shape, jnp.float32)
    block_outputs = []
    input_grads = []
    for batch_index in range(batches):
        qkv_weight, out_weight, up_weight, down_weight = (
            lax.all_gather(compute[0], "dp", axis=0, tiled=True),
            lax.all_gather(compute[1], "dp", axis=1, tiled=True),
            lax.all_gather(compute[2], "dp", axis=0, tiled=True),
            lax.all_gather(compute[3], "dp", axis=1, tiled=True),
        )
        tokens_here = block_input[batch_index, 0]
        normed, norm_pull = jax.vjp(layer_norm, tokens_here, vec_master[0], vec_master[1])
        gathered, image_row = (
            lax.all_gather(normed.astype(jnp.bfloat16), "tensor", axis=0, tiled=True),
            lax.all_gather(image_ids[batch_index, 0], "tensor", axis=0, tiled=True),
        )
        projected = jnp.einsum(
            "td,dce->cte", gathered, qkv_weight, preferred_element_type=jnp.float32
        )
        queries = (projected[0] + query_bias).astype(jnp.bfloat16)
        key_rows = projected[1].astype(jnp.bfloat16)
        values = (projected[2] + value_bias).astype(jnp.bfloat16)
        key_heads = key_rows.reshape(length, local_heads, HEAD)
        value_heads = values.reshape(length, local_heads, HEAD)
        query_blocks = queries.reshape(block_count, block_rows, local_heads, HEAD)
        image_blocks = image_row.reshape(block_count, block_rows)

        def attend(block_pair):
            query_block, image_block = block_pair
            scores = (
                jnp.einsum(
                    "qhe,khe->hqk", query_block, key_heads, preferred_element_type=jnp.float32
                )
                * score_scale
            )
            same_image = image_block[:, None] == image_row[None, :]
            scores = jnp.where(same_image[None], scores, mask_fill)
            row_max = jnp.max(scores, -1, keepdims=True)
            exp_scores = jnp.exp(scores - row_max)
            exp_total = jnp.sum(exp_scores, -1, keepdims=True)
            attn_probs = exp_scores / exp_total
            result = jnp.einsum(
                "hqk,khe->qhe",
                attn_probs.astype(jnp.bfloat16),
                value_heads,
                preferred_element_type=jnp.float32,
            )
            return (result.reshape(block_rows, head_cols), (row_max + jnp.log(exp_total))[..., 0])

        attended_blocks, log_sums = lax.map(attend, (query_blocks, image_blocks))
        attended = attended_blocks.reshape(length, head_cols).astype(jnp.bfloat16)
        attn_sum = lax.psum_scatter(
            jnp.dot(attended, out_weight, preferred_element_type=jnp.float32).astype(jnp.bfloat16),
            "tensor",
            scatter_dimension=0,
            tiled=True,
        ).astype(jnp.float32)
        middle = tokens_here + attn_sum + vec_master[2]
        normed_two, norm_pull_two = jax.vjp(layer_norm, middle, vec_master[3], vec_master[4])
        gathered_two = lax.all_gather(normed_two.astype(jnp.bfloat16), "tensor", axis=0, tiled=True)
        hidden = jnp.dot(gathered_two, up_weight, preferred_element_type=jnp.float32) + hidden_bias
        active, gelu_pull = jax.vjp(gelu_tanh, hidden)
        active_low = active.astype(jnp.bfloat16)
        project_row_piece = lax.slice_in_dim(
            active_low, 0, local_rows * lax.axis_size("tensor"), axis=0
        )
        mlp_sum = lax.psum_scatter(
            jnp.dot(project_row_piece, down_weight, preferred_element_type=jnp.float32).astype(
                jnp.bfloat16
            ),
            "tensor",
            scatter_dimension=0,
            tiled=True,
        ).astype(jnp.float32)
        block_outputs.append(middle + mlp_sum + vec_master[5])
        qkv_weight, out_weight, up_weight, down_weight = (
            lax.all_gather(compute[0], "dp", axis=0, tiled=True),
            lax.all_gather(compute[1], "dp", axis=1, tiled=True),
            lax.all_gather(compute[2], "dp", axis=0, tiled=True),
            lax.all_gather(compute[3], "dp", axis=1, tiled=True),
        )
        cotangent = out_cotangent[batch_index, 0]
        cot_full = lax.all_gather(cotangent.astype(jnp.bfloat16), "tensor", axis=0, tiled=True)
        down_term = jnp.dot(active_low.T, cot_full, preferred_element_type=jnp.float32)
        d_active = jnp.dot(cot_full, down_weight.T, preferred_element_type=jnp.float32)
        d_hidden = gelu_pull(d_active)[0].astype(jnp.bfloat16)
        up_term = jnp.dot(gathered_two.T, d_hidden, preferred_element_type=jnp.float32)
        d_normed_two = lax.psum_scatter(
            jnp.dot(d_hidden, up_weight.T, preferred_element_type=jnp.float32).astype(jnp.bfloat16),
            "tensor",
            scatter_dimension=0,
            tiled=True,
        ).astype(jnp.float32)
        d_middle, gain_two_grad, shift_two_grad = norm_pull_two(d_normed_two)
        d_middle = d_middle + cotangent
        mid_full = lax.all_gather(d_middle.astype(jnp.bfloat16), "tensor", axis=0, tiled=True)
        out_term = jnp.dot(attended.T, mid_full, preferred_element_type=jnp.float32)
        d_attended = jnp.dot(mid_full, out_weight.T, preferred_element_type=jnp.float32).astype(
            jnp.bfloat16
        )
        d_blocks = d_attended.reshape(block_count, block_rows, local_heads, HEAD)

        def attend_back(running, block_item):
            d_keys, d_values = running
            query_block, image_block, block_sums, d_block = block_item
            scores = (
                jnp.einsum(
                    "qhe,khe->hqk", query_block, key_heads, preferred_element_type=jnp.float32
                )
                * score_scale
            )
            same_image = image_block[:, None] == image_row[None, :]
            scores = jnp.where(same_image[None], scores, mask_fill)
            attn_probs = jnp.exp(scores - block_sums[:, :, None])
            d_probs = jnp.einsum(
                "qhe,khe->hqk", d_block, value_heads, preferred_element_type=jnp.float32
            )
            row_delta = jnp.sum(attn_probs * d_probs, -1, keepdims=True)
            d_scores = (attn_probs * (d_probs - row_delta)).astype(jnp.bfloat16)
            d_query = (
                jnp.einsum("hqk,khe->qhe", d_scores, key_heads, preferred_element_type=jnp.float32)
                * score_scale
            )
            d_keys = (
                d_keys
                + jnp.einsum(
                    "hqk,qhe->khe", d_scores, query_block, preferred_element_type=jnp.float32
                )
                * score_scale
            )
            d_values = d_values + jnp.einsum(
                "hqk,qhe->khe",
                attn_probs.astype(jnp.bfloat16),
                d_block,
                preferred_element_type=jnp.float32,
            )
            return ((d_keys, d_values), d_query)

        zero_heads = jnp.zeros((length, local_heads, HEAD), jnp.float32)
        (d_keys, d_values), d_queries = lax.scan(
            attend_back, (zero_heads, zero_heads), (query_blocks, image_blocks, log_sums, d_blocks)
        )
        d_query_low = d_queries.reshape(length, head_cols).astype(jnp.bfloat16)
        d_key_low = d_keys.reshape(length, head_cols).astype(jnp.bfloat16)
        d_value_low = d_values.reshape(length, head_cols).astype(jnp.bfloat16)
        d_projected = jnp.stack([d_query_low, d_key_low, d_value_low])
        qkv_term = jnp.einsum(
            "td,cte->dce", gathered, d_projected, preferred_element_type=jnp.float32
        )
        d_normed = lax.psum_scatter(
            jnp.einsum(
                "cte,dce->td", d_projected, qkv_weight, preferred_element_type=jnp.float32
            ).astype(jnp.bfloat16),
            "tensor",
            scatter_dimension=0,
            tiled=True,
        ).astype(jnp.float32)
        d_tokens, gain_one_grad, shift_one_grad = norm_pull(d_normed)
        input_grads.append(d_tokens + d_middle)
        vector_terms = vector_terms + jnp.stack(
            [
                gain_one_grad,
                shift_one_grad,
                jnp.sum(d_middle, 0),
                gain_two_grad,
                shift_two_grad,
                jnp.sum(cotangent, 0),
            ]
        )
        bias_terms = bias_terms + jnp.concatenate(
            [
                jnp.sum(d_query_low, 0, dtype=jnp.float32),
                jnp.sum(d_value_low, 0, dtype=jnp.float32),
                jnp.sum(d_hidden, 0, dtype=jnp.float32),
            ]
        )
        local_terms = (qkv_term, out_term, up_term, down_term)
        owned = (
            lax.psum_scatter(
                local_terms[0].astype(jnp.bfloat16), "dp", scatter_dimension=0, tiled=True
            ).astype(jnp.float32),
            lax.psum_scatter(
                local_terms[1].astype(jnp.bfloat16), "dp", scatter_dimension=1, tiled=True
            ).astype(jnp.float32),
            lax.psum_scatter(
                local_terms[2].astype(jnp.bfloat16), "dp", scatter_dimension=0, tiled=True
            ).astype(jnp.float32),
            lax.psum_scatter(
                local_terms[3].astype(jnp.bfloat16), "dp", scatter_dimension=1, tiled=True
            ).astype(jnp.float32),
        )
        weight_sums = tuple((total + term for total, term in zip(weight_sums, owned)))
    qkv_grad, out_grad, up_grad, down_grad = weight_sums
    tensor_index = lax.axis_index("tensor")
    placed = jnp.where(jnp.arange(splits)[:, None] == tensor_index, bias_terms[None, :], 0.0)
    vec_grad, bias_table = lax.psum((vector_terms, placed), ("dp", "tensor"))
    bias_grad = lax.dynamic_slice_in_dim(bias_table, tensor_index, 1, 0)
    qkv_second_new, qkv_master_new = adam_update(
        qkv_master, qkv_moment, qkv_second, qkv_grad, 0.09, 0.1
    )
    out_second_new, out_master_new = adam_update(
        out_master, out_moment, out_second, out_grad, 0.4, 0.1
    )
    up_second_new, up_master_new = adam_update(up_master, up_moment, up_second, up_grad, 0.09, 0.1)
    down_second_new, down_master_new = adam_update(
        down_master, down_moment, down_second, down_grad, 0.045, 0.1
    )
    vec_second_new, vec_master_new = adam_update(
        vec_master, vec_moment, vec_second, vec_grad, 0.6, 0.0
    )
    bias_second_new, bias_master_new = adam_update(
        bias_master, bias_moment, bias_second, bias_grad, 0.5, 0.0
    )
    block_output = jnp.stack(block_outputs)[:, None]
    input_grad = jnp.stack(input_grads)[:, None]
    return (
        block_output,
        input_grad,
        qkv_grad,
        qkv_second_new,
        qkv_master_new,
        out_grad,
        out_second_new,
        out_master_new,
        up_grad,
        up_second_new,
        up_master_new,
        down_grad,
        down_second_new,
        down_master_new,
        vec_grad,
        vec_second_new,
        vec_master_new,
        bias_grad,
        bias_second_new,
        bias_master_new,
    )


LANES = 128
TILE = 128
SPAN = 256
WIDE = 1152
BATCH = 8


def lane_window(head):
    first = head * HEAD
    low = first // LANES * LANES
    high = -(-(first + HEAD) // LANES) * LANES
    return low, high


def head_mask(head, rows):
    low, high = lane_window(head)
    lane = lax.broadcasted_iota(jnp.int32, (rows, high - low), 1) + low
    return (lane >= head * HEAD) & (lane < head * HEAD + HEAD)


def head_columns(head, columns):
    low, high = lane_window(head)
    high = min(high, columns)
    return slice(low, high), head_mask(head, TILE)[:, : high - low]


def padded(columns):
    return -(-columns // LANES) * LANES


def tile_spans(ids_smem, ids_ref, index, tiles):
    first_id = ids_smem[index * TILE]
    last_id = ids_smem[index * TILE + TILE - 1]
    ids = ids_ref[...]
    begin = jnp.sum((ids < first_id).astype(jnp.int32)) // TILE
    end = (jnp.sum((ids <= last_id).astype(jnp.int32)) + TILE - 1) // TILE
    count = (end - begin + 1) // 2
    return jnp.minimum(begin, tiles - 2 * count), count


def ids_column(ids_ref, index):
    row = ids_ref[:, pl.ds(pl.multiple_of(index * TILE, TILE), TILE)].astype(jnp.float32)
    square = jnp.broadcast_to(row, (TILE, TILE)).T
    return jnp.concatenate([square] * (SPAN // TILE), axis=1).astype(jnp.int32)


NT = (((1,), (1,)), ((), ()))
TN = (((0,), (0,)), ((), ()))


def attend_kernel(heads, length, ids_smem, ids_ref, q_ref, k_ref, v_ref, o_ref, lse_ref, top, total, acc):
    index = pl.program_id(0)
    columns = heads * HEAD
    scale = HEAD ** (-0.5) * math.log2(math.e)
    begin, count = tile_spans(ids_smem, ids_ref, index, length // TILE)
    own_ids = ids_column(ids_ref, index)
    top[...] = jnp.full(top.shape, mask_fill, jnp.float32)
    total[...] = jnp.zeros(total.shape, jnp.float32)
    acc[...] = jnp.zeros(acc.shape, jnp.float32)

    def window(low, high):
        return slice(low, min(high, columns))

    def step(item, carry):
        place = pl.multiple_of((begin + 2 * item) * TILE, TILE)
        keys = pl.ds(place, SPAN)
        same = own_ids == ids_ref[:, keys]
        for first in range(0, heads, BATCH):
            batch = range(first, min(first + BATCH, heads))
            held_scores = []
            for head in batch:
                cols, mask = head_columns(head, columns)
                query = q_ref[:, cols]
                query = jnp.where(mask, query, jnp.zeros_like(query))
                scores = lax.dot_general(query, k_ref[keys, cols], NT, preferred_element_type=jnp.float32)
                held_scores.append(jnp.where(same, scores * scale, mask_fill))
            tops = [jnp.maximum(top[head], jnp.max(scores, -1, keepdims=True)) for head, scores in zip(batch, held_scores)]
            parts = [
                jnp.exp2(scores - jnp.concatenate([now] * (SPAN // LANES), axis=1)) for now, scores in zip(tops, held_scores)
            ]
            sums = [jnp.sum(part, -1, keepdims=True) for part in parts]
            mixes = [
                jnp.dot(part.astype(jnp.bfloat16), v_ref[keys, head_columns(head, columns)[0]], preferred_element_type=jnp.float32)
                for head, part in zip(batch, parts)
            ]
            for head, now, part_sum, mixed in zip(batch, tops, sums, mixes):
                cols, mask = head_columns(head, columns)
                shrink = jnp.exp2(top[head] - now)
                total[head] = total[head] * shrink + part_sum
                top[head] = now
                width = cols.stop - cols.start
                wide = jnp.concatenate([shrink] * ((width + LANES - 1) // LANES), axis=1)[:, :width]
                held = acc[:, cols]
                acc[:, cols] = jnp.where(mask, held * wide + mixed, held)
        return carry

    lax.fori_loop(0, count, step, 0)
    sums = jnp.zeros((TILE, LANES), jnp.float32)
    lane = lax.broadcasted_iota(jnp.int32, (TILE, LANES), 1)
    for head in range(heads):
        low, high = lane_window(head)
        high = min(high, columns)
        cols = slice(low, high)
        mask = head_mask(head, TILE)[:, : high - low]
        inverse = 1.0 / total[head]
        wide = jnp.concatenate([inverse] * ((high - low + LANES - 1) // LANES), axis=1)[:, : high - low]
        held = acc[:, cols]
        acc[:, cols] = jnp.where(mask, held * wide, held)
        sums = jnp.where(lane == head, top[head] + jnp.log2(total[head]), sums)
    o_ref[...] = acc[...].astype(o_ref.dtype)
    lse_ref[...] = sums.T[:heads]


def attend(ids, query, key, value):
    length, columns = query.shape
    heads = columns // HEAD
    tiles = length // TILE
    whole = pl.BlockSpec((length, columns), lambda i, s: (0, 0))
    block = pl.BlockSpec((TILE, columns), lambda i, s: (i, 0))
    return pl.pallas_call(
        partial(attend_kernel, heads, length),
        grid_spec=pltpu.PrefetchScalarGridSpec(
            num_scalar_prefetch=1,
            grid=(tiles,),
            in_specs=[pl.BlockSpec((1, length), lambda i, s: (0, 0)), block, whole, whole],
            out_specs=[block, pl.BlockSpec((heads, TILE), lambda i, s: (0, i))],
            scratch_shapes=[
                pltpu.VMEM((heads, TILE, LANES), jnp.float32),
                pltpu.VMEM((heads, TILE, LANES), jnp.float32),
                pltpu.VMEM((TILE, columns), jnp.float32),
            ],
        ),
        out_shape=[
            jax.ShapeDtypeStruct((length, columns), jnp.bfloat16),
            jax.ShapeDtypeStruct((heads, length), jnp.float32),
        ],
        compiler_params=pltpu.CompilerParams(vmem_limit_bytes=36 << 20),
        cost_estimate=pl.CostEstimate(flops=4 * 10**9, bytes_accessed=10**6, transcendentals=0),
    )(ids, ids.reshape(1, length), query, key, value)


def attend_back_kernel(
    heads, length, ids_smem, ids_ref, q_ref, k_ref, v_ref, o_ref, g_ref, lse_ref,
    dq_ref, dk_ref, dv_ref, delta, dq_acc, dk_acc, dv_acc,
):
    index = pl.program_id(0)
    columns = heads * HEAD
    natural = HEAD ** (-0.5)
    scale = natural * math.log2(math.e)
    tiles = length // TILE
    begin, count = tile_spans(ids_smem, ids_ref, index, tiles)
    own_ids = ids_column(ids_ref, index)

    @pl.when(index == 0)
    def _():
        dq_acc[...] = jnp.zeros(dq_acc.shape, jnp.float32)
        row = lax.broadcasted_iota(jnp.int32, (heads, columns), 0)
        lane = lax.broadcasted_iota(jnp.int32, (heads, columns), 1)
        pick = ((lane >= row * HEAD) & (lane < row * HEAD + HEAD)).astype(jnp.bfloat16)
        product = g_ref[...].astype(jnp.float32) * o_ref[...].astype(jnp.float32)
        coarse = product.astype(jnp.bfloat16)
        fine = (product - coarse.astype(jnp.float32)).astype(jnp.bfloat16)
        delta[...] = lax.dot_general(pick, coarse, NT, preferred_element_type=jnp.float32) + lax.dot_general(
            pick, fine, NT, preferred_element_type=jnp.float32
        )

    dk_acc[...] = jnp.zeros(dk_acc.shape, jnp.float32)
    dv_acc[...] = jnp.zeros(dv_acc.shape, jnp.float32)

    def step(item, carry):
        place = pl.multiple_of((begin + 2 * item) * TILE, TILE)
        rows = pl.ds(place, SPAN)
        same = own_ids == ids_ref[:, rows]
        for first in range(0, heads, BATCH):
            batch = range(first, min(first + BATCH, heads))
            keys, scores, d_probs = [], [], []
            for head in batch:
                cols, mask = head_columns(head, columns)
                key = k_ref[:, cols]
                keys.append(jnp.where(mask, key, jnp.zeros_like(key)))
                value = v_ref[:, cols]
                value = jnp.where(mask, value, jnp.zeros_like(value))
                scores.append(lax.dot_general(keys[-1], q_ref[rows, cols], NT, preferred_element_type=jnp.float32))
                d_probs.append(lax.dot_general(value, g_ref[rows, cols], NT, preferred_element_type=jnp.float32))
            probs = [
                jnp.exp2(jnp.where(same, score * scale, mask_fill) - lse_ref[head : head + 1, rows])
                for head, score in zip(batch, scores)
            ]
            d_scores = [
                (prob * (d_prob - delta[head : head + 1, rows])).astype(jnp.bfloat16)
                for head, prob, d_prob in zip(batch, probs, d_probs)
            ]
            for head, key, prob, d_score in zip(batch, keys, probs, d_scores):
                cols, mask = head_columns(head, columns)
                d_value = jnp.dot(prob.astype(jnp.bfloat16), g_ref[rows, cols], preferred_element_type=jnp.float32)
                d_key = jnp.dot(d_score, q_ref[rows, cols], preferred_element_type=jnp.float32)
                d_query = lax.dot_general(d_score, key, TN, preferred_element_type=jnp.float32)
                dv_acc[:, cols] += jnp.where(mask, d_value, 0.0)
                dk_acc[:, cols] += jnp.where(mask, d_key, 0.0)
                dq_acc[rows, cols] += d_query
        return carry

    lax.fori_loop(0, count, step, 0)
    dk_ref[...] = (dk_acc[...] * natural).astype(dk_ref.dtype)
    dv_ref[...] = dv_acc[...].astype(dv_ref.dtype)

    @pl.when(index == tiles - 1)
    def _():
        dq_ref[...] = (dq_acc[...] * natural).astype(dq_ref.dtype)


def attend_back(ids, query, key, value, attended, grad, lse):
    length, columns = query.shape
    heads = columns // HEAD
    tiles = length // TILE
    whole = pl.BlockSpec((length, columns), lambda i, s: (0, 0))
    block = pl.BlockSpec((TILE, columns), lambda i, s: (i, 0))
    out = jax.ShapeDtypeStruct((length, columns), jnp.bfloat16)
    return pl.pallas_call(
        partial(attend_back_kernel, heads, length),
        grid_spec=pltpu.PrefetchScalarGridSpec(
            num_scalar_prefetch=1,
            grid=(tiles,),
            in_specs=[
                pl.BlockSpec((1, length), lambda i, s: (0, 0)),
                whole,
                block,
                block,
                whole,
                whole,
                pl.BlockSpec((heads, length), lambda i, s: (0, 0)),
            ],
            out_specs=[whole, block, block],
            scratch_shapes=[
                pltpu.VMEM((heads, length), jnp.float32),
                pltpu.VMEM((length, columns), jnp.float32),
                pltpu.VMEM((TILE, columns), jnp.float32),
                pltpu.VMEM((TILE, columns), jnp.float32),
            ],
        ),
        out_shape=[out, out, out],
        compiler_params=pltpu.CompilerParams(vmem_limit_bytes=36 << 20),
        cost_estimate=pl.CostEstimate(flops=2 * 10**9, bytes_accessed=10**6, transcendentals=0),
    )(ids, ids.reshape(1, length), query, key, value, attended, grad, lse)


def column_call(kernel, ins, outs, columns, flops, scratch=()):
    wide = min(WIDE, padded(columns))
    steps = -(-columns // wide)

    def spec(shape, cut):
        if cut:
            return pl.BlockSpec(shape[:-1] + (wide,), lambda i: (0,) * (len(shape) - 1) + (i,))
        return pl.BlockSpec(shape, lambda i: (0,) * len(shape))

    size = sum(math.prod(a.shape) * a.dtype.itemsize for a, _ in ins) + sum(
        math.prod(a.shape) * a.dtype.itemsize for a in outs
    )
    return pl.pallas_call(
        kernel,
        grid=(steps,),
        in_specs=[spec(a.shape, cut) for a, cut in ins],
        out_specs=[spec(a.shape, True) for a in outs],
        out_shape=outs,
        scratch_shapes=list(scratch),
        compiler_params=pltpu.CompilerParams(vmem_limit_bytes=44 << 20),
        cost_estimate=pl.CostEstimate(flops=flops // 8, bytes_accessed=size // 8, transcendentals=0),
    )(*[a for a, _ in ins])


def hidden_kernel(x_ref, w_ref, b_ref, active_ref, slope_ref):
    rows = 256
    for block in range(x_ref.shape[0] // rows):
        part = pl.ds(block * rows, rows)
        value = jnp.dot(x_ref[part, :], w_ref[...], preferred_element_type=jnp.float32) + b_ref[...]
        active, slope = gelu_pair(value)
        active_ref[part, :] = active.astype(jnp.bfloat16)
        slope_ref[part, :] = slope.astype(jnp.bfloat16)


def hidden_units(x, weight, bias):
    tokens, columns = x.shape[0], weight.shape[1]
    out = jax.ShapeDtypeStruct((tokens, columns), jnp.bfloat16)
    ins = [(x, False), (weight, True), (bias.reshape(1, columns), True)]
    return column_call(hidden_kernel, ins, [out, out], columns, 2 * tokens * x.shape[1] * columns)


def hidden_back_kernel(x_ref, w_ref, slope_ref, grad_ref, sum_ref):
    rows = 256
    total = jnp.zeros(sum_ref.shape, jnp.float32)
    for block in range(x_ref.shape[0] // rows):
        part = pl.ds(block * rows, rows)
        value = jnp.dot(x_ref[part, :], w_ref[...], preferred_element_type=jnp.float32)
        value = value * slope_ref[part, :].astype(jnp.float32)
        grad_ref[part, :] = value.astype(jnp.bfloat16)
        total = total + jnp.sum(value, 0, keepdims=True)
    sum_ref[...] = total


def hidden_back(x, weight, slope):
    tokens, columns = x.shape[0], weight.shape[1]
    outs = [jax.ShapeDtypeStruct((tokens, columns), jnp.bfloat16), jax.ShapeDtypeStruct((1, columns), jnp.float32)]
    ins = [(x, False), (weight, True), (slope, True)]
    return column_call(hidden_back_kernel, ins, outs, columns, 2 * tokens * x.shape[1] * columns)


def grad_kernel(chunks, stacked, x_ref, *refs):
    core = lax.axis_index("dp") % 2
    count = len(refs) - 4 if stacked else (len(refs) - 2) // 3
    turned, result = refs[-2:]
    dy_refs = refs[:count]
    outs = refs[count:-2]

    @pl.when(pl.program_id(0) == 0)
    def _():
        turned[...] = x_ref[...].T

    rows = turned.shape[0] // chunks
    for number, dy_ref in enumerate(dy_refs):
        if stacked:
            sent_ref, kept_ref = outs[0].at[number], outs[1].at[number]
        else:
            sent_ref, kept_ref = outs[number], outs[count + number]
        result[...] = jnp.dot(turned[...], dy_ref[...], preferred_element_type=jnp.float32)
        for spot in range(chunks // 2):
            sent = pl.multiple_of((2 * spot + 1 - core) * rows, 8)
            kept = pl.multiple_of((2 * spot + core) * rows, 8)
            sent_ref[spot] = result[pl.ds(sent, rows), :].astype(jnp.bfloat16)
            kept_ref[spot] = result[pl.ds(kept, rows), :].astype(jnp.bfloat16)


def weight_grads(x, parts, stacked=False):
    tokens, features = x.shape
    columns = parts[0].shape[1]
    count = len(parts)
    wide = min(WIDE, padded(columns))
    shape = (8, features // 16, columns)
    outs = [jax.ShapeDtypeStruct(shape, jnp.bfloat16)] * (2 * count)
    if stacked:
        outs = [jax.ShapeDtypeStruct((count,) + shape, jnp.bfloat16)] * 2
    results = column_call(
        partial(grad_kernel, 16, stacked),
        [(x, False)] + [(part, True) for part in parts],
        outs,
        columns,
        2 * tokens * features * columns * count,
        [pltpu.VMEM((features, tokens), jnp.bfloat16), pltpu.VMEM((features, wide), jnp.float32)],
    )
    return results if stacked else (results[:count], results[count:])


def block_call(kernel, ins, outs, columns):
    wide = min(768, padded(columns))

    def spec(shape):
        return pl.BlockSpec(shape[:-1] + (wide,), lambda i: (0,) * (len(shape) - 1) + (i,))

    size = sum(math.prod(a.shape) * 2 for a in list(ins) + list(outs))
    return pl.pallas_call(
        kernel,
        grid=(-(-columns // wide),),
        in_specs=[spec(a.shape) for a in ins],
        out_specs=[spec(a.shape) for a in outs],
        out_shape=outs,
        compiler_params=pltpu.CompilerParams(vmem_limit_bytes=58 << 20),
        cost_estimate=pl.CostEstimate(flops=0, bytes_accessed=size // 4, transcendentals=0),
    )(*ins)


def low_sum(*refs):
    total = refs[0].astype(jnp.float32)
    for ref in refs[1:]:
        total = total + ref.astype(jnp.float32)
    return total.astype(jnp.bfloat16)


def first_sums_kernel(kept_own, kept_other, core_own, core_other, near_own, near_other, far_own, near_sent, far_sent):
    y = lax.axis_index("dp") // 2 % 2
    for z in range(2):
        keep, send = 2 * z + y, 2 * z + 1 - y
        near_own[z] = low_sum(kept_own[keep], core_own[keep])
        near_other[z] = low_sum(kept_other[keep], core_other[keep])
        near_sent[0, z] = low_sum(kept_own[send], core_own[send])
        near_sent[1, z] = low_sum(kept_other[send], core_other[send])
    for spot in range(4):
        far_own[spot] = low_sum(kept_own[4 + spot], core_own[4 + spot])
        far_sent[spot] = low_sum(kept_other[4 + spot], core_other[4 + spot])


def middle_sums_kernel(near_own, near_other, near_got, far_own, far_got, own, far, near_sent, far_sent):
    y = lax.axis_index("dp") // 2 % 2
    for z in range(2):
        keep, send = 2 * z + y, 2 * z + 1 - y
        own[z] = low_sum(near_own[z], near_got[0, z])
        near_sent[z] = low_sum(near_other[z], near_got[1, z])
        far[z] = low_sum(far_own[keep], far_got[keep])
        far_sent[z] = low_sum(far_own[send], far_got[send])


def core_sums_kernel(kept, got, here, there):
    y = lax.axis_index("dp") // 2 % 2
    for lead in range(kept.shape[0]):
        for z in range(4):
            keep, send = 2 * z + y, 2 * z + 1 - y
            here[lead, z] = low_sum(kept[lead, keep], got[lead, keep])
            there[lead, z] = low_sum(kept[lead, send], got[lead, send])


def core_sums(kept, got):
    leads, rows, columns = kept.shape[0], kept.shape[2], kept.shape[3]
    out = jax.ShapeDtypeStruct((leads, 4, rows, columns), jnp.bfloat16)
    return block_call(core_sums_kernel, [kept, got], [out, out], columns)


def place_kernel(leads, ordered, steps, *refs):
    pieces = refs[: len(steps)]
    outs = refs[len(steps) : len(steps) + leads]
    sems = refs[len(steps) + leads]
    spot = lax.axis_index("dp")
    z, y, core = spot // 4, spot // 2 % 2, spot % 2
    copies = []
    for piece, (first_slot, y_step, core_step) in zip(pieces, steps):
        column = (y + y_step) % 2 * 2 + (core + core_step) % 2
        for slot in range(piece.shape[0]):
            number = first_slot + slot
            row = (number if ordered else (z + 4 - number) % 4) * 4 + column
            for lead in range(leads):
                copy = pltpu.make_async_copy(piece.at[slot, lead], outs[lead].at[row], sems.at[len(copies)])
                copy.start()
                copies.append(copy)
    for copy in copies:
        copy.wait()


def place(planes, ordered):
    pieces = sum(planes, [])
    leads, rows, columns = pieces[0].shape[1:]
    slots = pieces[0].shape[0]
    steps = [(start, step % 2, step // 2) for start in range(0, 4, slots) for step in range(4)]
    size = 16 * leads * rows * padded(columns) * 2
    placed = pl.pallas_call(
        partial(place_kernel, leads, ordered, steps),
        in_specs=[pl.BlockSpec(memory_space=pl.ANY)] * len(pieces),
        out_specs=[pl.BlockSpec(memory_space=pltpu.VMEM)] * leads,
        out_shape=[jax.ShapeDtypeStruct((16, rows, columns), jnp.bfloat16)] * leads,
        scratch_shapes=[pltpu.SemaphoreType.DMA((16 * leads,))],
        compiler_params=pltpu.CompilerParams(vmem_limit_bytes=size * 3 // 2 + (2 << 20)),
        cost_estimate=pl.CostEstimate(flops=0, bytes_accessed=size // 4, transcendentals=0),
    )(*pieces)
    return [part.reshape(16 * rows, columns) for part in placed]


def swap_x(value):
    return lax.ppermute(value, "tensor", [(0, 1), (1, 0)])


def swap_y(value):
    return lax.ppermute(value, "dp", [(spot, spot ^ 2) for spot in range(16)])


def swap_core(value):
    return lax.ppermute(value, "dp", [(spot, spot ^ 1) for spot in range(16)])


def move_z(value, steps):
    return lax.ppermute(value, "dp", [(spot, (spot + 4 * steps) % 16) for spot in range(16)])


def tie(*values):
    return lax.optimization_barrier(values)


def gather_z(shard):
    groups = [[spot + 4 * z for z in range(4)] for spot in range(4)]
    return lax.all_gather(shard, "dp", axis_index_groups=groups)


def both_cores(parts):
    return parts + [swap_core(part) for part in parts]


def add_low(*terms):
    total = terms[0].astype(jnp.float32)
    for term in terms[1:]:
        total = total + term.astype(jnp.float32)
    return total.astype(jnp.bfloat16)


def part_of(value, index, axis):
    return lax.dynamic_index_in_dim(value, index, axis, keepdims=False)


def y_parts(value):
    spot = lax.axis_index("dp")
    split = value.reshape((value.shape[0] // 2, 2) + value.shape[1:])
    return part_of(split, spot // 2 % 2, 1), part_of(split, 1 - spot // 2 % 2, 1)


class Planes:
    def __init__(self, kept, core):
        rows, self.columns = kept[0].shape[1:]
        self.two, self.four = [jax.ShapeDtypeStruct((n, rows, self.columns), jnp.bfloat16) for n in (2, 4)]
        pair = jax.ShapeDtypeStruct((2, 2, rows, self.columns), jnp.bfloat16)
        self.near_own, self.near_other, self.far_own, *self.sent = block_call(
            first_sums_kernel, [*kept, *core], [self.two, self.two, self.four, pair, self.four], self.columns
        )

    def first(self):
        self.got = [swap_y(self.sent[0]), swap_x(self.sent[1])]

    def middle(self):
        self.near_own, self.far_own, *self.sent = block_call(
            middle_sums_kernel,
            [self.near_own, self.near_other, self.got[0], self.far_own, self.got[1]],
            [self.two] * 4,
            self.columns,
        )

    def second(self):
        self.got = [swap_x(self.sent[0]), swap_y(self.sent[1])]

    def total(self):
        return jnp.concatenate([add_low(self.near_own, self.got[0]), add_low(self.far_own, self.got[1])])


def scatter_z(value):
    groups = [[spot + 4 * z for z in range(4)] for spot in range(4)]
    return lax.psum_scatter(value, "dp", axis_index_groups=groups)


def send_z(value):
    z = lax.axis_index("dp") // 4
    return [part_of(value, z, 0)] + [move_z(part_of(value, (z + steps) % 4, 0), steps) for steps in (1, 2, 3)]


def sum_terms(terms):
    total = terms[0].astype(jnp.float32)
    for term in terms[1:]:
        total = total + term.astype(jnp.float32)
    return total


def norm_forward(values):
    centre = values - jnp.mean(values, -1, keepdims=True)
    inverse = lax.rsqrt(jnp.mean(centre * centre, -1, keepdims=True) + norm_eps)
    return centre * inverse, inverse


def norm_back(grad, hat, inverse, gain):
    scaled = grad * gain
    mean_one = jnp.mean(scaled, -1, keepdims=True)
    mean_two = jnp.mean(scaled * hat, -1, keepdims=True)
    return (scaled - mean_one - hat * mean_two) * inverse


def gelu_pair(value):
    inner = math.sqrt(2.0 / math.pi)
    squared = value * value
    bent = jnp.tanh(inner * (value + 0.044715 * value * squared))
    half = 0.5 * (1.0 + bent)
    slope = half + 0.5 * value * (1.0 - bent * bent) * inner * (1.0 + 3 * 0.044715 * squared)
    return value * half, slope


def row_layer(
    block_input,
    image_ids,
    out_cotangent,
    qkv_master,
    qkv_moment,
    qkv_second,
    out_master,
    out_moment,
    out_second,
    up_master,
    up_moment,
    up_second,
    down_master,
    down_moment,
    down_second,
    vec_master,
    vec_moment,
    vec_second,
    bias_master,
    bias_moment,
    bias_second,
):
    low = jnp.bfloat16
    wide = jnp.float32
    mine = lax.axis_index("tensor")
    first = mine == 0
    half = block_input.shape[2]
    features = block_input.shape[3]
    head_cols = qkv_master.shape[2]

    def pick(pair, index):
        return lax.dynamic_index_in_dim(pair, index, 0, keepdims=False)

    def in_order(own, other, axis=0):
        return jnp.concatenate([jnp.where(first, own, other), jnp.where(first, other, own)], axis)

    def dot(spec, left, right):
        return jnp.einsum(spec, left, right, preferred_element_type=wide)

    inputs_own = pick(block_input[:, 0], mine)
    inputs_sent = pick(block_input[:, 0], 1 - mine)
    cot_own = pick(out_cotangent[:, 0], mine)
    cot_sent = pick(out_cotangent[:, 0], 1 - mine)
    inputs_low = inputs_sent.astype(low)
    early_shard = jnp.stack([qkv_master[:, 0], qkv_master[:, 1], qkv_master[:, 2]]).astype(low)
    early_shard, inputs_low = tie(early_shard, inputs_low)
    inputs_got = swap_x(inputs_low)
    early_one = move_z(early_shard, 1)
    early_three = move_z(early_shard, 3)
    early_shard, early_one = tie(early_shard, early_one)
    early_two = move_z(early_shard, 2)
    near = jnp.stack([early_shard, early_one])
    near_y, near_x = swap_y(near), swap_x(near)
    late_shard = jnp.stack([up_master, down_master.T]).astype(low)
    small = jnp.concatenate([pick(image_ids[:, 0], 1 - mine).astype(wide), bias_master[0]])
    cot_sum = jnp.sum(out_cotangent[:, 0], (0, 1))
    cot_low_sent = cot_sent.astype(low)
    late_shard, early_two, early_three = tie(late_shard, early_two, early_three)
    late_z = gather_z(late_shard)
    far = jnp.stack([early_two, early_three])
    far_y = swap_y(far)
    small, cot_sum, cot_low_sent, inputs_got, near_x, near_y, far, far_y = tie(
        small, cot_sum, cot_low_sent, inputs_got, near_x, near_y, far, far_y
    )
    small_got = swap_x(small[None])[0]
    far_x = swap_x(far)
    near_xy, far_yx = swap_y(near_x), swap_x(far_y)
    early_own = place([both_cores([near, near_y]), both_cores([far, far_y])], False)
    out_shard, early_own = tie(out_master.T.astype(low), early_own)
    out_whole = lax.all_gather(out_shard, ("tensor", "dp")).reshape(2, features, head_cols)
    inputs = in_order(inputs_own, inputs_got.astype(wide))
    ids = in_order(pick(image_ids[:, 0], mine), small_got[:half].astype(jnp.int32))
    biases = jnp.stack([bias_master[0], small_got[half:]])

    hat_one, inverse_one = norm_forward(inputs)
    normed = (hat_one * vec_master[0] + vec_master[1]).astype(low)
    def project(g, weights):
        query = (dot("td,de->te", normed, weights[0]) + biases[g, :head_cols]).astype(low)
        key = dot("td,de->te", normed, weights[1]).astype(low)
        value = (dot("td,de->te", normed, weights[2]) + biases[g, head_cols : 2 * head_cols]).astype(low)
        return query, key, value

    projected = [project(0, early_own), None]
    up_near, up_far = [late_z[start : start + 2, :1] for start in (0, 2)]
    projected[0], near_x, near_xy, far_x, up_near, up_far = tie(
        projected[0], near_x, near_xy, far_x, up_near, up_far
    )
    up_near_x, up_far_y = swap_x(up_near), swap_y(up_far)
    others = [both_cores([near_x, near_xy]), [far_x, swap_core(far_x)]]
    attended, log_sums = [None, None], [None, None]
    attended[0], log_sums[0] = attend(ids, *projected[0])
    others, attended[0], far_yx, up_near, up_far, up_near_x, up_far_y = tie(
        others, attended[0], far_yx, up_near, up_far, up_near_x, up_far_y
    )
    up_near_y, up_far_x = swap_y(up_near), swap_x(up_far)
    others[1] = [others[1][0], far_yx, others[1][1], swap_core(far_yx)]
    early_other = place(others, False)
    down_near, down_far = [late_z[start : start + 2, 1:] for start in (0, 2)]
    projected[1] = project(1, early_other)
    query_weight, key_weight, value_weight = zip(early_own, early_other)
    projected[1], up_near_x, up_far_y, up_near_y, up_far_x = tie(
        projected[1], up_near_x, up_far_y, up_near_y, up_far_x
    )
    up_near_xy, up_far_yx = swap_y(up_near_x), swap_x(up_far_y)
    attended[1], log_sums[1] = attend(ids, *projected[1])
    attended[1], up_near_xy, up_far_yx, down_near, down_far = tie(
        attended[1], up_near_xy, up_far_yx, down_near, down_far
    )
    down_near_x, down_far_y = swap_x(down_near), swap_y(down_far)
    cot_got = swap_x(cot_low_sent)
    out_weight = [pick(out_whole, mine), pick(out_whole, 1 - mine)]
    attn_sum = sum(dot("te,de->td", attended[g], out_weight[g]) for g in range(2)) + vec_master[2]
    middle = inputs + attn_sum
    hat_two, inverse_two = norm_forward(middle)
    normed_two = (hat_two * vec_master[3] + vec_master[4]).astype(low)
    normed_two, down_near, down_far, down_near_x, down_far_y = tie(
        normed_two, down_near, down_far, down_near_x, down_far_y
    )
    down_near_y, down_far_x = swap_y(down_near), swap_x(down_far)
    up_weight = [
        place([both_cores([up_near, up_near_y]), both_cores([up_far, up_far_y])], True)[0],
        place([both_cores([up_near_x, up_near_xy]), both_cores([up_far_x, up_far_yx])], True)[0],
    ]
    active, slope = [None, None], [None, None]
    active[0], slope[0] = hidden_units(normed_two, up_weight[0], biases[0, 2 * head_cols :])
    normed_two, active[0], down_near_x, down_far_y, down_near_y, down_far_x, cot_got = tie(
        normed_two, active[0], down_near_x, down_far_y, down_near_y, down_far_x, cot_got
    )
    down_near_xy, down_far_yx = swap_y(down_near_x), swap_x(down_far_y)
    active[1], slope[1] = hidden_units(normed_two, up_weight[1], biases[1, 2 * head_cols :])
    down_weight = [place([both_cores([down_near, down_near_y]), both_cores([down_far, down_far_y])], True)[0], None]
    active[1], down_weight[0] = tie(active[1], down_weight[0])
    cot_row = in_order(cot_own, cot_got.astype(wide))
    cot_low = cot_row.astype(low)
    down_sent, down_kept = weight_grads(cot_low, active)
    down_sent, down_near_xy, down_far_yx = tie(down_sent, down_near_xy, down_far_yx)
    down_weight[1] = place(
        [both_cores([down_near_x, down_near_xy]), both_cores([down_far_x, down_far_yx])], True
    )[0]
    added = attn_sum + sum(dot("tf,df->td", active[g], down_weight[g]) for g in range(2)) + vec_master[5]
    added = added.reshape(2, half, features)
    added_got = swap_x(pick(added, 1 - mine).astype(low))

    own, other = 0, 1
    down_core = [swap_core(part) for part in down_sent]
    d_hidden, hidden_sums = [None, None], [None, None]
    d_hidden[own], hidden_sums[own] = hidden_back(cot_low, down_weight[own], slope[own])
    d_hidden[own], down_core = tie(d_hidden[own], down_core)
    down = Planes(down_kept, down_core)
    cot_late, down.sent = tie(cot_low, down.sent)
    down.first()
    d_hidden[other], hidden_sums[other] = hidden_back(cot_late, down_weight[other], slope[other])
    up_sent, up_kept = weight_grads(normed_two, d_hidden)
    up_sent, down.got = tie(up_sent, down.got)
    up_core = [swap_core(part) for part in up_sent]
    down.middle()
    d_hidden, down.sent = tie(d_hidden, down.sent)
    down.second()
    d_normed_two = sum(dot("tf,df->td", d_hidden[g], up_weight[g]) for g in range(2))
    d_normed_two, up_core, down.got = tie(d_normed_two, up_core, down.got)
    up = Planes(up_kept, up_core)
    down_total = down.total()
    d_normed_two, up.sent, down_total = tie(d_normed_two, up.sent, down_total)
    up.first()
    down_term = scatter_z(down_total)
    mid_added = norm_back(d_normed_two, hat_two, inverse_two, vec_master[3])
    d_middle = cot_row + mid_added
    mid_low = d_middle.astype(low)
    d_attended = [dot("td,de->te", mid_low, out_weight[g]).astype(low) for g in range(2)]
    out_sent, out_kept = weight_grads(mid_low, attended)
    d_attended[other], out_sent, added_got = tie(d_attended[other], out_sent, added_got)
    out_core = [swap_core(part) for part in out_sent]

    def back(g, grad):
        return attend_back(ids, *projected[g], attended[g], grad, log_sums[g])

    d_other = back(other, d_attended[other])
    d_other, out_core, up.got = tie(d_other, out_core, up.got)
    up.middle()
    out_other = add_low(out_kept[other], out_core[other])
    out_own = add_low(out_kept[own], out_core[own])
    d_other, up.sent, out_other = tie(d_other, up.sent, out_other)
    up.second()
    out_there_x = swap_x(out_other)
    qkv_sent, qkv_kept = [None, None], [None, None]
    qkv_sent[other], qkv_kept[other] = weight_grads(normed, d_other, True)

    def normed_part(parts, g):
        weights = (query_weight, key_weight, value_weight)
        return sum(dot("te,de->td", part, weight[g]) for part, weight in zip(parts, weights))

    d_other, qkv_sent[other] = tie(d_other, qkv_sent[other])
    qkv_core_other = swap_core(qkv_sent[other])
    d_normed_other = normed_part(d_other, other)
    d_normed_other, up.got, qkv_core_other = tie(d_normed_other, up.got, qkv_core_other)
    up_total = up.total()
    qkv_other_here, qkv_other_there = core_sums(qkv_kept[other], qkv_core_other)
    d_attended[own], up_total, qkv_other_there = tie(d_attended[own], up_total, qkv_other_there)
    up_term = scatter_z(up_total)
    qkv_there_y = swap_y(qkv_other_there)
    d_own = back(own, d_attended[own])
    d_own, qkv_there_y, out_there_x = tie(tuple(d_own), qkv_there_y, out_there_x)
    qkv_other = add_low(qkv_other_here, qkv_there_y)
    out_here, out_there = y_parts(add_low(out_own, out_there_x))
    d_own, qkv_other, out_there = tie(d_own, qkv_other, out_there)
    qkv_there_x = swap_x(qkv_other)
    out_there_y = swap_y(out_there)
    qkv_sent[own], qkv_kept[own] = weight_grads(normed, d_own, True)
    d_own, qkv_sent[own], out_there_y = tie(d_own, qkv_sent[own], out_there_y)
    out_terms = send_z(add_low(out_here, out_there_y))
    qkv_core_own = swap_core(qkv_sent[own])
    d_normed_own = normed_part(d_own, own)
    d_normed_own, qkv_core_own, qkv_there_x = tie(d_normed_own, qkv_core_own, qkv_there_x)
    qkv_here, qkv_there = core_sums(qkv_kept[own], qkv_core_own)
    d_normed_own, qkv_there = tie(d_normed_own, qkv_there)
    qkv_there_y = swap_y(qkv_there)
    d_normed = d_normed_other + d_normed_own
    early = jnp.concatenate(
        [
            jnp.sum(d_middle, 0),
            jnp.sum(d_normed_two * hat_two, 0),
            jnp.sum(d_normed_two, 0),
            cot_sum,
        ]
    )

    def bias_rows(sums):
        return jnp.where(first, jnp.concatenate(sums), jnp.concatenate(sums[::-1]))

    sums = jnp.concatenate(
        [
            jnp.sum(d_normed * hat_one, 0),
            jnp.sum(d_normed, 0),
            early,
            bias_rows([jnp.sum(part[0], 0, dtype=wide) for part in (d_own, d_other)]),
            bias_rows([jnp.sum(part[2], 0, dtype=wide) for part in (d_own, d_other)]),
            bias_rows([part[0] for part in hidden_sums]),
        ]
    )
    in_added = (mid_added + norm_back(d_normed, hat_one, inverse_one, vec_master[0])).reshape(2, half, features)
    in_sent = pick(in_added, 1 - mine).astype(low)
    in_got = swap_x(in_sent)
    down_term, up_term, out_terms, added_got, in_sent = tie(down_term, up_term, out_terms, added_got, in_sent)
    block_here = inputs_own + pick(added, mine)
    block_there = pick(block_input[:, 0], 1 - mine) + added_got.astype(wide)
    block_output = in_order(block_here[None], block_there[None])[:, None]

    def update(name, grad):
        master, moment, second, rate, decay = states[name]
        second_new, master_new = adam_update(master, moment, second, grad, rate, decay)
        return grad, second_new, master_new

    states = {
        "qkv": (qkv_master, qkv_moment, qkv_second, 0.09, 0.1),
        "out": (out_master, out_moment, out_second, 0.4, 0.1),
        "up": (up_master, up_moment, up_second, 0.09, 0.1),
        "down": (down_master, down_moment, down_second, 0.045, 0.1),
        "vec": (vec_master, vec_moment, vec_second, 0.6, 0.0),
        "bias": (bias_master, bias_moment, bias_second, 0.5, 0.0),
    }
    up_new = update("up", up_term.astype(wide))
    down_new = update("down", down_term.astype(wide).T)
    out_new = update("out", sum_terms(out_terms).T)
    sums, qkv_there_y, block_output, up_new, down_new, out_new = tie(
        sums, qkv_there_y, block_output, up_new, down_new, out_new
    )
    qkv_terms = send_z(add_low(qkv_here, qkv_there_y, qkv_there_x).transpose(1, 0, 2, 3))
    sums = sums[None]
    sums = sums + move_z(sums, 1) + move_z(sums, 2) + move_z(sums, 3)
    sums, in_got = tie(sums, in_got)
    sums = sums + swap_core(sums)
    sums = sums + swap_y(sums)
    sums = (sums + swap_x(sums))[0]
    qkv_new = update("qkv", sum_terms(qkv_terms).transpose(1, 0, 2))
    grad_here = cot_own + pick(in_added, mine)
    grad_there = cot_sent + in_got.astype(wide)
    input_grad = in_order(grad_here[None], grad_there[None])[:, None]
    vec_grad = sums[: 6 * features].reshape(6, features)

    def group(start, size):
        return pick(sums[start : start + 2 * size].reshape(2, size), mine)

    start = 6 * features
    bias_grad = jnp.concatenate(
        [
            group(start, head_cols),
            group(start + 2 * head_cols, head_cols),
            group(start + 4 * head_cols, up_master.shape[1]),
        ]
    )[None]

    vec_new = update("vec", vec_grad)
    bias_new = update("bias", bias_grad)
    return (block_output, input_grad, *qkv_new, *out_new, *up_new, *down_new, *vec_new, *bias_new)


def solution(mesh):
    placed = (
        P(None, "dp", "tensor", None),
        P(None, "dp", "tensor"),
        P(None, "dp", "tensor", None),
        P("dp", None, "tensor"),
        P("dp", None, "tensor"),
        P("dp", None, "tensor"),
        P("tensor", "dp"),
        P("tensor", "dp"),
        P("tensor", "dp"),
        P("dp", "tensor"),
        P("dp", "tensor"),
        P("dp", "tensor"),
        P("tensor", "dp"),
        P("tensor", "dp"),
        P("tensor", "dp"),
        P(),
        P(),
        P(),
        P("tensor", None),
        P("tensor", None),
        P("tensor", None),
    )
    by_rows = dict(mesh.shape) == {"dp": 16, "tensor": 2}
    return jax.shard_map(
        row_layer if by_rows else split_layer,
        mesh=mesh,
        in_specs=placed,
        out_specs=(
            P(None, "dp", "tensor", None),
            P(None, "dp", "tensor", None),
            P("dp", None, "tensor"),
            P("dp", None, "tensor"),
            P("dp", None, "tensor"),
            P("tensor", "dp"),
            P("tensor", "dp"),
            P("tensor", "dp"),
            P("dp", "tensor"),
            P("dp", "tensor"),
            P("dp", "tensor"),
            P("tensor", "dp"),
            P("tensor", "dp"),
            P("tensor", "dp"),
            P(),
            P(),
            P(),
            P("tensor", None),
            P("tensor", None),
            P("tensor", None),
        ),
        check_vma=False,
    )
```

```python
import math
from functools import partial

import jax
import jax.numpy as jnp
from jax import lax
from jax.experimental import pallas as pl
from jax.experimental.pallas import tpu as pltpu
from jax.sharding import PartitionSpec as P

HEAD = 72
STEP = 10


norm_eps = 1e-06
mask_fill = -1e30
beta_one = 0.9
beta_two = 0.95
adam_eps = 1e-08


def layer_norm(values, scale_vec, shift_vec):
    centre = values - jnp.mean(values, -1, keepdims=True)
    spread = jnp.mean(centre * centre, -1, keepdims=True)
    return centre * lax.rsqrt(spread + norm_eps) * scale_vec + shift_vec


def adam_update(master, moment, second, gradient, step_rate, weight_decay):
    first_moment = beta_one * moment.astype(jnp.float32) + (1.0 - beta_one) * gradient
    second_new = beta_two * second + (1.0 - beta_two) * gradient * gradient
    update = (
        first_moment
        / (1.0 - beta_one**STEP)
        / (jnp.sqrt(second_new / (1.0 - beta_two**STEP)) + adam_eps)
        + weight_decay * master
    )
    return (second_new, master - step_rate * update)


def split_layer(
    block_input,
    image_ids,
    out_cotangent,
    qkv_master,
    qkv_moment,
    qkv_second,
    out_master,
    out_moment,
    out_second,
    up_master,
    up_moment,
    up_second,
    down_master,
    down_moment,
    down_second,
    vec_master,
    vec_moment,
    vec_second,
    bias_master,
    bias_moment,
    bias_second,
):
    batches = block_input.shape[0]
    local_rows = block_input.shape[2]
    features = block_input.shape[3]
    splits = lax.axis_size("tensor")
    length = local_rows * splits
    head_cols = qkv_master.shape[2]
    local_heads = head_cols // HEAD
    block_rows = min(512, length)
    block_count = length // block_rows
    score_scale = HEAD ** (-0.5)
    biases = bias_master[0]
    query_bias = biases[:head_cols]
    value_bias = biases[head_cols : 2 * head_cols]
    hidden_bias = biases[2 * head_cols :]
    compute = (
        qkv_master.astype(jnp.bfloat16),
        out_master.astype(jnp.bfloat16),
        up_master.astype(jnp.bfloat16),
        down_master.astype(jnp.bfloat16),
    )
    gelu_tanh = partial(jax.nn.gelu, approximate=True)
    weight_sums = (
        jnp.zeros_like(qkv_master),
        jnp.zeros_like(out_master),
        jnp.zeros_like(up_master),
        jnp.zeros_like(down_master),
    )
    vector_terms = jnp.zeros((6, features), jnp.float32)
    bias_terms = jnp.zeros(biases.shape, jnp.float32)
    block_outputs = []
    input_grads = []
    for batch_index in range(batches):
        qkv_weight, out_weight, up_weight, down_weight = (
            lax.all_gather(compute[0], "dp", axis=0, tiled=True),
            lax.all_gather(compute[1], "dp", axis=1, tiled=True),
            lax.all_gather(compute[2], "dp", axis=0, tiled=True),
            lax.all_gather(compute[3], "dp", axis=1, tiled=True),
        )
        tokens_here = block_input[batch_index, 0]
        normed, norm_pull = jax.vjp(layer_norm, tokens_here, vec_master[0], vec_master[1])
        gathered, image_row = (
            lax.all_gather(normed.astype(jnp.bfloat16), "tensor", axis=0, tiled=True),
            lax.all_gather(image_ids[batch_index, 0], "tensor", axis=0, tiled=True),
        )
        projected = jnp.einsum(
            "td,dce->cte", gathered, qkv_weight, preferred_element_type=jnp.float32
        )
        queries = (projected[0] + query_bias).astype(jnp.bfloat16)
        key_rows = projected[1].astype(jnp.bfloat16)
        values = (projected[2] + value_bias).astype(jnp.bfloat16)
        key_heads = key_rows.reshape(length, local_heads, HEAD)
        value_heads = values.reshape(length, local_heads, HEAD)
        query_blocks = queries.reshape(block_count, block_rows, local_heads, HEAD)
        image_blocks = image_row.reshape(block_count, block_rows)

        def attend(block_pair):
            query_block, image_block = block_pair
            scores = (
                jnp.einsum(
                    "qhe,khe->hqk", query_block, key_heads, preferred_element_type=jnp.float32
                )
                * score_scale
            )
            same_image = image_block[:, None] == image_row[None, :]
            scores = jnp.where(same_image[None], scores, mask_fill)
            row_max = jnp.max(scores, -1, keepdims=True)
            exp_scores = jnp.exp(scores - row_max)
            exp_total = jnp.sum(exp_scores, -1, keepdims=True)
            attn_probs = exp_scores / exp_total
            result = jnp.einsum(
                "hqk,khe->qhe",
                attn_probs.astype(jnp.bfloat16),
                value_heads,
                preferred_element_type=jnp.float32,
            )
            return (result.reshape(block_rows, head_cols), (row_max + jnp.log(exp_total))[..., 0])

        attended_blocks, log_sums = lax.map(attend, (query_blocks, image_blocks))
        attended = attended_blocks.reshape(length, head_cols).astype(jnp.bfloat16)
        attn_sum = lax.psum_scatter(
            jnp.dot(attended, out_weight, preferred_element_type=jnp.float32).astype(jnp.bfloat16),
            "tensor",
            scatter_dimension=0,
            tiled=True,
        ).astype(jnp.float32)
        middle = tokens_here + attn_sum + vec_master[2]
        normed_two, norm_pull_two = jax.vjp(layer_norm, middle, vec_master[3], vec_master[4])
        gathered_two = lax.all_gather(normed_two.astype(jnp.bfloat16), "tensor", axis=0, tiled=True)
        hidden = jnp.dot(gathered_two, up_weight, preferred_element_type=jnp.float32) + hidden_bias
        active, gelu_pull = jax.vjp(gelu_tanh, hidden)
        active_low = active.astype(jnp.bfloat16)
        project_row_piece = lax.slice_in_dim(
            active_low, 0, local_rows * lax.axis_size("tensor"), axis=0
        )
        mlp_sum = lax.psum_scatter(
            jnp.dot(project_row_piece, down_weight, preferred_element_type=jnp.float32).astype(
                jnp.bfloat16
            ),
            "tensor",
            scatter_dimension=0,
            tiled=True,
        ).astype(jnp.float32)
        block_outputs.append(middle + mlp_sum + vec_master[5])
        qkv_weight, out_weight, up_weight, down_weight = (
            lax.all_gather(compute[0], "dp", axis=0, tiled=True),
            lax.all_gather(compute[1], "dp", axis=1, tiled=True),
            lax.all_gather(compute[2], "dp", axis=0, tiled=True),
            lax.all_gather(compute[3], "dp", axis=1, tiled=True),
        )
        cotangent = out_cotangent[batch_index, 0]
        cot_full = lax.all_gather(cotangent.astype(jnp.bfloat16), "tensor", axis=0, tiled=True)
        down_term = jnp.dot(active_low.T, cot_full, preferred_element_type=jnp.float32)
        d_active = jnp.dot(cot_full, down_weight.T, preferred_element_type=jnp.float32)
        d_hidden = gelu_pull(d_active)[0].astype(jnp.bfloat16)
        up_term = jnp.dot(gathered_two.T, d_hidden, preferred_element_type=jnp.float32)
        d_normed_two = lax.psum_scatter(
            jnp.dot(d_hidden, up_weight.T, preferred_element_type=jnp.float32).astype(jnp.bfloat16),
            "tensor",
            scatter_dimension=0,
            tiled=True,
        ).astype(jnp.float32)
        d_middle, gain_two_grad, shift_two_grad = norm_pull_two(d_normed_two)
        d_middle = d_middle + cotangent
        mid_full = lax.all_gather(d_middle.astype(jnp.bfloat16), "tensor", axis=0, tiled=True)
        out_term = jnp.dot(attended.T, mid_full, preferred_element_type=jnp.float32)
        d_attended = jnp.dot(mid_full, out_weight.T, preferred_element_type=jnp.float32).astype(
            jnp.bfloat16
        )
        d_blocks = d_attended.reshape(block_count, block_rows, local_heads, HEAD)

        def attend_back(running, block_item):
            d_keys, d_values = running
            query_block, image_block, block_sums, d_block = block_item
            scores = (
                jnp.einsum(
                    "qhe,khe->hqk", query_block, key_heads, preferred_element_type=jnp.float32
                )
                * score_scale
            )
            same_image = image_block[:, None] == image_row[None, :]
            scores = jnp.where(same_image[None], scores, mask_fill)
            attn_probs = jnp.exp(scores - block_sums[:, :, None])
            d_probs = jnp.einsum(
                "qhe,khe->hqk", d_block, value_heads, preferred_element_type=jnp.float32
            )
            row_delta = jnp.sum(attn_probs * d_probs, -1, keepdims=True)
            d_scores = (attn_probs * (d_probs - row_delta)).astype(jnp.bfloat16)
            d_query = (
                jnp.einsum("hqk,khe->qhe", d_scores, key_heads, preferred_element_type=jnp.float32)
                * score_scale
            )
            d_keys = (
                d_keys
                + jnp.einsum(
                    "hqk,qhe->khe", d_scores, query_block, preferred_element_type=jnp.float32
                )
                * score_scale
            )
            d_values = d_values + jnp.einsum(
                "hqk,qhe->khe",
                attn_probs.astype(jnp.bfloat16),
                d_block,
                preferred_element_type=jnp.float32,
            )
            return ((d_keys, d_values), d_query)

        zero_heads = jnp.zeros((length, local_heads, HEAD), jnp.float32)
        (d_keys, d_values), d_queries = lax.scan(
            attend_back, (zero_heads, zero_heads), (query_blocks, image_blocks, log_sums, d_blocks)
        )
        d_query_low = d_queries.reshape(length, head_cols).astype(jnp.bfloat16)
        d_key_low = d_keys.reshape(length, head_cols).astype(jnp.bfloat16)
        d_value_low = d_values.reshape(length, head_cols).astype(jnp.bfloat16)
        d_projected = jnp.stack([d_query_low, d_key_low, d_value_low])
        qkv_term = jnp.einsum(
            "td,cte->dce", gathered, d_projected, preferred_element_type=jnp.float32
        )
        d_normed = lax.psum_scatter(
            jnp.einsum(
                "cte,dce->td", d_projected, qkv_weight, preferred_element_type=jnp.float32
            ).astype(jnp.bfloat16),
            "tensor",
            scatter_dimension=0,
            tiled=True,
        ).astype(jnp.float32)
        d_tokens, gain_one_grad, shift_one_grad = norm_pull(d_normed)
        input_grads.append(d_tokens + d_middle)
        vector_terms = vector_terms + jnp.stack(
            [
                gain_one_grad,
                shift_one_grad,
                jnp.sum(d_middle, 0),
                gain_two_grad,
                shift_two_grad,
                jnp.sum(cotangent, 0),
            ]
        )
        bias_terms = bias_terms + jnp.concatenate(
            [
                jnp.sum(d_query_low, 0, dtype=jnp.float32),
                jnp.sum(d_value_low, 0, dtype=jnp.float32),
                jnp.sum(d_hidden, 0, dtype=jnp.float32),
            ]
        )
        local_terms = (qkv_term, out_term, up_term, down_term)
        owned = (
            lax.psum_scatter(
                local_terms[0].astype(jnp.bfloat16), "dp", scatter_dimension=0, tiled=True
            ).astype(jnp.float32),
            lax.psum_scatter(
                local_terms[1].astype(jnp.bfloat16), "dp", scatter_dimension=1, tiled=True
            ).astype(jnp.float32),
            lax.psum_scatter(
                local_terms[2].astype(jnp.bfloat16), "dp", scatter_dimension=0, tiled=True
            ).astype(jnp.float32),
            lax.psum_scatter(
                local_terms[3].astype(jnp.bfloat16), "dp", scatter_dimension=1, tiled=True
            ).astype(jnp.float32),
        )
        weight_sums = tuple((total + term for total, term in zip(weight_sums, owned)))
    qkv_grad, out_grad, up_grad, down_grad = weight_sums
    tensor_index = lax.axis_index("tensor")
    placed = jnp.where(jnp.arange(splits)[:, None] == tensor_index, bias_terms[None, :], 0.0)
    vec_grad, bias_table = lax.psum((vector_terms, placed), ("dp", "tensor"))
    bias_grad = lax.dynamic_slice_in_dim(bias_table, tensor_index, 1, 0)
    qkv_second_new, qkv_master_new = adam_update(
        qkv_master, qkv_moment, qkv_second, qkv_grad, 0.09, 0.1
    )
    out_second_new, out_master_new = adam_update(
        out_master, out_moment, out_second, out_grad, 0.4, 0.1
    )
    up_second_new, up_master_new = adam_update(up_master, up_moment, up_second, up_grad, 0.09, 0.1)
    down_second_new, down_master_new = adam_update(
        down_master, down_moment, down_second, down_grad, 0.045, 0.1
    )
    vec_second_new, vec_master_new = adam_update(
        vec_master, vec_moment, vec_second, vec_grad, 0.6, 0.0
    )
    bias_second_new, bias_master_new = adam_update(
        bias_master, bias_moment, bias_second, bias_grad, 0.5, 0.0
    )
    block_output = jnp.stack(block_outputs)[:, None]
    input_grad = jnp.stack(input_grads)[:, None]
    return (
        block_output,
        input_grad,
        qkv_grad,
        qkv_second_new,
        qkv_master_new,
        out_grad,
        out_second_new,
        out_master_new,
        up_grad,
        up_second_new,
        up_master_new,
        down_grad,
        down_second_new,
        down_master_new,
        vec_grad,
        vec_second_new,
        vec_master_new,
        bias_grad,
        bias_second_new,
        bias_master_new,
    )


LANES = 128
TILE = 128
SPAN = 256
WIDE = 1152
BATCH = 8


def lane_window(head):
    first = head * HEAD
    low = first // LANES * LANES
    high = -(-(first + HEAD) // LANES) * LANES
    return low, high


def head_mask(head, rows):
    low, high = lane_window(head)
    lane = lax.broadcasted_iota(jnp.int32, (rows, high - low), 1) + low
    return (lane >= head * HEAD) & (lane < head * HEAD + HEAD)


def head_columns(head, columns):
    low, high = lane_window(head)
    high = min(high, columns)
    return slice(low, high), head_mask(head, TILE)[:, : high - low]


def padded(columns):
    return -(-columns // LANES) * LANES


def tile_spans(ids_smem, ids_ref, index, tiles):
    first_id = ids_smem[index * TILE]
    last_id = ids_smem[index * TILE + TILE - 1]
    ids = ids_ref[...]
    begin = jnp.sum((ids < first_id).astype(jnp.int32)) // TILE
    end = (jnp.sum((ids <= last_id).astype(jnp.int32)) + TILE - 1) // TILE
    count = (end - begin + 1) // 2
    return jnp.minimum(begin, tiles - 2 * count), count


def ids_column(ids_ref, index):
    row = ids_ref[:, pl.ds(pl.multiple_of(index * TILE, TILE), TILE)].astype(jnp.float32)
    square = jnp.broadcast_to(row, (TILE, TILE)).T
    return jnp.concatenate([square] * (SPAN // TILE), axis=1).astype(jnp.int32)


NT = (((1,), (1,)), ((), ()))
TN = (((0,), (0,)), ((), ()))


def attend_kernel(heads, length, ids_smem, ids_ref, q_ref, k_ref, v_ref, o_ref, lse_ref, top, total, acc):
    index = pl.program_id(0)
    columns = heads * HEAD
    scale = HEAD ** (-0.5) * math.log2(math.e)
    begin, count = tile_spans(ids_smem, ids_ref, index, length // TILE)
    own_ids = ids_column(ids_ref, index)
    top[...] = jnp.full(top.shape, mask_fill, jnp.float32)
    total[...] = jnp.zeros(total.shape, jnp.float32)
    acc[...] = jnp.zeros(acc.shape, jnp.float32)

    def window(low, high):
        return slice(low, min(high, columns))

    def step(item, carry):
        place = pl.multiple_of((begin + 2 * item) * TILE, TILE)
        keys = pl.ds(place, SPAN)
        same = own_ids == ids_ref[:, keys]
        for first in range(0, heads, BATCH):
            batch = range(first, min(first + BATCH, heads))
            held_scores = []
            for head in batch:
                cols, mask = head_columns(head, columns)
                query = q_ref[:, cols]
                query = jnp.where(mask, query, jnp.zeros_like(query))
                scores = lax.dot_general(query, k_ref[keys, cols], NT, preferred_element_type=jnp.float32)
                held_scores.append(jnp.where(same, scores * scale, mask_fill))
            tops = [jnp.maximum(top[head], jnp.max(scores, -1, keepdims=True)) for head, scores in zip(batch, held_scores)]
            parts = [
                jnp.exp2(scores - jnp.concatenate([now] * (SPAN // LANES), axis=1)) for now, scores in zip(tops, held_scores)
            ]
            sums = [jnp.sum(part, -1, keepdims=True) for part in parts]
            mixes = [
                jnp.dot(part.astype(jnp.bfloat16), v_ref[keys, head_columns(head, columns)[0]], preferred_element_type=jnp.float32)
                for head, part in zip(batch, parts)
            ]
            for head, now, part_sum, mixed in zip(batch, tops, sums, mixes):
                cols, mask = head_columns(head, columns)
                shrink = jnp.exp2(top[head] - now)
                total[head] = total[head] * shrink + part_sum
                top[head] = now
                width = cols.stop - cols.start
                wide = jnp.concatenate([shrink] * ((width + LANES - 1) // LANES), axis=1)[:, :width]
                held = acc[:, cols]
                acc[:, cols] = jnp.where(mask, held * wide + mixed, held)
        return carry

    lax.fori_loop(0, count, step, 0)
    sums = jnp.zeros((TILE, LANES), jnp.float32)
    lane = lax.broadcasted_iota(jnp.int32, (TILE, LANES), 1)
    for head in range(heads):
        low, high = lane_window(head)
        high = min(high, columns)
        cols = slice(low, high)
        mask = head_mask(head, TILE)[:, : high - low]
        inverse = 1.0 / total[head]
        wide = jnp.concatenate([inverse] * ((high - low + LANES - 1) // LANES), axis=1)[:, : high - low]
        held = acc[:, cols]
        acc[:, cols] = jnp.where(mask, held * wide, held)
        sums = jnp.where(lane == head, top[head] + jnp.log2(total[head]), sums)
    o_ref[...] = acc[...].astype(o_ref.dtype)
    lse_ref[...] = sums.T[:heads]


def attend(ids, query, key, value):
    length, columns = query.shape
    heads = columns // HEAD
    tiles = length // TILE
    whole = pl.BlockSpec((length, columns), lambda i, s: (0, 0))
    block = pl.BlockSpec((TILE, columns), lambda i, s: (i, 0))
    return pl.pallas_call(
        partial(attend_kernel, heads, length),
        grid_spec=pltpu.PrefetchScalarGridSpec(
            num_scalar_prefetch=1,
            grid=(tiles,),
            in_specs=[pl.BlockSpec((1, length), lambda i, s: (0, 0)), block, whole, whole],
            out_specs=[block, pl.BlockSpec((heads, TILE), lambda i, s: (0, i))],
            scratch_shapes=[
                pltpu.VMEM((heads, TILE, LANES), jnp.float32),
                pltpu.VMEM((heads, TILE, LANES), jnp.float32),
                pltpu.VMEM((TILE, columns), jnp.float32),
            ],
        ),
        out_shape=[
            jax.ShapeDtypeStruct((length, columns), jnp.bfloat16),
            jax.ShapeDtypeStruct((heads, length), jnp.float32),
        ],
        compiler_params=pltpu.CompilerParams(vmem_limit_bytes=36 << 20),
        cost_estimate=pl.CostEstimate(flops=4 * 10**9, bytes_accessed=10**6, transcendentals=0),
    )(ids, ids.reshape(1, length), query, key, value)


def attend_back_kernel(
    heads, length, ids_smem, ids_ref, q_ref, k_ref, v_ref, o_ref, g_ref, lse_ref,
    dq_ref, dk_ref, dv_ref, delta, dq_acc, dk_acc, dv_acc,
):
    index = pl.program_id(0)
    columns = heads * HEAD
    natural = HEAD ** (-0.5)
    scale = natural * math.log2(math.e)
    tiles = length // TILE
    begin, count = tile_spans(ids_smem, ids_ref, index, tiles)
    own_ids = ids_column(ids_ref, index)

    @pl.when(index == 0)
    def _():
        dq_acc[...] = jnp.zeros(dq_acc.shape, jnp.float32)
        row = lax.broadcasted_iota(jnp.int32, (heads, columns), 0)
        lane = lax.broadcasted_iota(jnp.int32, (heads, columns), 1)
        pick = ((lane >= row * HEAD) & (lane < row * HEAD + HEAD)).astype(jnp.bfloat16)
        product = g_ref[...].astype(jnp.float32) * o_ref[...].astype(jnp.float32)
        coarse = product.astype(jnp.bfloat16)
        fine = (product - coarse.astype(jnp.float32)).astype(jnp.bfloat16)
        delta[...] = lax.dot_general(pick, coarse, NT, preferred_element_type=jnp.float32) + lax.dot_general(
            pick, fine, NT, preferred_element_type=jnp.float32
        )

    dk_acc[...] = jnp.zeros(dk_acc.shape, jnp.float32)
    dv_acc[...] = jnp.zeros(dv_acc.shape, jnp.float32)

    def step(item, carry):
        place = pl.multiple_of((begin + 2 * item) * TILE, TILE)
        rows = pl.ds(place, SPAN)
        same = own_ids == ids_ref[:, rows]
        for first in range(0, heads, BATCH):
            batch = range(first, min(first + BATCH, heads))
            keys, scores, d_probs = [], [], []
            for head in batch:
                cols, mask = head_columns(head, columns)
                key = k_ref[:, cols]
                keys.append(jnp.where(mask, key, jnp.zeros_like(key)))
                value = v_ref[:, cols]
                value = jnp.where(mask, value, jnp.zeros_like(value))
                scores.append(lax.dot_general(keys[-1], q_ref[rows, cols], NT, preferred_element_type=jnp.float32))
                d_probs.append(lax.dot_general(value, g_ref[rows, cols], NT, preferred_element_type=jnp.float32))
            probs = [
                jnp.exp2(jnp.where(same, score * scale, mask_fill) - lse_ref[head : head + 1, rows])
                for head, score in zip(batch, scores)
            ]
            d_scores = [
                (prob * (d_prob - delta[head : head + 1, rows])).astype(jnp.bfloat16)
                for head, prob, d_prob in zip(batch, probs, d_probs)
            ]
            for head, key, prob, d_score in zip(batch, keys, probs, d_scores):
                cols, mask = head_columns(head, columns)
                d_value = jnp.dot(prob.astype(jnp.bfloat16), g_ref[rows, cols], preferred_element_type=jnp.float32)
                d_key = jnp.dot(d_score, q_ref[rows, cols], preferred_element_type=jnp.float32)
                d_query = lax.dot_general(d_score, key, TN, preferred_element_type=jnp.float32)
                dv_acc[:, cols] += jnp.where(mask, d_value, 0.0)
                dk_acc[:, cols] += jnp.where(mask, d_key, 0.0)
                dq_acc[rows, cols] += d_query
        return carry

    lax.fori_loop(0, count, step, 0)
    dk_ref[...] = (dk_acc[...] * natural).astype(dk_ref.dtype)
    dv_ref[...] = dv_acc[...].astype(dv_ref.dtype)

    @pl.when(index == tiles - 1)
    def _():
        dq_ref[...] = (dq_acc[...] * natural).astype(dq_ref.dtype)


def attend_back(ids, query, key, value, attended, grad, lse):
    length, columns = query.shape
    heads = columns // HEAD
    tiles = length // TILE
    whole = pl.BlockSpec((length, columns), lambda i, s: (0, 0))
    block = pl.BlockSpec((TILE, columns), lambda i, s: (i, 0))
    out = jax.ShapeDtypeStruct((length, columns), jnp.bfloat16)
    return pl.pallas_call(
        partial(attend_back_kernel, heads, length),
        grid_spec=pltpu.PrefetchScalarGridSpec(
            num_scalar_prefetch=1,
            grid=(tiles,),
            in_specs=[
                pl.BlockSpec((1, length), lambda i, s: (0, 0)),
                whole,
                block,
                block,
                whole,
                whole,
                pl.BlockSpec((heads, length), lambda i, s: (0, 0)),
            ],
            out_specs=[whole, block, block],
            scratch_shapes=[
                pltpu.VMEM((heads, length), jnp.float32),
                pltpu.VMEM((length, columns), jnp.float32),
                pltpu.VMEM((TILE, columns), jnp.float32),
                pltpu.VMEM((TILE, columns), jnp.float32),
            ],
        ),
        out_shape=[out, out, out],
        compiler_params=pltpu.CompilerParams(vmem_limit_bytes=36 << 20),
        cost_estimate=pl.CostEstimate(flops=2 * 10**9, bytes_accessed=10**6, transcendentals=0),
    )(ids, ids.reshape(1, length), query, key, value, attended, grad, lse)


def column_call(kernel, ins, outs, columns, flops, scratch=()):
    wide = min(WIDE, padded(columns))
    steps = -(-columns // wide)

    def spec(shape, cut):
        if cut:
            return pl.BlockSpec(shape[:-1] + (wide,), lambda i: (0,) * (len(shape) - 1) + (i,))
        return pl.BlockSpec(shape, lambda i: (0,) * len(shape))

    size = sum(math.prod(a.shape) * a.dtype.itemsize for a, _ in ins) + sum(
        math.prod(a.shape) * a.dtype.itemsize for a in outs
    )
    return pl.pallas_call(
        kernel,
        grid=(steps,),
        in_specs=[spec(a.shape, cut) for a, cut in ins],
        out_specs=[spec(a.shape, True) for a in outs],
        out_shape=outs,
        scratch_shapes=list(scratch),
        compiler_params=pltpu.CompilerParams(vmem_limit_bytes=44 << 20),
        cost_estimate=pl.CostEstimate(flops=flops // 8, bytes_accessed=size // 8, transcendentals=0),
    )(*[a for a, _ in ins])


def hidden_kernel(x_ref, w_ref, b_ref, active_ref, slope_ref):
    rows = 256
    for block in range(x_ref.shape[0] // rows):
        part = pl.ds(block * rows, rows)
        value = jnp.dot(x_ref[part, :], w_ref[...], preferred_element_type=jnp.float32) + b_ref[...]
        active, slope = gelu_pair(value)
        active_ref[part, :] = active.astype(jnp.bfloat16)
        slope_ref[part, :] = slope.astype(jnp.bfloat16)


def hidden_units(x, weight, bias):
    tokens, columns = x.shape[0], weight.shape[1]
    out = jax.ShapeDtypeStruct((tokens, columns), jnp.bfloat16)
    ins = [(x, False), (weight, True), (bias.reshape(1, columns), True)]
    return column_call(hidden_kernel, ins, [out, out], columns, 2 * tokens * x.shape[1] * columns)


def hidden_back_kernel(x_ref, w_ref, slope_ref, grad_ref, sum_ref):
    rows = 256
    total = jnp.zeros(sum_ref.shape, jnp.float32)
    for block in range(x_ref.shape[0] // rows):
        part = pl.ds(block * rows, rows)
        value = jnp.dot(x_ref[part, :], w_ref[...], preferred_element_type=jnp.float32)
        value = value * slope_ref[part, :].astype(jnp.float32)
        grad_ref[part, :] = value.astype(jnp.bfloat16)
        total = total + jnp.sum(value, 0, keepdims=True)
    sum_ref[...] = total


def hidden_back(x, weight, slope):
    tokens, columns = x.shape[0], weight.shape[1]
    outs = [jax.ShapeDtypeStruct((tokens, columns), jnp.bfloat16), jax.ShapeDtypeStruct((1, columns), jnp.float32)]
    ins = [(x, False), (weight, True), (slope, True)]
    return column_call(hidden_back_kernel, ins, outs, columns, 2 * tokens * x.shape[1] * columns)


def grad_kernel(chunks, stacked, x_ref, *refs):
    core = lax.axis_index("dp") % 2
    count = len(refs) - 4 if stacked else (len(refs) - 2) // 3
    turned, result = refs[-2:]
    dy_refs = refs[:count]
    outs = refs[count:-2]

    @pl.when(pl.program_id(0) == 0)
    def _():
        turned[...] = x_ref[...].T

    rows = turned.shape[0] // chunks
    for number, dy_ref in enumerate(dy_refs):
        if stacked:
            sent_ref, kept_ref = outs[0].at[number], outs[1].at[number]
        else:
            sent_ref, kept_ref = outs[number], outs[count + number]
        result[...] = jnp.dot(turned[...], dy_ref[...], preferred_element_type=jnp.float32)
        for spot in range(chunks // 2):
            sent = pl.multiple_of((2 * spot + 1 - core) * rows, 8)
            kept = pl.multiple_of((2 * spot + core) * rows, 8)
            sent_ref[spot] = result[pl.ds(sent, rows), :].astype(jnp.bfloat16)
            kept_ref[spot] = result[pl.ds(kept, rows), :].astype(jnp.bfloat16)


def weight_grads(x, parts, stacked=False):
    tokens, features = x.shape
    columns = parts[0].shape[1]
    count = len(parts)
    wide = min(WIDE, padded(columns))
    shape = (8, features // 16, columns)
    outs = [jax.ShapeDtypeStruct(shape, jnp.bfloat16)] * (2 * count)
    if stacked:
        outs = [jax.ShapeDtypeStruct((count,) + shape, jnp.bfloat16)] * 2
    results = column_call(
        partial(grad_kernel, 16, stacked),
        [(x, False)] + [(part, True) for part in parts],
        outs,
        columns,
        2 * tokens * features * columns * count,
        [pltpu.VMEM((features, tokens), jnp.bfloat16), pltpu.VMEM((features, wide), jnp.float32)],
    )
    return results if stacked else (results[:count], results[count:])


def block_call(kernel, ins, outs, columns):
    wide = min(768, padded(columns))

    def spec(shape):
        return pl.BlockSpec(shape[:-1] + (wide,), lambda i: (0,) * (len(shape) - 1) + (i,))

    size = sum(math.prod(a.shape) * 2 for a in list(ins) + list(outs))
    return pl.pallas_call(
        kernel,
        grid=(-(-columns // wide),),
        in_specs=[spec(a.shape) for a in ins],
        out_specs=[spec(a.shape) for a in outs],
        out_shape=outs,
        compiler_params=pltpu.CompilerParams(vmem_limit_bytes=58 << 20),
        cost_estimate=pl.CostEstimate(flops=0, bytes_accessed=size // 4, transcendentals=0),
    )(*ins)


def low_sum(*refs):
    total = refs[0].astype(jnp.float32)
    for ref in refs[1:]:
        total = total + ref.astype(jnp.float32)
    return total.astype(jnp.bfloat16)


def first_sums_kernel(kept_own, kept_other, core_own, core_other, near_own, near_other, far_own, near_sent, far_sent):
    y = lax.axis_index("dp") // 2 % 2
    for z in range(2):
        keep, send = 2 * z + y, 2 * z + 1 - y
        near_own[z] = low_sum(kept_own[keep], core_own[keep])
        near_other[z] = low_sum(kept_other[keep], core_other[keep])
        near_sent[0, z] = low_sum(kept_own[send], core_own[send])
        near_sent[1, z] = low_sum(kept_other[send], core_other[send])
    for spot in range(4):
        far_own[spot] = low_sum(kept_own[4 + spot], core_own[4 + spot])
        far_sent[spot] = low_sum(kept_other[4 + spot], core_other[4 + spot])


def middle_sums_kernel(near_own, near_other, near_got, far_own, far_got, own, far, near_sent, far_sent):
    y = lax.axis_index("dp") // 2 % 2
    for z in range(2):
        keep, send = 2 * z + y, 2 * z + 1 - y
        own[z] = low_sum(near_own[z], near_got[0, z])
        near_sent[z] = low_sum(near_other[z], near_got[1, z])
        far[z] = low_sum(far_own[keep], far_got[keep])
        far_sent[z] = low_sum(far_own[send], far_got[send])


def core_sums_kernel(kept, got, here, there):
    y = lax.axis_index("dp") // 2 % 2
    for lead in range(kept.shape[0]):
        for z in range(4):
            keep, send = 2 * z + y, 2 * z + 1 - y
            here[lead, z] = low_sum(kept[lead, keep], got[lead, keep])
            there[lead, z] = low_sum(kept[lead, send], got[lead, send])


def core_sums(kept, got):
    leads, rows, columns = kept.shape[0], kept.shape[2], kept.shape[3]
    out = jax.ShapeDtypeStruct((leads, 4, rows, columns), jnp.bfloat16)
    return block_call(core_sums_kernel, [kept, got], [out, out], columns)


def place_kernel(leads, ordered, steps, *refs):
    pieces = refs[: len(steps)]
    outs = refs[len(steps) : len(steps) + leads]
    sems = refs[len(steps) + leads]
    spot = lax.axis_index("dp")
    z, y, core = spot // 4, spot // 2 % 2, spot % 2
    copies = []
    for piece, (first_slot, y_step, core_step) in zip(pieces, steps):
        column = (y + y_step) % 2 * 2 + (core + core_step) % 2
        for slot in range(piece.shape[0]):
            number = first_slot + slot
            row = (number if ordered else (z + 4 - number) % 4) * 4 + column
            for lead in range(leads):
                copy = pltpu.make_async_copy(piece.at[slot, lead], outs[lead].at[row], sems.at[len(copies)])
                copy.start()
                copies.append(copy)
    for copy in copies:
        copy.wait()


def place(planes, ordered):
    pieces = sum(planes, [])
    leads, rows, columns = pieces[0].shape[1:]
    slots = pieces[0].shape[0]
    steps = [(start, step % 2, step // 2) for start in range(0, 4, slots) for step in range(4)]
    size = 16 * leads * rows * padded(columns) * 2
    placed = pl.pallas_call(
        partial(place_kernel, leads, ordered, steps),
        in_specs=[pl.BlockSpec(memory_space=pl.ANY)] * len(pieces),
        out_specs=[pl.BlockSpec(memory_space=pltpu.VMEM)] * leads,
        out_shape=[jax.ShapeDtypeStruct((16, rows, columns), jnp.bfloat16)] * leads,
        scratch_shapes=[pltpu.SemaphoreType.DMA((16 * leads,))],
        compiler_params=pltpu.CompilerParams(vmem_limit_bytes=size * 3 // 2 + (2 << 20)),
        cost_estimate=pl.CostEstimate(flops=0, bytes_accessed=size // 4, transcendentals=0),
    )(*pieces)
    return [part.reshape(16 * rows, columns) for part in placed]


def swap_x(value):
    return lax.ppermute(value, "tensor", [(0, 1), (1, 0)])


def swap_y(value):
    return lax.ppermute(value, "dp", [(spot, spot ^ 2) for spot in range(16)])


def swap_core(value):
    return lax.ppermute(value, "dp", [(spot, spot ^ 1) for spot in range(16)])


def move_z(value, steps):
    return lax.ppermute(value, "dp", [(spot, (spot + 4 * steps) % 16) for spot in range(16)])


def tie(*values):
    return lax.optimization_barrier(values)


def gather_z(shard):
    groups = [[spot + 4 * z for z in range(4)] for spot in range(4)]
    return lax.all_gather(shard, "dp", axis_index_groups=groups)


def both_cores(parts):
    return parts + [swap_core(part) for part in parts]


def add_low(*terms):
    total = terms[0].astype(jnp.float32)
    for term in terms[1:]:
        total = total + term.astype(jnp.float32)
    return total.astype(jnp.bfloat16)


def part_of(value, index, axis):
    return lax.dynamic_index_in_dim(value, index, axis, keepdims=False)


def y_parts(value):
    spot = lax.axis_index("dp")
    split = value.reshape((value.shape[0] // 2, 2) + value.shape[1:])
    return part_of(split, spot // 2 % 2, 1), part_of(split, 1 - spot // 2 % 2, 1)


class Planes:
    def __init__(self, kept, core):
        rows, self.columns = kept[0].shape[1:]
        self.two, self.four = [jax.ShapeDtypeStruct((n, rows, self.columns), jnp.bfloat16) for n in (2, 4)]
        pair = jax.ShapeDtypeStruct((2, 2, rows, self.columns), jnp.bfloat16)
        self.near_own, self.near_other, self.far_own, *self.sent = block_call(
            first_sums_kernel, [*kept, *core], [self.two, self.two, self.four, pair, self.four], self.columns
        )

    def first(self):
        self.got = [swap_y(self.sent[0]), swap_x(self.sent[1])]

    def middle(self):
        self.near_own, self.far_own, *self.sent = block_call(
            middle_sums_kernel,
            [self.near_own, self.near_other, self.got[0], self.far_own, self.got[1]],
            [self.two] * 4,
            self.columns,
        )

    def second(self):
        self.got = [swap_x(self.sent[0]), swap_y(self.sent[1])]

    def total(self):
        return jnp.concatenate([add_low(self.near_own, self.got[0]), add_low(self.far_own, self.got[1])])


def scatter_z(value):
    groups = [[spot + 4 * z for z in range(4)] for spot in range(4)]
    return lax.psum_scatter(value, "dp", axis_index_groups=groups)


def send_z(value):
    z = lax.axis_index("dp") // 4
    return [part_of(value, z, 0)] + [move_z(part_of(value, (z + steps) % 4, 0), steps) for steps in (1, 2, 3)]


def sum_terms(terms):
    total = terms[0].astype(jnp.float32)
    for term in terms[1:]:
        total = total + term.astype(jnp.float32)
    return total


def norm_forward(values):
    centre = values - jnp.mean(values, -1, keepdims=True)
    inverse = lax.rsqrt(jnp.mean(centre * centre, -1, keepdims=True) + norm_eps)
    return centre * inverse, inverse


def norm_back(grad, hat, inverse, gain):
    scaled = grad * gain
    mean_one = jnp.mean(scaled, -1, keepdims=True)
    mean_two = jnp.mean(scaled * hat, -1, keepdims=True)
    return (scaled - mean_one - hat * mean_two) * inverse


def gelu_pair(value):
    inner = math.sqrt(2.0 / math.pi)
    squared = value * value
    bent = jnp.tanh(inner * (value + 0.044715 * value * squared))
    half = 0.5 * (1.0 + bent)
    slope = half + 0.5 * value * (1.0 - bent * bent) * inner * (1.0 + 3 * 0.044715 * squared)
    return value * half, slope


def row_layer(
    block_input,
    image_ids,
    out_cotangent,
    qkv_master,
    qkv_moment,
    qkv_second,
    out_master,
    out_moment,
    out_second,
    up_master,
    up_moment,
    up_second,
    down_master,
    down_moment,
    down_second,
    vec_master,
    vec_moment,
    vec_second,
    bias_master,
    bias_moment,
    bias_second,
):
    low = jnp.bfloat16
    wide = jnp.float32
    mine = lax.axis_index("tensor")
    first = mine == 0
    half = block_input.shape[2]
    features = block_input.shape[3]
    head_cols = qkv_master.shape[2]

    def pick(pair, index):
        return lax.dynamic_index_in_dim(pair, index, 0, keepdims=False)

    def in_order(own, other, axis=0):
        return jnp.concatenate([jnp.where(first, own, other), jnp.where(first, other, own)], axis)

    def dot(spec, left, right):
        return jnp.einsum(spec, left, right, preferred_element_type=wide)

    inputs_own = pick(block_input[:, 0], mine)
    inputs_sent = pick(block_input[:, 0], 1 - mine)
    cot_own = pick(out_cotangent[:, 0], mine)
    cot_sent = pick(out_cotangent[:, 0], 1 - mine)
    inputs_low = inputs_sent.astype(low)
    early_shard = jnp.stack([qkv_master[:, 0], qkv_master[:, 1], qkv_master[:, 2]]).astype(low)
    early_shard, inputs_low = tie(early_shard, inputs_low)
    inputs_got = swap_x(inputs_low)
    early_one = move_z(early_shard, 1)
    early_three = move_z(early_shard, 3)
    early_shard, early_one = tie(early_shard, early_one)
    early_two = move_z(early_shard, 2)
    near = jnp.stack([early_shard, early_one])
    near_y = swap_y(near)
    late_shard = jnp.stack([up_master, down_master.T]).astype(low)
    small = jnp.concatenate([pick(image_ids[:, 0], 1 - mine).astype(wide), bias_master[0]])
    cot_sum = jnp.sum(out_cotangent[:, 0], (0, 1))
    cot_low_sent = cot_sent.astype(low)
    late_shard, cot_sum, cot_low_sent, early_two, early_three, inputs_got, near, near_y = tie(
        late_shard, cot_sum, cot_low_sent, early_two, early_three, inputs_got, near, near_y
    )
    late_z = gather_z(late_shard)
    far = jnp.stack([early_two, early_three])
    far_y, near_x, far_x = swap_y(far), swap_x(near), swap_x(far)
    small, far_y = tie(small, far_y)
    small_got = swap_x(small[None])[0]
    near_xy, far_yx = swap_y(near_x), swap_x(far_y)
    early_own = place([both_cores([near, near_y]), both_cores([far, far_y])], False)
    out_shard, early_own = tie(out_master.T.astype(low), early_own)
    out_whole = lax.all_gather(out_shard, ("tensor", "dp")).reshape(2, features, head_cols)
    inputs = in_order(inputs_own, inputs_got.astype(wide))
    ids = in_order(pick(image_ids[:, 0], mine), small_got[:half].astype(jnp.int32))
    biases = jnp.stack([bias_master[0], small_got[half:]])

    hat_one, inverse_one = norm_forward(inputs)
    normed = (hat_one * vec_master[0] + vec_master[1]).astype(low)
    def project(g, weights):
        query = (dot("td,de->te", normed, weights[0]) + biases[g, :head_cols]).astype(low)
        key = dot("td,de->te", normed, weights[1]).astype(low)
        value = (dot("td,de->te", normed, weights[2]) + biases[g, head_cols : 2 * head_cols]).astype(low)
        return query, key, value

    projected = [project(0, early_own), None]
    projected[0], near_x, far_x = tie(projected[0], near_x, far_x)
    others = [[near_x, swap_core(near_x)], [far_x, swap_core(far_x)]]
    up_near, up_far = [late_z[start : start + 2, :1] for start in (0, 2)]
    attended, log_sums = [None, None], [None, None]
    attended[0], log_sums[0] = attend(ids, *projected[0])
    others, attended[0], near_xy, far_yx = tie(others, attended[0], near_xy, far_yx)
    others[0] = [others[0][0], near_xy, others[0][1], swap_core(near_xy)]
    others[1] = [others[1][0], far_yx, others[1][1], swap_core(far_yx)]
    early_other = place(others, False)
    early_other, up_near, up_far = tie(early_other, up_near, up_far)
    up_near_x, up_far_y = swap_x(up_near), swap_y(up_far)
    down_near, down_far = [late_z[start : start + 2, 1:] for start in (0, 2)]
    projected[1] = project(1, early_other)
    query_weight, key_weight, value_weight = zip(early_own, early_other)
    projected[1], up_near, up_far, up_near_x, up_far_y = tie(projected[1], up_near, up_far, up_near_x, up_far_y)
    up_near_y, up_far_x = swap_y(up_near), swap_x(up_far)
    attended[1], log_sums[1] = attend(ids, *projected[1])
    attended[1], up_near_x, up_far_y, up_near_y, up_far_x = tie(
        attended[1], up_near_x, up_far_y, up_near_y, up_far_x
    )
    up_near_xy, up_far_yx = swap_y(up_near_x), swap_x(up_far_y)
    out_weight = [pick(out_whole, mine), pick(out_whole, 1 - mine)]
    out_weight, up_near_xy, up_far_yx, down_near, down_far = tie(
        out_weight, up_near_xy, up_far_yx, down_near, down_far
    )
    down_near_x, down_far_y = swap_x(down_near), swap_y(down_far)
    cot_got = swap_x(cot_low_sent)
    attn_sum = sum(dot("te,de->td", attended[g], out_weight[g]) for g in range(2)) + vec_master[2]
    middle = inputs + attn_sum
    hat_two, inverse_two = norm_forward(middle)
    normed_two = (hat_two * vec_master[3] + vec_master[4]).astype(low)
    normed_two, down_near, down_far, down_near_x, down_far_y = tie(
        normed_two, down_near, down_far, down_near_x, down_far_y
    )
    down_near_y, down_far_x = swap_y(down_near), swap_x(down_far)
    up_weight = [
        place([both_cores([up_near, up_near_y]), both_cores([up_far, up_far_y])], True)[0],
        place([both_cores([up_near_x, up_near_xy]), both_cores([up_far_x, up_far_yx])], True)[0],
    ]
    active, slope = [None, None], [None, None]
    active[0], slope[0] = hidden_units(normed_two, up_weight[0], biases[0, 2 * head_cols :])
    normed_two, active[0], down_near_x, down_far_y, down_near_y, down_far_x, cot_got = tie(
        normed_two, active[0], down_near_x, down_far_y, down_near_y, down_far_x, cot_got
    )
    down_near_xy, down_far_yx = swap_y(down_near_x), swap_x(down_far_y)
    active[1], slope[1] = hidden_units(normed_two, up_weight[1], biases[1, 2 * head_cols :])
    down_weight = [place([both_cores([down_near, down_near_y]), both_cores([down_far, down_far_y])], True)[0], None]
    active[1], down_weight[0] = tie(active[1], down_weight[0])
    cot_row = in_order(cot_own, cot_got.astype(wide))
    cot_low = cot_row.astype(low)
    down_sent, down_kept = weight_grads(cot_low, active)
    down_sent, down_near_xy, down_far_yx = tie(down_sent, down_near_xy, down_far_yx)
    down_weight[1] = place(
        [both_cores([down_near_x, down_near_xy]), both_cores([down_far_x, down_far_yx])], True
    )[0]
    added = attn_sum + sum(dot("tf,df->td", active[g], down_weight[g]) for g in range(2)) + vec_master[5]
    added = added.reshape(2, half, features)
    added_got = swap_x(pick(added, 1 - mine).astype(low))

    own, other = 0, 1
    down_core = [swap_core(part) for part in down_sent]
    d_hidden, hidden_sums = [None, None], [None, None]
    d_hidden[own], hidden_sums[own] = hidden_back(cot_low, down_weight[own], slope[own])
    d_hidden[own], down_core = tie(d_hidden[own], down_core)
    down = Planes(down_kept, down_core)
    cot_late, down.sent = tie(cot_low, down.sent)
    down.first()
    d_hidden[other], hidden_sums[other] = hidden_back(cot_late, down_weight[other], slope[other])
    up_sent, up_kept = weight_grads(normed_two, d_hidden)
    up_sent, down.got = tie(up_sent, down.got)
    up_core = [swap_core(part) for part in up_sent]
    down.middle()
    d_hidden, down.sent = tie(d_hidden, down.sent)
    down.second()
    d_normed_two = sum(dot("tf,df->td", d_hidden[g], up_weight[g]) for g in range(2))
    d_normed_two, up_core, down.got = tie(d_normed_two, up_core, down.got)
    up = Planes(up_kept, up_core)
    down_total = down.total()
    d_normed_two, up.sent, down_total = tie(d_normed_two, up.sent, down_total)
    up.first()
    down_term = scatter_z(down_total)
    mid_added = norm_back(d_normed_two, hat_two, inverse_two, vec_master[3])
    d_middle = cot_row + mid_added
    mid_low = d_middle.astype(low)
    d_attended = [dot("td,de->te", mid_low, out_weight[g]).astype(low) for g in range(2)]
    out_sent, out_kept = weight_grads(mid_low, attended)
    d_attended[other], out_sent, added_got = tie(d_attended[other], out_sent, added_got)
    out_core = [swap_core(part) for part in out_sent]

    def back(g, grad):
        return attend_back(ids, *projected[g], attended[g], grad, log_sums[g])

    d_other = back(other, d_attended[other])
    d_other, out_core, up.got = tie(d_other, out_core, up.got)
    up.middle()
    out_other = add_low(out_kept[other], out_core[other])
    out_own = add_low(out_kept[own], out_core[own])
    d_other, up.sent, out_other = tie(d_other, up.sent, out_other)
    up.second()
    out_there_x = swap_x(out_other)
    qkv_sent, qkv_kept = [None, None], [None, None]
    qkv_sent[other], qkv_kept[other] = weight_grads(normed, d_other, True)

    def normed_part(parts, g):
        weights = (query_weight, key_weight, value_weight)
        return sum(dot("te,de->td", part, weight[g]) for part, weight in zip(parts, weights))

    d_other, qkv_sent[other] = tie(d_other, qkv_sent[other])
    qkv_core_other = swap_core(qkv_sent[other])
    d_normed_other = normed_part(d_other, other)
    d_normed_other, up.got, qkv_core_other = tie(d_normed_other, up.got, qkv_core_other)
    up_total = up.total()
    qkv_other_here, qkv_other_there = core_sums(qkv_kept[other], qkv_core_other)
    d_attended[own], up_total, qkv_other_there = tie(d_attended[own], up_total, qkv_other_there)
    up_term = scatter_z(up_total)
    qkv_there_y = swap_y(qkv_other_there)
    d_own = back(own, d_attended[own])
    d_own, qkv_there_y, out_there_x = tie(tuple(d_own), qkv_there_y, out_there_x)
    qkv_other = add_low(qkv_other_here, qkv_there_y)
    out_here, out_there = y_parts(add_low(out_own, out_there_x))
    d_own, qkv_other, out_there = tie(d_own, qkv_other, out_there)
    qkv_there_x = swap_x(qkv_other)
    out_there_y = swap_y(out_there)
    qkv_sent[own], qkv_kept[own] = weight_grads(normed, d_own, True)
    d_own, qkv_sent[own], out_there_y = tie(d_own, qkv_sent[own], out_there_y)
    out_terms = send_z(add_low(out_here, out_there_y))
    qkv_core_own = swap_core(qkv_sent[own])
    d_normed_own = normed_part(d_own, own)
    d_normed_own, qkv_core_own, qkv_there_x = tie(d_normed_own, qkv_core_own, qkv_there_x)
    qkv_here, qkv_there = core_sums(qkv_kept[own], qkv_core_own)
    d_normed_own, qkv_there = tie(d_normed_own, qkv_there)
    qkv_there_y = swap_y(qkv_there)
    d_normed = d_normed_other + d_normed_own
    early = jnp.concatenate(
        [
            jnp.sum(d_middle, 0),
            jnp.sum(d_normed_two * hat_two, 0),
            jnp.sum(d_normed_two, 0),
            cot_sum,
        ]
    )

    def bias_rows(sums):
        return jnp.where(first, jnp.concatenate(sums), jnp.concatenate(sums[::-1]))

    sums = jnp.concatenate(
        [
            jnp.sum(d_normed * hat_one, 0),
            jnp.sum(d_normed, 0),
            early,
            bias_rows([jnp.sum(part[0], 0, dtype=wide) for part in (d_own, d_other)]),
            bias_rows([jnp.sum(part[2], 0, dtype=wide) for part in (d_own, d_other)]),
            bias_rows([part[0] for part in hidden_sums]),
        ]
    )
    in_added = (mid_added + norm_back(d_normed, hat_one, inverse_one, vec_master[0])).reshape(2, half, features)
    in_sent = pick(in_added, 1 - mine).astype(low)
    in_got = swap_x(in_sent)
    down_term, up_term, out_terms, added_got, in_sent = tie(down_term, up_term, out_terms, added_got, in_sent)
    block_here = inputs_own + pick(added, mine)
    block_there = pick(block_input[:, 0], 1 - mine) + added_got.astype(wide)
    block_output = in_order(block_here[None], block_there[None])[:, None]

    def update(name, grad):
        master, moment, second, rate, decay = states[name]
        second_new, master_new = adam_update(master, moment, second, grad, rate, decay)
        return grad, second_new, master_new

    states = {
        "qkv": (qkv_master, qkv_moment, qkv_second, 0.09, 0.1),
        "out": (out_master, out_moment, out_second, 0.4, 0.1),
        "up": (up_master, up_moment, up_second, 0.09, 0.1),
        "down": (down_master, down_moment, down_second, 0.045, 0.1),
        "vec": (vec_master, vec_moment, vec_second, 0.6, 0.0),
        "bias": (bias_master, bias_moment, bias_second, 0.5, 0.0),
    }
    up_new = update("up", up_term.astype(wide))
    down_new = update("down", down_term.astype(wide).T)
    out_new = update("out", sum_terms(out_terms).T)
    sums, qkv_there_y, block_output, up_new, down_new, out_new = tie(
        sums, qkv_there_y, block_output, up_new, down_new, out_new
    )
    qkv_terms = send_z(add_low(qkv_here, qkv_there_y, qkv_there_x).transpose(1, 0, 2, 3))
    sums = sums[None]
    sums = sums + move_z(sums, 1) + move_z(sums, 2) + move_z(sums, 3)
    sums, in_got = tie(sums, in_got)
    sums = sums + swap_core(sums)
    sums = sums + swap_y(sums)
    sums = (sums + swap_x(sums))[0]
    qkv_grad = sum_terms(qkv_terms).transpose(1, 0, 2)
    qkv_new = update("qkv", qkv_grad)
    grad_here = cot_own + pick(in_added, mine)
    grad_there = cot_sent + in_got.astype(wide)
    input_grad = in_order(grad_here[None], grad_there[None])[:, None]
    vec_grad = sums[: 6 * features].reshape(6, features)

    def group(start, size):
        return pick(sums[start : start + 2 * size].reshape(2, size), mine)

    start = 6 * features
    bias_grad = jnp.concatenate(
        [
            group(start, head_cols),
            group(start + 2 * head_cols, head_cols),
            group(start + 4 * head_cols, up_master.shape[1]),
        ]
    )[None]

    vec_new = update("vec", vec_grad)
    bias_new = update("bias", bias_grad)
    return (block_output, input_grad, *qkv_new, *out_new, *up_new, *down_new, *vec_new, *bias_new)


def solution(mesh):
    placed = (
        P(None, "dp", "tensor", None),
        P(None, "dp", "tensor"),
        P(None, "dp", "tensor", None),
        P("dp", None, "tensor"),
        P("dp", None, "tensor"),
        P("dp", None, "tensor"),
        P("tensor", "dp"),
        P("tensor", "dp"),
        P("tensor", "dp"),
        P("dp", "tensor"),
        P("dp", "tensor"),
        P("dp", "tensor"),
        P("tensor", "dp"),
        P("tensor", "dp"),
        P("tensor", "dp"),
        P(),
        P(),
        P(),
        P("tensor", None),
        P("tensor", None),
        P("tensor", None),
    )
    by_rows = dict(mesh.shape) == {"dp": 16, "tensor": 2}
    return jax.shard_map(
        row_layer if by_rows else split_layer,
        mesh=mesh,
        in_specs=placed,
        out_specs=(
            P(None, "dp", "tensor", None),
            P(None, "dp", "tensor", None),
            P("dp", None, "tensor"),
            P("dp", None, "tensor"),
            P("dp", None, "tensor"),
            P("tensor", "dp"),
            P("tensor", "dp"),
            P("tensor", "dp"),
            P("dp", "tensor"),
            P("dp", "tensor"),
            P("dp", "tensor"),
            P("tensor", "dp"),
            P("tensor", "dp"),
            P("tensor", "dp"),
            P(),
            P(),
            P(),
            P("tensor", None),
            P("tensor", None),
            P("tensor", None),
        ),
        check_vma=False,
    )
```

```python
import math
from functools import partial

import jax
import jax.numpy as jnp
from jax import lax
from jax.experimental import pallas as pl
from jax.experimental.pallas import tpu as pltpu
from jax.sharding import PartitionSpec as P

HEAD = 72
STEP = 10


norm_eps = 1e-06
mask_fill = -1e30
beta_one = 0.9
beta_two = 0.95
adam_eps = 1e-08


def layer_norm(values, scale_vec, shift_vec):
    centre = values - jnp.mean(values, -1, keepdims=True)
    spread = jnp.mean(centre * centre, -1, keepdims=True)
    return centre * lax.rsqrt(spread + norm_eps) * scale_vec + shift_vec


def adam_update(master, moment, second, gradient, step_rate, weight_decay):
    first_moment = beta_one * moment.astype(jnp.float32) + (1.0 - beta_one) * gradient
    second_new = beta_two * second + (1.0 - beta_two) * gradient * gradient
    update = (
        first_moment
        / (1.0 - beta_one**STEP)
        / (jnp.sqrt(second_new / (1.0 - beta_two**STEP)) + adam_eps)
        + weight_decay * master
    )
    return (second_new, master - step_rate * update)


def split_layer(
    block_input,
    image_ids,
    out_cotangent,
    qkv_master,
    qkv_moment,
    qkv_second,
    out_master,
    out_moment,
    out_second,
    up_master,
    up_moment,
    up_second,
    down_master,
    down_moment,
    down_second,
    vec_master,
    vec_moment,
    vec_second,
    bias_master,
    bias_moment,
    bias_second,
):
    batches = block_input.shape[0]
    local_rows = block_input.shape[2]
    features = block_input.shape[3]
    splits = lax.axis_size("tensor")
    length = local_rows * splits
    head_cols = qkv_master.shape[2]
    local_heads = head_cols // HEAD
    block_rows = min(512, length)
    block_count = length // block_rows
    score_scale = HEAD ** (-0.5)
    biases = bias_master[0]
    query_bias = biases[:head_cols]
    value_bias = biases[head_cols : 2 * head_cols]
    hidden_bias = biases[2 * head_cols :]
    compute = (
        qkv_master.astype(jnp.bfloat16),
        out_master.astype(jnp.bfloat16),
        up_master.astype(jnp.bfloat16),
        down_master.astype(jnp.bfloat16),
    )
    gelu_tanh = partial(jax.nn.gelu, approximate=True)
    weight_sums = (
        jnp.zeros_like(qkv_master),
        jnp.zeros_like(out_master),
        jnp.zeros_like(up_master),
        jnp.zeros_like(down_master),
    )
    vector_terms = jnp.zeros((6, features), jnp.float32)
    bias_terms = jnp.zeros(biases.shape, jnp.float32)
    block_outputs = []
    input_grads = []
    for batch_index in range(batches):
        qkv_weight, out_weight, up_weight, down_weight = (
            lax.all_gather(compute[0], "dp", axis=0, tiled=True),
            lax.all_gather(compute[1], "dp", axis=1, tiled=True),
            lax.all_gather(compute[2], "dp", axis=0, tiled=True),
            lax.all_gather(compute[3], "dp", axis=1, tiled=True),
        )
        tokens_here = block_input[batch_index, 0]
        normed, norm_pull = jax.vjp(layer_norm, tokens_here, vec_master[0], vec_master[1])
        gathered, image_row = (
            lax.all_gather(normed.astype(jnp.bfloat16), "tensor", axis=0, tiled=True),
            lax.all_gather(image_ids[batch_index, 0], "tensor", axis=0, tiled=True),
        )
        projected = jnp.einsum(
            "td,dce->cte", gathered, qkv_weight, preferred_element_type=jnp.float32
        )
        queries = (projected[0] + query_bias).astype(jnp.bfloat16)
        key_rows = projected[1].astype(jnp.bfloat16)
        values = (projected[2] + value_bias).astype(jnp.bfloat16)
        key_heads = key_rows.reshape(length, local_heads, HEAD)
        value_heads = values.reshape(length, local_heads, HEAD)
        query_blocks = queries.reshape(block_count, block_rows, local_heads, HEAD)
        image_blocks = image_row.reshape(block_count, block_rows)

        def attend(block_pair):
            query_block, image_block = block_pair
            scores = (
                jnp.einsum(
                    "qhe,khe->hqk", query_block, key_heads, preferred_element_type=jnp.float32
                )
                * score_scale
            )
            same_image = image_block[:, None] == image_row[None, :]
            scores = jnp.where(same_image[None], scores, mask_fill)
            row_max = jnp.max(scores, -1, keepdims=True)
            exp_scores = jnp.exp(scores - row_max)
            exp_total = jnp.sum(exp_scores, -1, keepdims=True)
            attn_probs = exp_scores / exp_total
            result = jnp.einsum(
                "hqk,khe->qhe",
                attn_probs.astype(jnp.bfloat16),
                value_heads,
                preferred_element_type=jnp.float32,
            )
            return (result.reshape(block_rows, head_cols), (row_max + jnp.log(exp_total))[..., 0])

        attended_blocks, log_sums = lax.map(attend, (query_blocks, image_blocks))
        attended = attended_blocks.reshape(length, head_cols).astype(jnp.bfloat16)
        attn_sum = lax.psum_scatter(
            jnp.dot(attended, out_weight, preferred_element_type=jnp.float32).astype(jnp.bfloat16),
            "tensor",
            scatter_dimension=0,
            tiled=True,
        ).astype(jnp.float32)
        middle = tokens_here + attn_sum + vec_master[2]
        normed_two, norm_pull_two = jax.vjp(layer_norm, middle, vec_master[3], vec_master[4])
        gathered_two = lax.all_gather(normed_two.astype(jnp.bfloat16), "tensor", axis=0, tiled=True)
        hidden = jnp.dot(gathered_two, up_weight, preferred_element_type=jnp.float32) + hidden_bias
        active, gelu_pull = jax.vjp(gelu_tanh, hidden)
        active_low = active.astype(jnp.bfloat16)
        project_row_piece = lax.slice_in_dim(
            active_low, 0, local_rows * lax.axis_size("tensor"), axis=0
        )
        mlp_sum = lax.psum_scatter(
            jnp.dot(project_row_piece, down_weight, preferred_element_type=jnp.float32).astype(
                jnp.bfloat16
            ),
            "tensor",
            scatter_dimension=0,
            tiled=True,
        ).astype(jnp.float32)
        block_outputs.append(middle + mlp_sum + vec_master[5])
        qkv_weight, out_weight, up_weight, down_weight = (
            lax.all_gather(compute[0], "dp", axis=0, tiled=True),
            lax.all_gather(compute[1], "dp", axis=1, tiled=True),
            lax.all_gather(compute[2], "dp", axis=0, tiled=True),
            lax.all_gather(compute[3], "dp", axis=1, tiled=True),
        )
        cotangent = out_cotangent[batch_index, 0]
        cot_full = lax.all_gather(cotangent.astype(jnp.bfloat16), "tensor", axis=0, tiled=True)
        down_term = jnp.dot(active_low.T, cot_full, preferred_element_type=jnp.float32)
        d_active = jnp.dot(cot_full, down_weight.T, preferred_element_type=jnp.float32)
        d_hidden = gelu_pull(d_active)[0].astype(jnp.bfloat16)
        up_term = jnp.dot(gathered_two.T, d_hidden, preferred_element_type=jnp.float32)
        d_normed_two = lax.psum_scatter(
            jnp.dot(d_hidden, up_weight.T, preferred_element_type=jnp.float32).astype(jnp.bfloat16),
            "tensor",
            scatter_dimension=0,
            tiled=True,
        ).astype(jnp.float32)
        d_middle, gain_two_grad, shift_two_grad = norm_pull_two(d_normed_two)
        d_middle = d_middle + cotangent
        mid_full = lax.all_gather(d_middle.astype(jnp.bfloat16), "tensor", axis=0, tiled=True)
        out_term = jnp.dot(attended.T, mid_full, preferred_element_type=jnp.float32)
        d_attended = jnp.dot(mid_full, out_weight.T, preferred_element_type=jnp.float32).astype(
            jnp.bfloat16
        )
        d_blocks = d_attended.reshape(block_count, block_rows, local_heads, HEAD)

        def attend_back(running, block_item):
            d_keys, d_values = running
            query_block, image_block, block_sums, d_block = block_item
            scores = (
                jnp.einsum(
                    "qhe,khe->hqk", query_block, key_heads, preferred_element_type=jnp.float32
                )
                * score_scale
            )
            same_image = image_block[:, None] == image_row[None, :]
            scores = jnp.where(same_image[None], scores, mask_fill)
            attn_probs = jnp.exp(scores - block_sums[:, :, None])
            d_probs = jnp.einsum(
                "qhe,khe->hqk", d_block, value_heads, preferred_element_type=jnp.float32
            )
            row_delta = jnp.sum(attn_probs * d_probs, -1, keepdims=True)
            d_scores = (attn_probs * (d_probs - row_delta)).astype(jnp.bfloat16)
            d_query = (
                jnp.einsum("hqk,khe->qhe", d_scores, key_heads, preferred_element_type=jnp.float32)
                * score_scale
            )
            d_keys = (
                d_keys
                + jnp.einsum(
                    "hqk,qhe->khe", d_scores, query_block, preferred_element_type=jnp.float32
                )
                * score_scale
            )
            d_values = d_values + jnp.einsum(
                "hqk,qhe->khe",
                attn_probs.astype(jnp.bfloat16),
                d_block,
                preferred_element_type=jnp.float32,
            )
            return ((d_keys, d_values), d_query)

        zero_heads = jnp.zeros((length, local_heads, HEAD), jnp.float32)
        (d_keys, d_values), d_queries = lax.scan(
            attend_back, (zero_heads, zero_heads), (query_blocks, image_blocks, log_sums, d_blocks)
        )
        d_query_low = d_queries.reshape(length, head_cols).astype(jnp.bfloat16)
        d_key_low = d_keys.reshape(length, head_cols).astype(jnp.bfloat16)
        d_value_low = d_values.reshape(length, head_cols).astype(jnp.bfloat16)
        d_projected = jnp.stack([d_query_low, d_key_low, d_value_low])
        qkv_term = jnp.einsum(
            "td,cte->dce", gathered, d_projected, preferred_element_type=jnp.float32
        )
        d_normed = lax.psum_scatter(
            jnp.einsum(
                "cte,dce->td", d_projected, qkv_weight, preferred_element_type=jnp.float32
            ).astype(jnp.bfloat16),
            "tensor",
            scatter_dimension=0,
            tiled=True,
        ).astype(jnp.float32)
        d_tokens, gain_one_grad, shift_one_grad = norm_pull(d_normed)
        input_grads.append(d_tokens + d_middle)
        vector_terms = vector_terms + jnp.stack(
            [
                gain_one_grad,
                shift_one_grad,
                jnp.sum(d_middle, 0),
                gain_two_grad,
                shift_two_grad,
                jnp.sum(cotangent, 0),
            ]
        )
        bias_terms = bias_terms + jnp.concatenate(
            [
                jnp.sum(d_query_low, 0, dtype=jnp.float32),
                jnp.sum(d_value_low, 0, dtype=jnp.float32),
                jnp.sum(d_hidden, 0, dtype=jnp.float32),
            ]
        )
        local_terms = (qkv_term, out_term, up_term, down_term)
        owned = (
            lax.psum_scatter(
                local_terms[0].astype(jnp.bfloat16), "dp", scatter_dimension=0, tiled=True
            ).astype(jnp.float32),
            lax.psum_scatter(
                local_terms[1].astype(jnp.bfloat16), "dp", scatter_dimension=1, tiled=True
            ).astype(jnp.float32),
            lax.psum_scatter(
                local_terms[2].astype(jnp.bfloat16), "dp", scatter_dimension=0, tiled=True
            ).astype(jnp.float32),
            lax.psum_scatter(
                local_terms[3].astype(jnp.bfloat16), "dp", scatter_dimension=1, tiled=True
            ).astype(jnp.float32),
        )
        weight_sums = tuple((total + term for total, term in zip(weight_sums, owned)))
    qkv_grad, out_grad, up_grad, down_grad = weight_sums
    tensor_index = lax.axis_index("tensor")
    placed = jnp.where(jnp.arange(splits)[:, None] == tensor_index, bias_terms[None, :], 0.0)
    vec_grad, bias_table = lax.psum((vector_terms, placed), ("dp", "tensor"))
    bias_grad = lax.dynamic_slice_in_dim(bias_table, tensor_index, 1, 0)
    qkv_second_new, qkv_master_new = adam_update(
        qkv_master, qkv_moment, qkv_second, qkv_grad, 0.09, 0.1
    )
    out_second_new, out_master_new = adam_update(
        out_master, out_moment, out_second, out_grad, 0.4, 0.1
    )
    up_second_new, up_master_new = adam_update(up_master, up_moment, up_second, up_grad, 0.09, 0.1)
    down_second_new, down_master_new = adam_update(
        down_master, down_moment, down_second, down_grad, 0.045, 0.1
    )
    vec_second_new, vec_master_new = adam_update(
        vec_master, vec_moment, vec_second, vec_grad, 0.6, 0.0
    )
    bias_second_new, bias_master_new = adam_update(
        bias_master, bias_moment, bias_second, bias_grad, 0.5, 0.0
    )
    block_output = jnp.stack(block_outputs)[:, None]
    input_grad = jnp.stack(input_grads)[:, None]
    return (
        block_output,
        input_grad,
        qkv_grad,
        qkv_second_new,
        qkv_master_new,
        out_grad,
        out_second_new,
        out_master_new,
        up_grad,
        up_second_new,
        up_master_new,
        down_grad,
        down_second_new,
        down_master_new,
        vec_grad,
        vec_second_new,
        vec_master_new,
        bias_grad,
        bias_second_new,
        bias_master_new,
    )


LANES = 128
TILE = 128
SPAN = 256
WIDE = 1152
BATCH = 8


def lane_window(head):
    first = head * HEAD
    low = first // LANES * LANES
    high = -(-(first + HEAD) // LANES) * LANES
    return low, high


def head_mask(head, rows):
    low, high = lane_window(head)
    lane = lax.broadcasted_iota(jnp.int32, (rows, high - low), 1) + low
    return (lane >= head * HEAD) & (lane < head * HEAD + HEAD)


def head_columns(head, columns):
    low, high = lane_window(head)
    high = min(high, columns)
    return slice(low, high), head_mask(head, TILE)[:, : high - low]


def padded(columns):
    return -(-columns // LANES) * LANES


def tile_spans(ids_smem, ids_ref, index, tiles):
    first_id = ids_smem[index * TILE]
    last_id = ids_smem[index * TILE + TILE - 1]
    ids = ids_ref[...]
    begin = jnp.sum((ids < first_id).astype(jnp.int32)) // TILE
    end = (jnp.sum((ids <= last_id).astype(jnp.int32)) + TILE - 1) // TILE
    count = (end - begin + 1) // 2
    return jnp.minimum(begin, tiles - 2 * count), count


def ids_column(ids_ref, index):
    row = ids_ref[:, pl.ds(pl.multiple_of(index * TILE, TILE), TILE)].astype(jnp.float32)
    square = jnp.broadcast_to(row, (TILE, TILE)).T
    return jnp.concatenate([square] * (SPAN // TILE), axis=1).astype(jnp.int32)


NT = (((1,), (1,)), ((), ()))
TN = (((0,), (0,)), ((), ()))


def attend_kernel(heads, length, ids_smem, ids_ref, q_ref, k_ref, v_ref, o_ref, lse_ref, top, total, acc):
    index = pl.program_id(0)
    columns = heads * HEAD
    scale = HEAD ** (-0.5) * math.log2(math.e)
    begin, count = tile_spans(ids_smem, ids_ref, index, length // TILE)
    own_ids = ids_column(ids_ref, index)
    top[...] = jnp.full(top.shape, mask_fill, jnp.float32)
    total[...] = jnp.zeros(total.shape, jnp.float32)
    acc[...] = jnp.zeros(acc.shape, jnp.float32)

    def window(low, high):
        return slice(low, min(high, columns))

    def step(item, carry):
        place = pl.multiple_of((begin + 2 * item) * TILE, TILE)
        keys = pl.ds(place, SPAN)
        same = own_ids == ids_ref[:, keys]
        for first in range(0, heads, BATCH):
            batch = range(first, min(first + BATCH, heads))
            held_scores = []
            for head in batch:
                cols, mask = head_columns(head, columns)
                query = q_ref[:, cols]
                query = jnp.where(mask, query, jnp.zeros_like(query))
                scores = lax.dot_general(query, k_ref[keys, cols], NT, preferred_element_type=jnp.float32)
                held_scores.append(jnp.where(same, scores * scale, mask_fill))
            tops = [jnp.maximum(top[head], jnp.max(scores, -1, keepdims=True)) for head, scores in zip(batch, held_scores)]
            parts = [
                jnp.exp2(scores - jnp.concatenate([now] * (SPAN // LANES), axis=1)) for now, scores in zip(tops, held_scores)
            ]
            sums = [jnp.sum(part, -1, keepdims=True) for part in parts]
            mixes = [
                jnp.dot(part.astype(jnp.bfloat16), v_ref[keys, head_columns(head, columns)[0]], preferred_element_type=jnp.float32)
                for head, part in zip(batch, parts)
            ]
            for head, now, part_sum, mixed in zip(batch, tops, sums, mixes):
                cols, mask = head_columns(head, columns)
                shrink = jnp.exp2(top[head] - now)
                total[head] = total[head] * shrink + part_sum
                top[head] = now
                width = cols.stop - cols.start
                wide = jnp.concatenate([shrink] * ((width + LANES - 1) // LANES), axis=1)[:, :width]
                held = acc[:, cols]
                acc[:, cols] = jnp.where(mask, held * wide + mixed, held)
        return carry

    lax.fori_loop(0, count, step, 0)
    sums = jnp.zeros((TILE, LANES), jnp.float32)
    lane = lax.broadcasted_iota(jnp.int32, (TILE, LANES), 1)
    for head in range(heads):
        low, high = lane_window(head)
        high = min(high, columns)
        cols = slice(low, high)
        mask = head_mask(head, TILE)[:, : high - low]
        inverse = 1.0 / total[head]
        wide = jnp.concatenate([inverse] * ((high - low + LANES - 1) // LANES), axis=1)[:, : high - low]
        held = acc[:, cols]
        acc[:, cols] = jnp.where(mask, held * wide, held)
        sums = jnp.where(lane == head, top[head] + jnp.log2(total[head]), sums)
    o_ref[...] = acc[...].astype(o_ref.dtype)
    lse_ref[...] = sums.T[:heads]


def attend(ids, query, key, value):
    length, columns = query.shape
    heads = columns // HEAD
    tiles = length // TILE
    whole = pl.BlockSpec((length, columns), lambda i, s: (0, 0))
    block = pl.BlockSpec((TILE, columns), lambda i, s: (i, 0))
    return pl.pallas_call(
        partial(attend_kernel, heads, length),
        grid_spec=pltpu.PrefetchScalarGridSpec(
            num_scalar_prefetch=1,
            grid=(tiles,),
            in_specs=[pl.BlockSpec((1, length), lambda i, s: (0, 0)), block, whole, whole],
            out_specs=[block, pl.BlockSpec((heads, TILE), lambda i, s: (0, i))],
            scratch_shapes=[
                pltpu.VMEM((heads, TILE, LANES), jnp.float32),
                pltpu.VMEM((heads, TILE, LANES), jnp.float32),
                pltpu.VMEM((TILE, columns), jnp.float32),
            ],
        ),
        out_shape=[
            jax.ShapeDtypeStruct((length, columns), jnp.bfloat16),
            jax.ShapeDtypeStruct((heads, length), jnp.float32),
        ],
        compiler_params=pltpu.CompilerParams(vmem_limit_bytes=36 << 20),
        cost_estimate=pl.CostEstimate(flops=4 * 10**9, bytes_accessed=10**6, transcendentals=0),
    )(ids, ids.reshape(1, length), query, key, value)


def attend_back_kernel(
    heads, length, ids_smem, ids_ref, q_ref, k_ref, v_ref, o_ref, g_ref, lse_ref,
    dq_ref, dk_ref, dv_ref, delta, dq_acc, dk_acc, dv_acc,
):
    index = pl.program_id(0)
    columns = heads * HEAD
    natural = HEAD ** (-0.5)
    scale = natural * math.log2(math.e)
    tiles = length // TILE
    begin, count = tile_spans(ids_smem, ids_ref, index, tiles)
    own_ids = ids_column(ids_ref, index)

    @pl.when(index == 0)
    def _():
        dq_acc[...] = jnp.zeros(dq_acc.shape, jnp.float32)
        row = lax.broadcasted_iota(jnp.int32, (heads, columns), 0)
        lane = lax.broadcasted_iota(jnp.int32, (heads, columns), 1)
        pick = ((lane >= row * HEAD) & (lane < row * HEAD + HEAD)).astype(jnp.bfloat16)
        product = g_ref[...].astype(jnp.float32) * o_ref[...].astype(jnp.float32)
        coarse = product.astype(jnp.bfloat16)
        fine = (product - coarse.astype(jnp.float32)).astype(jnp.bfloat16)
        delta[...] = lax.dot_general(pick, coarse, NT, preferred_element_type=jnp.float32) + lax.dot_general(
            pick, fine, NT, preferred_element_type=jnp.float32
        )

    dk_acc[...] = jnp.zeros(dk_acc.shape, jnp.float32)
    dv_acc[...] = jnp.zeros(dv_acc.shape, jnp.float32)

    def step(item, carry):
        place = pl.multiple_of((begin + 2 * item) * TILE, TILE)
        rows = pl.ds(place, SPAN)
        same = own_ids == ids_ref[:, rows]
        for first in range(0, heads, BATCH):
            batch = range(first, min(first + BATCH, heads))
            keys, scores, d_probs = [], [], []
            for head in batch:
                cols, mask = head_columns(head, columns)
                key = k_ref[:, cols]
                keys.append(jnp.where(mask, key, jnp.zeros_like(key)))
                value = v_ref[:, cols]
                value = jnp.where(mask, value, jnp.zeros_like(value))
                scores.append(lax.dot_general(keys[-1], q_ref[rows, cols], NT, preferred_element_type=jnp.float32))
                d_probs.append(lax.dot_general(value, g_ref[rows, cols], NT, preferred_element_type=jnp.float32))
            probs = [
                jnp.exp2(jnp.where(same, score * scale, mask_fill) - lse_ref[head : head + 1, rows])
                for head, score in zip(batch, scores)
            ]
            d_scores = [
                (prob * (d_prob - delta[head : head + 1, rows])).astype(jnp.bfloat16)
                for head, prob, d_prob in zip(batch, probs, d_probs)
            ]
            for head, key, prob, d_score in zip(batch, keys, probs, d_scores):
                cols, mask = head_columns(head, columns)
                d_value = jnp.dot(prob.astype(jnp.bfloat16), g_ref[rows, cols], preferred_element_type=jnp.float32)
                d_key = jnp.dot(d_score, q_ref[rows, cols], preferred_element_type=jnp.float32)
                d_query = lax.dot_general(d_score, key, TN, preferred_element_type=jnp.float32)
                dv_acc[:, cols] += jnp.where(mask, d_value, 0.0)
                dk_acc[:, cols] += jnp.where(mask, d_key, 0.0)
                dq_acc[rows, cols] += d_query
        return carry

    lax.fori_loop(0, count, step, 0)
    dk_ref[...] = (dk_acc[...] * natural).astype(dk_ref.dtype)
    dv_ref[...] = dv_acc[...].astype(dv_ref.dtype)

    @pl.when(index == tiles - 1)
    def _():
        dq_ref[...] = (dq_acc[...] * natural).astype(dq_ref.dtype)


def attend_back(ids, query, key, value, attended, grad, lse):
    length, columns = query.shape
    heads = columns // HEAD
    tiles = length // TILE
    whole = pl.BlockSpec((length, columns), lambda i, s: (0, 0))
    block = pl.BlockSpec((TILE, columns), lambda i, s: (i, 0))
    out = jax.ShapeDtypeStruct((length, columns), jnp.bfloat16)
    return pl.pallas_call(
        partial(attend_back_kernel, heads, length),
        grid_spec=pltpu.PrefetchScalarGridSpec(
            num_scalar_prefetch=1,
            grid=(tiles,),
            in_specs=[
                pl.BlockSpec((1, length), lambda i, s: (0, 0)),
                whole,
                block,
                block,
                whole,
                whole,
                pl.BlockSpec((heads, length), lambda i, s: (0, 0)),
            ],
            out_specs=[whole, block, block],
            scratch_shapes=[
                pltpu.VMEM((heads, length), jnp.float32),
                pltpu.VMEM((length, columns), jnp.float32),
                pltpu.VMEM((TILE, columns), jnp.float32),
                pltpu.VMEM((TILE, columns), jnp.float32),
            ],
        ),
        out_shape=[out, out, out],
        compiler_params=pltpu.CompilerParams(vmem_limit_bytes=36 << 20),
        cost_estimate=pl.CostEstimate(flops=2 * 10**9, bytes_accessed=10**6, transcendentals=0),
    )(ids, ids.reshape(1, length), query, key, value, attended, grad, lse)


def column_call(kernel, ins, outs, columns, flops, scratch=()):
    wide = min(WIDE, padded(columns))
    steps = -(-columns // wide)

    def spec(shape, cut):
        if cut:
            return pl.BlockSpec(shape[:-1] + (wide,), lambda i: (0,) * (len(shape) - 1) + (i,))
        return pl.BlockSpec(shape, lambda i: (0,) * len(shape))

    size = sum(math.prod(a.shape) * a.dtype.itemsize for a, _ in ins) + sum(
        math.prod(a.shape) * a.dtype.itemsize for a in outs
    )
    return pl.pallas_call(
        kernel,
        grid=(steps,),
        in_specs=[spec(a.shape, cut) for a, cut in ins],
        out_specs=[spec(a.shape, True) for a in outs],
        out_shape=outs,
        scratch_shapes=list(scratch),
        compiler_params=pltpu.CompilerParams(vmem_limit_bytes=44 << 20),
        cost_estimate=pl.CostEstimate(flops=flops // 8, bytes_accessed=size // 8, transcendentals=0),
    )(*[a for a, _ in ins])


def hidden_kernel(x_ref, w_ref, b_ref, active_ref, slope_ref):
    rows = 256
    for block in range(x_ref.shape[0] // rows):
        part = pl.ds(block * rows, rows)
        value = jnp.dot(x_ref[part, :], w_ref[...], preferred_element_type=jnp.float32) + b_ref[...]
        active, slope = gelu_pair(value)
        active_ref[part, :] = active.astype(jnp.bfloat16)
        slope_ref[part, :] = slope.astype(jnp.bfloat16)


def hidden_units(x, weight, bias):
    tokens, columns = x.shape[0], weight.shape[1]
    out = jax.ShapeDtypeStruct((tokens, columns), jnp.bfloat16)
    ins = [(x, False), (weight, True), (bias.reshape(1, columns), True)]
    return column_call(hidden_kernel, ins, [out, out], columns, 2 * tokens * x.shape[1] * columns)


def hidden_back_kernel(x_ref, w_ref, slope_ref, grad_ref, sum_ref):
    rows = 256
    total = jnp.zeros(sum_ref.shape, jnp.float32)
    for block in range(x_ref.shape[0] // rows):
        part = pl.ds(block * rows, rows)
        value = jnp.dot(x_ref[part, :], w_ref[...], preferred_element_type=jnp.float32)
        value = value * slope_ref[part, :].astype(jnp.float32)
        grad_ref[part, :] = value.astype(jnp.bfloat16)
        total = total + jnp.sum(value, 0, keepdims=True)
    sum_ref[...] = total


def hidden_back(x, weight, slope):
    tokens, columns = x.shape[0], weight.shape[1]
    outs = [jax.ShapeDtypeStruct((tokens, columns), jnp.bfloat16), jax.ShapeDtypeStruct((1, columns), jnp.float32)]
    ins = [(x, False), (weight, True), (slope, True)]
    return column_call(hidden_back_kernel, ins, outs, columns, 2 * tokens * x.shape[1] * columns)


def grad_kernel(chunks, stacked, x_ref, *refs):
    core = lax.axis_index("dp") % 2
    count = len(refs) - 4 if stacked else (len(refs) - 2) // 3
    turned, result = refs[-2:]
    dy_refs = refs[:count]
    outs = refs[count:-2]

    @pl.when(pl.program_id(0) == 0)
    def _():
        turned[...] = x_ref[...].T

    rows = turned.shape[0] // chunks
    for number, dy_ref in enumerate(dy_refs):
        if stacked:
            sent_ref, kept_ref = outs[0].at[number], outs[1].at[number]
        else:
            sent_ref, kept_ref = outs[number], outs[count + number]
        result[...] = jnp.dot(turned[...], dy_ref[...], preferred_element_type=jnp.float32)
        for spot in range(chunks // 2):
            sent = pl.multiple_of((2 * spot + 1 - core) * rows, 8)
            kept = pl.multiple_of((2 * spot + core) * rows, 8)
            sent_ref[spot] = result[pl.ds(sent, rows), :].astype(jnp.bfloat16)
            kept_ref[spot] = result[pl.ds(kept, rows), :].astype(jnp.bfloat16)


def weight_grads(x, parts, stacked=False):
    tokens, features = x.shape
    columns = parts[0].shape[1]
    count = len(parts)
    wide = min(WIDE, padded(columns))
    shape = (8, features // 16, columns)
    outs = [jax.ShapeDtypeStruct(shape, jnp.bfloat16)] * (2 * count)
    if stacked:
        outs = [jax.ShapeDtypeStruct((count,) + shape, jnp.bfloat16)] * 2
    results = column_call(
        partial(grad_kernel, 16, stacked),
        [(x, False)] + [(part, True) for part in parts],
        outs,
        columns,
        2 * tokens * features * columns * count,
        [pltpu.VMEM((features, tokens), jnp.bfloat16), pltpu.VMEM((features, wide), jnp.float32)],
    )
    return results if stacked else (results[:count], results[count:])


def block_call(kernel, ins, outs, columns):
    wide = min(768, padded(columns))

    def spec(shape):
        return pl.BlockSpec(shape[:-1] + (wide,), lambda i: (0,) * (len(shape) - 1) + (i,))

    size = sum(math.prod(a.shape) * 2 for a in list(ins) + list(outs))
    return pl.pallas_call(
        kernel,
        grid=(-(-columns // wide),),
        in_specs=[spec(a.shape) for a in ins],
        out_specs=[spec(a.shape) for a in outs],
        out_shape=outs,
        compiler_params=pltpu.CompilerParams(vmem_limit_bytes=58 << 20),
        cost_estimate=pl.CostEstimate(flops=0, bytes_accessed=size // 4, transcendentals=0),
    )(*ins)


def low_sum(*refs):
    total = refs[0].astype(jnp.float32)
    for ref in refs[1:]:
        total = total + ref.astype(jnp.float32)
    return total.astype(jnp.bfloat16)


def first_sums_kernel(kept_own, kept_other, core_own, core_other, near_own, near_other, far_own, near_sent, far_sent):
    y = lax.axis_index("dp") // 2 % 2
    for z in range(2):
        keep, send = 2 * z + y, 2 * z + 1 - y
        near_own[z] = low_sum(kept_own[keep], core_own[keep])
        near_other[z] = low_sum(kept_other[keep], core_other[keep])
        near_sent[0, z] = low_sum(kept_own[send], core_own[send])
        near_sent[1, z] = low_sum(kept_other[send], core_other[send])
    for spot in range(4):
        far_own[spot] = low_sum(kept_own[4 + spot], core_own[4 + spot])
        far_sent[spot] = low_sum(kept_other[4 + spot], core_other[4 + spot])


def middle_sums_kernel(near_own, near_other, near_got, far_own, far_got, own, far, near_sent, far_sent):
    y = lax.axis_index("dp") // 2 % 2
    for z in range(2):
        keep, send = 2 * z + y, 2 * z + 1 - y
        own[z] = low_sum(near_own[z], near_got[0, z])
        near_sent[z] = low_sum(near_other[z], near_got[1, z])
        far[z] = low_sum(far_own[keep], far_got[keep])
        far_sent[z] = low_sum(far_own[send], far_got[send])


def core_sums_kernel(kept, got, here, there):
    y = lax.axis_index("dp") // 2 % 2
    for lead in range(kept.shape[0]):
        for z in range(4):
            keep, send = 2 * z + y, 2 * z + 1 - y
            here[lead, z] = low_sum(kept[lead, keep], got[lead, keep])
            there[lead, z] = low_sum(kept[lead, send], got[lead, send])


def core_sums(kept, got):
    leads, rows, columns = kept.shape[0], kept.shape[2], kept.shape[3]
    out = jax.ShapeDtypeStruct((leads, 4, rows, columns), jnp.bfloat16)
    return block_call(core_sums_kernel, [kept, got], [out, out], columns)


def place_kernel(leads, ordered, steps, *refs):
    pieces = refs[: len(steps)]
    outs = refs[len(steps) : len(steps) + leads]
    sems = refs[len(steps) + leads]
    spot = lax.axis_index("dp")
    z, y, core = spot // 4, spot // 2 % 2, spot % 2
    copies = []
    for piece, (first_slot, y_step, core_step) in zip(pieces, steps):
        column = (y + y_step) % 2 * 2 + (core + core_step) % 2
        for slot in range(piece.shape[0]):
            number = first_slot + slot
            row = (number if ordered else (z + 4 - number) % 4) * 4 + column
            for lead in range(leads):
                copy = pltpu.make_async_copy(piece.at[slot, lead], outs[lead].at[row], sems.at[len(copies)])
                copy.start()
                copies.append(copy)
    for copy in copies:
        copy.wait()


def place(planes, ordered):
    pieces = sum(planes, [])
    leads, rows, columns = pieces[0].shape[1:]
    slots = pieces[0].shape[0]
    steps = [(start, step % 2, step // 2) for start in range(0, 4, slots) for step in range(4)]
    size = 16 * leads * rows * padded(columns) * 2
    placed = pl.pallas_call(
        partial(place_kernel, leads, ordered, steps),
        in_specs=[pl.BlockSpec(memory_space=pl.ANY)] * len(pieces),
        out_specs=[pl.BlockSpec(memory_space=pltpu.VMEM)] * leads,
        out_shape=[jax.ShapeDtypeStruct((16, rows, columns), jnp.bfloat16)] * leads,
        scratch_shapes=[pltpu.SemaphoreType.DMA((16 * leads,))],
        compiler_params=pltpu.CompilerParams(vmem_limit_bytes=size * 3 // 2 + (2 << 20)),
        cost_estimate=pl.CostEstimate(flops=0, bytes_accessed=size // 4, transcendentals=0),
    )(*pieces)
    return [part.reshape(16 * rows, columns) for part in placed]


def swap_x(value):
    return lax.ppermute(value, "tensor", [(0, 1), (1, 0)])


def swap_y(value):
    return lax.ppermute(value, "dp", [(spot, spot ^ 2) for spot in range(16)])


def swap_core(value):
    return lax.ppermute(value, "dp", [(spot, spot ^ 1) for spot in range(16)])


def move_z(value, steps):
    return lax.ppermute(value, "dp", [(spot, (spot + 4 * steps) % 16) for spot in range(16)])


def tie(*values):
    return lax.optimization_barrier(values)


def gather_z(shard):
    groups = [[spot + 4 * z for z in range(4)] for spot in range(4)]
    return lax.all_gather(shard, "dp", axis_index_groups=groups)


def both_cores(parts):
    return parts + [swap_core(part) for part in parts]


def add_low(*terms):
    total = terms[0].astype(jnp.float32)
    for term in terms[1:]:
        total = total + term.astype(jnp.float32)
    return total.astype(jnp.bfloat16)


def part_of(value, index, axis):
    return lax.dynamic_index_in_dim(value, index, axis, keepdims=False)


def y_parts(value):
    spot = lax.axis_index("dp")
    split = value.reshape((value.shape[0] // 2, 2) + value.shape[1:])
    return part_of(split, spot // 2 % 2, 1), part_of(split, 1 - spot // 2 % 2, 1)


class Planes:
    def __init__(self, kept, core):
        rows, self.columns = kept[0].shape[1:]
        self.two, self.four = [jax.ShapeDtypeStruct((n, rows, self.columns), jnp.bfloat16) for n in (2, 4)]
        pair = jax.ShapeDtypeStruct((2, 2, rows, self.columns), jnp.bfloat16)
        self.near_own, self.near_other, self.far_own, *self.sent = block_call(
            first_sums_kernel, [*kept, *core], [self.two, self.two, self.four, pair, self.four], self.columns
        )

    def first(self):
        self.got = [swap_y(self.sent[0]), swap_x(self.sent[1])]

    def middle(self):
        self.near_own, self.far_own, *self.sent = block_call(
            middle_sums_kernel,
            [self.near_own, self.near_other, self.got[0], self.far_own, self.got[1]],
            [self.two] * 4,
            self.columns,
        )

    def second(self):
        self.got = [swap_x(self.sent[0]), swap_y(self.sent[1])]

    def total(self):
        return jnp.concatenate([add_low(self.near_own, self.got[0]), add_low(self.far_own, self.got[1])])


def scatter_z(value):
    groups = [[spot + 4 * z for z in range(4)] for spot in range(4)]
    return lax.psum_scatter(value, "dp", axis_index_groups=groups)


def send_z(value):
    z = lax.axis_index("dp") // 4
    return [part_of(value, z, 0)] + [move_z(part_of(value, (z + steps) % 4, 0), steps) for steps in (1, 2, 3)]


def sum_terms(terms):
    total = terms[0].astype(jnp.float32)
    for term in terms[1:]:
        total = total + term.astype(jnp.float32)
    return total


def norm_forward(values):
    centre = values - jnp.mean(values, -1, keepdims=True)
    inverse = lax.rsqrt(jnp.mean(centre * centre, -1, keepdims=True) + norm_eps)
    return centre * inverse, inverse


def norm_back(grad, hat, inverse, gain):
    scaled = grad * gain
    mean_one = jnp.mean(scaled, -1, keepdims=True)
    mean_two = jnp.mean(scaled * hat, -1, keepdims=True)
    return (scaled - mean_one - hat * mean_two) * inverse


def gelu_pair(value):
    inner = math.sqrt(2.0 / math.pi)
    squared = value * value
    bent = jnp.tanh(inner * (value + 0.044715 * value * squared))
    half = 0.5 * (1.0 + bent)
    slope = half + 0.5 * value * (1.0 - bent * bent) * inner * (1.0 + 3 * 0.044715 * squared)
    return value * half, slope


def row_layer(
    block_input,
    image_ids,
    out_cotangent,
    qkv_master,
    qkv_moment,
    qkv_second,
    out_master,
    out_moment,
    out_second,
    up_master,
    up_moment,
    up_second,
    down_master,
    down_moment,
    down_second,
    vec_master,
    vec_moment,
    vec_second,
    bias_master,
    bias_moment,
    bias_second,
):
    low = jnp.bfloat16
    wide = jnp.float32
    mine = lax.axis_index("tensor")
    first = mine == 0
    half = block_input.shape[2]
    features = block_input.shape[3]
    head_cols = qkv_master.shape[2]

    def pick(pair, index):
        return lax.dynamic_index_in_dim(pair, index, 0, keepdims=False)

    def in_order(own, other, axis=0):
        return jnp.concatenate([jnp.where(first, own, other), jnp.where(first, other, own)], axis)

    def dot(spec, left, right):
        return jnp.einsum(spec, left, right, preferred_element_type=wide)

    inputs_own = pick(block_input[:, 0], mine)
    inputs_sent = pick(block_input[:, 0], 1 - mine)
    cot_own = pick(out_cotangent[:, 0], mine)
    cot_sent = pick(out_cotangent[:, 0], 1 - mine)
    inputs_low = inputs_sent.astype(low)
    early_shard = jnp.stack([qkv_master[:, 0], qkv_master[:, 1], qkv_master[:, 2]]).astype(low)
    early_shard, inputs_low = tie(early_shard, inputs_low)
    inputs_got = swap_x(inputs_low)
    early_one = move_z(early_shard, 1)
    early_three = move_z(early_shard, 3)
    early_shard, early_one = tie(early_shard, early_one)
    early_two = move_z(early_shard, 2)
    near = jnp.stack([early_shard, early_one])
    near_y = swap_y(near)
    late_shard = jnp.stack([up_master, down_master.T]).astype(low)
    small = jnp.concatenate([pick(image_ids[:, 0], 1 - mine).astype(wide), bias_master[0]])
    cot_sum = jnp.sum(out_cotangent[:, 0], (0, 1))
    cot_low_sent = cot_sent.astype(low)
    late_shard, cot_sum, cot_low_sent, early_two, early_three, inputs_got, near, near_y = tie(
        late_shard, cot_sum, cot_low_sent, early_two, early_three, inputs_got, near, near_y
    )
    late_z = gather_z(late_shard)
    far = jnp.stack([early_two, early_three])
    far_y, near_x, far_x = swap_y(far), swap_x(near), swap_x(far)
    small, far_y = tie(small, far_y)
    small_got = swap_x(small[None])[0]
    near_xy, far_yx = swap_y(near_x), swap_x(far_y)
    early_own = place([both_cores([near, near_y]), both_cores([far, far_y])], False)
    out_shard, early_own = tie(out_master.T.astype(low), early_own)
    out_whole = lax.all_gather(out_shard, ("tensor", "dp")).reshape(2, features, head_cols)
    inputs = in_order(inputs_own, inputs_got.astype(wide))
    ids = in_order(pick(image_ids[:, 0], mine), small_got[:half].astype(jnp.int32))
    biases = jnp.stack([bias_master[0], small_got[half:]])

    hat_one, inverse_one = norm_forward(inputs)
    normed = (hat_one * vec_master[0] + vec_master[1]).astype(low)
    def project(g, weights):
        query = (dot("td,de->te", normed, weights[0]) + biases[g, :head_cols]).astype(low)
        key = dot("td,de->te", normed, weights[1]).astype(low)
        value = (dot("td,de->te", normed, weights[2]) + biases[g, head_cols : 2 * head_cols]).astype(low)
        return query, key, value

    projected = [project(0, early_own), None]
    projected[0], near_x, far_x = tie(projected[0], near_x, far_x)
    others = [[near_x, swap_core(near_x)], [far_x, swap_core(far_x)]]
    up_near, up_far = [late_z[start : start + 2, :1] for start in (0, 2)]
    attended, log_sums = [None, None], [None, None]
    attended[0], log_sums[0] = attend(ids, *projected[0])
    others, attended[0], near_xy, far_yx, up_near, up_far = tie(
        others, attended[0], near_xy, far_yx, up_near, up_far
    )
    up_near_x, up_far_y = swap_x(up_near), swap_y(up_far)
    others[0] = [others[0][0], near_xy, others[0][1], swap_core(near_xy)]
    others[1] = [others[1][0], far_yx, others[1][1], swap_core(far_yx)]
    early_other = place(others, False)
    down_near, down_far = [late_z[start : start + 2, 1:] for start in (0, 2)]
    projected[1] = project(1, early_other)
    query_weight, key_weight, value_weight = zip(early_own, early_other)
    projected[1], up_near, up_far, up_near_x, up_far_y = tie(projected[1], up_near, up_far, up_near_x, up_far_y)
    up_near_y, up_far_x = swap_y(up_near), swap_x(up_far)
    attended[1], log_sums[1] = attend(ids, *projected[1])
    attended[1], up_near_x, up_far_y, up_near_y, up_far_x = tie(
        attended[1], up_near_x, up_far_y, up_near_y, up_far_x
    )
    up_near_xy, up_far_yx = swap_y(up_near_x), swap_x(up_far_y)
    out_weight = [pick(out_whole, mine), pick(out_whole, 1 - mine)]
    out_weight, up_near_xy, up_far_yx, down_near, down_far = tie(
        out_weight, up_near_xy, up_far_yx, down_near, down_far
    )
    down_near_x, down_far_y = swap_x(down_near), swap_y(down_far)
    cot_got = swap_x(cot_low_sent)
    attn_sum = sum(dot("te,de->td", attended[g], out_weight[g]) for g in range(2)) + vec_master[2]
    middle = inputs + attn_sum
    hat_two, inverse_two = norm_forward(middle)
    normed_two = (hat_two * vec_master[3] + vec_master[4]).astype(low)
    up_weight = [
        place([both_cores([up_near, up_near_y]), both_cores([up_far, up_far_y])], True)[0],
        place([both_cores([up_near_x, up_near_xy]), both_cores([up_far_x, up_far_yx])], True)[0],
    ]
    active, slope = [None, None], [None, None]
    active[0], slope[0] = hidden_units(normed_two, up_weight[0], biases[0, 2 * head_cols :])
    normed_two, active[0], down_near, down_far, down_near_x, down_far_y, cot_got = tie(
        normed_two, active[0], down_near, down_far, down_near_x, down_far_y, cot_got
    )
    down_near_y, down_far_x = swap_y(down_near), swap_x(down_far)
    active[1], slope[1] = hidden_units(normed_two, up_weight[1], biases[1, 2 * head_cols :])
    active[1], down_near_x, down_far_y, down_near_y, down_far_x = tie(
        active[1], down_near_x, down_far_y, down_near_y, down_far_x
    )
    down_near_xy, down_far_yx = swap_y(down_near_x), swap_x(down_far_y)
    down_weight = [place([both_cores([down_near, down_near_y]), both_cores([down_far, down_far_y])], True)[0], None]
    active[1], down_weight[0] = tie(active[1], down_weight[0])
    cot_row = in_order(cot_own, cot_got.astype(wide))
    cot_low = cot_row.astype(low)
    down_sent, down_kept = weight_grads(cot_low, active)
    down_sent, down_near_xy, down_far_yx = tie(down_sent, down_near_xy, down_far_yx)
    down_weight[1] = place(
        [both_cores([down_near_x, down_near_xy]), both_cores([down_far_x, down_far_yx])], True
    )[0]
    added = attn_sum + sum(dot("tf,df->td", active[g], down_weight[g]) for g in range(2)) + vec_master[5]
    added = added.reshape(2, half, features)
    added_got = swap_x(pick(added, 1 - mine).astype(low))

    own, other = 0, 1
    down_core = [swap_core(part) for part in down_sent]
    d_hidden, hidden_sums = [None, None], [None, None]
    d_hidden[own], hidden_sums[own] = hidden_back(cot_low, down_weight[own], slope[own])
    d_hidden[own], down_core = tie(d_hidden[own], down_core)
    down = Planes(down_kept, down_core)
    cot_late, down.sent = tie(cot_low, down.sent)
    down.first()
    d_hidden[other], hidden_sums[other] = hidden_back(cot_late, down_weight[other], slope[other])
    up_sent, up_kept = weight_grads(normed_two, d_hidden)
    up_sent, down.got = tie(up_sent, down.got)
    up_core = [swap_core(part) for part in up_sent]
    down.middle()
    d_hidden, down.sent = tie(d_hidden, down.sent)
    down.second()
    d_normed_two = sum(dot("tf,df->td", d_hidden[g], up_weight[g]) for g in range(2))
    d_normed_two, up_core, down.got = tie(d_normed_two, up_core, down.got)
    up = Planes(up_kept, up_core)
    down_total = down.total()
    d_normed_two, up.sent, down_total = tie(d_normed_two, up.sent, down_total)
    up.first()
    down_term = scatter_z(down_total)
    mid_added = norm_back(d_normed_two, hat_two, inverse_two, vec_master[3])
    d_middle = cot_row + mid_added
    mid_low = d_middle.astype(low)
    d_attended = [dot("td,de->te", mid_low, out_weight[g]).astype(low) for g in range(2)]
    out_sent, out_kept = weight_grads(mid_low, attended)
    d_attended[other], out_sent, added_got = tie(d_attended[other], out_sent, added_got)
    out_core = [swap_core(part) for part in out_sent]

    def back(g, grad):
        return attend_back(ids, *projected[g], attended[g], grad, log_sums[g])

    d_other = back(other, d_attended[other])
    d_other, out_core, up.got = tie(d_other, out_core, up.got)
    up.middle()
    out_other = add_low(out_kept[other], out_core[other])
    out_own = add_low(out_kept[own], out_core[own])
    d_other, up.sent, out_other = tie(d_other, up.sent, out_other)
    up.second()
    out_there_x = swap_x(out_other)
    qkv_sent, qkv_kept = [None, None], [None, None]
    qkv_sent[other], qkv_kept[other] = weight_grads(normed, d_other, True)

    def normed_part(parts, g):
        weights = (query_weight, key_weight, value_weight)
        return sum(dot("te,de->td", part, weight[g]) for part, weight in zip(parts, weights))

    d_other, qkv_sent[other] = tie(d_other, qkv_sent[other])
    qkv_core_other = swap_core(qkv_sent[other])
    d_normed_other = normed_part(d_other, other)
    d_normed_other, up.got, qkv_core_other = tie(d_normed_other, up.got, qkv_core_other)
    up_total = up.total()
    qkv_other_here, qkv_other_there = core_sums(qkv_kept[other], qkv_core_other)
    d_attended[own], up_total, qkv_other_there = tie(d_attended[own], up_total, qkv_other_there)
    up_term = scatter_z(up_total)
    qkv_there_y = swap_y(qkv_other_there)
    d_own = back(own, d_attended[own])
    d_own, qkv_there_y, out_there_x = tie(tuple(d_own), qkv_there_y, out_there_x)
    qkv_other = add_low(qkv_other_here, qkv_there_y)
    out_here, out_there = y_parts(add_low(out_own, out_there_x))
    d_own, qkv_other, out_there = tie(d_own, qkv_other, out_there)
    qkv_there_x = swap_x(qkv_other)
    out_there_y = swap_y(out_there)
    qkv_sent[own], qkv_kept[own] = weight_grads(normed, d_own, True)
    d_own, qkv_sent[own], out_there_y = tie(d_own, qkv_sent[own], out_there_y)
    out_terms = send_z(add_low(out_here, out_there_y))
    qkv_core_own = swap_core(qkv_sent[own])
    d_normed_own = normed_part(d_own, own)
    d_normed_own, qkv_core_own, qkv_there_x = tie(d_normed_own, qkv_core_own, qkv_there_x)
    qkv_here, qkv_there = core_sums(qkv_kept[own], qkv_core_own)
    d_normed_own, qkv_there = tie(d_normed_own, qkv_there)
    qkv_there_y = swap_y(qkv_there)
    d_normed = d_normed_other + d_normed_own
    early = jnp.concatenate(
        [
            jnp.sum(d_middle, 0),
            jnp.sum(d_normed_two * hat_two, 0),
            jnp.sum(d_normed_two, 0),
            cot_sum,
        ]
    )

    def bias_rows(sums):
        return jnp.where(first, jnp.concatenate(sums), jnp.concatenate(sums[::-1]))

    sums = jnp.concatenate(
        [
            jnp.sum(d_normed * hat_one, 0),
            jnp.sum(d_normed, 0),
            early,
            bias_rows([jnp.sum(part[0], 0, dtype=wide) for part in (d_own, d_other)]),
            bias_rows([jnp.sum(part[2], 0, dtype=wide) for part in (d_own, d_other)]),
            bias_rows([part[0] for part in hidden_sums]),
        ]
    )
    in_added = (mid_added + norm_back(d_normed, hat_one, inverse_one, vec_master[0])).reshape(2, half, features)
    in_sent = pick(in_added, 1 - mine).astype(low)
    in_got = swap_x(in_sent)
    down_term, up_term, out_terms, added_got, in_sent = tie(down_term, up_term, out_terms, added_got, in_sent)
    block_here = inputs_own + pick(added, mine)
    block_there = pick(block_input[:, 0], 1 - mine) + added_got.astype(wide)
    block_output = in_order(block_here[None], block_there[None])[:, None]

    def update(name, grad):
        master, moment, second, rate, decay = states[name]
        second_new, master_new = adam_update(master, moment, second, grad, rate, decay)
        return grad, second_new, master_new

    states = {
        "qkv": (qkv_master, qkv_moment, qkv_second, 0.09, 0.1),
        "out": (out_master, out_moment, out_second, 0.4, 0.1),
        "up": (up_master, up_moment, up_second, 0.09, 0.1),
        "down": (down_master, down_moment, down_second, 0.045, 0.1),
        "vec": (vec_master, vec_moment, vec_second, 0.6, 0.0),
        "bias": (bias_master, bias_moment, bias_second, 0.5, 0.0),
    }
    up_new = update("up", up_term.astype(wide))
    down_new = update("down", down_term.astype(wide).T)
    out_new = update("out", sum_terms(out_terms).T)
    sums, qkv_there_y, block_output, up_new, down_new, out_new = tie(
        sums, qkv_there_y, block_output, up_new, down_new, out_new
    )
    qkv_terms = send_z(add_low(qkv_here, qkv_there_y, qkv_there_x).transpose(1, 0, 2, 3))
    sums = sums[None]
    sums = sums + move_z(sums, 1) + move_z(sums, 2) + move_z(sums, 3)
    sums, in_got = tie(sums, in_got)
    sums = sums + swap_core(sums)
    sums = sums + swap_y(sums)
    sums = (sums + swap_x(sums))[0]
    qkv_grad = sum_terms(qkv_terms).transpose(1, 0, 2)
    qkv_new = update("qkv", qkv_grad)
    grad_here = cot_own + pick(in_added, mine)
    grad_there = cot_sent + in_got.astype(wide)
    input_grad = in_order(grad_here[None], grad_there[None])[:, None]
    vec_grad = sums[: 6 * features].reshape(6, features)

    def group(start, size):
        return pick(sums[start : start + 2 * size].reshape(2, size), mine)

    start = 6 * features
    bias_grad = jnp.concatenate(
        [
            group(start, head_cols),
            group(start + 2 * head_cols, head_cols),
            group(start + 4 * head_cols, up_master.shape[1]),
        ]
    )[None]

    vec_new = update("vec", vec_grad)
    bias_new = update("bias", bias_grad)
    return (block_output, input_grad, *qkv_new, *out_new, *up_new, *down_new, *vec_new, *bias_new)


def solution(mesh):
    placed = (
        P(None, "dp", "tensor", None),
        P(None, "dp", "tensor"),
        P(None, "dp", "tensor", None),
        P("dp", None, "tensor"),
        P("dp", None, "tensor"),
        P("dp", None, "tensor"),
        P("tensor", "dp"),
        P("tensor", "dp"),
        P("tensor", "dp"),
        P("dp", "tensor"),
        P("dp", "tensor"),
        P("dp", "tensor"),
        P("tensor", "dp"),
        P("tensor", "dp"),
        P("tensor", "dp"),
        P(),
        P(),
        P(),
        P("tensor", None),
        P("tensor", None),
        P("tensor", None),
    )
    by_rows = dict(mesh.shape) == {"dp": 16, "tensor": 2}
    return jax.shard_map(
        row_layer if by_rows else split_layer,
        mesh=mesh,
        in_specs=placed,
        out_specs=(
            P(None, "dp", "tensor", None),
            P(None, "dp", "tensor", None),
            P("dp", None, "tensor"),
            P("dp", None, "tensor"),
            P("dp", None, "tensor"),
            P("tensor", "dp"),
            P("tensor", "dp"),
            P("tensor", "dp"),
            P("dp", "tensor"),
            P("dp", "tensor"),
            P("dp", "tensor"),
            P("tensor", "dp"),
            P("tensor", "dp"),
            P("tensor", "dp"),
            P(),
            P(),
            P(),
            P("tensor", None),
            P("tensor", None),
            P("tensor", None),
        ),
        check_vma=False,
    )
```

```python
import math
from functools import partial

import jax
import jax.numpy as jnp
from jax import lax
from jax.experimental import pallas as pl
from jax.experimental.pallas import tpu as pltpu
from jax.sharding import PartitionSpec as P

HEAD = 72
STEP = 10


norm_eps = 1e-06
mask_fill = -1e30
beta_one = 0.9
beta_two = 0.95
adam_eps = 1e-08


def layer_norm(values, scale_vec, shift_vec):
    centre = values - jnp.mean(values, -1, keepdims=True)
    spread = jnp.mean(centre * centre, -1, keepdims=True)
    return centre * lax.rsqrt(spread + norm_eps) * scale_vec + shift_vec


def adam_update(master, moment, second, gradient, step_rate, weight_decay):
    first_moment = beta_one * moment.astype(jnp.float32) + (1.0 - beta_one) * gradient
    second_new = beta_two * second + (1.0 - beta_two) * gradient * gradient
    update = (
        first_moment
        / (1.0 - beta_one**STEP)
        / (jnp.sqrt(second_new / (1.0 - beta_two**STEP)) + adam_eps)
        + weight_decay * master
    )
    return (second_new, master - step_rate * update)


def split_layer(
    block_input,
    image_ids,
    out_cotangent,
    qkv_master,
    qkv_moment,
    qkv_second,
    out_master,
    out_moment,
    out_second,
    up_master,
    up_moment,
    up_second,
    down_master,
    down_moment,
    down_second,
    vec_master,
    vec_moment,
    vec_second,
    bias_master,
    bias_moment,
    bias_second,
):
    batches = block_input.shape[0]
    local_rows = block_input.shape[2]
    features = block_input.shape[3]
    splits = lax.axis_size("tensor")
    length = local_rows * splits
    head_cols = qkv_master.shape[2]
    local_heads = head_cols // HEAD
    block_rows = min(512, length)
    block_count = length // block_rows
    score_scale = HEAD ** (-0.5)
    biases = bias_master[0]
    query_bias = biases[:head_cols]
    value_bias = biases[head_cols : 2 * head_cols]
    hidden_bias = biases[2 * head_cols :]
    compute = (
        qkv_master.astype(jnp.bfloat16),
        out_master.astype(jnp.bfloat16),
        up_master.astype(jnp.bfloat16),
        down_master.astype(jnp.bfloat16),
    )
    gelu_tanh = partial(jax.nn.gelu, approximate=True)
    weight_sums = (
        jnp.zeros_like(qkv_master),
        jnp.zeros_like(out_master),
        jnp.zeros_like(up_master),
        jnp.zeros_like(down_master),
    )
    vector_terms = jnp.zeros((6, features), jnp.float32)
    bias_terms = jnp.zeros(biases.shape, jnp.float32)
    block_outputs = []
    input_grads = []
    for batch_index in range(batches):
        qkv_weight, out_weight, up_weight, down_weight = (
            lax.all_gather(compute[0], "dp", axis=0, tiled=True),
            lax.all_gather(compute[1], "dp", axis=1, tiled=True),
            lax.all_gather(compute[2], "dp", axis=0, tiled=True),
            lax.all_gather(compute[3], "dp", axis=1, tiled=True),
        )
        tokens_here = block_input[batch_index, 0]
        normed, norm_pull = jax.vjp(layer_norm, tokens_here, vec_master[0], vec_master[1])
        gathered, image_row = (
            lax.all_gather(normed.astype(jnp.bfloat16), "tensor", axis=0, tiled=True),
            lax.all_gather(image_ids[batch_index, 0], "tensor", axis=0, tiled=True),
        )
        projected = jnp.einsum(
            "td,dce->cte", gathered, qkv_weight, preferred_element_type=jnp.float32
        )
        queries = (projected[0] + query_bias).astype(jnp.bfloat16)
        key_rows = projected[1].astype(jnp.bfloat16)
        values = (projected[2] + value_bias).astype(jnp.bfloat16)
        key_heads = key_rows.reshape(length, local_heads, HEAD)
        value_heads = values.reshape(length, local_heads, HEAD)
        query_blocks = queries.reshape(block_count, block_rows, local_heads, HEAD)
        image_blocks = image_row.reshape(block_count, block_rows)

        def attend(block_pair):
            query_block, image_block = block_pair
            scores = (
                jnp.einsum(
                    "qhe,khe->hqk", query_block, key_heads, preferred_element_type=jnp.float32
                )
                * score_scale
            )
            same_image = image_block[:, None] == image_row[None, :]
            scores = jnp.where(same_image[None], scores, mask_fill)
            row_max = jnp.max(scores, -1, keepdims=True)
            exp_scores = jnp.exp(scores - row_max)
            exp_total = jnp.sum(exp_scores, -1, keepdims=True)
            attn_probs = exp_scores / exp_total
            result = jnp.einsum(
                "hqk,khe->qhe",
                attn_probs.astype(jnp.bfloat16),
                value_heads,
                preferred_element_type=jnp.float32,
            )
            return (result.reshape(block_rows, head_cols), (row_max + jnp.log(exp_total))[..., 0])

        attended_blocks, log_sums = lax.map(attend, (query_blocks, image_blocks))
        attended = attended_blocks.reshape(length, head_cols).astype(jnp.bfloat16)
        attn_sum = lax.psum_scatter(
            jnp.dot(attended, out_weight, preferred_element_type=jnp.float32).astype(jnp.bfloat16),
            "tensor",
            scatter_dimension=0,
            tiled=True,
        ).astype(jnp.float32)
        middle = tokens_here + attn_sum + vec_master[2]
        normed_two, norm_pull_two = jax.vjp(layer_norm, middle, vec_master[3], vec_master[4])
        gathered_two = lax.all_gather(normed_two.astype(jnp.bfloat16), "tensor", axis=0, tiled=True)
        hidden = jnp.dot(gathered_two, up_weight, preferred_element_type=jnp.float32) + hidden_bias
        active, gelu_pull = jax.vjp(gelu_tanh, hidden)
        active_low = active.astype(jnp.bfloat16)
        project_row_piece = lax.slice_in_dim(
            active_low, 0, local_rows * lax.axis_size("tensor"), axis=0
        )
        mlp_sum = lax.psum_scatter(
            jnp.dot(project_row_piece, down_weight, preferred_element_type=jnp.float32).astype(
                jnp.bfloat16
            ),
            "tensor",
            scatter_dimension=0,
            tiled=True,
        ).astype(jnp.float32)
        block_outputs.append(middle + mlp_sum + vec_master[5])
        qkv_weight, out_weight, up_weight, down_weight = (
            lax.all_gather(compute[0], "dp", axis=0, tiled=True),
            lax.all_gather(compute[1], "dp", axis=1, tiled=True),
            lax.all_gather(compute[2], "dp", axis=0, tiled=True),
            lax.all_gather(compute[3], "dp", axis=1, tiled=True),
        )
        cotangent = out_cotangent[batch_index, 0]
        cot_full = lax.all_gather(cotangent.astype(jnp.bfloat16), "tensor", axis=0, tiled=True)
        down_term = jnp.dot(active_low.T, cot_full, preferred_element_type=jnp.float32)
        d_active = jnp.dot(cot_full, down_weight.T, preferred_element_type=jnp.float32)
        d_hidden = gelu_pull(d_active)[0].astype(jnp.bfloat16)
        up_term = jnp.dot(gathered_two.T, d_hidden, preferred_element_type=jnp.float32)
        d_normed_two = lax.psum_scatter(
            jnp.dot(d_hidden, up_weight.T, preferred_element_type=jnp.float32).astype(jnp.bfloat16),
            "tensor",
            scatter_dimension=0,
            tiled=True,
        ).astype(jnp.float32)
        d_middle, gain_two_grad, shift_two_grad = norm_pull_two(d_normed_two)
        d_middle = d_middle + cotangent
        mid_full = lax.all_gather(d_middle.astype(jnp.bfloat16), "tensor", axis=0, tiled=True)
        out_term = jnp.dot(attended.T, mid_full, preferred_element_type=jnp.float32)
        d_attended = jnp.dot(mid_full, out_weight.T, preferred_element_type=jnp.float32).astype(
            jnp.bfloat16
        )
        d_blocks = d_attended.reshape(block_count, block_rows, local_heads, HEAD)

        def attend_back(running, block_item):
            d_keys, d_values = running
            query_block, image_block, block_sums, d_block = block_item
            scores = (
                jnp.einsum(
                    "qhe,khe->hqk", query_block, key_heads, preferred_element_type=jnp.float32
                )
                * score_scale
            )
            same_image = image_block[:, None] == image_row[None, :]
            scores = jnp.where(same_image[None], scores, mask_fill)
            attn_probs = jnp.exp(scores - block_sums[:, :, None])
            d_probs = jnp.einsum(
                "qhe,khe->hqk", d_block, value_heads, preferred_element_type=jnp.float32
            )
            row_delta = jnp.sum(attn_probs * d_probs, -1, keepdims=True)
            d_scores = (attn_probs * (d_probs - row_delta)).astype(jnp.bfloat16)
            d_query = (
                jnp.einsum("hqk,khe->qhe", d_scores, key_heads, preferred_element_type=jnp.float32)
                * score_scale
            )
            d_keys = (
                d_keys
                + jnp.einsum(
                    "hqk,qhe->khe", d_scores, query_block, preferred_element_type=jnp.float32
                )
                * score_scale
            )
            d_values = d_values + jnp.einsum(
                "hqk,qhe->khe",
                attn_probs.astype(jnp.bfloat16),
                d_block,
                preferred_element_type=jnp.float32,
            )
            return ((d_keys, d_values), d_query)

        zero_heads = jnp.zeros((length, local_heads, HEAD), jnp.float32)
        (d_keys, d_values), d_queries = lax.scan(
            attend_back, (zero_heads, zero_heads), (query_blocks, image_blocks, log_sums, d_blocks)
        )
        d_query_low = d_queries.reshape(length, head_cols).astype(jnp.bfloat16)
        d_key_low = d_keys.reshape(length, head_cols).astype(jnp.bfloat16)
        d_value_low = d_values.reshape(length, head_cols).astype(jnp.bfloat16)
        d_projected = jnp.stack([d_query_low, d_key_low, d_value_low])
        qkv_term = jnp.einsum(
            "td,cte->dce", gathered, d_projected, preferred_element_type=jnp.float32
        )
        d_normed = lax.psum_scatter(
            jnp.einsum(
                "cte,dce->td", d_projected, qkv_weight, preferred_element_type=jnp.float32
            ).astype(jnp.bfloat16),
            "tensor",
            scatter_dimension=0,
            tiled=True,
        ).astype(jnp.float32)
        d_tokens, gain_one_grad, shift_one_grad = norm_pull(d_normed)
        input_grads.append(d_tokens + d_middle)
        vector_terms = vector_terms + jnp.stack(
            [
                gain_one_grad,
                shift_one_grad,
                jnp.sum(d_middle, 0),
                gain_two_grad,
                shift_two_grad,
                jnp.sum(cotangent, 0),
            ]
        )
        bias_terms = bias_terms + jnp.concatenate(
            [
                jnp.sum(d_query_low, 0, dtype=jnp.float32),
                jnp.sum(d_value_low, 0, dtype=jnp.float32),
                jnp.sum(d_hidden, 0, dtype=jnp.float32),
            ]
        )
        local_terms = (qkv_term, out_term, up_term, down_term)
        owned = (
            lax.psum_scatter(
                local_terms[0].astype(jnp.bfloat16), "dp", scatter_dimension=0, tiled=True
            ).astype(jnp.float32),
            lax.psum_scatter(
                local_terms[1].astype(jnp.bfloat16), "dp", scatter_dimension=1, tiled=True
            ).astype(jnp.float32),
            lax.psum_scatter(
                local_terms[2].astype(jnp.bfloat16), "dp", scatter_dimension=0, tiled=True
            ).astype(jnp.float32),
            lax.psum_scatter(
                local_terms[3].astype(jnp.bfloat16), "dp", scatter_dimension=1, tiled=True
            ).astype(jnp.float32),
        )
        weight_sums = tuple((total + term for total, term in zip(weight_sums, owned)))
    qkv_grad, out_grad, up_grad, down_grad = weight_sums
    tensor_index = lax.axis_index("tensor")
    placed = jnp.where(jnp.arange(splits)[:, None] == tensor_index, bias_terms[None, :], 0.0)
    vec_grad, bias_table = lax.psum((vector_terms, placed), ("dp", "tensor"))
    bias_grad = lax.dynamic_slice_in_dim(bias_table, tensor_index, 1, 0)
    qkv_second_new, qkv_master_new = adam_update(
        qkv_master, qkv_moment, qkv_second, qkv_grad, 0.09, 0.1
    )
    out_second_new, out_master_new = adam_update(
        out_master, out_moment, out_second, out_grad, 0.4, 0.1
    )
    up_second_new, up_master_new = adam_update(up_master, up_moment, up_second, up_grad, 0.09, 0.1)
    down_second_new, down_master_new = adam_update(
        down_master, down_moment, down_second, down_grad, 0.045, 0.1
    )
    vec_second_new, vec_master_new = adam_update(
        vec_master, vec_moment, vec_second, vec_grad, 0.6, 0.0
    )
    bias_second_new, bias_master_new = adam_update(
        bias_master, bias_moment, bias_second, bias_grad, 0.5, 0.0
    )
    block_output = jnp.stack(block_outputs)[:, None]
    input_grad = jnp.stack(input_grads)[:, None]
    return (
        block_output,
        input_grad,
        qkv_grad,
        qkv_second_new,
        qkv_master_new,
        out_grad,
        out_second_new,
        out_master_new,
        up_grad,
        up_second_new,
        up_master_new,
        down_grad,
        down_second_new,
        down_master_new,
        vec_grad,
        vec_second_new,
        vec_master_new,
        bias_grad,
        bias_second_new,
        bias_master_new,
    )


LANES = 128
TILE = 128
SPAN = 256
WIDE = 1152
BATCH = 8


def lane_window(head):
    first = head * HEAD
    low = first // LANES * LANES
    high = -(-(first + HEAD) // LANES) * LANES
    return low, high


def head_mask(head, rows):
    low, high = lane_window(head)
    lane = lax.broadcasted_iota(jnp.int32, (rows, high - low), 1) + low
    return (lane >= head * HEAD) & (lane < head * HEAD + HEAD)


def head_columns(head, columns):
    low, high = lane_window(head)
    high = min(high, columns)
    return slice(low, high), head_mask(head, TILE)[:, : high - low]


def padded(columns):
    return -(-columns // LANES) * LANES


def tile_spans(ids_smem, ids_ref, index, tiles):
    first_id = ids_smem[index * TILE]
    last_id = ids_smem[index * TILE + TILE - 1]
    ids = ids_ref[...]
    begin = jnp.sum((ids < first_id).astype(jnp.int32)) // TILE
    end = (jnp.sum((ids <= last_id).astype(jnp.int32)) + TILE - 1) // TILE
    count = (end - begin + 1) // 2
    return jnp.minimum(begin, tiles - 2 * count), count


def ids_column(ids_ref, index):
    row = ids_ref[:, pl.ds(pl.multiple_of(index * TILE, TILE), TILE)].astype(jnp.float32)
    square = jnp.broadcast_to(row, (TILE, TILE)).T
    return jnp.concatenate([square] * (SPAN // TILE), axis=1).astype(jnp.int32)


NT = (((1,), (1,)), ((), ()))
TN = (((0,), (0,)), ((), ()))


def attend_kernel(heads, length, ids_smem, ids_ref, q_ref, k_ref, v_ref, o_ref, lse_ref, top, total, acc):
    index = pl.program_id(0)
    columns = heads * HEAD
    scale = HEAD ** (-0.5) * math.log2(math.e)
    begin, count = tile_spans(ids_smem, ids_ref, index, length // TILE)
    own_ids = ids_column(ids_ref, index)
    top[...] = jnp.full(top.shape, mask_fill, jnp.float32)
    total[...] = jnp.zeros(total.shape, jnp.float32)
    acc[...] = jnp.zeros(acc.shape, jnp.float32)

    def window(low, high):
        return slice(low, min(high, columns))

    def step(item, carry):
        place = pl.multiple_of((begin + 2 * item) * TILE, TILE)
        keys = pl.ds(place, SPAN)
        same = own_ids == ids_ref[:, keys]
        for first in range(0, heads, BATCH):
            batch = range(first, min(first + BATCH, heads))
            held_scores = []
            for head in batch:
                cols, mask = head_columns(head, columns)
                query = q_ref[:, cols]
                query = jnp.where(mask, query, jnp.zeros_like(query))
                scores = lax.dot_general(query, k_ref[keys, cols], NT, preferred_element_type=jnp.float32)
                held_scores.append(jnp.where(same, scores * scale, mask_fill))
            tops = [jnp.maximum(top[head], jnp.max(scores, -1, keepdims=True)) for head, scores in zip(batch, held_scores)]
            parts = [
                jnp.exp2(scores - jnp.concatenate([now] * (SPAN // LANES), axis=1)) for now, scores in zip(tops, held_scores)
            ]
            sums = [jnp.sum(part, -1, keepdims=True) for part in parts]
            mixes = [
                jnp.dot(part.astype(jnp.bfloat16), v_ref[keys, head_columns(head, columns)[0]], preferred_element_type=jnp.float32)
                for head, part in zip(batch, parts)
            ]
            for head, now, part_sum, mixed in zip(batch, tops, sums, mixes):
                cols, mask = head_columns(head, columns)
                shrink = jnp.exp2(top[head] - now)
                total[head] = total[head] * shrink + part_sum
                top[head] = now
                width = cols.stop - cols.start
                wide = jnp.concatenate([shrink] * ((width + LANES - 1) // LANES), axis=1)[:, :width]
                held = acc[:, cols]
                acc[:, cols] = jnp.where(mask, held * wide + mixed, held)
        return carry

    lax.fori_loop(0, count, step, 0)
    sums = jnp.zeros((TILE, LANES), jnp.float32)
    lane = lax.broadcasted_iota(jnp.int32, (TILE, LANES), 1)
    for head in range(heads):
        low, high = lane_window(head)
        high = min(high, columns)
        cols = slice(low, high)
        mask = head_mask(head, TILE)[:, : high - low]
        inverse = 1.0 / total[head]
        wide = jnp.concatenate([inverse] * ((high - low + LANES - 1) // LANES), axis=1)[:, : high - low]
        held = acc[:, cols]
        acc[:, cols] = jnp.where(mask, held * wide, held)
        sums = jnp.where(lane == head, top[head] + jnp.log2(total[head]), sums)
    o_ref[...] = acc[...].astype(o_ref.dtype)
    lse_ref[...] = sums.T[:heads]


def attend(ids, query, key, value):
    length, columns = query.shape
    heads = columns // HEAD
    tiles = length // TILE
    whole = pl.BlockSpec((length, columns), lambda i, s: (0, 0))
    block = pl.BlockSpec((TILE, columns), lambda i, s: (i, 0))
    return pl.pallas_call(
        partial(attend_kernel, heads, length),
        grid_spec=pltpu.PrefetchScalarGridSpec(
            num_scalar_prefetch=1,
            grid=(tiles,),
            in_specs=[pl.BlockSpec((1, length), lambda i, s: (0, 0)), block, whole, whole],
            out_specs=[block, pl.BlockSpec((heads, TILE), lambda i, s: (0, i))],
            scratch_shapes=[
                pltpu.VMEM((heads, TILE, LANES), jnp.float32),
                pltpu.VMEM((heads, TILE, LANES), jnp.float32),
                pltpu.VMEM((TILE, columns), jnp.float32),
            ],
        ),
        out_shape=[
            jax.ShapeDtypeStruct((length, columns), jnp.bfloat16),
            jax.ShapeDtypeStruct((heads, length), jnp.float32),
        ],
        compiler_params=pltpu.CompilerParams(vmem_limit_bytes=36 << 20),
        cost_estimate=pl.CostEstimate(flops=4 * 10**9, bytes_accessed=10**6, transcendentals=0),
    )(ids, ids.reshape(1, length), query, key, value)


def attend_back_kernel(
    heads, length, ids_smem, ids_ref, q_ref, k_ref, v_ref, o_ref, g_ref, lse_ref,
    dq_ref, dk_ref, dv_ref, delta, dq_acc, dk_acc, dv_acc,
):
    index = pl.program_id(0)
    columns = heads * HEAD
    natural = HEAD ** (-0.5)
    scale = natural * math.log2(math.e)
    tiles = length // TILE
    begin, count = tile_spans(ids_smem, ids_ref, index, tiles)
    own_ids = ids_column(ids_ref, index)

    @pl.when(index == 0)
    def _():
        dq_acc[...] = jnp.zeros(dq_acc.shape, jnp.float32)
        row = lax.broadcasted_iota(jnp.int32, (heads, columns), 0)
        lane = lax.broadcasted_iota(jnp.int32, (heads, columns), 1)
        pick = ((lane >= row * HEAD) & (lane < row * HEAD + HEAD)).astype(jnp.bfloat16)
        product = g_ref[...].astype(jnp.float32) * o_ref[...].astype(jnp.float32)
        coarse = product.astype(jnp.bfloat16)
        fine = (product - coarse.astype(jnp.float32)).astype(jnp.bfloat16)
        delta[...] = lax.dot_general(pick, coarse, NT, preferred_element_type=jnp.float32) + lax.dot_general(
            pick, fine, NT, preferred_element_type=jnp.float32
        )

    dk_acc[...] = jnp.zeros(dk_acc.shape, jnp.float32)
    dv_acc[...] = jnp.zeros(dv_acc.shape, jnp.float32)

    def step(item, carry):
        place = pl.multiple_of((begin + 2 * item) * TILE, TILE)
        rows = pl.ds(place, SPAN)
        same = own_ids == ids_ref[:, rows]
        for first in range(0, heads, BATCH):
            batch = range(first, min(first + BATCH, heads))
            keys, scores, d_probs = [], [], []
            for head in batch:
                cols, mask = head_columns(head, columns)
                key = k_ref[:, cols]
                keys.append(jnp.where(mask, key, jnp.zeros_like(key)))
                value = v_ref[:, cols]
                value = jnp.where(mask, value, jnp.zeros_like(value))
                scores.append(lax.dot_general(keys[-1], q_ref[rows, cols], NT, preferred_element_type=jnp.float32))
                d_probs.append(lax.dot_general(value, g_ref[rows, cols], NT, preferred_element_type=jnp.float32))
            probs = [
                jnp.exp2(jnp.where(same, score * scale, mask_fill) - lse_ref[head : head + 1, rows])
                for head, score in zip(batch, scores)
            ]
            d_scores = [
                (prob * (d_prob - delta[head : head + 1, rows])).astype(jnp.bfloat16)
                for head, prob, d_prob in zip(batch, probs, d_probs)
            ]
            for head, key, prob, d_score in zip(batch, keys, probs, d_scores):
                cols, mask = head_columns(head, columns)
                d_value = jnp.dot(prob.astype(jnp.bfloat16), g_ref[rows, cols], preferred_element_type=jnp.float32)
                d_key = jnp.dot(d_score, q_ref[rows, cols], preferred_element_type=jnp.float32)
                d_query = lax.dot_general(d_score, key, TN, preferred_element_type=jnp.float32)
                dv_acc[:, cols] += jnp.where(mask, d_value, 0.0)
                dk_acc[:, cols] += jnp.where(mask, d_key, 0.0)
                dq_acc[rows, cols] += d_query
        return carry

    lax.fori_loop(0, count, step, 0)
    dk_ref[...] = (dk_acc[...] * natural).astype(dk_ref.dtype)
    dv_ref[...] = dv_acc[...].astype(dv_ref.dtype)

    @pl.when(index == tiles - 1)
    def _():
        dq_ref[...] = (dq_acc[...] * natural).astype(dq_ref.dtype)


def attend_back(ids, query, key, value, attended, grad, lse):
    length, columns = query.shape
    heads = columns // HEAD
    tiles = length // TILE
    whole = pl.BlockSpec((length, columns), lambda i, s: (0, 0))
    block = pl.BlockSpec((TILE, columns), lambda i, s: (i, 0))
    out = jax.ShapeDtypeStruct((length, columns), jnp.bfloat16)
    return pl.pallas_call(
        partial(attend_back_kernel, heads, length),
        grid_spec=pltpu.PrefetchScalarGridSpec(
            num_scalar_prefetch=1,
            grid=(tiles,),
            in_specs=[
                pl.BlockSpec((1, length), lambda i, s: (0, 0)),
                whole,
                block,
                block,
                whole,
                whole,
                pl.BlockSpec((heads, length), lambda i, s: (0, 0)),
            ],
            out_specs=[whole, block, block],
            scratch_shapes=[
                pltpu.VMEM((heads, length), jnp.float32),
                pltpu.VMEM((length, columns), jnp.float32),
                pltpu.VMEM((TILE, columns), jnp.float32),
                pltpu.VMEM((TILE, columns), jnp.float32),
            ],
        ),
        out_shape=[out, out, out],
        compiler_params=pltpu.CompilerParams(vmem_limit_bytes=36 << 20),
        cost_estimate=pl.CostEstimate(flops=2 * 10**9, bytes_accessed=10**6, transcendentals=0),
    )(ids, ids.reshape(1, length), query, key, value, attended, grad, lse)


def column_call(kernel, ins, outs, columns, flops, scratch=()):
    wide = min(WIDE, padded(columns))
    steps = -(-columns // wide)

    def spec(shape, cut):
        if cut:
            return pl.BlockSpec(shape[:-1] + (wide,), lambda i: (0,) * (len(shape) - 1) + (i,))
        return pl.BlockSpec(shape, lambda i: (0,) * len(shape))

    size = sum(math.prod(a.shape) * a.dtype.itemsize for a, _ in ins) + sum(
        math.prod(a.shape) * a.dtype.itemsize for a in outs
    )
    return pl.pallas_call(
        kernel,
        grid=(steps,),
        in_specs=[spec(a.shape, cut) for a, cut in ins],
        out_specs=[spec(a.shape, True) for a in outs],
        out_shape=outs,
        scratch_shapes=list(scratch),
        compiler_params=pltpu.CompilerParams(vmem_limit_bytes=44 << 20),
        cost_estimate=pl.CostEstimate(flops=flops // 8, bytes_accessed=size // 8, transcendentals=0),
    )(*[a for a, _ in ins])


def hidden_kernel(x_ref, w_ref, b_ref, active_ref, slope_ref):
    rows = 256
    for block in range(x_ref.shape[0] // rows):
        part = pl.ds(block * rows, rows)
        value = jnp.dot(x_ref[part, :], w_ref[...], preferred_element_type=jnp.float32) + b_ref[...]
        active, slope = gelu_pair(value)
        active_ref[part, :] = active.astype(jnp.bfloat16)
        slope_ref[part, :] = slope.astype(jnp.bfloat16)


def hidden_units(x, weight, bias):
    tokens, columns = x.shape[0], weight.shape[1]
    out = jax.ShapeDtypeStruct((tokens, columns), jnp.bfloat16)
    ins = [(x, False), (weight, True), (bias.reshape(1, columns), True)]
    return column_call(hidden_kernel, ins, [out, out], columns, 2 * tokens * x.shape[1] * columns)


def hidden_back_kernel(x_ref, w_ref, slope_ref, grad_ref, sum_ref):
    rows = 256
    total = jnp.zeros(sum_ref.shape, jnp.float32)
    for block in range(x_ref.shape[0] // rows):
        part = pl.ds(block * rows, rows)
        value = jnp.dot(x_ref[part, :], w_ref[...], preferred_element_type=jnp.float32)
        value = value * slope_ref[part, :].astype(jnp.float32)
        grad_ref[part, :] = value.astype(jnp.bfloat16)
        total = total + jnp.sum(value, 0, keepdims=True)
    sum_ref[...] = total


def hidden_back(x, weight, slope):
    tokens, columns = x.shape[0], weight.shape[1]
    outs = [jax.ShapeDtypeStruct((tokens, columns), jnp.bfloat16), jax.ShapeDtypeStruct((1, columns), jnp.float32)]
    ins = [(x, False), (weight, True), (slope, True)]
    return column_call(hidden_back_kernel, ins, outs, columns, 2 * tokens * x.shape[1] * columns)


def grad_kernel(chunks, stacked, x_ref, *refs):
    core = lax.axis_index("dp") % 2
    count = len(refs) - 4 if stacked else (len(refs) - 2) // 3
    turned, result = refs[-2:]
    dy_refs = refs[:count]
    outs = refs[count:-2]

    @pl.when(pl.program_id(0) == 0)
    def _():
        turned[...] = x_ref[...].T

    rows = turned.shape[0] // chunks
    for number, dy_ref in enumerate(dy_refs):
        if stacked:
            sent_ref, kept_ref = outs[0].at[number], outs[1].at[number]
        else:
            sent_ref, kept_ref = outs[number], outs[count + number]
        result[...] = jnp.dot(turned[...], dy_ref[...], preferred_element_type=jnp.float32)
        for spot in range(chunks // 2):
            sent = pl.multiple_of((2 * spot + 1 - core) * rows, 8)
            kept = pl.multiple_of((2 * spot + core) * rows, 8)
            sent_ref[spot] = result[pl.ds(sent, rows), :].astype(jnp.bfloat16)
            kept_ref[spot] = result[pl.ds(kept, rows), :].astype(jnp.bfloat16)


def weight_grads(x, parts, stacked=False):
    tokens, features = x.shape
    columns = parts[0].shape[1]
    count = len(parts)
    wide = min(WIDE, padded(columns))
    shape = (8, features // 16, columns)
    outs = [jax.ShapeDtypeStruct(shape, jnp.bfloat16)] * (2 * count)
    if stacked:
        outs = [jax.ShapeDtypeStruct((count,) + shape, jnp.bfloat16)] * 2
    results = column_call(
        partial(grad_kernel, 16, stacked),
        [(x, False)] + [(part, True) for part in parts],
        outs,
        columns,
        2 * tokens * features * columns * count,
        [pltpu.VMEM((features, tokens), jnp.bfloat16), pltpu.VMEM((features, wide), jnp.float32)],
    )
    return results if stacked else (results[:count], results[count:])


def block_call(kernel, ins, outs, columns):
    wide = min(768, padded(columns))

    def spec(shape):
        return pl.BlockSpec(shape[:-1] + (wide,), lambda i: (0,) * (len(shape) - 1) + (i,))

    size = sum(math.prod(a.shape) * 2 for a in list(ins) + list(outs))
    return pl.pallas_call(
        kernel,
        grid=(-(-columns // wide),),
        in_specs=[spec(a.shape) for a in ins],
        out_specs=[spec(a.shape) for a in outs],
        out_shape=outs,
        compiler_params=pltpu.CompilerParams(vmem_limit_bytes=58 << 20),
        cost_estimate=pl.CostEstimate(flops=0, bytes_accessed=size // 4, transcendentals=0),
    )(*ins)


def low_sum(*refs):
    total = refs[0].astype(jnp.float32)
    for ref in refs[1:]:
        total = total + ref.astype(jnp.float32)
    return total.astype(jnp.bfloat16)


def first_sums_kernel(kept_own, kept_other, core_own, core_other, near_own, near_other, far_own, near_sent, far_sent):
    y = lax.axis_index("dp") // 2 % 2
    for z in range(2):
        keep, send = 2 * z + y, 2 * z + 1 - y
        near_own[z] = low_sum(kept_own[keep], core_own[keep])
        near_other[z] = low_sum(kept_other[keep], core_other[keep])
        near_sent[0, z] = low_sum(kept_own[send], core_own[send])
        near_sent[1, z] = low_sum(kept_other[send], core_other[send])
    for spot in range(4):
        far_own[spot] = low_sum(kept_own[4 + spot], core_own[4 + spot])
        far_sent[spot] = low_sum(kept_other[4 + spot], core_other[4 + spot])


def middle_sums_kernel(near_own, near_other, near_got, far_own, far_got, own, far, near_sent, far_sent):
    y = lax.axis_index("dp") // 2 % 2
    for z in range(2):
        keep, send = 2 * z + y, 2 * z + 1 - y
        own[z] = low_sum(near_own[z], near_got[0, z])
        near_sent[z] = low_sum(near_other[z], near_got[1, z])
        far[z] = low_sum(far_own[keep], far_got[keep])
        far_sent[z] = low_sum(far_own[send], far_got[send])


def core_sums_kernel(kept, got, here, there):
    y = lax.axis_index("dp") // 2 % 2
    for lead in range(kept.shape[0]):
        for z in range(4):
            keep, send = 2 * z + y, 2 * z + 1 - y
            here[lead, z] = low_sum(kept[lead, keep], got[lead, keep])
            there[lead, z] = low_sum(kept[lead, send], got[lead, send])


def core_sums(kept, got):
    leads, rows, columns = kept.shape[0], kept.shape[2], kept.shape[3]
    out = jax.ShapeDtypeStruct((leads, 4, rows, columns), jnp.bfloat16)
    return block_call(core_sums_kernel, [kept, got], [out, out], columns)


def place_kernel(leads, ordered, steps, *refs):
    pieces = refs[: len(steps)]
    outs = refs[len(steps) : len(steps) + leads]
    sems = refs[len(steps) + leads]
    spot = lax.axis_index("dp")
    z, y, core = spot // 4, spot // 2 % 2, spot % 2
    copies = []
    for piece, (first_slot, y_step, core_step) in zip(pieces, steps):
        column = (y + y_step) % 2 * 2 + (core + core_step) % 2
        for slot in range(piece.shape[0]):
            number = first_slot + slot
            row = (number if ordered else (z + 4 - number) % 4) * 4 + column
            for lead in range(leads):
                copy = pltpu.make_async_copy(piece.at[slot, lead], outs[lead].at[row], sems.at[len(copies)])
                copy.start()
                copies.append(copy)
    for copy in copies:
        copy.wait()


def place(planes, ordered):
    pieces = sum(planes, [])
    leads, rows, columns = pieces[0].shape[1:]
    slots = pieces[0].shape[0]
    steps = [(start, step % 2, step // 2) for start in range(0, 4, slots) for step in range(4)]
    size = 16 * leads * rows * padded(columns) * 2
    placed = pl.pallas_call(
        partial(place_kernel, leads, ordered, steps),
        in_specs=[pl.BlockSpec(memory_space=pl.ANY)] * len(pieces),
        out_specs=[pl.BlockSpec(memory_space=pltpu.VMEM)] * leads,
        out_shape=[jax.ShapeDtypeStruct((16, rows, columns), jnp.bfloat16)] * leads,
        scratch_shapes=[pltpu.SemaphoreType.DMA((16 * leads,))],
        compiler_params=pltpu.CompilerParams(vmem_limit_bytes=size * 3 // 2 + (2 << 20)),
        cost_estimate=pl.CostEstimate(flops=0, bytes_accessed=size // 4, transcendentals=0),
    )(*pieces)
    return [part.reshape(16 * rows, columns) for part in placed]


def swap_x(value):
    return lax.ppermute(value, "tensor", [(0, 1), (1, 0)])


def swap_y(value):
    return lax.ppermute(value, "dp", [(spot, spot ^ 2) for spot in range(16)])


def swap_core(value):
    return lax.ppermute(value, "dp", [(spot, spot ^ 1) for spot in range(16)])


def move_z(value, steps):
    return lax.ppermute(value, "dp", [(spot, (spot + 4 * steps) % 16) for spot in range(16)])


def tie(*values):
    return lax.optimization_barrier(values)


def gather_z(shard):
    groups = [[spot + 4 * z for z in range(4)] for spot in range(4)]
    return lax.all_gather(shard, "dp", axis_index_groups=groups)


def both_cores(parts):
    return parts + [swap_core(part) for part in parts]


def add_low(*terms):
    total = terms[0].astype(jnp.float32)
    for term in terms[1:]:
        total = total + term.astype(jnp.float32)
    return total.astype(jnp.bfloat16)


def part_of(value, index, axis):
    return lax.dynamic_index_in_dim(value, index, axis, keepdims=False)


def y_parts(value):
    spot = lax.axis_index("dp")
    split = value.reshape((value.shape[0] // 2, 2) + value.shape[1:])
    return part_of(split, spot // 2 % 2, 1), part_of(split, 1 - spot // 2 % 2, 1)


class Planes:
    def __init__(self, kept, core):
        rows, self.columns = kept[0].shape[1:]
        self.two, self.four = [jax.ShapeDtypeStruct((n, rows, self.columns), jnp.bfloat16) for n in (2, 4)]
        pair = jax.ShapeDtypeStruct((2, 2, rows, self.columns), jnp.bfloat16)
        self.near_own, self.near_other, self.far_own, *self.sent = block_call(
            first_sums_kernel, [*kept, *core], [self.two, self.two, self.four, pair, self.four], self.columns
        )

    def first(self):
        self.got = [swap_y(self.sent[0]), swap_x(self.sent[1])]

    def middle(self):
        self.near_own, self.far_own, *self.sent = block_call(
            middle_sums_kernel,
            [self.near_own, self.near_other, self.got[0], self.far_own, self.got[1]],
            [self.two] * 4,
            self.columns,
        )

    def second(self):
        self.got = [swap_x(self.sent[0]), swap_y(self.sent[1])]

    def total(self):
        return jnp.concatenate([add_low(self.near_own, self.got[0]), add_low(self.far_own, self.got[1])])


def scatter_z(value):
    groups = [[spot + 4 * z for z in range(4)] for spot in range(4)]
    return lax.psum_scatter(value, "dp", axis_index_groups=groups)


def send_z(value):
    z = lax.axis_index("dp") // 4
    return [part_of(value, z, 0)] + [move_z(part_of(value, (z + steps) % 4, 0), steps) for steps in (1, 2, 3)]


def sum_terms(terms):
    total = terms[0].astype(jnp.float32)
    for term in terms[1:]:
        total = total + term.astype(jnp.float32)
    return total


def norm_forward(values):
    centre = values - jnp.mean(values, -1, keepdims=True)
    inverse = lax.rsqrt(jnp.mean(centre * centre, -1, keepdims=True) + norm_eps)
    return centre * inverse, inverse


def norm_back(grad, hat, inverse, gain):
    scaled = grad * gain
    mean_one = jnp.mean(scaled, -1, keepdims=True)
    mean_two = jnp.mean(scaled * hat, -1, keepdims=True)
    return (scaled - mean_one - hat * mean_two) * inverse


def gelu_pair(value):
    inner = math.sqrt(2.0 / math.pi)
    squared = value * value
    bent = jnp.tanh(inner * (value + 0.044715 * value * squared))
    half = 0.5 * (1.0 + bent)
    slope = half + 0.5 * value * (1.0 - bent * bent) * inner * (1.0 + 3 * 0.044715 * squared)
    return value * half, slope


def row_layer(
    block_input,
    image_ids,
    out_cotangent,
    qkv_master,
    qkv_moment,
    qkv_second,
    out_master,
    out_moment,
    out_second,
    up_master,
    up_moment,
    up_second,
    down_master,
    down_moment,
    down_second,
    vec_master,
    vec_moment,
    vec_second,
    bias_master,
    bias_moment,
    bias_second,
):
    low = jnp.bfloat16
    wide = jnp.float32
    mine = lax.axis_index("tensor")
    first = mine == 0
    half = block_input.shape[2]
    features = block_input.shape[3]
    head_cols = qkv_master.shape[2]

    def pick(pair, index):
        return lax.dynamic_index_in_dim(pair, index, 0, keepdims=False)

    def in_order(own, other, axis=0):
        return jnp.concatenate([jnp.where(first, own, other), jnp.where(first, other, own)], axis)

    def dot(spec, left, right):
        return jnp.einsum(spec, left, right, preferred_element_type=wide)

    inputs_own = pick(block_input[:, 0], mine)
    inputs_sent = pick(block_input[:, 0], 1 - mine)
    cot_own = pick(out_cotangent[:, 0], mine)
    cot_sent = pick(out_cotangent[:, 0], 1 - mine)
    inputs_low = inputs_sent.astype(low)
    early_shard = jnp.stack([qkv_master[:, 0], qkv_master[:, 1], qkv_master[:, 2]]).astype(low)
    early_shard, inputs_low = tie(early_shard, inputs_low)
    inputs_got = swap_x(inputs_low)
    early_one = move_z(early_shard, 1)
    early_three = move_z(early_shard, 3)
    early_shard, early_one = tie(early_shard, early_one)
    early_two = move_z(early_shard, 2)
    near = jnp.stack([early_shard, early_one])
    near_y = swap_y(near)
    late_shard = jnp.stack([up_master, down_master.T]).astype(low)
    small = jnp.concatenate([pick(image_ids[:, 0], 1 - mine).astype(wide), bias_master[0]])
    cot_sum = jnp.sum(out_cotangent[:, 0], (0, 1))
    cot_low_sent = cot_sent.astype(low)
    late_shard, cot_sum, cot_low_sent, early_two, early_three, inputs_got, near, near_y = tie(
        late_shard, cot_sum, cot_low_sent, early_two, early_three, inputs_got, near, near_y
    )
    late_z = gather_z(late_shard)
    far = jnp.stack([early_two, early_three])
    far_y, near_x, far_x = swap_y(far), swap_x(near), swap_x(far)
    small, far_y = tie(small, far_y)
    small_got = swap_x(small[None])[0]
    near_xy, far_yx = swap_y(near_x), swap_x(far_y)
    early_own = place([both_cores([near, near_y]), both_cores([far, far_y])], False)
    out_shard, early_own = tie(out_master.T.astype(low), early_own)
    out_whole = lax.all_gather(out_shard, ("tensor", "dp")).reshape(2, features, head_cols)
    inputs = in_order(inputs_own, inputs_got.astype(wide))
    ids = in_order(pick(image_ids[:, 0], mine), small_got[:half].astype(jnp.int32))
    biases = jnp.stack([bias_master[0], small_got[half:]])

    hat_one, inverse_one = norm_forward(inputs)
    normed = (hat_one * vec_master[0] + vec_master[1]).astype(low)
    def project(g, weights):
        query = (dot("td,de->te", normed, weights[0]) + biases[g, :head_cols]).astype(low)
        key = dot("td,de->te", normed, weights[1]).astype(low)
        value = (dot("td,de->te", normed, weights[2]) + biases[g, head_cols : 2 * head_cols]).astype(low)
        return query, key, value

    projected = [project(0, early_own), None]
    projected[0], near_x, far_x = tie(projected[0], near_x, far_x)
    others = [[near_x, swap_core(near_x)], [far_x, swap_core(far_x)]]
    up_near, up_far = [late_z[start : start + 2, :1] for start in (0, 2)]
    attended, log_sums = [None, None], [None, None]
    attended[0], log_sums[0] = attend(ids, *projected[0])
    others, attended[0], near_xy, far_yx, up_near, up_far = tie(
        others, attended[0], near_xy, far_yx, up_near, up_far
    )
    up_near_x, up_far_y = swap_x(up_near), swap_y(up_far)
    others[0] = [others[0][0], near_xy, others[0][1], swap_core(near_xy)]
    others[1] = [others[1][0], far_yx, others[1][1], swap_core(far_yx)]
    early_other = place(others, False)
    down_near, down_far = [late_z[start : start + 2, 1:] for start in (0, 2)]
    projected[1] = project(1, early_other)
    query_weight, key_weight, value_weight = zip(early_own, early_other)
    projected[1], up_near, up_far, up_near_x, up_far_y = tie(projected[1], up_near, up_far, up_near_x, up_far_y)
    up_near_y, up_far_x = swap_y(up_near), swap_x(up_far)
    attended[1], log_sums[1] = attend(ids, *projected[1])
    attended[1], up_near_x, up_far_y, up_near_y, up_far_x = tie(
        attended[1], up_near_x, up_far_y, up_near_y, up_far_x
    )
    up_near_xy, up_far_yx = swap_y(up_near_x), swap_x(up_far_y)
    out_weight = [pick(out_whole, mine), pick(out_whole, 1 - mine)]
    out_weight, up_near_xy, up_far_yx, down_near, down_far = tie(
        out_weight, up_near_xy, up_far_yx, down_near, down_far
    )
    down_near_x, down_far_y = swap_x(down_near), swap_y(down_far)
    cot_got = swap_x(cot_low_sent)
    attn_sum = sum(dot("te,de->td", attended[g], out_weight[g]) for g in range(2)) + vec_master[2]
    middle = inputs + attn_sum
    hat_two, inverse_two = norm_forward(middle)
    normed_two = (hat_two * vec_master[3] + vec_master[4]).astype(low)
    up_weight = [
        place([both_cores([up_near, up_near_y]), both_cores([up_far, up_far_y])], True)[0],
        place([both_cores([up_near_x, up_near_xy]), both_cores([up_far_x, up_far_yx])], True)[0],
    ]
    normed_two, up_weight = tie(normed_two, up_weight)
    active, slope = [None, None], [None, None]
    active[0], slope[0] = hidden_units(normed_two, up_weight[0], biases[0, 2 * head_cols :])
    normed_two, active[0], down_near, down_far, down_near_x, down_far_y, cot_got = tie(
        normed_two, active[0], down_near, down_far, down_near_x, down_far_y, cot_got
    )
    down_near_y, down_far_x = swap_y(down_near), swap_x(down_far)
    active[1], slope[1] = hidden_units(normed_two, up_weight[1], biases[1, 2 * head_cols :])
    active[1], down_near_x, down_far_y, down_near_y, down_far_x = tie(
        active[1], down_near_x, down_far_y, down_near_y, down_far_x
    )
    down_near_xy, down_far_yx = swap_y(down_near_x), swap_x(down_far_y)
    down_weight = [place([both_cores([down_near, down_near_y]), both_cores([down_far, down_far_y])], True)[0], None]
    active[1], down_weight[0] = tie(active[1], down_weight[0])
    cot_row = in_order(cot_own, cot_got.astype(wide))
    cot_low = cot_row.astype(low)
    down_sent, down_kept = weight_grads(cot_low, active)
    down_sent, down_near_xy, down_far_yx = tie(down_sent, down_near_xy, down_far_yx)
    down_weight[1] = place(
        [both_cores([down_near_x, down_near_xy]), both_cores([down_far_x, down_far_yx])], True
    )[0]
    added = attn_sum + sum(dot("tf,df->td", active[g], down_weight[g]) for g in range(2)) + vec_master[5]
    added = added.reshape(2, half, features)
    added_got = swap_x(pick(added, 1 - mine).astype(low))

    own, other = 0, 1
    down_core = [swap_core(part) for part in down_sent]
    d_hidden, hidden_sums = [None, None], [None, None]
    d_hidden[own], hidden_sums[own] = hidden_back(cot_low, down_weight[own], slope[own])
    d_hidden[own], down_core = tie(d_hidden[own], down_core)
    down = Planes(down_kept, down_core)
    cot_late, down.sent = tie(cot_low, down.sent)
    down.first()
    d_hidden[other], hidden_sums[other] = hidden_back(cot_late, down_weight[other], slope[other])
    up_sent, up_kept = weight_grads(normed_two, d_hidden)
    up_sent, down.got = tie(up_sent, down.got)
    up_core = [swap_core(part) for part in up_sent]
    down.middle()
    d_hidden, down.sent = tie(d_hidden, down.sent)
    down.second()
    d_normed_two = sum(dot("tf,df->td", d_hidden[g], up_weight[g]) for g in range(2))
    d_normed_two, up_core, down.got = tie(d_normed_two, up_core, down.got)
    up = Planes(up_kept, up_core)
    down_total = down.total()
    d_normed_two, up.sent, down_total = tie(d_normed_two, up.sent, down_total)
    up.first()
    down_term = scatter_z(down_total)
    mid_added = norm_back(d_normed_two, hat_two, inverse_two, vec_master[3])
    d_middle = cot_row + mid_added
    mid_low = d_middle.astype(low)
    d_attended = [dot("td,de->te", mid_low, out_weight[g]).astype(low) for g in range(2)]
    out_sent, out_kept = weight_grads(mid_low, attended)
    d_attended[other], out_sent, added_got = tie(d_attended[other], out_sent, added_got)
    out_core = [swap_core(part) for part in out_sent]

    def back(g, grad):
        return attend_back(ids, *projected[g], attended[g], grad, log_sums[g])

    d_other = back(other, d_attended[other])
    d_other, out_core, up.got = tie(d_other, out_core, up.got)
    up.middle()
    out_other = add_low(out_kept[other], out_core[other])
    out_own = add_low(out_kept[own], out_core[own])
    d_other, up.sent, out_other = tie(d_other, up.sent, out_other)
    up.second()
    out_there_x = swap_x(out_other)
    qkv_sent, qkv_kept = [None, None], [None, None]
    qkv_sent[other], qkv_kept[other] = weight_grads(normed, d_other, True)

    def normed_part(parts, g):
        weights = (query_weight, key_weight, value_weight)
        return sum(dot("te,de->td", part, weight[g]) for part, weight in zip(parts, weights))

    d_other, qkv_sent[other] = tie(d_other, qkv_sent[other])
    qkv_core_other = swap_core(qkv_sent[other])
    d_normed_other = normed_part(d_other, other)
    d_normed_other, up.got, qkv_core_other = tie(d_normed_other, up.got, qkv_core_other)
    up_total = up.total()
    qkv_other_here, qkv_other_there = core_sums(qkv_kept[other], qkv_core_other)
    d_attended[own], up_total, qkv_other_there = tie(d_attended[own], up_total, qkv_other_there)
    up_term = scatter_z(up_total)
    qkv_there_y = swap_y(qkv_other_there)
    d_own = back(own, d_attended[own])
    d_own, qkv_there_y, out_there_x = tie(tuple(d_own), qkv_there_y, out_there_x)
    qkv_other = add_low(qkv_other_here, qkv_there_y)
    out_here, out_there = y_parts(add_low(out_own, out_there_x))
    d_own, qkv_other, out_there = tie(d_own, qkv_other, out_there)
    qkv_there_x = swap_x(qkv_other)
    out_there_y = swap_y(out_there)
    qkv_sent[own], qkv_kept[own] = weight_grads(normed, d_own, True)
    d_own, qkv_sent[own], out_there_y = tie(d_own, qkv_sent[own], out_there_y)
    out_terms = send_z(add_low(out_here, out_there_y))
    qkv_core_own = swap_core(qkv_sent[own])
    d_normed_own = normed_part(d_own, own)
    d_normed_own, qkv_core_own, qkv_there_x = tie(d_normed_own, qkv_core_own, qkv_there_x)
    qkv_here, qkv_there = core_sums(qkv_kept[own], qkv_core_own)
    d_normed_own, qkv_there = tie(d_normed_own, qkv_there)
    qkv_there_y = swap_y(qkv_there)
    d_normed = d_normed_other + d_normed_own
    early = jnp.concatenate(
        [
            jnp.sum(d_middle, 0),
            jnp.sum(d_normed_two * hat_two, 0),
            jnp.sum(d_normed_two, 0),
            cot_sum,
        ]
    )

    def bias_rows(sums):
        return jnp.where(first, jnp.concatenate(sums), jnp.concatenate(sums[::-1]))

    sums = jnp.concatenate(
        [
            jnp.sum(d_normed * hat_one, 0),
            jnp.sum(d_normed, 0),
            early,
            bias_rows([jnp.sum(part[0], 0, dtype=wide) for part in (d_own, d_other)]),
            bias_rows([jnp.sum(part[2], 0, dtype=wide) for part in (d_own, d_other)]),
            bias_rows([part[0] for part in hidden_sums]),
        ]
    )
    in_added = (mid_added + norm_back(d_normed, hat_one, inverse_one, vec_master[0])).reshape(2, half, features)
    in_sent = pick(in_added, 1 - mine).astype(low)
    in_got = swap_x(in_sent)
    down_term, up_term, out_terms, added_got, in_sent = tie(down_term, up_term, out_terms, added_got, in_sent)
    block_here = inputs_own + pick(added, mine)
    block_there = pick(block_input[:, 0], 1 - mine) + added_got.astype(wide)
    block_output = in_order(block_here[None], block_there[None])[:, None]

    def update(name, grad):
        master, moment, second, rate, decay = states[name]
        second_new, master_new = adam_update(master, moment, second, grad, rate, decay)
        return grad, second_new, master_new

    states = {
        "qkv": (qkv_master, qkv_moment, qkv_second, 0.09, 0.1),
        "out": (out_master, out_moment, out_second, 0.4, 0.1),
        "up": (up_master, up_moment, up_second, 0.09, 0.1),
        "down": (down_master, down_moment, down_second, 0.045, 0.1),
        "vec": (vec_master, vec_moment, vec_second, 0.6, 0.0),
        "bias": (bias_master, bias_moment, bias_second, 0.5, 0.0),
    }
    up_new = update("up", up_term.astype(wide))
    down_new = update("down", down_term.astype(wide).T)
    out_new = update("out", sum_terms(out_terms).T)
    sums, qkv_there_y, block_output, up_new, down_new, out_new = tie(
        sums, qkv_there_y, block_output, up_new, down_new, out_new
    )
    qkv_terms = send_z(add_low(qkv_here, qkv_there_y, qkv_there_x).transpose(1, 0, 2, 3))
    sums = sums[None]
    sums = sums + move_z(sums, 1) + move_z(sums, 2) + move_z(sums, 3)
    sums, in_got = tie(sums, in_got)
    sums = sums + swap_core(sums)
    sums = sums + swap_y(sums)
    sums = (sums + swap_x(sums))[0]
    qkv_grad = sum_terms(qkv_terms).transpose(1, 0, 2)
    qkv_new = update("qkv", qkv_grad)
    grad_here = cot_own + pick(in_added, mine)
    grad_there = cot_sent + in_got.astype(wide)
    input_grad = in_order(grad_here[None], grad_there[None])[:, None]
    vec_grad = sums[: 6 * features].reshape(6, features)

    def group(start, size):
        return pick(sums[start : start + 2 * size].reshape(2, size), mine)

    start = 6 * features
    bias_grad = jnp.concatenate(
        [
            group(start, head_cols),
            group(start + 2 * head_cols, head_cols),
            group(start + 4 * head_cols, up_master.shape[1]),
        ]
    )[None]

    vec_new = update("vec", vec_grad)
    bias_new = update("bias", bias_grad)
    return (block_output, input_grad, *qkv_new, *out_new, *up_new, *down_new, *vec_new, *bias_new)


def solution(mesh):
    placed = (
        P(None, "dp", "tensor", None),
        P(None, "dp", "tensor"),
        P(None, "dp", "tensor", None),
        P("dp", None, "tensor"),
        P("dp", None, "tensor"),
        P("dp", None, "tensor"),
        P("tensor", "dp"),
        P("tensor", "dp"),
        P("tensor", "dp"),
        P("dp", "tensor"),
        P("dp", "tensor"),
        P("dp", "tensor"),
        P("tensor", "dp"),
        P("tensor", "dp"),
        P("tensor", "dp"),
        P(),
        P(),
        P(),
        P("tensor", None),
        P("tensor", None),
        P("tensor", None),
    )
    by_rows = dict(mesh.shape) == {"dp": 16, "tensor": 2}
    return jax.shard_map(
        row_layer if by_rows else split_layer,
        mesh=mesh,
        in_specs=placed,
        out_specs=(
            P(None, "dp", "tensor", None),
            P(None, "dp", "tensor", None),
            P("dp", None, "tensor"),
            P("dp", None, "tensor"),
            P("dp", None, "tensor"),
            P("tensor", "dp"),
            P("tensor", "dp"),
            P("tensor", "dp"),
            P("dp", "tensor"),
            P("dp", "tensor"),
            P("dp", "tensor"),
            P("tensor", "dp"),
            P("tensor", "dp"),
            P("tensor", "dp"),
            P(),
            P(),
            P(),
            P("tensor", None),
            P("tensor", None),
            P("tensor", None),
        ),
        check_vma=False,
    )
```
